32 devices in a mesh: mid: 8 (over z, y), off: 4 (over x, core).
Axes of the slice: x: 2, y: 2, z: 4, core: 2. Of those that a mesh axis runs over, the one named last changes fastest.
Arguments:
- traces: bfloat16 [4096, 512], P(('mid', 'off')), may hold values from -16 to 16
- kernels: bfloat16 [8, 512, 512], replicated, may hold values from -0.25 to 0.25
- send_list: int32 [8, 4, 4], P('mid'), may hold values from 0 to 7, as said below
- aper_slot: int32 [8, 4096], P(None, ('mid', 'off')), may hold values from 0 to 23, as said below
- aper_pattern: int32 [8, 4096], P(None, ('mid', 'off')), may hold values from 0 to 7
- trace_bin: int32 [4096], P(('mid', 'off')), may hold values from 0 to 15
- trace_count: int32 [4096], P(('mid', 'off')), may hold values from 5 to 8, as said below
Outputs:
- solution: float32 [64, 64, 512], P('mid', 'off')
- residual: float32 [64, 64, 512], P('mid', 'off')
The draws below stay inside these ranges and needn't reach their ends.
Inputs may be any that keep to these rules, and one draw needn't show every extreme that they name: Each row send_list[i, k, :] holds 4 different cells of tile i. `aper_slot`: with r = j % 5, entry j of every list names one of the 8 own cells of the trace's tile when r == 0, and otherwise one of slots 8 + (r - 1) * 4 to 8 + r * 4 - 1, the cells that arrive from direction r - 1. Only the first trace_count[t] entries of a list are live.
All inputs are finite; a program needn't handle non-finite values.
Results may differ from the reference program's by a relative error of at most 0.015.
Values may be sent and summed in bfloat16 or wider, within the bound.
No kernel may reach another device: no remote copies, remote signals or barrier semaphores. Data moves between devices by JAX's collectives and lax.ppermute only.
A program may use at most 64 MiB of HBM per device.

```python
import jax
import jax.numpy as jnp
from jax import lax

NT = 512
NOFF = 64
PATTERNS = 8
REACH = 2
APER = 8
ITERS = 2
CELLS = 8
SEND = 4
TR_DEV = 128
TILES = 8
OFF_DEV = 16
TRACES = 4096
DIRS = 4
SLOTS = 24
N_MID = 8
N_OFF = 4


def draw_traces(key, part):
    key = jax.random.fold_in(key, 11)
    rising = jnp.arange(TRACES, dtype=jnp.float32) / (TRACES - 1)
    values = jnp.clip(jax.random.normal(key, (TRACES, NT), jnp.float32), -4.0, 4.0)
    row_scale = 1.0 + 2.0 * rising
    return (values * row_scale[:, None]).astype(jnp.bfloat16)


def draw_send_list(key, part):
    key = jax.random.fold_in(key, 12)
    scores = jax.random.randint(key, (TILES, DIRS, CELLS), 0, 1 << 20) * CELLS + jnp.arange(CELLS, dtype=jnp.int32)
    return jnp.argsort(scores, axis=-1)[:, :, :SEND].astype(jnp.int32)


def draw_aper_slot(key, part):
    key = jax.random.fold_in(key, 13)
    region = jnp.arange(APER, dtype=jnp.int32) % (DIRS + 1)
    region_base = jnp.where(region == 0, 0, CELLS + (region - 1) * SEND)
    region_size = jnp.where(region == 0, CELLS, SEND)
    random_bits = jax.random.randint(key, (APER, TRACES), 0, 1 << 20)
    slot_ids = region_base[:, None] + random_bits % region_size[:, None]
    slot_ids = slot_ids.at[0, 0].set(0).at[DIRS, 0].set(SLOTS - 1)
    return slot_ids.astype(jnp.int32)


def draw_trace_count(key, part):
    key = jax.random.fold_in(key, 14)
    groups = NOFF // OFF_DEV
    trace_ids = jnp.arange(TRACES, dtype=jnp.int32)
    upper_half = trace_ids // TR_DEV % groups >= groups // 2
    flipped = jax.random.randint(key, (TRACES,), 0, 8) == 0
    fewest = 2 * REACH + 1
    lower_counts = jnp.where(flipped, fewest + 1, fewest)
    upper_counts = jnp.where(flipped, max(APER - 1, fewest), APER)
    counts = jnp.where(upper_half, upper_counts, lower_counts)
    counts = counts.at[0].set(fewest).at[TRACES - 1].set(APER)
    return counts.astype(jnp.int32)


def touch_ends(drawn, rng, least, high):
    place = [jax.random.randint(jax.random.fold_in(rng, axis), (), 0, length) for axis, length in enumerate(drawn.shape)]
    widest = drawn.shape.index(max(drawn.shape))
    neighbour = place[:widest] + [(place[widest] + 1) % drawn.shape[widest]] + place[widest + 1:]
    return drawn.at[tuple(place)].set(least).at[tuple(neighbour)].set(high)


def bell_draw(key, shape, scale, limit, kind=jnp.bfloat16):
    values = jax.random.normal(key, shape, jnp.float32) * scale
    return jnp.minimum(jnp.maximum(values, -limit), limit).astype(kind)


def setup_inputs(seed: int = 0) -> dict:
    arg_keys = jax.random.split(jax.random.key(seed), 8)
    return {
        "traces": draw_traces(jax.random.fold_in(arg_keys[7], 71), 0),
        "kernels": bell_draw(arg_keys[1], (PATTERNS, NT, NT), NT ** -0.5, 0.25),
        "send_list": draw_send_list(jax.random.fold_in(arg_keys[7], 71), 0),
        "aper_slot": draw_aper_slot(jax.random.fold_in(arg_keys[7], 71), 0),
        "aper_pattern": touch_ends(jax.random.randint(arg_keys[4], (APER, TRACES), 0, PATTERNS), jax.random.fold_in(arg_keys[4], 1), 0, PATTERNS - 1).astype(jnp.int32),
        "trace_bin": touch_ends(jax.random.randint(arg_keys[5], (TRACES,), 0, OFF_DEV), jax.random.fold_in(arg_keys[5], 1), 0, OFF_DEV - 1).astype(jnp.int32),
        "trace_count": draw_trace_count(jax.random.fold_in(arg_keys[7], 71), 0),
    }


smooth_weight = 2.0


def direction_shift(course):
    return (course // 2 + 1) * (1 - 2 * (course % 2))


def cell_lookup(send_list):
    tile_ids = jnp.arange(N_MID, dtype=jnp.int32)
    own_cells = tile_ids[:, None] * CELLS + jnp.arange(CELLS, dtype=jnp.int32)[None, :]
    columns_list = [own_cells]
    for course in range(2 * REACH):
        source = tile_ids - direction_shift(course)
        valid_mask = (source >= 0) & (source < N_MID)
        safe_source = jnp.clip(source, 0, N_MID - 1).astype(jnp.int32)
        cell_ids = safe_source[:, None] * CELLS + send_list[safe_source, course, :]
        columns_list.append(jnp.where(valid_mask[:, None], cell_ids, CELLS * N_MID))
    return jnp.concatenate(columns_list, axis=1).astype(jnp.int32)


def entry_tables(send_list, aper_slot, trace_bin, trace_count):
    lookup = cell_lookup(send_list)
    trace_ids = jnp.arange(TR_DEV * N_MID * N_OFF, dtype=jnp.int32)
    tile_index = trace_ids // (TR_DEV * N_OFF)
    offset_bin = ((trace_ids // TR_DEV) % N_OFF) * (NOFF // N_OFF) + trace_bin
    cell_index = lookup[tile_index[None, :], aper_slot]
    valid_mask = (cell_index < CELLS * N_MID) & (jnp.arange(APER, dtype=jnp.int32)[:, None] < trace_count[None, :])
    entry_index = jnp.where(valid_mask, cell_index * NOFF + offset_bin[None, :], CELLS * N_MID * NOFF)
    return entry_index.astype(jnp.int32), valid_mask


def by_tiles(array):
    return jnp.transpose(array.reshape(array.shape[0], N_MID, -1), (1, 0, 2))


def forward_tile(flat_field, kernels, entry_index, valid_mask, patterns):
    safe_index = jnp.where(valid_mask, entry_index, 0).astype(jnp.int32)
    blocks = flat_field[safe_index].astype(jnp.float32) * valid_mask[..., None].astype(jnp.float32)
    chooser = (patterns[None] == jnp.arange(PATTERNS, dtype=jnp.int32)[:, None, None]).astype(jnp.float32)
    pattern_sums = jnp.einsum("pjt,jtn->ptn", chooser, blocks).astype(jnp.bfloat16)
    return jnp.einsum("ptn,pnm->tm", pattern_sums.astype(jnp.float32), kernels.astype(jnp.float32))


def adjoint_tile(accumulated, values, entry_index, valid_mask, patterns, kernels):
    spread = jnp.einsum("tm,pnm->ptn", values.astype(jnp.float32), kernels.astype(jnp.float32))
    chooser = (patterns[None] == jnp.arange(PATTERNS, dtype=jnp.int32)[:, None, None]).astype(jnp.float32)
    chooser = chooser * valid_mask[None].astype(jnp.float32)
    entries = jnp.einsum("pjt,ptn->jtn", chooser, spread)
    return accumulated.at[entry_index.reshape(-1)].add(entries.reshape(-1, NT), mode="drop")


def smoothing(field):
    padded = jnp.pad(field, ((0, 0), (1, 1), (0, 0)))
    return smooth_weight * (2.0 * field - padded[:, :-2] - padded[:, 2:])


def reference(traces, kernels, send_list, aper_slot, aper_pattern, trace_bin, trace_count):
    entry_index, valid_mask = entry_tables(send_list, aper_slot, trace_bin, trace_count)
    tiled = (by_tiles(entry_index), by_tiles(valid_mask), by_tiles(aper_pattern))
    model_rows = CELLS * N_MID * NOFF
    model_shape = (CELLS * N_MID, NOFF, NT)

    def adjoint_all(values_tiled):
        def advance(accumulated, pieces):
            values, index_tile, mask_tile, pattern_tile = pieces
            return adjoint_tile(accumulated, values, index_tile, mask_tile, pattern_tile, kernels), None
        accumulated, _ = lax.scan(advance, jnp.zeros((model_rows, NT), jnp.float32), (values_tiled,) + tiled)
        return accumulated.reshape(model_shape)

    def normal_all(field):
        flat_field = field.astype(jnp.bfloat16).reshape(model_rows, NT)

        def advance(accumulated, pieces):
            index_tile, mask_tile, pattern_tile = pieces
            applied = forward_tile(flat_field, kernels, index_tile, mask_tile, pattern_tile).astype(jnp.bfloat16)
            return adjoint_tile(accumulated, applied, index_tile, mask_tile, pattern_tile, kernels), None
        accumulated, _ = lax.scan(advance, jnp.zeros((model_rows, NT), jnp.float32), tiled)
        return accumulated.reshape(model_shape) + smoothing(field)

    residual = adjoint_all(traces.reshape(N_MID, N_OFF * TR_DEV, NT))
    direction = residual
    solution = jnp.zeros_like(residual)
    norm_now = jnp.sum(residual * residual)
    for iteration in range(ITERS):
        applied = normal_all(direction)
        step_size = norm_now / jnp.sum(direction * applied)
        solution = solution + step_size * direction
        residual = residual - step_size * applied
        if iteration + 1 < ITERS:
            norm_next = jnp.sum(residual * residual)
            direction = residual + (norm_next / norm_now) * direction
            norm_now = norm_next
    return solution, residual
```

```python
import functools

import jax
import jax.numpy as jnp
from jax import lax
from jax.experimental import pallas as pl
from jax.experimental.pallas import tpu as pltpu
from jax.sharding import PartitionSpec as P

NOFF = 64
PATTERNS = 8
REACH = 2
APER = 8
ITERS = 2
CELLS = 8
KEYS = PATTERNS * CELLS
ROOM = 32
LANES = 128
TOGETHER = LANES // ROOM


smooth_weight = 2.0


def padded_2(x, sides, width):
    for axis, dim in sides:
        peers, length = (lax.axis_size(axis), x.shape[dim])
        up = [(i, (i + 1) % peers) for i in range(peers - 1)]
        down = [(j, i) for i, j in up]
        last = lax.slice_in_dim(x, length - width, length, axis=dim)
        first = lax.slice_in_dim(x, 0, width, axis=dim)
        before = lax.ppermute(last, axis, up)
        after = lax.ppermute(first, axis, down)
        x = jnp.concatenate([before, x, after], axis=dim)
    return x


def from_behind(x, axis, by):
    peers = lax.axis_size(axis)
    pairs = [(i, i + by) for i in range(peers) if 0 <= i + by < peers]
    return lax.ppermute(x, axis, pairs)


def direction_shift(course):
    return (course // 2 + 1) * (1 - 2 * (course % 2))


def offset_laplace(padded):
    return smooth_weight * (2.0 * padded[:, 1:-1] - padded[:, :-2] - padded[:, 2:])


def smoothing(field):
    padded = padded_2(field, (("off", 1),), 1)
    smoothed = offset_laplace(padded)
    return smoothed


def deliver(outgoing):
    arrived = [None] * (2 * REACH)
    for course in range(2 * REACH):
        arrived[course] = from_behind(outgoing[course], "mid", direction_shift(course))
    return arrived


def give_back(returning):
    landed = [None] * (2 * REACH)
    for course in range(2 * REACH):
        landed[course] = from_behind(returning[course], "mid", -direction_shift(course))
    return landed


def shards_by_tile(
    traces, kernels, send_list, aper_slot, aper_pattern, trace_bin, trace_count
):
    off_dev = NOFF // lax.axis_size("off")
    trace_rows = traces.shape[0]
    samples = traces.shape[1]
    chosen_cells = send_list[0]
    send_count = chosen_cells.shape[1]
    slot_count = CELLS + 2 * REACH * send_count
    live_mask = jnp.arange(APER, dtype=jnp.int32)[:, None] < trace_count[None, :]
    row_index = (aper_slot * off_dev + trace_bin[None, :]).reshape(-1)
    pattern_ids = jnp.arange(PATTERNS, dtype=jnp.int32)[:, None, None]
    chooser = ((aper_pattern[None] == pattern_ids) & live_mask[None]).astype(
        jnp.bfloat16
    )
    pick_rows = (
        aper_pattern * trace_rows + jnp.arange(trace_rows, dtype=jnp.int32)[None, :]
    ).reshape(-1)
    live_column = live_mask.reshape(-1, 1).astype(jnp.float32)

    def forward(field_bf):
        outgoing = [field_bf[chosen_cells[course]] for course in range(2 * REACH)]
        arrived = deliver(outgoing)
        slot_rows = jnp.concatenate([field_bf] + arrived, 0).reshape(-1, samples)
        blocks = slot_rows[row_index].reshape(APER, trace_rows, samples)
        pattern_sums = jnp.einsum(
            "pjt,jtn->ptn", chooser, blocks, preferred_element_type=jnp.float32
        ).astype(jnp.bfloat16)
        return jnp.einsum(
            "ptn,pnm->tm", pattern_sums, kernels, preferred_element_type=jnp.float32
        )

    def adjoint(values_bf):
        spread = jnp.einsum(
            "tm,pnm->ptn", values_bf, kernels, preferred_element_type=jnp.float32
        ).reshape(-1, samples)
        entries = spread[pick_rows] * live_column
        slot_sums = (
            jnp.zeros((slot_count * off_dev, samples), jnp.float32)
            .at[row_index]
            .add(entries)
        )
        slot_sums = slot_sums.reshape(slot_count, off_dev, samples)
        returning = [
            slot_sums[CELLS + course * send_count : CELLS + (course + 1) * send_count]
            for course in range(2 * REACH)
        ]
        landed = give_back(returning)
        accumulated = slot_sums[:CELLS]
        for course in range(2 * REACH):
            accumulated = accumulated.at[chosen_cells[course]].add(landed[course])
        return accumulated

    def global_total(value):
        return lax.psum(value, ("mid", "off"))

    residual = adjoint(traces)
    direction = residual
    solution = jnp.zeros_like(residual)
    norm_now = global_total(jnp.sum(residual * residual))
    for iteration in range(ITERS):
        applied = adjoint(
            forward(direction.astype(jnp.bfloat16)).astype(jnp.bfloat16)
        ) + smoothing(direction)
        step_size = norm_now / global_total(jnp.sum(direction * applied))
        solution = solution + step_size * direction
        residual = residual - step_size * applied
        if iteration + 1 < ITERS:
            norm_next = global_total(jnp.sum(residual * residual))
            direction = residual + norm_next / norm_now * direction
            norm_now = norm_next
    return (solution, residual)


def path_rank(m, tiles):
    return m ^ ((m >> 1) & 1) if tiles % 4 == 0 else m


def flipped():
    return lax.axis_index("off") % 2 > 0


def own_block(tiles):
    block = path_rank(lax.axis_index("mid"), tiles)
    return jnp.where(flipped(), tiles - 1 - block, block)


def dot_back(rows, kernel):
    return lax.dot_general(
        rows, kernel, (((1,), (1,)), ((), ())), preferred_element_type=jnp.float32
    )


SLOT, PATTERN, WITHIN, COUNT, SENT = 0, APER, 2 * APER, 2 * APER + 1, 2 * APER + 2


def share_kernel(
    tiles, bins, room, sends_arg, slot_arg, pattern_arg, bin_arg, count_arg, traces_arg,
    out_ref, full_ref, sends_ref, slot_ref, pattern_ref, bin_ref, count_ref, traces_ref,
    staged,
):
    rows, samples = traces_ref.shape
    stages = [
        pltpu.make_async_copy(arg, ref, staged.at[i])
        for i, (arg, ref) in enumerate(
            [
                (bin_arg, bin_ref),
                (slot_arg, slot_ref),
                (pattern_arg, pattern_ref),
                (count_arg, count_ref),
                (sends_arg, sends_ref),
                (traces_arg, traces_ref),
            ]
        )
    ]
    for stage in stages:
        stage.start()
    for stage in stages:
        stage.wait()
    offset_bin = bin_ref[...]
    block = lax.div(offset_bin, bins)
    within = offset_bin - block * bins
    chunk = path_rank(jnp.where(flipped(), tiles - 1 - block, block), tiles)
    belongs = lax.broadcasted_iota(jnp.int32, (tiles, rows), 0) == chunk
    belongs = jnp.where(belongs, 1.0, 0.0)
    earlier = lax.broadcasted_iota(jnp.int32, (rows, rows), 0) < (
        lax.broadcasted_iota(jnp.int32, (rows, rows), 1)
    )
    rank = jnp.dot(
        belongs.astype(jnp.bfloat16),
        jnp.where(earlier, 1.0, 0.0).astype(jnp.bfloat16),
        preferred_element_type=jnp.float32,
    )
    rank = jnp.sum(rank * belongs, 0, keepdims=True).astype(jnp.int32)
    full = jnp.max(rank, axis=1, keepdims=True) >= room
    full_ref[...] = jnp.broadcast_to(jnp.where(full, 1.0, 0.0), full_ref.shape)
    target = jnp.where(rank < room, chunk * room + rank, -1)
    chosen = lax.broadcasted_iota(jnp.int32, (tiles * room, rows), 0) == target
    chosen = jnp.where(chosen, 1.0, 0.0).astype(jnp.bfloat16)
    picked = jnp.dot(chosen, traces_ref[...], preferred_element_type=jnp.float32)
    out_ref[:, :, :samples] = picked.reshape(tiles, room, samples).astype(jnp.bfloat16)
    place = lax.axis_index("mid")
    lane = lax.broadcasted_iota(jnp.int32, (1, LANES), 1)
    target = chunk * LANES + lax.rem(place, TOGETHER) * room + rank
    chosen = lax.broadcasted_iota(jnp.int32, (tiles * LANES, rows), 0) == (
        jnp.where(rank < room, target, -1)
    )
    chosen = jnp.where(chosen, 1.0, 0.0).astype(jnp.bfloat16)
    lists = jnp.concatenate(
        [
            slot_ref[...].astype(jnp.float32),
            pattern_ref[...].astype(jnp.float32),
            within.astype(jnp.float32),
            count_ref[...].astype(jnp.float32),
            jnp.zeros((room - SENT, rows), jnp.float32),
        ],
        0,
    ).astype(jnp.bfloat16)
    lists = dot_back(lists, chosen)
    _, courses, send = sends_ref.shape
    line = lax.broadcasted_iota(jnp.int32, (room, LANES), 0)
    sent = jnp.zeros((room, LANES), jnp.int32)
    for course in range(courses):
        reader = lax.rem(place + direction_shift(course) + TOGETHER, TOGETHER)
        here = lax.div(lane, room) == reader
        for m in range(send):
            value = jnp.where(here, sends_ref[0, course, m], 0)
            sent += jnp.where(line == sent_row(course, send) + m, value, 0)
    sent = sent.astype(jnp.float32)
    for m in range(tiles):
        out_ref[m, :, samples:] = (
            lists[:, m * LANES : (m + 1) * LANES] + sent
        ).astype(jnp.bfloat16)


def sent_row(course, send):
    return SENT + max(course - 1, 0) * send


def fill_picks(tiles, bins, send, landed_ref, picks_ref):
    samples = landed_ref.shape[2] - LANES
    keys = lax.broadcasted_iota(jnp.int32, (KEYS, LANES), 0)
    member = lax.div(lax.broadcasted_iota(jnp.int32, (1, LANES), 1), ROOM)
    blocks = [
        landed_ref[tile, :, samples:].astype(jnp.float32).astype(jnp.int32)
        for tile in range(tiles)
    ]
    for group in range(tiles // TOGETHER):
        readers = range(group * TOGETHER, (group + 1) * TOGETHER)
        lists = sum(blocks[tile][:SENT] for tile in readers)
        within, count = lists[WITHIN : WITHIN + 1], lists[COUNT : COUNT + 1]
        wanted = []
        for region in range(2 * REACH + 1):
            course = region - 1
            shift = direction_shift(course) if region else 0
            owners = [tile - shift for tile in readers if 0 <= tile - shift < tiles]
            sent = 0
            for owner in owners if region else ():
                row = sent_row(course, send)
                values = blocks[owner][row : row + send]
                sent += jnp.where(member == (owner + shift) % TOGETHER, values, 0)
            for entry in range(region, APER, 2 * REACH + 1):
                cell = lists[SLOT + entry : SLOT + entry + 1]
                if region:
                    place = cell - (CELLS + course * send)
                    cell = sent[:1]
                    for other in range(1, send):
                        cell = jnp.where(place == other, sent[other : other + 1], cell)
                pattern = lists[PATTERN + entry : PATTERN + entry + 1]
                key = jnp.where(count > entry, pattern * CELLS + cell, -1)
                for owner in owners:
                    there = member == (owner + shift) % TOGETHER
                    wanted.append((owner, jnp.where(there, key, -1)))
        for tile in range(tiles):
            for b in range(bins):
                total = jnp.zeros((KEYS, LANES), jnp.float32)
                for owner, key in wanted:
                    if owner == tile:
                        hit = keys == jnp.where(within == b, key, -1)
                        total += jnp.where(hit, 1.0, 0.0)
                picks_ref[b, :, tile, :, group * LANES : (group + 1) * LANES] = (
                    total.reshape(PATTERNS, CELLS, LANES)
                )


def two_parts(x):
    high = x.astype(jnp.bfloat16)
    low = (x - high.astype(jnp.float32)).astype(jnp.bfloat16)
    return jnp.concatenate([high, low], 0)


def store_parts(parts_ref, b, x):
    shape = (PATTERNS, *parts_ref.shape[3:])
    high = x.astype(jnp.bfloat16)
    parts_ref[:, 0, b] = high.reshape(shape)
    low = (x - high.astype(jnp.float32)).astype(jnp.bfloat16)
    parts_ref[:, 1, b] = low.reshape(shape)


def back_projected(kernels_ref, parts_ref):
    _, _, bins, side, samples = parts_ref.shape
    rows = bins * side
    both = jnp.zeros((2 * rows, samples), jnp.float32)
    for p in range(PATTERNS):
        both += dot_back(parts_ref[p].reshape(2 * rows, samples), kernels_ref[p])
    return both[:rows] + both[rows:]


def project(field, kernels_ref, rows_ref):
    bins, _, side, samples = rows_ref.shape
    rows = bins * side
    for p in range(PATTERNS):
        u = jnp.dot(field, kernels_ref[p], preferred_element_type=jnp.float32)
        u = u[:rows] + u[rows:] if field.shape[0] > rows else u
        rows_ref[:, p] = u.astype(jnp.bfloat16).reshape(bins, side, samples)


def mixed(gram_ref, rows_ref, b):
    _, _, side, samples = rows_ref.shape
    return jnp.dot(
        gram_ref[b],
        rows_ref[b].reshape(PATTERNS * side, samples),
        preferred_element_type=jnp.float32,
    )


def smoothed(field, before, after):
    side = before.shape[0]
    lower = jnp.concatenate([before, field[:-side]], 0)
    upper = jnp.concatenate([field[side:], after], 0)
    return smooth_weight * (2.0 * field - lower - upper)


def first_kernel(
    tiles, bins, send, landed_ref, kernels_arg,
    start_ref, local_ref, gram_ref, up_ref, down_ref, kernels_ref,
    picks_ref, rows_ref, parts_ref, arrived,
):
    copies = [
        pltpu.make_async_copy(kernels_arg.at[p], kernels_ref.at[p], arrived.at[p])
        for p in range(PATTERNS)
    ]
    for copy in copies:
        copy.start()
    side = tiles * CELLS
    samples = start_ref.shape[1]
    fill_picks(tiles, bins, send, landed_ref, picks_ref)
    traces = landed_ref[:, :, :samples].reshape(-1, samples)
    for b in range(bins):
        picks = picks_ref[b].reshape(PATTERNS * side, -1).astype(jnp.bfloat16)
        gram_ref[b] = dot_back(picks, picks).astype(jnp.bfloat16)
        sums = jnp.dot(picks, traces, preferred_element_type=jnp.float32)
        parts_ref[:, 0, b] = sums.astype(jnp.bfloat16).reshape(PATTERNS, side, samples)
    start = jnp.zeros((bins * side, samples), jnp.float32)
    for p in range(PATTERNS):
        copies[p].wait()
        start += dot_back(parts_ref[p, 0].reshape(bins * side, samples), kernels_ref[p])
    start = start.astype(jnp.bfloat16)
    start_ref[...] = start
    field = start.astype(jnp.float32)
    nothing = jnp.zeros((side, samples), jnp.float32)
    project(start, kernels_ref, rows_ref)
    for b in range(bins):
        store_parts(parts_ref, b, mixed(gram_ref, rows_ref, b))
    local = back_projected(kernels_ref, parts_ref) + smoothed(field, nothing, nothing)
    local_ref[...] = local
    up_ref[:side] = start[-side:]
    up_ref[side:] = local[-side:].astype(jnp.bfloat16)
    down_ref[:side] = start[:side]
    down_ref[side:] = local[:side].astype(jnp.bfloat16)


FULL, STEP, GROW = 4, 5, 6


def ahead_kernel(local_ref, gram_ref, kernels_ref, rows_ref, mixed_ref):
    project(two_parts(local_ref[...]), kernels_ref, rows_ref)
    for b in range(rows_ref.shape[0]):
        mixed_ref[b] = mixed(gram_ref, rows_ref, b)


def second_kernel(
    tiles, offs, start_ref, local_ref, gram_ref, kernels_ref, before_ref, after_ref,
    full_ref, ahead_ref, mixed_ref,
    once_ref, smooth_ref, parts_ref, sums_ref, rows_ref,
):
    bins, _, side, samples = rows_ref.shape
    start = start_ref[...].astype(jnp.float32)
    place = lax.axis_index("off") * tiles + own_block(tiles)
    ends = [place > 0, place < offs * tiles - 1]
    beyond, outer = [], []
    for end, (edge_ref, own) in enumerate(
        [(before_ref, start[:side]), (after_ref, start[-side:])]
    ):
        edge = edge_ref[...].astype(jnp.float32)
        there = jnp.where(ends[end], smooth_weight, 0.0)
        beyond.append(-smooth_weight * edge[:side])
        outer.append(edge[side:] - there * own)
    inner = [jnp.zeros(((bins - 2) * side, samples), jnp.float32)] if bins > 2 else []
    beyond = jnp.concatenate([beyond[0], *inner, beyond[1]], 0)
    once = local_ref[...] + beyond
    once_ref[...] = once
    smooth = smoothed(once, outer[0], outer[1])
    smooth_ref[...] = smooth
    project(beyond.astype(jnp.bfloat16), kernels_ref, rows_ref)
    square = 0.0
    for b in range(bins):
        both = mixed_ref[b] + mixed(gram_ref, rows_ref, b)
        store_parts(parts_ref, b, both)
        rows = ahead_ref[b].astype(jnp.float32) + rows_ref[b].astype(jnp.float32)
        square += total(rows.reshape(both.shape) * both)
    products = [
        total(start * start),
        total(start * once),
        total(once * once),
        total(once * smooth) + square,
    ]
    lane = lax.broadcasted_iota(jnp.int32, (1, LANES), 1)
    line = jnp.where(lane == FULL, full_ref[:1], 0.0)
    for i, product in enumerate(products):
        line = jnp.where(lane == i, product, line)
    sums_ref[...] = jnp.broadcast_to(line, sums_ref.shape)


def last_kernel(parts_ref, kernels_ref, out_ref):
    out_ref[...] = back_projected(kernels_ref, parts_ref)


def pack_kernel(
    sums_ref, start_ref, once_ref, smooth_ref, normal_ref, out_ref, lines_ref
):
    tiles = out_ref.shape[0]
    size = out_ref.shape[1] // 3
    ss, so, oo = (sums_ref[:1, i : i + 1] for i in range(3))
    step, grow = own_scales(ss, so, oo)
    lane = lax.broadcasted_iota(jnp.int32, lines_ref.shape, 1)
    line = jnp.where(lane == STEP, step, sums_ref[:1])
    line = jnp.where(lane == GROW, grow, line)
    own = lax.broadcasted_iota(jnp.int32, lines_ref.shape, 0) == lax.axis_index("mid")
    lines_ref[...] = jnp.where(own, line, 0.0)
    start, once = start_ref[...].astype(jnp.float32), once_ref[...]
    twice = normal_ref[...] + smooth_ref[...]
    basis = [start, start - step * once, grow * once - step * twice]
    for i, vector in enumerate(basis):
        vector = vector.reshape(-1, tiles, CELLS, vector.shape[1])
        for tile in range(tiles):
            out_ref[tile, i * size : (i + 1) * size] = (
                vector[:, tile].reshape(size, -1).astype(jnp.bfloat16)
            )


def total(x):
    return jnp.sum(jnp.sum(x, 0, keepdims=True), 1, keepdims=True)


def own_scales(ss, so, oo):
    step = ss / so
    step = jnp.where(step > 0.0, jnp.clip(step, 1e-8, 1e3), 1.0)
    grow = step * step * oo / ss
    return step, jnp.where(grow > 0.0, jnp.clip(grow, 0.0, 1e3), 1.0)


def place_kernel(bins, lines_ref, landed_ref, solution_ref, residual_ref, full_ref):
    tiles = landed_ref.shape[0]
    size = bins * CELLS
    samples = solution_ref.shape[2]
    sums = jnp.sum(lines_ref[...], 0, keepdims=True)
    full_ref[0] = jnp.sum(sums[:, FULL : FULL + 1]).astype(jnp.int32)
    ss, so, oo, ot = (sums[:, i : i + 1] for i in range(4))
    step_0 = ss / so
    norm_1 = step_0 * step_0 * oo - ss
    grow = 1.0 + norm_1 / ss
    step_1 = norm_1 / (grow * grow * so - 2.0 * step_0 * grow * oo + step_0 * step_0 * ot)
    near = step_0 + step_1 * grow
    far = step_1 * step_0
    fields = [[], []]
    for block in range(tiles):
        source = jnp.where(
            flipped(), path_rank(tiles - 1 - block, tiles), path_rank(block, tiles)
        )
        line = lines_ref[pl.ds(source, 1), :]
        inverse = 1.0 / line[:, STEP : STEP + 1]
        there = line[:, GROW : GROW + 1]
        start, first, second = (
            landed_ref[source, i * size : (i + 1) * size].astype(jnp.float32)
            for i in range(3)
        )
        far_once = far * inverse
        near_once = near * inverse - far_once * there * inverse
        solution = (near - far_once) * start + far_once * first
        residual = (1.0 - near_once) * start + near_once * first - far_once * second
        fields[0].append(solution.reshape(bins, CELLS, samples))
        fields[1].append(residual.reshape(bins, CELLS, samples))
    solution_ref[...] = jnp.swapaxes(jnp.concatenate(fields[0], 0), 0, 1)
    residual_ref[...] = jnp.swapaxes(jnp.concatenate(fields[1], 0), 0, 1)


def copy_kernel(*refs):
    *refs, arrived = refs
    half = len(refs) // 2
    copies = [
        pltpu.make_async_copy(refs[i], refs[half + i], arrived.at[i]) for i in range(half)
    ]
    for copy in copies:
        copy.start()
    for copy in copies:
        copy.wait()


VMEM = pl.BlockSpec(memory_space=pltpu.VMEM)
HBM = pl.BlockSpec(memory_space=pltpu.HBM)


SMEM = pl.BlockSpec(memory_space=pltpu.SMEM)


def local_call(kernel, name, in_specs, out_shape, scratch=(), out_specs=None, cost=0):
    return pl.pallas_call(
        kernel,
        out_shape=out_shape,
        in_specs=in_specs,
        out_specs=out_specs or jax.tree.map(lambda _: VMEM, out_shape),
        scratch_shapes=list(scratch),
        cost_estimate=pl.CostEstimate(
            flops=cost, bytes_accessed=cost // 256, transcendentals=0
        )
        if cost
        else None,
        compiler_params=pltpu.CompilerParams(vmem_limit_bytes=32 * 1024 * 1024),
        name=name,
    )


def shards_by_bin(
    traces, kernels, send_list, aper_slot, aper_pattern, trace_bin, trace_count
):
    tiles, offs = lax.axis_size("mid"), lax.axis_size("off")
    bins = NOFF // offs // tiles
    trace_rows, samples = traces.shape
    send = send_list.shape[2]
    rows = bins * tiles * CELLS
    side = tiles * CELLS
    sums = bins * (CELLS + 2 * REACH * send)

    def array(*shape, dtype=jnp.float32):
        return jax.ShapeDtypeStruct(shape, dtype)

    bf16 = functools.partial(array, dtype=jnp.bfloat16)
    in_hbm = functools.partial(
        pltpu.with_memory_space_constraint, memory_space=pltpu.HBM
    )
    lists = (send_list, aper_slot, aper_pattern, trace_bin, trace_count)
    shared, full = local_call(
        functools.partial(share_kernel, tiles, bins, ROOM),
        "share",
        [HBM] * 6,
        (bf16(tiles, ROOM, samples + LANES), array(8, LANES)),
        [
            pltpu.SMEM(send_list.shape, jnp.int32),
            pltpu.VMEM(aper_slot.shape, jnp.int32),
            pltpu.VMEM(aper_pattern.shape, jnp.int32),
            pltpu.VMEM((1, trace_rows), jnp.int32),
            pltpu.VMEM((1, trace_rows), jnp.int32),
            pltpu.VMEM(traces.shape, jnp.bfloat16),
            pltpu.SemaphoreType.DMA((6,)),
        ],
    )(
        in_hbm(send_list),
        in_hbm(aper_slot),
        in_hbm(aper_pattern),
        in_hbm(trace_bin[None]),
        in_hbm(trace_count[None]),
        in_hbm(traces),
    )
    landed = lax.all_to_all(shared, "mid", 0, 0)
    pattern_rows = pltpu.VMEM((bins, PATTERNS, side, samples), jnp.bfloat16)
    parts_type = bf16(PATTERNS, 2, bins, side, samples)
    start, local, gram, up, down, held = local_call(
        functools.partial(first_kernel, tiles, bins, send),
        "first",
        [VMEM, HBM],
        (
            bf16(rows, samples),
            array(rows, samples),
            bf16(bins, tiles * KEYS, tiles * KEYS),
            bf16(2 * side, samples),
            bf16(2 * side, samples),
            bf16(*kernels.shape),
        ),
        [
            pltpu.VMEM((bins, PATTERNS, tiles, CELLS, tiles * ROOM), jnp.float32),
            pattern_rows,
            pltpu.VMEM(parts_type.shape, parts_type.dtype),
            pltpu.SemaphoreType.DMA((PATTERNS,)),
        ],
    )(landed, in_hbm(kernels))

    path = [path_rank(m, tiles) for m in range(tiles)]
    chain = [m * offs + o for o in range(offs) for m in (path[::-1] if o % 2 else path)]
    pairs = list(zip(chain[:-1], chain[1:]))
    before = lax.ppermute(up, ("mid", "off"), pairs)
    after = lax.ppermute(down, ("mid", "off"), [(j, i) for i, j in pairs])

    flops = 2 * rows * PATTERNS * samples * samples
    ahead, mixed_ahead = local_call(
        ahead_kernel,
        "ahead",
        [VMEM] * 3,
        (
            bf16(*pattern_rows.shape),
            array(bins, PATTERNS * side, samples),
        ),
        cost=3 * flops,
    )(local, gram, held)
    field = array(rows, samples)
    once, smooth, parts, products = local_call(
        functools.partial(second_kernel, tiles, offs),
        "second",
        [VMEM] * 9,
        (field, field, parts_type, array(8, LANES)),
        [pattern_rows],
        cost=2 * flops,
    )(start, local, gram, held, before, after, full, ahead, mixed_ahead)

    def exchanged(x, axis):
        step = 1
        while step < lax.axis_size(axis):
            pairs = [(i, i ^ step) for i in range(lax.axis_size(axis))]
            x = x + lax.ppermute(x, axis, pairs)
            step *= 2
        return x

    projected = local_call(last_kernel, "last", [VMEM] * 2, field, cost=2 * flops)(
        parts, held
    )
    packed, lines = local_call(
        pack_kernel,
        "pack",
        [VMEM] * 5,
        (bf16(tiles, 3 * bins * CELLS, samples), array(tiles, LANES)),
    )(exchanged(products, "off"), start, once, smooth, projected)
    landed = lax.all_to_all(packed, "mid", 0, 0)
    lines = exchanged(lines, "mid")
    out_type = array(CELLS, bins * tiles, samples)
    *outputs, full = local_call(
        functools.partial(place_kernel, bins),
        "place",
        [VMEM] * 2,
        (out_type, out_type, array(1, dtype=jnp.int32)),
        out_specs=(VMEM, VMEM, SMEM),
    )(lines, landed)

    def again():
        arguments = [in_hbm(x) for x in (traces, kernels, *lists[:3])]
        arguments += [in_hbm(x[None]) for x in lists[3:]]
        *copies, bins_again, count_again = local_call(
            copy_kernel,
            "again",
            [HBM] * len(arguments),
            tuple(array(*x.shape, dtype=x.dtype) for x in arguments),
            [pltpu.SemaphoreType.DMA((len(arguments),))],
            out_specs=(HBM,) * len(arguments),
        )(*arguments)
        return *copies, bins_again[0], count_again[0]

    _, *outputs = lax.while_loop(
        lambda state: state[0] > 0,
        lambda _: (jnp.int32(0), *shards_by_tile(*again())),
        (full[0], *outputs),
    )
    return tuple(outputs)


def fits_by_bin(tiles, offs, send, trace_rows, samples):
    return (
        (NOFF // offs) % (2 * tiles) == 0
        and offs & (offs - 1) == 0
        and tiles & (tiles - 1) == 0
        and tiles % TOGETHER == 0
        and SENT + (2 * REACH - 1) * send <= ROOM
        and trace_rows == LANES
        and samples % LANES == 0
    )


def solution(mesh):
    in_specs = (
        P(("mid", "off"), None),
        P(),
        P("mid", None, None),
        P(None, ("mid", "off")),
        P(None, ("mid", "off")),
        P(("mid", "off")),
        P(("mid", "off")),
    )
    out_specs = (P("mid", "off", None), P("mid", "off", None))

    def shards(traces, kernels, send_list, *lists):
        fits = fits_by_bin(
            mesh.shape["mid"], mesh.shape["off"], send_list.shape[2], *traces.shape
        )
        form = shards_by_bin if fits else shards_by_tile
        return form(traces, kernels, send_list, *lists)

    return jax.shard_map(
        shards, mesh=mesh, in_specs=in_specs, out_specs=out_specs, check_vma=False
    )
```

```python
import functools

import jax
import jax.numpy as jnp
from jax import lax
from jax.experimental import pallas as pl
from jax.experimental.pallas import tpu as pltpu
from jax.sharding import PartitionSpec as P

NOFF = 64
PATTERNS = 8
REACH = 2
APER = 8
ITERS = 2
CELLS = 8
KEYS = PATTERNS * CELLS
ROOM = 32
LANES = 128
TOGETHER = LANES // ROOM


smooth_weight = 2.0


def padded_2(x, sides, width):
    for axis, dim in sides:
        peers, length = (lax.axis_size(axis), x.shape[dim])
        up = [(i, (i + 1) % peers) for i in range(peers - 1)]
        down = [(j, i) for i, j in up]
        last = lax.slice_in_dim(x, length - width, length, axis=dim)
        first = lax.slice_in_dim(x, 0, width, axis=dim)
        before = lax.ppermute(last, axis, up)
        after = lax.ppermute(first, axis, down)
        x = jnp.concatenate([before, x, after], axis=dim)
    return x


def from_behind(x, axis, by):
    peers = lax.axis_size(axis)
    pairs = [(i, i + by) for i in range(peers) if 0 <= i + by < peers]
    return lax.ppermute(x, axis, pairs)


def direction_shift(course):
    return (course // 2 + 1) * (1 - 2 * (course % 2))


def offset_laplace(padded):
    return smooth_weight * (2.0 * padded[:, 1:-1] - padded[:, :-2] - padded[:, 2:])


def smoothing(field):
    padded = padded_2(field, (("off", 1),), 1)
    smoothed = offset_laplace(padded)
    return smoothed


def deliver(outgoing):
    arrived = [None] * (2 * REACH)
    for course in range(2 * REACH):
        arrived[course] = from_behind(outgoing[course], "mid", direction_shift(course))
    return arrived


def give_back(returning):
    landed = [None] * (2 * REACH)
    for course in range(2 * REACH):
        landed[course] = from_behind(returning[course], "mid", -direction_shift(course))
    return landed


def shards_by_tile(
    traces, kernels, send_list, aper_slot, aper_pattern, trace_bin, trace_count
):
    off_dev = NOFF // lax.axis_size("off")
    trace_rows = traces.shape[0]
    samples = traces.shape[1]
    chosen_cells = send_list[0]
    send_count = chosen_cells.shape[1]
    slot_count = CELLS + 2 * REACH * send_count
    live_mask = jnp.arange(APER, dtype=jnp.int32)[:, None] < trace_count[None, :]
    row_index = (aper_slot * off_dev + trace_bin[None, :]).reshape(-1)
    pattern_ids = jnp.arange(PATTERNS, dtype=jnp.int32)[:, None, None]
    chooser = ((aper_pattern[None] == pattern_ids) & live_mask[None]).astype(
        jnp.bfloat16
    )
    pick_rows = (
        aper_pattern * trace_rows + jnp.arange(trace_rows, dtype=jnp.int32)[None, :]
    ).reshape(-1)
    live_column = live_mask.reshape(-1, 1).astype(jnp.float32)

    def forward(field_bf):
        outgoing = [field_bf[chosen_cells[course]] for course in range(2 * REACH)]
        arrived = deliver(outgoing)
        slot_rows = jnp.concatenate([field_bf] + arrived, 0).reshape(-1, samples)
        blocks = slot_rows[row_index].reshape(APER, trace_rows, samples)
        pattern_sums = jnp.einsum(
            "pjt,jtn->ptn", chooser, blocks, preferred_element_type=jnp.float32
        ).astype(jnp.bfloat16)
        return jnp.einsum(
            "ptn,pnm->tm", pattern_sums, kernels, preferred_element_type=jnp.float32
        )

    def adjoint(values_bf):
        spread = jnp.einsum(
            "tm,pnm->ptn", values_bf, kernels, preferred_element_type=jnp.float32
        ).reshape(-1, samples)
        entries = spread[pick_rows] * live_column
        slot_sums = (
            jnp.zeros((slot_count * off_dev, samples), jnp.float32)
            .at[row_index]
            .add(entries)
        )
        slot_sums = slot_sums.reshape(slot_count, off_dev, samples)
        returning = [
            slot_sums[CELLS + course * send_count : CELLS + (course + 1) * send_count]
            for course in range(2 * REACH)
        ]
        landed = give_back(returning)
        accumulated = slot_sums[:CELLS]
        for course in range(2 * REACH):
            accumulated = accumulated.at[chosen_cells[course]].add(landed[course])
        return accumulated

    def global_total(value):
        return lax.psum(value, ("mid", "off"))

    residual = adjoint(traces)
    direction = residual
    solution = jnp.zeros_like(residual)
    norm_now = global_total(jnp.sum(residual * residual))
    for iteration in range(ITERS):
        applied = adjoint(
            forward(direction.astype(jnp.bfloat16)).astype(jnp.bfloat16)
        ) + smoothing(direction)
        step_size = norm_now / global_total(jnp.sum(direction * applied))
        solution = solution + step_size * direction
        residual = residual - step_size * applied
        if iteration + 1 < ITERS:
            norm_next = global_total(jnp.sum(residual * residual))
            direction = residual + norm_next / norm_now * direction
            norm_now = norm_next
    return (solution, residual)


def path_rank(m, tiles):
    return m ^ ((m >> 1) & 1) if tiles % 4 == 0 else m


def flipped():
    return lax.axis_index("off") % 2 > 0


def own_block(tiles):
    block = path_rank(lax.axis_index("mid"), tiles)
    return jnp.where(flipped(), tiles - 1 - block, block)


def dot_back(rows, kernel):
    return lax.dot_general(
        rows, kernel, (((1,), (1,)), ((), ())), preferred_element_type=jnp.float32
    )


SLOT, PATTERN, WITHIN, COUNT, SENT = 0, APER, 2 * APER, 2 * APER + 1, 2 * APER + 2


def share_kernel(
    tiles, bins, room, sends_arg, slot_arg, pattern_arg, bin_arg, count_arg, traces_arg,
    out_ref, full_ref, sends_ref, slot_ref, pattern_ref, bin_ref, count_ref, traces_ref,
    staged,
):
    rows, samples = traces_ref.shape
    stages = [
        pltpu.make_async_copy(arg, ref, staged.at[i])
        for i, (arg, ref) in enumerate(
            [
                (bin_arg, bin_ref),
                (slot_arg, slot_ref),
                (pattern_arg, pattern_ref),
                (count_arg, count_ref),
                (sends_arg, sends_ref),
                (traces_arg, traces_ref),
            ]
        )
    ]
    for stage in stages:
        stage.start()
    for stage in stages:
        stage.wait()
    offset_bin = bin_ref[...]
    block = lax.div(offset_bin, bins)
    within = offset_bin - block * bins
    chunk = path_rank(jnp.where(flipped(), tiles - 1 - block, block), tiles)
    belongs = lax.broadcasted_iota(jnp.int32, (tiles, rows), 0) == chunk
    belongs = jnp.where(belongs, 1.0, 0.0)
    earlier = lax.broadcasted_iota(jnp.int32, (rows, rows), 0) < (
        lax.broadcasted_iota(jnp.int32, (rows, rows), 1)
    )
    rank = jnp.dot(
        belongs.astype(jnp.bfloat16),
        jnp.where(earlier, 1.0, 0.0).astype(jnp.bfloat16),
        preferred_element_type=jnp.float32,
    )
    rank = jnp.sum(rank * belongs, 0, keepdims=True).astype(jnp.int32)
    full = jnp.max(rank, axis=1, keepdims=True) >= room
    full_ref[...] = jnp.broadcast_to(jnp.where(full, 1.0, 0.0), full_ref.shape)
    target = jnp.where(rank < room, chunk * room + rank, -1)
    chosen = lax.broadcasted_iota(jnp.int32, (tiles * room, rows), 0) == target
    chosen = jnp.where(chosen, 1.0, 0.0).astype(jnp.bfloat16)
    picked = jnp.dot(chosen, traces_ref[...], preferred_element_type=jnp.float32)
    out_ref[:, :, :samples] = picked.reshape(tiles, room, samples).astype(jnp.bfloat16)
    place = lax.axis_index("mid")
    lane = lax.broadcasted_iota(jnp.int32, (1, LANES), 1)
    target = chunk * LANES + lax.rem(place, TOGETHER) * room + rank
    chosen = lax.broadcasted_iota(jnp.int32, (tiles * LANES, rows), 0) == (
        jnp.where(rank < room, target, -1)
    )
    chosen = jnp.where(chosen, 1.0, 0.0).astype(jnp.bfloat16)
    lists = jnp.concatenate(
        [
            slot_ref[...].astype(jnp.float32),
            pattern_ref[...].astype(jnp.float32),
            within.astype(jnp.float32),
            count_ref[...].astype(jnp.float32),
            jnp.zeros((room - SENT, rows), jnp.float32),
        ],
        0,
    ).astype(jnp.bfloat16)
    lists = dot_back(lists, chosen)
    _, courses, send = sends_ref.shape
    line = lax.broadcasted_iota(jnp.int32, (room, LANES), 0)
    sent = jnp.zeros((room, LANES), jnp.int32)
    for course in range(courses):
        reader = lax.rem(place + direction_shift(course) + TOGETHER, TOGETHER)
        here = lax.div(lane, room) == reader
        for m in range(send):
            value = jnp.where(here, sends_ref[0, course, m], 0)
            sent += jnp.where(line == sent_row(course, send) + m, value, 0)
    sent = sent.astype(jnp.float32)
    for m in range(tiles):
        out_ref[m, :, samples:] = (
            lists[:, m * LANES : (m + 1) * LANES] + sent
        ).astype(jnp.bfloat16)


def sent_row(course, send):
    return SENT + max(course - 1, 0) * send


def fill_picks(tiles, bins, send, landed_ref, picks_ref):
    samples = landed_ref.shape[2] - LANES
    keys = lax.broadcasted_iota(jnp.int32, (KEYS, LANES), 0)
    member = lax.div(lax.broadcasted_iota(jnp.int32, (1, LANES), 1), ROOM)
    blocks = [
        landed_ref[tile, :, samples:].astype(jnp.float32).astype(jnp.int32)
        for tile in range(tiles)
    ]
    for group in range(tiles // TOGETHER):
        readers = range(group * TOGETHER, (group + 1) * TOGETHER)
        lists = sum(blocks[tile][:SENT] for tile in readers)
        within, count = lists[WITHIN : WITHIN + 1], lists[COUNT : COUNT + 1]
        wanted = []
        for region in range(2 * REACH + 1):
            course = region - 1
            shift = direction_shift(course) if region else 0
            owners = [tile - shift for tile in readers if 0 <= tile - shift < tiles]
            sent = 0
            for owner in owners if region else ():
                row = sent_row(course, send)
                values = blocks[owner][row : row + send]
                sent += jnp.where(member == (owner + shift) % TOGETHER, values, 0)
            for entry in range(region, APER, 2 * REACH + 1):
                cell = lists[SLOT + entry : SLOT + entry + 1]
                if region:
                    place = cell - (CELLS + course * send)
                    cell = sent[:1]
                    for other in range(1, send):
                        cell = jnp.where(place == other, sent[other : other + 1], cell)
                pattern = lists[PATTERN + entry : PATTERN + entry + 1]
                key = jnp.where(count > entry, pattern * CELLS + cell, -1)
                for owner in owners:
                    there = member == (owner + shift) % TOGETHER
                    wanted.append((owner, jnp.where(there, key, -1)))
        for tile in range(tiles):
            for b in range(bins):
                total = jnp.zeros((KEYS, LANES), jnp.float32)
                for owner, key in wanted:
                    if owner == tile:
                        hit = keys == jnp.where(within == b, key, -1)
                        total += jnp.where(hit, 1.0, 0.0)
                picks_ref[b, :, tile, :, group * LANES : (group + 1) * LANES] = (
                    total.reshape(PATTERNS, CELLS, LANES)
                )


def two_parts(x):
    high = x.astype(jnp.bfloat16)
    low = (x - high.astype(jnp.float32)).astype(jnp.bfloat16)
    return jnp.concatenate([high, low], 0)


def store_parts(parts_ref, b, x):
    shape = (PATTERNS, *parts_ref.shape[3:])
    high = x.astype(jnp.bfloat16)
    parts_ref[:, 0, b] = high.reshape(shape)
    low = (x - high.astype(jnp.float32)).astype(jnp.bfloat16)
    parts_ref[:, 1, b] = low.reshape(shape)


def back_projected(kernels_ref, parts_ref):
    _, _, bins, side, samples = parts_ref.shape
    rows = bins * side
    both = jnp.zeros((2 * rows, samples), jnp.float32)
    for p in range(PATTERNS):
        both += dot_back(parts_ref[p].reshape(2 * rows, samples), kernels_ref[p])
    return both[:rows] + both[rows:]


def project(field, kernels_ref, rows_ref):
    bins, _, side, samples = rows_ref.shape
    rows = bins * side
    for p in range(PATTERNS):
        u = jnp.dot(field, kernels_ref[p], preferred_element_type=jnp.float32)
        u = u[:rows] + u[rows:] if field.shape[0] > rows else u
        rows_ref[:, p] = u.astype(jnp.bfloat16).reshape(bins, side, samples)


def mixed(gram_ref, rows_ref, b):
    _, _, side, samples = rows_ref.shape
    return jnp.dot(
        gram_ref[b],
        rows_ref[b].reshape(PATTERNS * side, samples),
        preferred_element_type=jnp.float32,
    )


def smoothed(field, before, after):
    side = before.shape[0]
    lower = jnp.concatenate([before, field[:-side]], 0)
    upper = jnp.concatenate([field[side:], after], 0)
    return smooth_weight * (2.0 * field - lower - upper)


def first_kernel(
    tiles, bins, send, landed_ref, kernels_arg,
    start_ref, local_ref, gram_ref, up_ref, down_ref, kernels_ref,
    picks_ref, rows_ref, parts_ref, arrived,
):
    copies = [
        pltpu.make_async_copy(kernels_arg.at[p], kernels_ref.at[p], arrived.at[p])
        for p in range(PATTERNS)
    ]
    for copy in copies:
        copy.start()
    side = tiles * CELLS
    samples = start_ref.shape[1]
    fill_picks(tiles, bins, send, landed_ref, picks_ref)
    traces = landed_ref[:, :, :samples].reshape(-1, samples)
    for b in range(bins):
        picks = picks_ref[b].reshape(PATTERNS * side, -1).astype(jnp.bfloat16)
        gram_ref[b] = dot_back(picks, picks).astype(jnp.bfloat16)
        sums = jnp.dot(picks, traces, preferred_element_type=jnp.float32)
        parts_ref[:, 0, b] = sums.astype(jnp.bfloat16).reshape(PATTERNS, side, samples)
    start = jnp.zeros((bins * side, samples), jnp.float32)
    for p in range(PATTERNS):
        copies[p].wait()
        start += dot_back(parts_ref[p, 0].reshape(bins * side, samples), kernels_ref[p])
    start = start.astype(jnp.bfloat16)
    start_ref[...] = start
    field = start.astype(jnp.float32)
    nothing = jnp.zeros((side, samples), jnp.float32)
    project(start, kernels_ref, rows_ref)
    for b in range(bins):
        store_parts(parts_ref, b, mixed(gram_ref, rows_ref, b))
    local = back_projected(kernels_ref, parts_ref) + smoothed(field, nothing, nothing)
    local_ref[...] = local
    up_ref[:side] = start[-side:]
    up_ref[side:] = local[-side:].astype(jnp.bfloat16)
    down_ref[:side] = start[:side]
    down_ref[side:] = local[:side].astype(jnp.bfloat16)


FULL, STEP, GROW = 4, 5, 6


def store_chunks(out_ref, row, field):
    tiles, samples = out_ref.shape[0], field.shape[1]
    field = field.reshape(-1, tiles, CELLS, samples)
    size = field.shape[0] * CELLS
    for tile in range(tiles):
        out_ref[tile, row : row + size, :samples] = (
            field[:, tile].reshape(size, samples).astype(jnp.bfloat16)
        )


def ahead_kernel(
    start_ref, local_ref, gram_ref, kernels_ref, rows_ref, mixed_ref, chunks_ref
):
    store_chunks(chunks_ref, 0, start_ref[...].astype(jnp.float32))
    project(two_parts(local_ref[...]), kernels_ref, rows_ref)
    for b in range(rows_ref.shape[0]):
        mixed_ref[b] = mixed(gram_ref, rows_ref, b)


def second_kernel(
    tiles, offs, start_ref, local_ref, gram_ref, kernels_ref, before_ref, after_ref,
    full_ref, ahead_ref, mixed_ref,
    once_ref, smooth_ref, parts_ref, sums_ref, rows_ref,
):
    bins, _, side, samples = rows_ref.shape
    start = start_ref[...].astype(jnp.float32)
    place = lax.axis_index("off") * tiles + own_block(tiles)
    ends = [place > 0, place < offs * tiles - 1]
    beyond, outer = [], []
    for end, (edge_ref, own) in enumerate(
        [(before_ref, start[:side]), (after_ref, start[-side:])]
    ):
        edge = edge_ref[...].astype(jnp.float32)
        there = jnp.where(ends[end], smooth_weight, 0.0)
        beyond.append(-smooth_weight * edge[:side])
        outer.append(edge[side:] - there * own)
    inner = [jnp.zeros(((bins - 2) * side, samples), jnp.float32)] if bins > 2 else []
    beyond = jnp.concatenate([beyond[0], *inner, beyond[1]], 0)
    once = local_ref[...] + beyond
    once_ref[...] = once
    smooth = smoothed(once, outer[0], outer[1])
    smooth_ref[...] = smooth
    project(beyond.astype(jnp.bfloat16), kernels_ref, rows_ref)
    square = 0.0
    for b in range(bins):
        both = mixed_ref[b] + mixed(gram_ref, rows_ref, b)
        store_parts(parts_ref, b, both)
        rows = ahead_ref[b].astype(jnp.float32) + rows_ref[b].astype(jnp.float32)
        square += total(rows.reshape(both.shape) * both)
    products = [
        total(start * start),
        total(start * once),
        total(once * once),
        total(once * smooth) + square,
    ]
    lane = lax.broadcasted_iota(jnp.int32, (1, LANES), 1)
    line = jnp.where(lane == FULL, full_ref[:1], 0.0)
    for i, product in enumerate(products):
        line = jnp.where(lane == i, product, line)
    sums_ref[...] = jnp.broadcast_to(line, sums_ref.shape)


def last_kernel(parts_ref, kernels_ref, out_ref):
    out_ref[...] = back_projected(kernels_ref, parts_ref)


def pack_kernel(sums_ref, start_ref, once_ref, smooth_ref, normal_ref, out_ref):
    tiles, size, width = out_ref.shape
    samples = width - LANES
    ss, so, oo = (sums_ref[:1, i : i + 1] for i in range(3))
    step, grow = own_scales(ss, so, oo)
    start, once = start_ref[...].astype(jnp.float32), once_ref[...]
    twice = normal_ref[...] + smooth_ref[...]
    store_chunks(out_ref, 0, start - step * once)
    store_chunks(out_ref, size // 2, grow * once - step * twice)
    lane = lax.broadcasted_iota(jnp.int32, (1, LANES), 1)
    rest = jnp.where(lane == STEP, step, sums_ref[:1])
    rest = jnp.where(lane == GROW, grow, rest)
    parts = []
    for _ in range(3):
        part = rest.astype(jnp.bfloat16).astype(jnp.float32)
        rest = rest - part
        parts.append(jnp.broadcast_to(part, (8, LANES)))
    parts.append(jnp.zeros((size - 24, LANES), jnp.float32))
    parts = jnp.concatenate(parts, 0).astype(jnp.bfloat16)
    for tile in range(tiles):
        out_ref[tile, :, samples:] = parts


def line_of(chunk):
    chunk = chunk.astype(jnp.float32)
    return chunk[:1] + chunk[8:9] + chunk[16:17]


def total(x):
    return jnp.sum(jnp.sum(x, 0, keepdims=True), 1, keepdims=True)


def own_scales(ss, so, oo):
    step = ss / so
    step = jnp.where(step > 0.0, jnp.clip(step, 1e-8, 1e3), 1.0)
    grow = step * step * oo / ss
    return step, jnp.where(grow > 0.0, jnp.clip(grow, 0.0, 1e3), 1.0)


def place_kernel(bins, starts_ref, landed_ref, solution_ref, residual_ref, full_ref):
    tiles = landed_ref.shape[0]
    size = bins * CELLS
    samples = solution_ref.shape[2]
    sums = sum(line_of(landed_ref[tile, :, samples:]) for tile in range(tiles))
    full_ref[0] = jnp.sum(sums[:, FULL : FULL + 1]).astype(jnp.int32)
    ss, so, oo, ot = (sums[:, i : i + 1] for i in range(4))
    step_0 = ss / so
    norm_1 = step_0 * step_0 * oo - ss
    grow = 1.0 + norm_1 / ss
    step_1 = norm_1 / (grow * grow * so - 2.0 * step_0 * grow * oo + step_0 * step_0 * ot)
    near = step_0 + step_1 * grow
    far = step_1 * step_0
    fields = [[], []]
    for block in range(tiles):
        source = jnp.where(
            flipped(), path_rank(tiles - 1 - block, tiles), path_rank(block, tiles)
        )
        line = line_of(landed_ref[source, :, samples:])
        inverse = 1.0 / line[:, STEP : STEP + 1]
        there = line[:, GROW : GROW + 1]
        start = starts_ref[source].astype(jnp.float32)
        first, second = (
            landed_ref[source, i * size : (i + 1) * size, :samples].astype(jnp.float32)
            for i in range(2)
        )
        far_once = far * inverse
        near_once = near * inverse - far_once * there * inverse
        solution = (near - far_once) * start + far_once * first
        residual = (1.0 - near_once) * start + near_once * first - far_once * second
        fields[0].append(solution.reshape(bins, CELLS, samples))
        fields[1].append(residual.reshape(bins, CELLS, samples))
    solution_ref[...] = jnp.swapaxes(jnp.concatenate(fields[0], 0), 0, 1)
    residual_ref[...] = jnp.swapaxes(jnp.concatenate(fields[1], 0), 0, 1)


def copy_kernel(*refs):
    *refs, arrived = refs
    half = len(refs) // 2
    copies = [
        pltpu.make_async_copy(refs[i], refs[half + i], arrived.at[i]) for i in range(half)
    ]
    for copy in copies:
        copy.start()
    for copy in copies:
        copy.wait()


VMEM = pl.BlockSpec(memory_space=pltpu.VMEM)
HBM = pl.BlockSpec(memory_space=pltpu.HBM)


SMEM = pl.BlockSpec(memory_space=pltpu.SMEM)


def local_call(kernel, name, in_specs, out_shape, scratch=(), out_specs=None, cost=0):
    return pl.pallas_call(
        kernel,
        out_shape=out_shape,
        in_specs=in_specs,
        out_specs=out_specs or jax.tree.map(lambda _: VMEM, out_shape),
        scratch_shapes=list(scratch),
        cost_estimate=pl.CostEstimate(
            flops=cost, bytes_accessed=cost // 256, transcendentals=0
        )
        if cost
        else None,
        compiler_params=pltpu.CompilerParams(vmem_limit_bytes=32 * 1024 * 1024),
        name=name,
    )


def shards_by_bin(
    traces, kernels, send_list, aper_slot, aper_pattern, trace_bin, trace_count
):
    tiles, offs = lax.axis_size("mid"), lax.axis_size("off")
    bins = NOFF // offs // tiles
    trace_rows, samples = traces.shape
    send = send_list.shape[2]
    rows = bins * tiles * CELLS
    side = tiles * CELLS
    sums = bins * (CELLS + 2 * REACH * send)

    def array(*shape, dtype=jnp.float32):
        return jax.ShapeDtypeStruct(shape, dtype)

    bf16 = functools.partial(array, dtype=jnp.bfloat16)
    in_hbm = functools.partial(
        pltpu.with_memory_space_constraint, memory_space=pltpu.HBM
    )
    lists = (send_list, aper_slot, aper_pattern, trace_bin, trace_count)
    shared, full = local_call(
        functools.partial(share_kernel, tiles, bins, ROOM),
        "share",
        [HBM] * 6,
        (bf16(tiles, ROOM, samples + LANES), array(8, LANES)),
        [
            pltpu.SMEM(send_list.shape, jnp.int32),
            pltpu.VMEM(aper_slot.shape, jnp.int32),
            pltpu.VMEM(aper_pattern.shape, jnp.int32),
            pltpu.VMEM((1, trace_rows), jnp.int32),
            pltpu.VMEM((1, trace_rows), jnp.int32),
            pltpu.VMEM(traces.shape, jnp.bfloat16),
            pltpu.SemaphoreType.DMA((6,)),
        ],
    )(
        in_hbm(send_list),
        in_hbm(aper_slot),
        in_hbm(aper_pattern),
        in_hbm(trace_bin[None]),
        in_hbm(trace_count[None]),
        in_hbm(traces),
    )
    landed = lax.all_to_all(shared, "mid", 0, 0)
    pattern_rows = pltpu.VMEM((bins, PATTERNS, side, samples), jnp.bfloat16)
    parts_type = bf16(PATTERNS, 2, bins, side, samples)
    start, local, gram, up, down, held = local_call(
        functools.partial(first_kernel, tiles, bins, send),
        "first",
        [VMEM, HBM],
        (
            bf16(rows, samples),
            array(rows, samples),
            bf16(bins, tiles * KEYS, tiles * KEYS),
            bf16(2 * side, samples),
            bf16(2 * side, samples),
            bf16(*kernels.shape),
        ),
        [
            pltpu.VMEM((bins, PATTERNS, tiles, CELLS, tiles * ROOM), jnp.float32),
            pattern_rows,
            pltpu.VMEM(parts_type.shape, parts_type.dtype),
            pltpu.SemaphoreType.DMA((PATTERNS,)),
        ],
    )(landed, in_hbm(kernels))

    path = [path_rank(m, tiles) for m in range(tiles)]
    chain = [m * offs + o for o in range(offs) for m in (path[::-1] if o % 2 else path)]
    pairs = list(zip(chain[:-1], chain[1:]))
    before = lax.ppermute(up, ("mid", "off"), pairs)
    after = lax.ppermute(down, ("mid", "off"), [(j, i) for i, j in pairs])

    flops = 2 * rows * PATTERNS * samples * samples
    ahead, mixed_ahead, chunks = local_call(
        ahead_kernel,
        "ahead",
        [VMEM] * 4,
        (
            bf16(*pattern_rows.shape),
            array(bins, PATTERNS * side, samples),
            bf16(tiles, bins * CELLS, samples),
        ),
        cost=3 * flops,
    )(start, local, gram, held)
    starts = lax.all_to_all(chunks, "mid", 0, 0)
    field = array(rows, samples)
    once, smooth, parts, products = local_call(
        functools.partial(second_kernel, tiles, offs),
        "second",
        [VMEM] * 9,
        (field, field, parts_type, array(8, LANES)),
        [pattern_rows],
        cost=2 * flops,
    )(start, local, gram, held, before, after, full, ahead, mixed_ahead)

    projected = local_call(last_kernel, "last", [VMEM] * 2, field, cost=2 * flops)(
        parts, held
    )
    step = 1
    while step < offs:
        partners = [(i, i ^ step) for i in range(offs)]
        products = products + lax.ppermute(products, "off", partners)
        step *= 2
    packed = local_call(
        pack_kernel,
        "pack",
        [VMEM] * 5,
        bf16(tiles, 2 * bins * CELLS, samples + LANES),
    )(products, start, once, smooth, projected)
    landed = lax.all_to_all(packed, "mid", 0, 0)
    out_type = array(CELLS, bins * tiles, samples)
    *outputs, full = local_call(
        functools.partial(place_kernel, bins),
        "place",
        [VMEM] * 2,
        (out_type, out_type, array(1, dtype=jnp.int32)),
        out_specs=(VMEM, VMEM, SMEM),
    )(starts, landed)

    def again():
        arguments = [in_hbm(x) for x in (traces, kernels, *lists[:3])]
        arguments += [in_hbm(x[None]) for x in lists[3:]]
        *copies, bins_again, count_again = local_call(
            copy_kernel,
            "again",
            [HBM] * len(arguments),
            tuple(array(*x.shape, dtype=x.dtype) for x in arguments),
            [pltpu.SemaphoreType.DMA((len(arguments),))],
            out_specs=(HBM,) * len(arguments),
        )(*arguments)
        return *copies, bins_again[0], count_again[0]

    _, *outputs = lax.while_loop(
        lambda state: state[0] > 0,
        lambda _: (jnp.int32(0), *shards_by_tile(*again())),
        (full[0], *outputs),
    )
    return tuple(outputs)


def fits_by_bin(tiles, offs, send, trace_rows, samples):
    return (
        (NOFF // offs) % (2 * tiles) == 0
        and offs & (offs - 1) == 0
        and tiles % TOGETHER == 0
        and SENT + (2 * REACH - 1) * send <= ROOM
        and trace_rows == LANES
        and samples % LANES == 0
    )


def solution(mesh):
    in_specs = (
        P(("mid", "off"), None),
        P(),
        P("mid", None, None),
        P(None, ("mid", "off")),
        P(None, ("mid", "off")),
        P(("mid", "off")),
        P(("mid", "off")),
    )
    out_specs = (P("mid", "off", None), P("mid", "off", None))

    def shards(traces, kernels, send_list, *lists):
        fits = fits_by_bin(
            mesh.shape["mid"], mesh.shape["off"], send_list.shape[2], *traces.shape
        )
        form = shards_by_bin if fits else shards_by_tile
        return form(traces, kernels, send_list, *lists)

    return jax.shard_map(
        shards, mesh=mesh, in_specs=in_specs, out_specs=out_specs, check_vma=False
    )
```

```python
import functools

import jax
import jax.numpy as jnp
from jax import lax
from jax.experimental import pallas as pl
from jax.experimental.pallas import tpu as pltpu
from jax.sharding import PartitionSpec as P

NOFF = 64
PATTERNS = 8
REACH = 2
APER = 8
ITERS = 2
CELLS = 8
KEYS = PATTERNS * CELLS
ROOM = 32
LANES = 128
TOGETHER = LANES // ROOM


smooth_weight = 2.0


def padded_2(x, sides, width):
    for axis, dim in sides:
        peers, length = (lax.axis_size(axis), x.shape[dim])
        up = [(i, (i + 1) % peers) for i in range(peers - 1)]
        down = [(j, i) for i, j in up]
        last = lax.slice_in_dim(x, length - width, length, axis=dim)
        first = lax.slice_in_dim(x, 0, width, axis=dim)
        before = lax.ppermute(last, axis, up)
        after = lax.ppermute(first, axis, down)
        x = jnp.concatenate([before, x, after], axis=dim)
    return x


def from_behind(x, axis, by):
    peers = lax.axis_size(axis)
    pairs = [(i, i + by) for i in range(peers) if 0 <= i + by < peers]
    return lax.ppermute(x, axis, pairs)


def direction_shift(course):
    return (course // 2 + 1) * (1 - 2 * (course % 2))


def offset_laplace(padded):
    return smooth_weight * (2.0 * padded[:, 1:-1] - padded[:, :-2] - padded[:, 2:])


def smoothing(field):
    padded = padded_2(field, (("off", 1),), 1)
    smoothed = offset_laplace(padded)
    return smoothed


def deliver(outgoing):
    arrived = [None] * (2 * REACH)
    for course in range(2 * REACH):
        arrived[course] = from_behind(outgoing[course], "mid", direction_shift(course))
    return arrived


def give_back(returning):
    landed = [None] * (2 * REACH)
    for course in range(2 * REACH):
        landed[course] = from_behind(returning[course], "mid", -direction_shift(course))
    return landed


def shards_by_tile(
    traces, kernels, send_list, aper_slot, aper_pattern, trace_bin, trace_count
):
    off_dev = NOFF // lax.axis_size("off")
    trace_rows = traces.shape[0]
    samples = traces.shape[1]
    chosen_cells = send_list[0]
    send_count = chosen_cells.shape[1]
    slot_count = CELLS + 2 * REACH * send_count
    live_mask = jnp.arange(APER, dtype=jnp.int32)[:, None] < trace_count[None, :]
    row_index = (aper_slot * off_dev + trace_bin[None, :]).reshape(-1)
    pattern_ids = jnp.arange(PATTERNS, dtype=jnp.int32)[:, None, None]
    chooser = ((aper_pattern[None] == pattern_ids) & live_mask[None]).astype(
        jnp.bfloat16
    )
    pick_rows = (
        aper_pattern * trace_rows + jnp.arange(trace_rows, dtype=jnp.int32)[None, :]
    ).reshape(-1)
    live_column = live_mask.reshape(-1, 1).astype(jnp.float32)

    def forward(field_bf):
        outgoing = [field_bf[chosen_cells[course]] for course in range(2 * REACH)]
        arrived = deliver(outgoing)
        slot_rows = jnp.concatenate([field_bf] + arrived, 0).reshape(-1, samples)
        blocks = slot_rows[row_index].reshape(APER, trace_rows, samples)
        pattern_sums = jnp.einsum(
            "pjt,jtn->ptn", chooser, blocks, preferred_element_type=jnp.float32
        ).astype(jnp.bfloat16)
        return jnp.einsum(
            "ptn,pnm->tm", pattern_sums, kernels, preferred_element_type=jnp.float32
        )

    def adjoint(values_bf):
        spread = jnp.einsum(
            "tm,pnm->ptn", values_bf, kernels, preferred_element_type=jnp.float32
        ).reshape(-1, samples)
        entries = spread[pick_rows] * live_column
        slot_sums = (
            jnp.zeros((slot_count * off_dev, samples), jnp.float32)
            .at[row_index]
            .add(entries)
        )
        slot_sums = slot_sums.reshape(slot_count, off_dev, samples)
        returning = [
            slot_sums[CELLS + course * send_count : CELLS + (course + 1) * send_count]
            for course in range(2 * REACH)
        ]
        landed = give_back(returning)
        accumulated = slot_sums[:CELLS]
        for course in range(2 * REACH):
            accumulated = accumulated.at[chosen_cells[course]].add(landed[course])
        return accumulated

    def global_total(value):
        return lax.psum(value, ("mid", "off"))

    residual = adjoint(traces)
    direction = residual
    solution = jnp.zeros_like(residual)
    norm_now = global_total(jnp.sum(residual * residual))
    for iteration in range(ITERS):
        applied = adjoint(
            forward(direction.astype(jnp.bfloat16)).astype(jnp.bfloat16)
        ) + smoothing(direction)
        step_size = norm_now / global_total(jnp.sum(direction * applied))
        solution = solution + step_size * direction
        residual = residual - step_size * applied
        if iteration + 1 < ITERS:
            norm_next = global_total(jnp.sum(residual * residual))
            direction = residual + norm_next / norm_now * direction
            norm_now = norm_next
    return (solution, residual)


def path_rank(m, tiles):
    return m ^ ((m >> 1) & 1) if tiles % 4 == 0 else m


def flipped():
    return lax.axis_index("off") % 2 > 0


def own_block(tiles):
    block = path_rank(lax.axis_index("mid"), tiles)
    return jnp.where(flipped(), tiles - 1 - block, block)


def dot_back(rows, kernel):
    return lax.dot_general(
        rows, kernel, (((1,), (1,)), ((), ())), preferred_element_type=jnp.float32
    )


SLOT, PATTERN, WITHIN, COUNT = 0, APER, 4, 5


def share_kernel(
    tiles, bins, room, sends_arg, slot_arg, pattern_arg, bin_arg, count_arg, traces_arg,
    out_ref, full_ref, sends_ref, slot_ref, pattern_ref, bin_ref, count_ref, traces_ref,
    staged,
):
    rows, samples = traces_ref.shape
    stages = [
        pltpu.make_async_copy(arg, ref, staged.at[i])
        for i, (arg, ref) in enumerate(
            [
                (bin_arg, bin_ref),
                (slot_arg, slot_ref),
                (pattern_arg, pattern_ref),
                (count_arg, count_ref),
                (sends_arg, sends_ref),
                (traces_arg, traces_ref),
            ]
        )
    ]
    for stage in stages:
        stage.start()
    for stage in stages:
        stage.wait()
    offset_bin = bin_ref[...]
    block = lax.div(offset_bin, bins)
    within = offset_bin - block * bins
    chunk = path_rank(jnp.where(flipped(), tiles - 1 - block, block), tiles)
    belongs = lax.broadcasted_iota(jnp.int32, (tiles, rows), 0) == chunk
    belongs = jnp.where(belongs, 1.0, 0.0)
    earlier = lax.broadcasted_iota(jnp.int32, (rows, rows), 0) < (
        lax.broadcasted_iota(jnp.int32, (rows, rows), 1)
    )
    rank = jnp.dot(
        belongs.astype(jnp.bfloat16),
        jnp.where(earlier, 1.0, 0.0).astype(jnp.bfloat16),
        preferred_element_type=jnp.float32,
    )
    rank = jnp.sum(rank * belongs, 0, keepdims=True).astype(jnp.int32)
    full = jnp.max(rank, axis=1, keepdims=True) >= room
    full_ref[...] = jnp.broadcast_to(jnp.where(full, 1.0, 0.0), full_ref.shape)
    target = jnp.where(rank < room, chunk * room + rank, -1)
    chosen = lax.broadcasted_iota(jnp.int32, (tiles * room, rows), 0) == target
    chosen = jnp.where(chosen, 1.0, 0.0).astype(jnp.bfloat16)
    picked = jnp.dot(chosen, traces_ref[...], preferred_element_type=jnp.float32)
    picked = picked.reshape(tiles, room, samples).astype(jnp.bfloat16)
    pieces = samples // LANES
    for i in range(pieces):
        out_ref[:, i * room : (i + 1) * room] = picked[:, :, i * LANES : (i + 1) * LANES]
    place = lax.axis_index("mid")
    lane = lax.broadcasted_iota(jnp.int32, (1, LANES), 1)
    target = chunk * LANES + lax.rem(place, TOGETHER) * room + rank
    chosen = lax.broadcasted_iota(jnp.int32, (tiles * LANES, rows), 0) == (
        jnp.where(rank < room, target, -1)
    )
    chosen = jnp.where(chosen, 1.0, 0.0).astype(jnp.bfloat16)
    lists = jnp.concatenate(
        [
            slot_ref[...].astype(jnp.float32),
            pattern_ref[...].astype(jnp.float32),
            jnp.zeros((WITHIN, rows), jnp.float32),
            within.astype(jnp.float32),
            count_ref[...].astype(jnp.float32),
            jnp.zeros((APER - COUNT - 1, rows), jnp.float32),
        ],
        0,
    ).astype(jnp.bfloat16)
    lists = dot_back(lists, chosen)
    _, courses, send = sends_ref.shape
    line = lax.broadcasted_iota(jnp.int32, (2 * APER, LANES), 0)
    sent = jnp.zeros((2 * APER, LANES), jnp.int32)
    for course in range(courses):
        reader = lax.rem(place + direction_shift(course) + TOGETHER, TOGETHER)
        here = lax.div(lane, room) == reader
        for m in range(send):
            value = jnp.where(here, sends_ref[0, course, m], 0)
            sent += jnp.where(line == sent_row(course, send) + m, value, 0)
    sent = sent.astype(jnp.float32)
    for m in range(tiles):
        own = lists[:, m * LANES : (m + 1) * LANES]
        moved = pltpu.roll(own[2 * APER :], room, 1)
        out_ref[m, pieces * room :] = (
            own[: 2 * APER] + jnp.concatenate([moved, jnp.zeros_like(moved)], 0) + sent
        ).astype(jnp.bfloat16)


def sent_row(course, send):
    return send if course == 3 else 0


def fill_picks(tiles, bins, send, landed_ref, picks_ref):
    keys = lax.broadcasted_iota(jnp.int32, (KEYS, LANES), 0)
    member = lax.div(lax.broadcasted_iota(jnp.int32, (1, LANES), 1), ROOM)
    blocks = [
        landed_ref[tile, -2 * APER :].astype(jnp.float32).astype(jnp.int32)
        for tile in range(tiles)
    ]
    for group in range(tiles // TOGETHER):
        readers = range(group * TOGETHER, (group + 1) * TOGETHER)
        lists, moved = 0, 0
        for tile in readers:
            lists += jnp.where(member == tile % TOGETHER, blocks[tile], 0)
            past = member == (tile + 1) % TOGETHER
            moved += jnp.where(past, blocks[tile][:APER], 0)
        moved = pltpu.roll(moved, LANES - ROOM, 1)
        within, count = moved[WITHIN : WITHIN + 1], moved[COUNT : COUNT + 1]
        wanted = []
        for region in range(2 * REACH + 1):
            course = region - 1
            shift = direction_shift(course) if region else 0
            owners = [tile - shift for tile in readers if 0 <= tile - shift < tiles]
            sent = 0
            for owner in owners if region else ():
                row = sent_row(course, send)
                values = blocks[owner][row : row + send]
                sent += jnp.where(member == (owner + shift) % TOGETHER, values, 0)
            for entry in range(region, APER, 2 * REACH + 1):
                cell = lists[SLOT + entry : SLOT + entry + 1]
                if region:
                    place = cell - (CELLS + course * send)
                    cell = sent[:1]
                    for other in range(1, send):
                        cell = jnp.where(place == other, sent[other : other + 1], cell)
                pattern = lists[PATTERN + entry : PATTERN + entry + 1]
                key = jnp.where(count > entry, pattern * CELLS + cell, -1)
                for owner in owners:
                    there = member == (owner + shift) % TOGETHER
                    wanted.append((owner, jnp.where(there, key, -1)))
        for tile in range(tiles):
            for b in range(bins):
                total = jnp.zeros((KEYS, LANES), jnp.float32)
                for owner, key in wanted:
                    if owner == tile:
                        hit = keys == jnp.where(within == b, key, -1)
                        total += jnp.where(hit, 1.0, 0.0)
                picks_ref[b, :, tile, :, group * LANES : (group + 1) * LANES] = (
                    total.reshape(PATTERNS, CELLS, LANES)
                )


def two_parts(x):
    high = x.astype(jnp.bfloat16)
    low = (x - high.astype(jnp.float32)).astype(jnp.bfloat16)
    return jnp.concatenate([high, low], 0)


def store_parts(parts_ref, b, x):
    shape = (PATTERNS, *parts_ref.shape[3:])
    high = x.astype(jnp.bfloat16)
    parts_ref[:, 0, b] = high.reshape(shape)
    low = (x - high.astype(jnp.float32)).astype(jnp.bfloat16)
    parts_ref[:, 1, b] = low.reshape(shape)


def back_projected(kernels_ref, parts_ref):
    _, _, bins, side, samples = parts_ref.shape
    rows = bins * side
    both = jnp.zeros((2 * rows, samples), jnp.float32)
    for p in range(PATTERNS):
        both += dot_back(parts_ref[p].reshape(2 * rows, samples), kernels_ref[p])
    return both[:rows] + both[rows:]


def project(field, kernels_ref, rows_ref):
    bins, _, side, samples = rows_ref.shape
    rows = bins * side
    for p in range(PATTERNS):
        u = jnp.dot(field, kernels_ref[p], preferred_element_type=jnp.float32)
        u = u[:rows] + u[rows:] if field.shape[0] > rows else u
        rows_ref[:, p] = u.astype(jnp.bfloat16).reshape(bins, side, samples)


def mixed(gram_ref, rows_ref, b):
    _, _, side, samples = rows_ref.shape
    return jnp.dot(
        gram_ref[b],
        rows_ref[b].reshape(PATTERNS * side, samples),
        preferred_element_type=jnp.float32,
    )


def smoothed(field, before, after):
    side = before.shape[0]
    lower = jnp.concatenate([before, field[:-side]], 0)
    upper = jnp.concatenate([field[side:], after], 0)
    return smooth_weight * (2.0 * field - lower - upper)


def first_kernel(
    tiles, bins, send, landed_ref, kernels_arg,
    start_ref, local_ref, gram_ref, up_ref, down_ref, kernels_ref,
    picks_ref, rows_ref, parts_ref, arrived,
):
    copies = [
        pltpu.make_async_copy(kernels_arg.at[p], kernels_ref.at[p], arrived.at[p])
        for p in range(PATTERNS)
    ]
    for copy in copies:
        copy.start()
    side = tiles * CELLS
    samples = start_ref.shape[1]
    fill_picks(tiles, bins, send, landed_ref, picks_ref)
    traces = jnp.concatenate(
        [
            landed_ref[:, i * ROOM : (i + 1) * ROOM].reshape(-1, LANES)
            for i in range(samples // LANES)
        ],
        1,
    )
    for b in range(bins):
        picks = picks_ref[b].reshape(PATTERNS * side, -1).astype(jnp.bfloat16)
        gram_ref[b] = dot_back(picks, picks).astype(jnp.bfloat16)
        sums = jnp.dot(picks, traces, preferred_element_type=jnp.float32)
        parts_ref[:, 0, b] = sums.astype(jnp.bfloat16).reshape(PATTERNS, side, samples)
    start = jnp.zeros((bins * side, samples), jnp.float32)
    for p in range(PATTERNS):
        copies[p].wait()
        start += dot_back(parts_ref[p, 0].reshape(bins * side, samples), kernels_ref[p])
    start = start.astype(jnp.bfloat16)
    start_ref[...] = start
    field = start.astype(jnp.float32)
    nothing = jnp.zeros((side, samples), jnp.float32)
    project(start, kernels_ref, rows_ref)
    for b in range(bins):
        store_parts(parts_ref, b, mixed(gram_ref, rows_ref, b))
    local = back_projected(kernels_ref, parts_ref) + smoothed(field, nothing, nothing)
    local_ref[...] = local
    up_ref[:side] = start[-side:]
    up_ref[side:] = local[-side:].astype(jnp.bfloat16)
    down_ref[:side] = start[:side]
    down_ref[side:] = local[:side].astype(jnp.bfloat16)


FULL, STEP, GROW = 4, 5, 6


def ahead_kernel(local_ref, gram_ref, kernels_ref, rows_ref, mixed_ref):
    project(two_parts(local_ref[...]), kernels_ref, rows_ref)
    for b in range(rows_ref.shape[0]):
        mixed_ref[b] = mixed(gram_ref, rows_ref, b)


def second_kernel(
    tiles, offs, start_ref, local_ref, gram_ref, kernels_ref, before_ref, after_ref,
    full_ref, ahead_ref, mixed_ref,
    once_ref, smooth_ref, parts_ref, sums_ref, rows_ref,
):
    bins, _, side, samples = rows_ref.shape
    start = start_ref[...].astype(jnp.float32)
    place = lax.axis_index("off") * tiles + own_block(tiles)
    ends = [place > 0, place < offs * tiles - 1]
    beyond, outer = [], []
    for end, (edge_ref, own) in enumerate(
        [(before_ref, start[:side]), (after_ref, start[-side:])]
    ):
        edge = edge_ref[...].astype(jnp.float32)
        there = jnp.where(ends[end], smooth_weight, 0.0)
        beyond.append(-smooth_weight * edge[:side])
        outer.append(edge[side:] - there * own)
    inner = [jnp.zeros(((bins - 2) * side, samples), jnp.float32)] if bins > 2 else []
    beyond = jnp.concatenate([beyond[0], *inner, beyond[1]], 0)
    once = local_ref[...] + beyond
    once_ref[...] = once
    smooth = smoothed(once, outer[0], outer[1])
    smooth_ref[...] = smooth
    project(beyond.astype(jnp.bfloat16), kernels_ref, rows_ref)
    square = 0.0
    for b in range(bins):
        both = mixed_ref[b] + mixed(gram_ref, rows_ref, b)
        store_parts(parts_ref, b, both)
        rows = ahead_ref[b].astype(jnp.float32) + rows_ref[b].astype(jnp.float32)
        square += total(rows.reshape(both.shape) * both)
    products = [
        total(start * start),
        total(start * once),
        total(once * once),
        total(once * smooth) + square,
    ]
    lane = lax.broadcasted_iota(jnp.int32, (1, LANES), 1)
    line = jnp.where(lane == FULL, full_ref[:1], 0.0)
    for i, product in enumerate(products):
        line = jnp.where(lane == i, product, line)
    sums_ref[...] = jnp.broadcast_to(line, sums_ref.shape)


def last_kernel(parts_ref, kernels_ref, out_ref):
    out_ref[...] = back_projected(kernels_ref, parts_ref)


def pack_kernel(sums_ref, start_ref, once_ref, smooth_ref, normal_ref, out_ref):
    tiles = out_ref.shape[0]
    ss, so, oo = (sums_ref[:1, i : i + 1] for i in range(3))
    step, grow = own_scales(ss, so, oo)
    start, once = start_ref[...].astype(jnp.float32), once_ref[...]
    twice = normal_ref[...] + smooth_ref[...]
    row = 0
    for field in (start, start - step * once, grow * once - step * twice):
        samples = field.shape[1]
        field = field.reshape(-1, tiles, CELLS, samples)
        size = field.shape[0] * CELLS
        for i in range(0, samples, LANES):
            for tile in range(tiles):
                piece = field[:, tile, :, i : i + LANES].reshape(size, LANES)
                out_ref[tile, row : row + size] = piece.astype(jnp.bfloat16)
            row += size
    lane = lax.broadcasted_iota(jnp.int32, (1, LANES), 1)
    rest = jnp.where(lane == STEP, step, sums_ref[:1])
    rest = jnp.where(lane == GROW, grow, rest)
    line = lax.broadcasted_iota(jnp.int32, (16, LANES), 0)
    parts = jnp.zeros((16, LANES), jnp.float32)
    for i in range(3):
        part = rest.astype(jnp.bfloat16).astype(jnp.float32)
        rest = rest - part
        parts = jnp.where(line == i, part, parts)
    for tile in range(tiles):
        out_ref[tile, row:] = parts.astype(jnp.bfloat16)


def total(x):
    return jnp.sum(jnp.sum(x, 0, keepdims=True), 1, keepdims=True)


def own_scales(ss, so, oo):
    step = ss / so
    step = jnp.where(step > 0.0, jnp.clip(step, 1e-8, 1e3), 1.0)
    grow = step * step * oo / ss
    return step, jnp.where(grow > 0.0, jnp.clip(grow, 0.0, 1e3), 1.0)


def place_kernel(bins, landed_ref, solution_ref, residual_ref, full_ref):
    tiles, length, _ = landed_ref.shape
    size = bins * CELLS
    samples = solution_ref.shape[2]
    pieces = samples // LANES

    def line_of(source):
        parts = landed_ref[source, length - 16 :].astype(jnp.float32)
        return jnp.sum(parts, 0, keepdims=True)

    def vector(source, i):
        part = [
            landed_ref[source, (i * pieces + j) * size : (i * pieces + j + 1) * size]
            for j in range(pieces)
        ]
        return jnp.concatenate(part, 1).astype(jnp.float32)

    sums = sum(line_of(tile) for tile in range(tiles))
    full_ref[0] = jnp.sum(sums[:, FULL : FULL + 1]).astype(jnp.int32)
    ss, so, oo, ot = (sums[:, i : i + 1] for i in range(4))
    step_0 = ss / so
    norm_1 = step_0 * step_0 * oo - ss
    grow = 1.0 + norm_1 / ss
    step_1 = norm_1 / (grow * grow * so - 2.0 * step_0 * grow * oo + step_0 * step_0 * ot)
    near = step_0 + step_1 * grow
    far = step_1 * step_0
    fields = [[], []]
    for block in range(tiles):
        source = jnp.where(
            flipped(), path_rank(tiles - 1 - block, tiles), path_rank(block, tiles)
        )
        line = line_of(source)
        inverse = 1.0 / line[:, STEP : STEP + 1]
        there = line[:, GROW : GROW + 1]
        start, first, second = (vector(source, i) for i in range(3))
        far_once = far * inverse
        near_once = near * inverse - far_once * there * inverse
        solution = (near - far_once) * start + far_once * first
        residual = (1.0 - near_once) * start + near_once * first - far_once * second
        fields[0].append(solution.reshape(bins, CELLS, samples))
        fields[1].append(residual.reshape(bins, CELLS, samples))
    solution_ref[...] = jnp.swapaxes(jnp.concatenate(fields[0], 0), 0, 1)
    residual_ref[...] = jnp.swapaxes(jnp.concatenate(fields[1], 0), 0, 1)


def copy_kernel(*refs):
    *refs, arrived = refs
    half = len(refs) // 2
    copies = [
        pltpu.make_async_copy(refs[i], refs[half + i], arrived.at[i]) for i in range(half)
    ]
    for copy in copies:
        copy.start()
    for copy in copies:
        copy.wait()


VMEM = pl.BlockSpec(memory_space=pltpu.VMEM)
HBM = pl.BlockSpec(memory_space=pltpu.HBM)


SMEM = pl.BlockSpec(memory_space=pltpu.SMEM)


def local_call(kernel, name, in_specs, out_shape, scratch=(), out_specs=None, cost=0):
    return pl.pallas_call(
        kernel,
        out_shape=out_shape,
        in_specs=in_specs,
        out_specs=out_specs or jax.tree.map(lambda _: VMEM, out_shape),
        scratch_shapes=list(scratch),
        cost_estimate=pl.CostEstimate(
            flops=cost, bytes_accessed=cost // 256, transcendentals=0
        )
        if cost
        else None,
        compiler_params=pltpu.CompilerParams(vmem_limit_bytes=32 * 1024 * 1024),
        name=name,
    )


def shards_by_bin(
    traces, kernels, send_list, aper_slot, aper_pattern, trace_bin, trace_count
):
    tiles, offs = lax.axis_size("mid"), lax.axis_size("off")
    bins = NOFF // offs // tiles
    trace_rows, samples = traces.shape
    send = send_list.shape[2]
    rows = bins * tiles * CELLS
    side = tiles * CELLS
    sums = bins * (CELLS + 2 * REACH * send)

    def array(*shape, dtype=jnp.float32):
        return jax.ShapeDtypeStruct(shape, dtype)

    bf16 = functools.partial(array, dtype=jnp.bfloat16)
    in_hbm = functools.partial(
        pltpu.with_memory_space_constraint, memory_space=pltpu.HBM
    )
    lists = (send_list, aper_slot, aper_pattern, trace_bin, trace_count)
    shared, full = local_call(
        functools.partial(share_kernel, tiles, bins, ROOM),
        "share",
        [HBM] * 6,
        (
            bf16(tiles, samples // LANES * ROOM + 2 * APER, LANES),
            array(8, LANES),
        ),
        [
            pltpu.SMEM(send_list.shape, jnp.int32),
            pltpu.VMEM(aper_slot.shape, jnp.int32),
            pltpu.VMEM(aper_pattern.shape, jnp.int32),
            pltpu.VMEM((1, trace_rows), jnp.int32),
            pltpu.VMEM((1, trace_rows), jnp.int32),
            pltpu.VMEM(traces.shape, jnp.bfloat16),
            pltpu.SemaphoreType.DMA((6,)),
        ],
    )(
        in_hbm(send_list),
        in_hbm(aper_slot),
        in_hbm(aper_pattern),
        in_hbm(trace_bin[None]),
        in_hbm(trace_count[None]),
        in_hbm(traces),
    )
    landed = lax.all_to_all(shared, "mid", 0, 0)
    pattern_rows = pltpu.VMEM((bins, PATTERNS, side, samples), jnp.bfloat16)
    parts_type = bf16(PATTERNS, 2, bins, side, samples)
    start, local, gram, up, down, held = local_call(
        functools.partial(first_kernel, tiles, bins, send),
        "first",
        [VMEM, HBM],
        (
            bf16(rows, samples),
            array(rows, samples),
            bf16(bins, tiles * KEYS, tiles * KEYS),
            bf16(2 * side, samples),
            bf16(2 * side, samples),
            bf16(*kernels.shape),
        ),
        [
            pltpu.VMEM((bins, PATTERNS, tiles, CELLS, tiles * ROOM), jnp.float32),
            pattern_rows,
            pltpu.VMEM(parts_type.shape, parts_type.dtype),
            pltpu.SemaphoreType.DMA((PATTERNS,)),
        ],
    )(landed, in_hbm(kernels))

    path = [path_rank(m, tiles) for m in range(tiles)]
    chain = [m * offs + o for o in range(offs) for m in (path[::-1] if o % 2 else path)]
    pairs = list(zip(chain[:-1], chain[1:]))
    before = lax.ppermute(up, ("mid", "off"), pairs)
    after = lax.ppermute(down, ("mid", "off"), [(j, i) for i, j in pairs])

    flops = 2 * rows * PATTERNS * samples * samples
    ahead, mixed_ahead = local_call(
        ahead_kernel,
        "ahead",
        [VMEM] * 3,
        (bf16(*pattern_rows.shape), array(bins, PATTERNS * side, samples)),
        cost=3 * flops,
    )(local, gram, held)
    field = array(rows, samples)
    once, smooth, parts, products = local_call(
        functools.partial(second_kernel, tiles, offs),
        "second",
        [VMEM] * 9,
        (field, field, parts_type, array(8, LANES)),
        [pattern_rows],
        cost=2 * flops,
    )(start, local, gram, held, before, after, full, ahead, mixed_ahead)

    projected = local_call(last_kernel, "last", [VMEM] * 2, field, cost=2 * flops)(
        parts, held
    )
    step = 1
    while step < offs:
        partners = [(i, i ^ step) for i in range(offs)]
        products = products + lax.ppermute(products, "off", partners)
        step *= 2
    packed = local_call(
        pack_kernel,
        "pack",
        [VMEM] * 5,
        bf16(tiles, samples // LANES * 3 * bins * CELLS + 16, LANES),
    )(products, start, once, smooth, projected)
    landed = lax.all_to_all(packed, "mid", 0, 0)
    out_type = array(CELLS, bins * tiles, samples)
    *outputs, full = local_call(
        functools.partial(place_kernel, bins),
        "place",
        [VMEM],
        (out_type, out_type, array(1, dtype=jnp.int32)),
        out_specs=(VMEM, VMEM, SMEM),
    )(landed)

    def again():
        arguments = [in_hbm(x) for x in (traces, kernels, *lists[:3])]
        arguments += [in_hbm(x[None]) for x in lists[3:]]
        *copies, bins_again, count_again = local_call(
            copy_kernel,
            "again",
            [HBM] * len(arguments),
            tuple(array(*x.shape, dtype=x.dtype) for x in arguments),
            [pltpu.SemaphoreType.DMA((len(arguments),))],
            out_specs=(HBM,) * len(arguments),
        )(*arguments)
        return *copies, bins_again[0], count_again[0]

    _, *outputs = lax.while_loop(
        lambda state: state[0] > 0,
        lambda _: (jnp.int32(0), *shards_by_tile(*again())),
        (full[0], *outputs),
    )
    return tuple(outputs)


def fits_by_bin(tiles, offs, send, trace_rows, samples):
    return (
        (NOFF // offs) % (2 * tiles) == 0
        and offs & (offs - 1) == 0
        and tiles % TOGETHER == 0
        and send == WITHIN
        and trace_rows == LANES
        and samples % LANES == 0
    )


def solution(mesh):
    in_specs = (
        P(("mid", "off"), None),
        P(),
        P("mid", None, None),
        P(None, ("mid", "off")),
        P(None, ("mid", "off")),
        P(("mid", "off")),
        P(("mid", "off")),
    )
    out_specs = (P("mid", "off", None), P("mid", "off", None))

    def shards(traces, kernels, send_list, *lists):
        fits = fits_by_bin(
            mesh.shape["mid"], mesh.shape["off"], send_list.shape[2], *traces.shape
        )
        form = shards_by_bin if fits else shards_by_tile
        return form(traces, kernels, send_list, *lists)

    return jax.shard_map(
        shards, mesh=mesh, in_specs=in_specs, out_specs=out_specs, check_vma=False
    )
```

```python
import functools

import jax
import jax.numpy as jnp
from jax import lax
from jax.experimental import pallas as pl
from jax.experimental.pallas import tpu as pltpu
from jax.sharding import PartitionSpec as P

NOFF = 64
PATTERNS = 8
REACH = 2
APER = 8
ITERS = 2
CELLS = 8
KEYS = PATTERNS * CELLS
ROOM = 32
LANES = 128
TOGETHER = LANES // ROOM


smooth_weight = 2.0


def padded_2(x, sides, width):
    for axis, dim in sides:
        peers, length = (lax.axis_size(axis), x.shape[dim])
        up = [(i, (i + 1) % peers) for i in range(peers - 1)]
        down = [(j, i) for i, j in up]
        last = lax.slice_in_dim(x, length - width, length, axis=dim)
        first = lax.slice_in_dim(x, 0, width, axis=dim)
        before = lax.ppermute(last, axis, up)
        after = lax.ppermute(first, axis, down)
        x = jnp.concatenate([before, x, after], axis=dim)
    return x


def from_behind(x, axis, by):
    peers = lax.axis_size(axis)
    pairs = [(i, i + by) for i in range(peers) if 0 <= i + by < peers]
    return lax.ppermute(x, axis, pairs)


def direction_shift(course):
    return (course // 2 + 1) * (1 - 2 * (course % 2))


def offset_laplace(padded):
    return smooth_weight * (2.0 * padded[:, 1:-1] - padded[:, :-2] - padded[:, 2:])


def smoothing(field):
    padded = padded_2(field, (("off", 1),), 1)
    smoothed = offset_laplace(padded)
    return smoothed


def deliver(outgoing):
    arrived = [None] * (2 * REACH)
    for course in range(2 * REACH):
        arrived[course] = from_behind(outgoing[course], "mid", direction_shift(course))
    return arrived


def give_back(returning):
    landed = [None] * (2 * REACH)
    for course in range(2 * REACH):
        landed[course] = from_behind(returning[course], "mid", -direction_shift(course))
    return landed


def shards_by_tile(
    traces, kernels, send_list, aper_slot, aper_pattern, trace_bin, trace_count
):
    off_dev = NOFF // lax.axis_size("off")
    trace_rows = traces.shape[0]
    samples = traces.shape[1]
    chosen_cells = send_list[0]
    send_count = chosen_cells.shape[1]
    slot_count = CELLS + 2 * REACH * send_count
    live_mask = jnp.arange(APER, dtype=jnp.int32)[:, None] < trace_count[None, :]
    row_index = (aper_slot * off_dev + trace_bin[None, :]).reshape(-1)
    pattern_ids = jnp.arange(PATTERNS, dtype=jnp.int32)[:, None, None]
    chooser = ((aper_pattern[None] == pattern_ids) & live_mask[None]).astype(
        jnp.bfloat16
    )
    pick_rows = (
        aper_pattern * trace_rows + jnp.arange(trace_rows, dtype=jnp.int32)[None, :]
    ).reshape(-1)
    live_column = live_mask.reshape(-1, 1).astype(jnp.float32)

    def forward(field_bf):
        outgoing = [field_bf[chosen_cells[course]] for course in range(2 * REACH)]
        arrived = deliver(outgoing)
        slot_rows = jnp.concatenate([field_bf] + arrived, 0).reshape(-1, samples)
        blocks = slot_rows[row_index].reshape(APER, trace_rows, samples)
        pattern_sums = jnp.einsum(
            "pjt,jtn->ptn", chooser, blocks, preferred_element_type=jnp.float32
        ).astype(jnp.bfloat16)
        return jnp.einsum(
            "ptn,pnm->tm", pattern_sums, kernels, preferred_element_type=jnp.float32
        )

    def adjoint(values_bf):
        spread = jnp.einsum(
            "tm,pnm->ptn", values_bf, kernels, preferred_element_type=jnp.float32
        ).reshape(-1, samples)
        entries = spread[pick_rows] * live_column
        slot_sums = (
            jnp.zeros((slot_count * off_dev, samples), jnp.float32)
            .at[row_index]
            .add(entries)
        )
        slot_sums = slot_sums.reshape(slot_count, off_dev, samples)
        returning = [
            slot_sums[CELLS + course * send_count : CELLS + (course + 1) * send_count]
            for course in range(2 * REACH)
        ]
        landed = give_back(returning)
        accumulated = slot_sums[:CELLS]
        for course in range(2 * REACH):
            accumulated = accumulated.at[chosen_cells[course]].add(landed[course])
        return accumulated

    def global_total(value):
        return lax.psum(value, ("mid", "off"))

    residual = adjoint(traces)
    direction = residual
    solution = jnp.zeros_like(residual)
    norm_now = global_total(jnp.sum(residual * residual))
    for iteration in range(ITERS):
        applied = adjoint(
            forward(direction.astype(jnp.bfloat16)).astype(jnp.bfloat16)
        ) + smoothing(direction)
        step_size = norm_now / global_total(jnp.sum(direction * applied))
        solution = solution + step_size * direction
        residual = residual - step_size * applied
        if iteration + 1 < ITERS:
            norm_next = global_total(jnp.sum(residual * residual))
            direction = residual + norm_next / norm_now * direction
            norm_now = norm_next
    return (solution, residual)


def path_rank(m, tiles):
    return m ^ ((m >> 1) & 1) if tiles % 4 == 0 else m


def lay_out(chunks_ref, out_refs):
    place = lax.axis_index("mid")
    for i, out_ref in enumerate(out_refs):
        out_ref[...] = chunks_ref[place ^ i]


def gather_in(landed_refs, chunks_ref):
    place = lax.axis_index("mid")
    for i, landed_ref in enumerate(landed_refs):
        chunks_ref[place ^ i] = landed_ref[...]


def swapped(chunks):
    peers = range(len(chunks))
    return chunks[:1] + [
        lax.ppermute(chunk, "mid", [(m, m ^ i) for m in peers])
        for i, chunk in enumerate(chunks)
        if i
    ]


def flipped():
    return lax.axis_index("off") % 2 > 0


def own_block(tiles):
    block = path_rank(lax.axis_index("mid"), tiles)
    return jnp.where(flipped(), tiles - 1 - block, block)


def dot_back(rows, kernel):
    return lax.dot_general(
        rows, kernel, (((1,), (1,)), ((), ())), preferred_element_type=jnp.float32
    )


SLOT, PATTERN, WITHIN, COUNT, FLAG = 0, APER, 4, 5, 6


def share_kernel(
    tiles, bins, room, sends_arg, slot_arg, pattern_arg, bin_arg, count_arg, traces_arg,
    out_ref, sends_ref, slot_ref, pattern_ref, bin_ref, count_ref, traces_ref,
    staged,
):
    rows, samples = traces_ref.shape
    stages = [
        pltpu.make_async_copy(arg, ref, staged.at[i])
        for i, (arg, ref) in enumerate(
            [
                (bin_arg, bin_ref),
                (slot_arg, slot_ref),
                (pattern_arg, pattern_ref),
                (count_arg, count_ref),
                (sends_arg, sends_ref),
                (traces_arg, traces_ref),
            ]
        )
    ]
    for stage in stages:
        stage.start()
    stages[0].wait()
    offset_bin = bin_ref[...]
    block = lax.div(offset_bin, bins)
    within = offset_bin - block * bins
    chunk = path_rank(jnp.where(flipped(), tiles - 1 - block, block), tiles)
    belongs = lax.broadcasted_iota(jnp.int32, (tiles, rows), 0) == chunk
    belongs = jnp.where(belongs, 1.0, 0.0)
    earlier = lax.broadcasted_iota(jnp.int32, (rows, rows), 0) < (
        lax.broadcasted_iota(jnp.int32, (rows, rows), 1)
    )
    rank = jnp.dot(
        belongs.astype(jnp.bfloat16),
        jnp.where(earlier, 1.0, 0.0).astype(jnp.bfloat16),
        preferred_element_type=jnp.float32,
    )
    rank = jnp.sum(rank * belongs, 0, keepdims=True).astype(jnp.int32)
    full = jnp.max(rank, axis=1, keepdims=True) >= room
    target = jnp.where(rank < room, chunk * room + rank, -1)
    picks = lax.broadcasted_iota(jnp.int32, (tiles * room, rows), 0) == target
    picks = jnp.where(picks, 1.0, 0.0).astype(jnp.bfloat16)
    place = lax.axis_index("mid")
    lane = lax.broadcasted_iota(jnp.int32, (1, LANES), 1)
    target = chunk * LANES + lax.rem(place, TOGETHER) * room + rank
    chosen = lax.broadcasted_iota(jnp.int32, (tiles * LANES, rows), 0) == (
        jnp.where(rank < room, target, -1)
    )
    chosen = jnp.where(chosen, 1.0, 0.0).astype(jnp.bfloat16)
    for stage in stages[1:5]:
        stage.wait()
    lists = jnp.concatenate(
        [
            slot_ref[...].astype(jnp.float32),
            pattern_ref[...].astype(jnp.float32),
            jnp.zeros((WITHIN, rows), jnp.float32),
            within.astype(jnp.float32),
            count_ref[...].astype(jnp.float32),
            jnp.zeros((APER - COUNT - 1, rows), jnp.float32),
        ],
        0,
    ).astype(jnp.bfloat16)
    lists = dot_back(lists, chosen)
    _, courses, send = sends_ref.shape
    line = lax.broadcasted_iota(jnp.int32, (2 * APER, LANES), 0)
    sent = jnp.zeros((2 * APER, LANES), jnp.int32)
    for course in range(courses):
        reader = lax.rem(place + direction_shift(course) + TOGETHER, TOGETHER)
        here = lax.div(lane, room) == reader
        for m in range(send):
            value = jnp.where(here, sends_ref[0, course, m], 0)
            sent += jnp.where(line == sent_row(course, send) + m, value, 0)
    past = lax.div(lane, room) == lax.rem(place + 1, TOGETHER)
    sent += jnp.where(past & (line == FLAG) & full, 1, 0)
    sent = sent.astype(jnp.float32)
    pieces = samples // LANES
    for m in range(tiles):
        own = lists[:, m * LANES : (m + 1) * LANES]
        moved = pltpu.roll(own[2 * APER :], room, 1)
        out_ref[m, pieces * room :] = (
            own[: 2 * APER] + jnp.concatenate([moved, jnp.zeros_like(moved)], 0) + sent
        ).astype(jnp.bfloat16)
    stages[5].wait()
    picked = jnp.dot(picks, traces_ref[...], preferred_element_type=jnp.float32)
    picked = picked.reshape(tiles, room, samples).astype(jnp.bfloat16)
    for i in range(pieces):
        out_ref[:, i * room : (i + 1) * room] = picked[:, :, i * LANES : (i + 1) * LANES]


def sent_row(course, send):
    return send if course == 3 else 0


def fill_picks(tiles, bins, send, landed_ref, picks_ref):
    flags = 0
    keys = lax.broadcasted_iota(jnp.int32, (KEYS, LANES), 0)
    member = lax.div(lax.broadcasted_iota(jnp.int32, (1, LANES), 1), ROOM)
    blocks = [
        landed_ref[tile, -2 * APER :].astype(jnp.float32).astype(jnp.int32)
        for tile in range(tiles)
    ]
    for group in range(tiles // TOGETHER):
        readers = range(group * TOGETHER, (group + 1) * TOGETHER)
        lists, moved = 0, 0
        for tile in readers:
            lists += jnp.where(member == tile % TOGETHER, blocks[tile], 0)
            past = member == (tile + 1) % TOGETHER
            moved += jnp.where(past, blocks[tile][:APER], 0)
        moved = pltpu.roll(moved, LANES - ROOM, 1)
        flags += moved[FLAG : FLAG + 1]
        within, count = moved[WITHIN : WITHIN + 1], moved[COUNT : COUNT + 1]
        wanted = []
        for region in range(2 * REACH + 1):
            course = region - 1
            shift = direction_shift(course) if region else 0
            owners = [tile - shift for tile in readers if 0 <= tile - shift < tiles]
            sent = 0
            for owner in owners if region else ():
                row = sent_row(course, send)
                values = blocks[owner][row : row + send]
                sent += jnp.where(member == (owner + shift) % TOGETHER, values, 0)
            for entry in range(region, APER, 2 * REACH + 1):
                cell = lists[SLOT + entry : SLOT + entry + 1]
                if region:
                    place = cell - (CELLS + course * send)
                    cell = sent[:1]
                    for other in range(1, send):
                        cell = jnp.where(place == other, sent[other : other + 1], cell)
                pattern = lists[PATTERN + entry : PATTERN + entry + 1]
                key = jnp.where(count > entry, pattern * CELLS + cell, -1)
                for owner in owners:
                    there = member == (owner + shift) % TOGETHER
                    wanted.append((owner, jnp.where(there, key, -1)))
        for tile in range(tiles):
            for b in range(bins):
                total = jnp.zeros((KEYS, LANES), jnp.float32)
                for owner, key in wanted:
                    if owner == tile:
                        hit = keys == jnp.where(within == b, key, -1)
                        total += jnp.where(hit, 1.0, 0.0)
                picks_ref[b, :, tile, :, group * LANES : (group + 1) * LANES] = (
                    total.reshape(PATTERNS, CELLS, LANES)
                )
    return flags.astype(jnp.float32)


def two_parts(x):
    high = x.astype(jnp.bfloat16)
    low = (x - high.astype(jnp.float32)).astype(jnp.bfloat16)
    return jnp.concatenate([high, low], 0)


def store_parts(parts_ref, b, x):
    shape = (PATTERNS, *parts_ref.shape[3:])
    high = x.astype(jnp.bfloat16)
    parts_ref[:, 0, b] = high.reshape(shape)
    low = (x - high.astype(jnp.float32)).astype(jnp.bfloat16)
    parts_ref[:, 1, b] = low.reshape(shape)


def back_projected(kernels_ref, parts_ref):
    _, _, bins, side, samples = parts_ref.shape
    rows = bins * side
    both = jnp.zeros((2 * rows, samples), jnp.float32)
    for p in range(PATTERNS):
        both += dot_back(parts_ref[p].reshape(2 * rows, samples), kernels_ref[p])
    return both[:rows] + both[rows:]


def project(field, kernels_ref, rows_ref):
    bins, _, side, samples = rows_ref.shape
    rows = bins * side
    for p in range(PATTERNS):
        u = jnp.dot(field, kernels_ref[p], preferred_element_type=jnp.float32)
        u = u[:rows] + u[rows:] if field.shape[0] > rows else u
        rows_ref[:, p] = u.astype(jnp.bfloat16).reshape(bins, side, samples)


def mixed(gram_ref, rows_ref, b):
    _, _, side, samples = rows_ref.shape
    return jnp.dot(
        gram_ref[b],
        rows_ref[b].reshape(PATTERNS * side, samples),
        preferred_element_type=jnp.float32,
    )


def smoothed(field, before, after):
    side = before.shape[0]
    lower = jnp.concatenate([before, field[:-side]], 0)
    upper = jnp.concatenate([field[side:], after], 0)
    return smooth_weight * (2.0 * field - lower - upper)


def first_kernel(
    tiles, bins, send, landed_ref, kernels_arg,
    start_ref, local_ref, gram_ref, up_ref, down_ref, full_ref, kernels_ref,
    picks_ref, rows_ref, parts_ref, arrived,
):
    copies = [
        pltpu.make_async_copy(kernels_arg.at[p], kernels_ref.at[p], arrived.at[p])
        for p in range(PATTERNS)
    ]
    for copy in copies:
        copy.start()
    side = tiles * CELLS
    samples = start_ref.shape[1]
    flags = total(fill_picks(tiles, bins, send, landed_ref, picks_ref))
    full_ref[...] = jnp.broadcast_to(flags, full_ref.shape)
    traces = jnp.concatenate(
        [
            landed_ref[:, i * ROOM : (i + 1) * ROOM].reshape(-1, LANES)
            for i in range(samples // LANES)
        ],
        1,
    )
    for b in range(bins):
        picks = picks_ref[b].reshape(PATTERNS * side, -1).astype(jnp.bfloat16)
        gram_ref[b] = dot_back(picks, picks).astype(jnp.bfloat16)
        sums = jnp.dot(picks, traces, preferred_element_type=jnp.float32)
        parts_ref[:, 0, b] = sums.astype(jnp.bfloat16).reshape(PATTERNS, side, samples)
    start = jnp.zeros((bins * side, samples), jnp.float32)
    for p in range(PATTERNS):
        copies[p].wait()
        start += dot_back(parts_ref[p, 0].reshape(bins * side, samples), kernels_ref[p])
    start = start.astype(jnp.bfloat16)
    start_ref[...] = start
    field = start.astype(jnp.float32)
    nothing = jnp.zeros((side, samples), jnp.float32)
    project(start, kernels_ref, rows_ref)
    for b in range(bins):
        store_parts(parts_ref, b, mixed(gram_ref, rows_ref, b))
    local = back_projected(kernels_ref, parts_ref) + smoothed(field, nothing, nothing)
    local_ref[...] = local
    up_ref[:side] = start[-side:]
    up_ref[side:] = local[-side:].astype(jnp.bfloat16)
    down_ref[:side] = start[:side]
    down_ref[side:] = local[:side].astype(jnp.bfloat16)


FULL, STEP, GROW = 4, 5, 6


def ahead_kernel(local_ref, gram_ref, kernels_ref, rows_ref, mixed_ref):
    project(two_parts(local_ref[...]), kernels_ref, rows_ref)
    for b in range(rows_ref.shape[0]):
        mixed_ref[b] = mixed(gram_ref, rows_ref, b)


def second_kernel(
    tiles, offs, start_ref, local_ref, gram_ref, kernels_ref, before_ref, after_ref,
    full_ref, ahead_ref, mixed_ref,
    once_ref, smooth_ref, parts_ref, sums_ref, rows_ref,
):
    bins, _, side, samples = rows_ref.shape
    start = start_ref[...].astype(jnp.float32)
    place = lax.axis_index("off") * tiles + own_block(tiles)
    ends = [place > 0, place < offs * tiles - 1]
    beyond, outer = [], []
    for end, (edge_ref, own) in enumerate(
        [(before_ref, start[:side]), (after_ref, start[-side:])]
    ):
        edge = edge_ref[...].astype(jnp.float32)
        there = jnp.where(ends[end], smooth_weight, 0.0)
        beyond.append(-smooth_weight * edge[:side])
        outer.append(edge[side:] - there * own)
    inner = [jnp.zeros(((bins - 2) * side, samples), jnp.float32)] if bins > 2 else []
    beyond = jnp.concatenate([beyond[0], *inner, beyond[1]], 0)
    once = local_ref[...] + beyond
    once_ref[...] = once
    smooth = smoothed(once, outer[0], outer[1])
    smooth_ref[...] = smooth
    project(beyond.astype(jnp.bfloat16), kernels_ref, rows_ref)
    square = 0.0
    for b in range(bins):
        both = mixed_ref[b] + mixed(gram_ref, rows_ref, b)
        store_parts(parts_ref, b, both)
        rows = ahead_ref[b].astype(jnp.float32) + rows_ref[b].astype(jnp.float32)
        square += total(rows.reshape(both.shape) * both)
    products = [
        total(start * start),
        total(start * once),
        total(once * once),
        total(once * smooth) + square,
    ]
    lane = lax.broadcasted_iota(jnp.int32, (1, LANES), 1)
    line = jnp.where(lane == FULL, full_ref[:1], 0.0)
    for i, product in enumerate(products):
        line = jnp.where(lane == i, product, line)
    sums_ref[...] = jnp.broadcast_to(line, sums_ref.shape)


def last_kernel(parts_ref, kernels_ref, out_ref):
    out_ref[...] = back_projected(kernels_ref, parts_ref)


def pack_kernel(sums_ref, start_ref, once_ref, smooth_ref, normal_ref, *refs):
    full_ref, *out_refs, out_ref = refs
    tiles = len(out_refs)
    full_ref[0] = jnp.sum(sums_ref[:1, FULL : FULL + 1]).astype(jnp.int32)
    ss, so, oo = (sums_ref[:1, i : i + 1] for i in range(3))
    step, grow = own_scales(ss, so, oo)
    start, once = start_ref[...].astype(jnp.float32), once_ref[...]
    twice = normal_ref[...] + smooth_ref[...]
    row = 0
    for field in (start, start - step * once, grow * once - step * twice):
        samples = field.shape[1]
        field = field.reshape(-1, tiles, CELLS, samples)
        size = field.shape[0] * CELLS
        for i in range(0, samples, LANES):
            for tile in range(tiles):
                piece = field[:, tile, :, i : i + LANES].reshape(size, LANES)
                out_ref[tile, row : row + size] = piece.astype(jnp.bfloat16)
            row += size
    lane = lax.broadcasted_iota(jnp.int32, (1, LANES), 1)
    rest = jnp.where(lane == STEP, step, sums_ref[:1])
    rest = jnp.where(lane == GROW, grow, rest)
    line = lax.broadcasted_iota(jnp.int32, (16, LANES), 0)
    parts = jnp.zeros((16, LANES), jnp.float32)
    for i in range(3):
        part = rest.astype(jnp.bfloat16).astype(jnp.float32)
        rest = rest - part
        parts = jnp.where(line == i, part, parts)
    for tile in range(tiles):
        out_ref[tile, row:] = parts.astype(jnp.bfloat16)
    lay_out(out_ref, out_refs)


def total(x):
    return jnp.sum(jnp.sum(x, 0, keepdims=True), 1, keepdims=True)


def own_scales(ss, so, oo):
    step = ss / so
    step = jnp.where(step > 0.0, jnp.clip(step, 1e-8, 1e3), 1.0)
    grow = step * step * oo / ss
    return step, jnp.where(grow > 0.0, jnp.clip(grow, 0.0, 1e3), 1.0)


def place_kernel(bins, *refs):
    *landed_refs, solution_ref, residual_ref, landed_ref = refs
    gather_in(landed_refs, landed_ref)
    tiles, length, _ = landed_ref.shape
    size = bins * CELLS
    samples = solution_ref.shape[2]
    pieces = samples // LANES

    def line_of(source):
        parts = landed_ref[source, length - 16 :].astype(jnp.float32)
        return jnp.sum(parts, 0, keepdims=True)

    def vector(source, i):
        part = [
            landed_ref[source, (i * pieces + j) * size : (i * pieces + j + 1) * size]
            for j in range(pieces)
        ]
        return jnp.concatenate(part, 1).astype(jnp.float32)

    sums = sum(line_of(tile) for tile in range(tiles))
    ss, so, oo, ot = (sums[:, i : i + 1] for i in range(4))
    step_0 = ss / so
    norm_1 = step_0 * step_0 * oo - ss
    grow = 1.0 + norm_1 / ss
    step_1 = norm_1 / (grow * grow * so - 2.0 * step_0 * grow * oo + step_0 * step_0 * ot)
    near = step_0 + step_1 * grow
    far = step_1 * step_0
    fields = [[], []]
    for block in range(tiles):
        source = jnp.where(
            flipped(), path_rank(tiles - 1 - block, tiles), path_rank(block, tiles)
        )
        line = line_of(source)
        inverse = 1.0 / line[:, STEP : STEP + 1]
        there = line[:, GROW : GROW + 1]
        start, first, second = (vector(source, i) for i in range(3))
        far_once = far * inverse
        near_once = near * inverse - far_once * there * inverse
        solution = (near - far_once) * start + far_once * first
        residual = (1.0 - near_once) * start + near_once * first - far_once * second
        fields[0].append(solution.reshape(bins, CELLS, samples))
        fields[1].append(residual.reshape(bins, CELLS, samples))
    solution_ref[...] = jnp.swapaxes(jnp.concatenate(fields[0], 0), 0, 1)
    residual_ref[...] = jnp.swapaxes(jnp.concatenate(fields[1], 0), 0, 1)


def copy_kernel(*refs):
    *refs, arrived = refs
    half = len(refs) // 2
    copies = [
        pltpu.make_async_copy(refs[i], refs[half + i], arrived.at[i]) for i in range(half)
    ]
    for copy in copies:
        copy.start()
    for copy in copies:
        copy.wait()


VMEM = pl.BlockSpec(memory_space=pltpu.VMEM)
HBM = pl.BlockSpec(memory_space=pltpu.HBM)


SMEM = pl.BlockSpec(memory_space=pltpu.SMEM)


def local_call(kernel, name, in_specs, out_shape, scratch=(), out_specs=None, cost=0):
    return pl.pallas_call(
        kernel,
        out_shape=out_shape,
        in_specs=in_specs,
        out_specs=out_specs or jax.tree.map(lambda _: VMEM, out_shape),
        scratch_shapes=list(scratch),
        cost_estimate=pl.CostEstimate(
            flops=cost, bytes_accessed=cost // 256, transcendentals=0
        )
        if cost
        else None,
        compiler_params=pltpu.CompilerParams(vmem_limit_bytes=32 * 1024 * 1024),
        name=name,
    )


def shards_by_bin(
    traces, kernels, send_list, aper_slot, aper_pattern, trace_bin, trace_count
):
    tiles, offs = lax.axis_size("mid"), lax.axis_size("off")
    bins = NOFF // offs // tiles
    trace_rows, samples = traces.shape
    send = send_list.shape[2]
    rows = bins * tiles * CELLS
    side = tiles * CELLS
    sums = bins * (CELLS + 2 * REACH * send)

    def array(*shape, dtype=jnp.float32):
        return jax.ShapeDtypeStruct(shape, dtype)

    bf16 = functools.partial(array, dtype=jnp.bfloat16)
    in_hbm = functools.partial(
        pltpu.with_memory_space_constraint, memory_space=pltpu.HBM
    )
    lists = (send_list, aper_slot, aper_pattern, trace_bin, trace_count)
    shared = local_call(
        functools.partial(share_kernel, tiles, bins, ROOM),
        "share",
        [HBM] * 6,
        bf16(tiles, samples // LANES * ROOM + 2 * APER, LANES),
        [
            pltpu.SMEM(send_list.shape, jnp.int32),
            pltpu.VMEM(aper_slot.shape, jnp.int32),
            pltpu.VMEM(aper_pattern.shape, jnp.int32),
            pltpu.VMEM((1, trace_rows), jnp.int32),
            pltpu.VMEM((1, trace_rows), jnp.int32),
            pltpu.VMEM(traces.shape, jnp.bfloat16),
            pltpu.SemaphoreType.DMA((6,)),
        ],
    )(
        in_hbm(send_list),
        in_hbm(aper_slot),
        in_hbm(aper_pattern),
        in_hbm(trace_bin[None]),
        in_hbm(trace_count[None]),
        in_hbm(traces),
    )
    landed = lax.all_to_all(shared, "mid", 0, 0)
    pattern_rows = pltpu.VMEM((bins, PATTERNS, side, samples), jnp.bfloat16)
    parts_type = bf16(PATTERNS, 2, bins, side, samples)
    start, local, gram, up, down, full, held = local_call(
        functools.partial(first_kernel, tiles, bins, send),
        "first",
        [VMEM, HBM],
        (
            bf16(rows, samples),
            array(rows, samples),
            bf16(bins, tiles * KEYS, tiles * KEYS),
            bf16(2 * side, samples),
            bf16(2 * side, samples),
            array(8, LANES),
            bf16(*kernels.shape),
        ),
        [
            pltpu.VMEM((bins, PATTERNS, tiles, CELLS, tiles * ROOM), jnp.float32),
            pattern_rows,
            pltpu.VMEM(parts_type.shape, parts_type.dtype),
            pltpu.SemaphoreType.DMA((PATTERNS,)),
        ],
    )(landed, in_hbm(kernels))

    path = [path_rank(m, tiles) for m in range(tiles)]
    chain = [m * offs + o for o in range(offs) for m in (path[::-1] if o % 2 else path)]
    pairs = list(zip(chain[:-1], chain[1:]))
    before = lax.ppermute(up, ("mid", "off"), pairs)
    after = lax.ppermute(down, ("mid", "off"), [(j, i) for i, j in pairs])

    flops = 2 * rows * PATTERNS * samples * samples
    ahead, mixed_ahead = local_call(
        ahead_kernel,
        "ahead",
        [VMEM] * 3,
        (bf16(*pattern_rows.shape), array(bins, PATTERNS * side, samples)),
        cost=3 * flops,
    )(local, gram, held)
    field = array(rows, samples)
    once, smooth, parts, products = local_call(
        functools.partial(second_kernel, tiles, offs),
        "second",
        [VMEM] * 9,
        (field, field, parts_type, array(8, LANES)),
        [pattern_rows],
        cost=2 * flops,
    )(start, local, gram, held, before, after, full, ahead, mixed_ahead)

    projected = local_call(last_kernel, "last", [VMEM] * 2, field, cost=2 * flops)(
        parts, held
    )
    step = 1
    while step < offs:
        partners = [(i, i ^ step) for i in range(offs)]
        products = products + lax.ppermute(products, "off", partners)
        step *= 2
    chunk = bf16(samples // LANES * 3 * bins * CELLS + 16, LANES)
    chunks = pltpu.VMEM((tiles, *chunk.shape), chunk.dtype)
    full, *packed = local_call(
        pack_kernel,
        "pack",
        [VMEM] * 5,
        (array(1, dtype=jnp.int32), *[chunk] * tiles),
        [chunks],
        out_specs=(SMEM, *[VMEM] * tiles),
    )(products, start, once, smooth, projected)
    landed = swapped(packed)

    def again():
        arguments = [in_hbm(x) for x in (traces, kernels, *lists[:3])]
        arguments += [in_hbm(x[None]) for x in lists[3:]]
        *copies, bins_again, count_again = local_call(
            copy_kernel,
            "again",
            [HBM] * len(arguments),
            tuple(array(*x.shape, dtype=x.dtype) for x in arguments),
            [pltpu.SemaphoreType.DMA((len(arguments),))],
            out_specs=(HBM,) * len(arguments),
        )(*arguments)
        return *copies, bins_again[0], count_again[0]

    def placed():
        out_type = pltpu.HBM((CELLS, bins * tiles, samples), jnp.float32)
        return local_call(
            functools.partial(place_kernel, bins),
            "place",
            [VMEM] * tiles,
            (out_type, out_type),
            [chunks],
            out_specs=(VMEM, VMEM),
        )(*landed)

    return lax.cond(full[0] > 0, lambda: shards_by_tile(*again()), placed)


def fits_by_bin(tiles, offs, send, trace_rows, samples):
    return (
        (NOFF // offs) % (2 * tiles) == 0
        and offs & (offs - 1) == 0
        and tiles & (tiles - 1) == 0
        and tiles % TOGETHER == 0
        and send == WITHIN
        and trace_rows == LANES
        and samples % LANES == 0
    )


def solution(mesh):
    in_specs = (
        P(("mid", "off"), None),
        P(),
        P("mid", None, None),
        P(None, ("mid", "off")),
        P(None, ("mid", "off")),
        P(("mid", "off")),
        P(("mid", "off")),
    )
    out_specs = (P("mid", "off", None), P("mid", "off", None))

    def shards(traces, kernels, send_list, *lists):
        fits = fits_by_bin(
            mesh.shape["mid"], mesh.shape["off"], send_list.shape[2], *traces.shape
        )
        form = shards_by_bin if fits else shards_by_tile
        return form(traces, kernels, send_list, *lists)

    return jax.shard_map(
        shards, mesh=mesh, in_specs=in_specs, out_specs=out_specs, check_vma=False
    )
```

```python
import functools

import jax
import jax.numpy as jnp
from jax import lax
from jax.experimental import pallas as pl
from jax.experimental.pallas import tpu as pltpu
from jax.sharding import PartitionSpec as P

NOFF = 64
PATTERNS = 8
REACH = 2
APER = 8
ITERS = 2
CELLS = 8
KEYS = PATTERNS * CELLS
ROOM = 32
LANES = 128
TOGETHER = LANES // ROOM


smooth_weight = 2.0


def padded_2(x, sides, width):
    for axis, dim in sides:
        peers, length = (lax.axis_size(axis), x.shape[dim])
        up = [(i, (i + 1) % peers) for i in range(peers - 1)]
        down = [(j, i) for i, j in up]
        last = lax.slice_in_dim(x, length - width, length, axis=dim)
        first = lax.slice_in_dim(x, 0, width, axis=dim)
        before = lax.ppermute(last, axis, up)
        after = lax.ppermute(first, axis, down)
        x = jnp.concatenate([before, x, after], axis=dim)
    return x


def from_behind(x, axis, by):
    peers = lax.axis_size(axis)
    pairs = [(i, i + by) for i in range(peers) if 0 <= i + by < peers]
    return lax.ppermute(x, axis, pairs)


def direction_shift(course):
    return (course // 2 + 1) * (1 - 2 * (course % 2))


def offset_laplace(padded):
    return smooth_weight * (2.0 * padded[:, 1:-1] - padded[:, :-2] - padded[:, 2:])


def smoothing(field):
    padded = padded_2(field, (("off", 1),), 1)
    smoothed = offset_laplace(padded)
    return smoothed


def deliver(outgoing):
    arrived = [None] * (2 * REACH)
    for course in range(2 * REACH):
        arrived[course] = from_behind(outgoing[course], "mid", direction_shift(course))
    return arrived


def give_back(returning):
    landed = [None] * (2 * REACH)
    for course in range(2 * REACH):
        landed[course] = from_behind(returning[course], "mid", -direction_shift(course))
    return landed


def shards_by_tile(
    traces, kernels, send_list, aper_slot, aper_pattern, trace_bin, trace_count
):
    off_dev = NOFF // lax.axis_size("off")
    trace_rows = traces.shape[0]
    samples = traces.shape[1]
    chosen_cells = send_list[0]
    send_count = chosen_cells.shape[1]
    slot_count = CELLS + 2 * REACH * send_count
    live_mask = jnp.arange(APER, dtype=jnp.int32)[:, None] < trace_count[None, :]
    row_index = (aper_slot * off_dev + trace_bin[None, :]).reshape(-1)
    pattern_ids = jnp.arange(PATTERNS, dtype=jnp.int32)[:, None, None]
    chooser = ((aper_pattern[None] == pattern_ids) & live_mask[None]).astype(
        jnp.bfloat16
    )
    pick_rows = (
        aper_pattern * trace_rows + jnp.arange(trace_rows, dtype=jnp.int32)[None, :]
    ).reshape(-1)
    live_column = live_mask.reshape(-1, 1).astype(jnp.float32)

    def forward(field_bf):
        outgoing = [field_bf[chosen_cells[course]] for course in range(2 * REACH)]
        arrived = deliver(outgoing)
        slot_rows = jnp.concatenate([field_bf] + arrived, 0).reshape(-1, samples)
        blocks = slot_rows[row_index].reshape(APER, trace_rows, samples)
        pattern_sums = jnp.einsum(
            "pjt,jtn->ptn", chooser, blocks, preferred_element_type=jnp.float32
        ).astype(jnp.bfloat16)
        return jnp.einsum(
            "ptn,pnm->tm", pattern_sums, kernels, preferred_element_type=jnp.float32
        )

    def adjoint(values_bf):
        spread = jnp.einsum(
            "tm,pnm->ptn", values_bf, kernels, preferred_element_type=jnp.float32
        ).reshape(-1, samples)
        entries = spread[pick_rows] * live_column
        slot_sums = (
            jnp.zeros((slot_count * off_dev, samples), jnp.float32)
            .at[row_index]
            .add(entries)
        )
        slot_sums = slot_sums.reshape(slot_count, off_dev, samples)
        returning = [
            slot_sums[CELLS + course * send_count : CELLS + (course + 1) * send_count]
            for course in range(2 * REACH)
        ]
        landed = give_back(returning)
        accumulated = slot_sums[:CELLS]
        for course in range(2 * REACH):
            accumulated = accumulated.at[chosen_cells[course]].add(landed[course])
        return accumulated

    def global_total(value):
        return lax.psum(value, ("mid", "off"))

    residual = adjoint(traces)
    direction = residual
    solution = jnp.zeros_like(residual)
    norm_now = global_total(jnp.sum(residual * residual))
    for iteration in range(ITERS):
        applied = adjoint(
            forward(direction.astype(jnp.bfloat16)).astype(jnp.bfloat16)
        ) + smoothing(direction)
        step_size = norm_now / global_total(jnp.sum(direction * applied))
        solution = solution + step_size * direction
        residual = residual - step_size * applied
        if iteration + 1 < ITERS:
            norm_next = global_total(jnp.sum(residual * residual))
            direction = residual + norm_next / norm_now * direction
            norm_now = norm_next
    return (solution, residual)


def path_rank(m, tiles):
    return m ^ ((m >> 1) & 1) if tiles % 4 == 0 else m


def turns(peers):
    far, near = range(peers // 2, peers), range(peers // 2)
    return [i for pair in zip(near, far) for i in pair]


def lay_out(chunks_ref, out_refs):
    place = lax.axis_index("mid")
    for i, out_ref in zip(turns(len(out_refs)), out_refs):
        out_ref[...] = chunks_ref[place ^ i]


def gather_in(landed_refs, chunks_ref):
    place = lax.axis_index("mid")
    for i, landed_ref in zip(turns(len(landed_refs)), landed_refs):
        chunks_ref[place ^ i] = landed_ref[...]


def swapped(chunks):
    peers = range(len(chunks))
    return [
        lax.ppermute(chunk, "mid", [(m, m ^ i) for m in peers]) if i else chunk
        for i, chunk in zip(turns(len(chunks)), chunks)
    ]


def flipped():
    return lax.axis_index("off") % 2 > 0


def own_block(tiles):
    block = path_rank(lax.axis_index("mid"), tiles)
    return jnp.where(flipped(), tiles - 1 - block, block)


def dot_back(rows, kernel):
    return lax.dot_general(
        rows, kernel, (((1,), (1,)), ((), ())), preferred_element_type=jnp.float32
    )


SLOT, PATTERN, WITHIN, COUNT, FLAG = 0, APER, 4, 5, 6


def share_kernel(
    tiles, bins, room, sends_arg, slot_arg, pattern_arg, bin_arg, count_arg, traces_arg,
    kernels_arg, out_ref, kernels_ref, sends_ref, slot_ref, pattern_ref, bin_ref, count_ref, traces_ref,
    staged, arrived,
):
    rows, samples = traces_ref.shape
    stages = [
        pltpu.make_async_copy(arg, ref, staged.at[i])
        for i, (arg, ref) in enumerate(
            [
                (bin_arg, bin_ref),
                (slot_arg, slot_ref),
                (pattern_arg, pattern_ref),
                (count_arg, count_ref),
                (sends_arg, sends_ref),
                (traces_arg, traces_ref),
            ]
        )
    ]
    kernels = pltpu.make_async_copy(
        kernels_arg.at[: PATTERNS // 2], kernels_ref, arrived
    )
    for stage in stages + [kernels]:
        stage.start()
    stages[0].wait()
    offset_bin = bin_ref[...]
    block = lax.div(offset_bin, bins)
    within = offset_bin - block * bins
    chunk = path_rank(jnp.where(flipped(), tiles - 1 - block, block), tiles)
    belongs = lax.broadcasted_iota(jnp.int32, (tiles, rows), 0) == chunk
    belongs = jnp.where(belongs, 1.0, 0.0)
    earlier = lax.broadcasted_iota(jnp.int32, (rows, rows), 0) < (
        lax.broadcasted_iota(jnp.int32, (rows, rows), 1)
    )
    rank = jnp.dot(
        belongs.astype(jnp.bfloat16),
        jnp.where(earlier, 1.0, 0.0).astype(jnp.bfloat16),
        preferred_element_type=jnp.float32,
    )
    rank = jnp.sum(rank * belongs, 0, keepdims=True).astype(jnp.int32)
    full = jnp.max(rank, axis=1, keepdims=True) >= room
    target = jnp.where(rank < room, chunk * room + rank, -1)
    picks = lax.broadcasted_iota(jnp.int32, (tiles * room, rows), 0) == target
    picks = jnp.where(picks, 1.0, 0.0).astype(jnp.bfloat16)
    place = lax.axis_index("mid")
    lane = lax.broadcasted_iota(jnp.int32, (1, LANES), 1)
    target = chunk * LANES + lax.rem(place, TOGETHER) * room + rank
    chosen = lax.broadcasted_iota(jnp.int32, (tiles * LANES, rows), 0) == (
        jnp.where(rank < room, target, -1)
    )
    chosen = jnp.where(chosen, 1.0, 0.0).astype(jnp.bfloat16)
    for stage in stages[1:5]:
        stage.wait()
    lists = jnp.concatenate(
        [
            slot_ref[...].astype(jnp.float32),
            pattern_ref[...].astype(jnp.float32),
            jnp.zeros((WITHIN, rows), jnp.float32),
            within.astype(jnp.float32),
            count_ref[...].astype(jnp.float32),
            jnp.zeros((APER - COUNT - 1, rows), jnp.float32),
        ],
        0,
    ).astype(jnp.bfloat16)
    lists = dot_back(lists, chosen)
    _, courses, send = sends_ref.shape
    line = lax.broadcasted_iota(jnp.int32, (2 * APER, LANES), 0)
    sent = jnp.zeros((2 * APER, LANES), jnp.int32)
    for course in range(courses):
        reader = lax.rem(place + direction_shift(course) + TOGETHER, TOGETHER)
        here = lax.div(lane, room) == reader
        for m in range(send):
            value = jnp.where(here, sends_ref[0, course, m], 0)
            sent += jnp.where(line == sent_row(course, send) + m, value, 0)
    past = lax.div(lane, room) == lax.rem(place + 1, TOGETHER)
    sent += jnp.where(past & (line == FLAG) & full, 1, 0)
    sent = sent.astype(jnp.float32)
    pieces = samples // LANES
    for m in range(tiles):
        own = lists[:, m * LANES : (m + 1) * LANES]
        moved = pltpu.roll(own[2 * APER :], room, 1)
        out_ref[m, pieces * room :] = (
            own[: 2 * APER] + jnp.concatenate([moved, jnp.zeros_like(moved)], 0) + sent
        ).astype(jnp.bfloat16)
    stages[5].wait()
    picked = jnp.dot(picks, traces_ref[...], preferred_element_type=jnp.float32)
    picked = picked.reshape(tiles, room, samples).astype(jnp.bfloat16)
    for i in range(pieces):
        out_ref[:, i * room : (i + 1) * room] = picked[:, :, i * LANES : (i + 1) * LANES]
    kernels.wait()


def sent_row(course, send):
    return send if course == 3 else 0


def fill_picks(tiles, bins, send, landed_ref, picks_ref):
    flags = 0
    keys = lax.broadcasted_iota(jnp.int32, (KEYS, LANES), 0)
    member = lax.div(lax.broadcasted_iota(jnp.int32, (1, LANES), 1), ROOM)
    blocks = [
        landed_ref[tile, -2 * APER :].astype(jnp.float32).astype(jnp.int32)
        for tile in range(tiles)
    ]
    for group in range(tiles // TOGETHER):
        readers = range(group * TOGETHER, (group + 1) * TOGETHER)
        lists, moved = 0, 0
        for tile in readers:
            lists += jnp.where(member == tile % TOGETHER, blocks[tile], 0)
            past = member == (tile + 1) % TOGETHER
            moved += jnp.where(past, blocks[tile][:APER], 0)
        moved = pltpu.roll(moved, LANES - ROOM, 1)
        flags += moved[FLAG : FLAG + 1]
        within, count = moved[WITHIN : WITHIN + 1], moved[COUNT : COUNT + 1]
        wanted = []
        for region in range(2 * REACH + 1):
            course = region - 1
            shift = direction_shift(course) if region else 0
            owners = [tile - shift for tile in readers if 0 <= tile - shift < tiles]
            sent = 0
            for owner in owners if region else ():
                row = sent_row(course, send)
                values = blocks[owner][row : row + send]
                sent += jnp.where(member == (owner + shift) % TOGETHER, values, 0)
            for entry in range(region, APER, 2 * REACH + 1):
                cell = lists[SLOT + entry : SLOT + entry + 1]
                if region:
                    place = cell - (CELLS + course * send)
                    cell = sent[:1]
                    for other in range(1, send):
                        cell = jnp.where(place == other, sent[other : other + 1], cell)
                pattern = lists[PATTERN + entry : PATTERN + entry + 1]
                key = jnp.where(count > entry, pattern * CELLS + cell, -1)
                for owner in owners:
                    there = member == (owner + shift) % TOGETHER
                    wanted.append((owner, jnp.where(there, key, -1)))
        for tile in range(tiles):
            for b in range(bins):
                total = jnp.zeros((KEYS, LANES), jnp.float32)
                for owner, key in wanted:
                    if owner == tile:
                        hit = keys == jnp.where(within == b, key, -1)
                        total += jnp.where(hit, 1.0, 0.0)
                picks_ref[b, :, tile, :, group * LANES : (group + 1) * LANES] = (
                    total.reshape(PATTERNS, CELLS, LANES)
                )
    return flags.astype(jnp.float32)


def two_parts(x):
    high = x.astype(jnp.bfloat16)
    low = (x - high.astype(jnp.float32)).astype(jnp.bfloat16)
    return jnp.concatenate([high, low], 0)


def store_parts(parts_ref, b, x):
    shape = (PATTERNS, *parts_ref.shape[3:])
    high = x.astype(jnp.bfloat16)
    parts_ref[:, 0, b] = high.reshape(shape)
    low = (x - high.astype(jnp.float32)).astype(jnp.bfloat16)
    parts_ref[:, 1, b] = low.reshape(shape)


def kernel_of(kernels, p):
    half, place = divmod(p, PATTERNS // 2)
    return kernels[half][place]


def back_projected(kernels, parts_ref):
    _, _, bins, side, samples = parts_ref.shape
    rows = bins * side
    both = jnp.zeros((2 * rows, samples), jnp.float32)
    for p in range(PATTERNS):
        both += dot_back(
            parts_ref[p].reshape(2 * rows, samples), kernel_of(kernels, p)
        )
    return both[:rows] + both[rows:]


def project(field, kernels, rows_ref):
    bins, _, side, samples = rows_ref.shape
    rows = bins * side
    for p in range(PATTERNS):
        u = jnp.dot(field, kernel_of(kernels, p), preferred_element_type=jnp.float32)
        u = u[:rows] + u[rows:] if field.shape[0] > rows else u
        rows_ref[:, p] = u.astype(jnp.bfloat16).reshape(bins, side, samples)


def mixed(gram_ref, rows_ref, b):
    _, _, side, samples = rows_ref.shape
    return jnp.dot(
        gram_ref[b],
        rows_ref[b].reshape(PATTERNS * side, samples),
        preferred_element_type=jnp.float32,
    )


def smoothed(field, before, after):
    side = before.shape[0]
    lower = jnp.concatenate([before, field[:-side]], 0)
    upper = jnp.concatenate([field[side:], after], 0)
    return smooth_weight * (2.0 * field - lower - upper)


def first_kernel(
    tiles, bins, send, landed_ref, lower_ref, kernels_arg,
    start_ref, local_ref, gram_ref, up_ref, down_ref, full_ref, upper_ref,
    picks_ref, rows_ref, parts_ref, arrived,
):
    half = PATTERNS // 2
    copies = [
        pltpu.make_async_copy(kernels_arg.at[half + p], upper_ref.at[p], arrived.at[p])
        for p in range(half)
    ]
    for copy in copies:
        copy.start()
    kernels = (lower_ref, upper_ref)
    side = tiles * CELLS
    samples = start_ref.shape[1]
    flags = total(fill_picks(tiles, bins, send, landed_ref, picks_ref))
    full_ref[...] = jnp.broadcast_to(flags, full_ref.shape)
    traces = jnp.concatenate(
        [
            landed_ref[:, i * ROOM : (i + 1) * ROOM].reshape(-1, LANES)
            for i in range(samples // LANES)
        ],
        1,
    )
    for b in range(bins):
        picks = picks_ref[b].reshape(PATTERNS * side, -1).astype(jnp.bfloat16)
        gram_ref[b] = dot_back(picks, picks).astype(jnp.bfloat16)
        sums = jnp.dot(picks, traces, preferred_element_type=jnp.float32)
        parts_ref[:, 0, b] = sums.astype(jnp.bfloat16).reshape(PATTERNS, side, samples)
    start = jnp.zeros((bins * side, samples), jnp.float32)
    for p in range(PATTERNS):
        if p >= half:
            copies[p - half].wait()
        rows = parts_ref[p, 0].reshape(bins * side, samples)
        start += dot_back(rows, kernel_of(kernels, p))
    start = start.astype(jnp.bfloat16)
    start_ref[...] = start
    field = start.astype(jnp.float32)
    nothing = jnp.zeros((side, samples), jnp.float32)
    project(start, kernels, rows_ref)
    for b in range(bins):
        store_parts(parts_ref, b, mixed(gram_ref, rows_ref, b))
    local = back_projected(kernels, parts_ref) + smoothed(field, nothing, nothing)
    local_ref[...] = local
    up_ref[:side] = start[-side:]
    up_ref[side:] = local[-side:].astype(jnp.bfloat16)
    down_ref[:side] = start[:side]
    down_ref[side:] = local[:side].astype(jnp.bfloat16)


FULL, STEP, GROW = 4, 5, 6


def ahead_kernel(local_ref, gram_ref, lower_ref, upper_ref, rows_ref, mixed_ref):
    project(two_parts(local_ref[...]), (lower_ref, upper_ref), rows_ref)
    for b in range(rows_ref.shape[0]):
        mixed_ref[b] = mixed(gram_ref, rows_ref, b)


def second_kernel(
    tiles, offs, start_ref, local_ref, gram_ref, lower_ref, upper_ref, before_ref, after_ref,
    full_ref, ahead_ref, mixed_ref,
    once_ref, smooth_ref, parts_ref, sums_ref, rows_ref,
):
    bins, _, side, samples = rows_ref.shape
    start = start_ref[...].astype(jnp.float32)
    place = lax.axis_index("off") * tiles + own_block(tiles)
    ends = [place > 0, place < offs * tiles - 1]
    beyond, outer = [], []
    for end, (edge_ref, own) in enumerate(
        [(before_ref, start[:side]), (after_ref, start[-side:])]
    ):
        edge = edge_ref[...].astype(jnp.float32)
        there = jnp.where(ends[end], smooth_weight, 0.0)
        beyond.append(-smooth_weight * edge[:side])
        outer.append(edge[side:] - there * own)
    inner = [jnp.zeros(((bins - 2) * side, samples), jnp.float32)] if bins > 2 else []
    beyond = jnp.concatenate([beyond[0], *inner, beyond[1]], 0)
    once = local_ref[...] + beyond
    once_ref[...] = once
    smooth = smoothed(once, outer[0], outer[1])
    smooth_ref[...] = smooth
    project(beyond.astype(jnp.bfloat16), (lower_ref, upper_ref), rows_ref)
    square = 0.0
    for b in range(bins):
        both = mixed_ref[b] + mixed(gram_ref, rows_ref, b)
        store_parts(parts_ref, b, both)
        rows = ahead_ref[b].astype(jnp.float32) + rows_ref[b].astype(jnp.float32)
        square += total(rows.reshape(both.shape) * both)
    products = [
        total(start * start),
        total(start * once),
        total(once * once),
        total(once * smooth) + square,
    ]
    lane = lax.broadcasted_iota(jnp.int32, (1, LANES), 1)
    line = jnp.where(lane == FULL, full_ref[:1], 0.0)
    for i, product in enumerate(products):
        line = jnp.where(lane == i, product, line)
    sums_ref[...] = jnp.broadcast_to(line, sums_ref.shape)


def last_kernel(parts_ref, lower_ref, upper_ref, out_ref):
    out_ref[...] = back_projected((lower_ref, upper_ref), parts_ref)


def pack_kernel(sums_ref, start_ref, once_ref, smooth_ref, normal_ref, *refs):
    *out_refs, out_ref = refs
    tiles = len(out_refs)
    ss, so, oo = (sums_ref[:1, i : i + 1] for i in range(3))
    step, grow = own_scales(ss, so, oo)
    start, once = start_ref[...].astype(jnp.float32), once_ref[...]
    twice = normal_ref[...] + smooth_ref[...]
    row = 0
    for field in (start, start - step * once, grow * once - step * twice):
        samples = field.shape[1]
        field = field.reshape(-1, tiles, CELLS, samples)
        size = field.shape[0] * CELLS
        for i in range(0, samples, LANES):
            for tile in range(tiles):
                piece = field[:, tile, :, i : i + LANES].reshape(size, LANES)
                out_ref[tile, row : row + size] = piece.astype(jnp.bfloat16)
            row += size
    lane = lax.broadcasted_iota(jnp.int32, (1, LANES), 1)
    rest = jnp.where(lane == STEP, step, sums_ref[:1])
    rest = jnp.where(lane == GROW, grow, rest)
    line = lax.broadcasted_iota(jnp.int32, (16, LANES), 0)
    parts = jnp.zeros((16, LANES), jnp.float32)
    for i in range(3):
        part = rest.astype(jnp.bfloat16).astype(jnp.float32)
        rest = rest - part
        parts = jnp.where(line == i, part, parts)
    for tile in range(tiles):
        out_ref[tile, row:] = parts.astype(jnp.bfloat16)
    lay_out(out_ref, out_refs)


def total(x):
    return jnp.sum(jnp.sum(x, 0, keepdims=True), 1, keepdims=True)


def own_scales(ss, so, oo):
    step = ss / so
    step = jnp.where(step > 0.0, jnp.clip(step, 1e-8, 1e3), 1.0)
    grow = step * step * oo / ss
    return step, jnp.where(grow > 0.0, jnp.clip(grow, 0.0, 1e3), 1.0)


def place_kernel(bins, *refs):
    *landed_refs, solution_ref, residual_ref, landed_ref = refs
    gather_in(landed_refs, landed_ref)
    tiles, length, _ = landed_ref.shape
    size = bins * CELLS
    samples = solution_ref.shape[2]
    pieces = samples // LANES

    def line_of(source):
        parts = landed_ref[source, length - 16 :].astype(jnp.float32)
        return jnp.sum(parts, 0, keepdims=True)

    def vector(source, i):
        part = [
            landed_ref[source, (i * pieces + j) * size : (i * pieces + j + 1) * size]
            for j in range(pieces)
        ]
        return jnp.concatenate(part, 1).astype(jnp.float32)

    sums = sum(line_of(tile) for tile in range(tiles))
    ss, so, oo, ot = (sums[:, i : i + 1] for i in range(4))
    step_0 = ss / so
    norm_1 = step_0 * step_0 * oo - ss
    grow = 1.0 + norm_1 / ss
    step_1 = norm_1 / (grow * grow * so - 2.0 * step_0 * grow * oo + step_0 * step_0 * ot)
    near = step_0 + step_1 * grow
    far = step_1 * step_0
    fields = [[], []]
    for block in range(tiles):
        source = jnp.where(
            flipped(), path_rank(tiles - 1 - block, tiles), path_rank(block, tiles)
        )
        line = line_of(source)
        inverse = 1.0 / line[:, STEP : STEP + 1]
        there = line[:, GROW : GROW + 1]
        start, first, second = (vector(source, i) for i in range(3))
        far_once = far * inverse
        near_once = near * inverse - far_once * there * inverse
        solution = (near - far_once) * start + far_once * first
        residual = (1.0 - near_once) * start + near_once * first - far_once * second
        fields[0].append(solution.reshape(bins, CELLS, samples))
        fields[1].append(residual.reshape(bins, CELLS, samples))
    solution_ref[...] = jnp.swapaxes(jnp.concatenate(fields[0], 0), 0, 1)
    residual_ref[...] = jnp.swapaxes(jnp.concatenate(fields[1], 0), 0, 1)


def copy_kernel(*refs):
    *refs, arrived = refs
    half = len(refs) // 2
    copies = [
        pltpu.make_async_copy(refs[i], refs[half + i], arrived.at[i]) for i in range(half)
    ]
    for copy in copies:
        copy.start()
    for copy in copies:
        copy.wait()


VMEM = pl.BlockSpec(memory_space=pltpu.VMEM)
HBM = pl.BlockSpec(memory_space=pltpu.HBM)


def local_call(kernel, name, in_specs, out_shape, scratch=(), out_specs=None, cost=0):
    return pl.pallas_call(
        kernel,
        out_shape=out_shape,
        in_specs=in_specs,
        out_specs=out_specs or jax.tree.map(lambda _: VMEM, out_shape),
        scratch_shapes=list(scratch),
        cost_estimate=pl.CostEstimate(
            flops=cost, bytes_accessed=cost // 256, transcendentals=0
        )
        if cost
        else None,
        compiler_params=pltpu.CompilerParams(vmem_limit_bytes=32 * 1024 * 1024),
        name=name,
    )


def shards_by_bin(
    traces, kernels, send_list, aper_slot, aper_pattern, trace_bin, trace_count
):
    tiles, offs = lax.axis_size("mid"), lax.axis_size("off")
    bins = NOFF // offs // tiles
    trace_rows, samples = traces.shape
    send = send_list.shape[2]
    rows = bins * tiles * CELLS
    side = tiles * CELLS
    sums = bins * (CELLS + 2 * REACH * send)

    def array(*shape, dtype=jnp.float32):
        return jax.ShapeDtypeStruct(shape, dtype)

    bf16 = functools.partial(array, dtype=jnp.bfloat16)
    in_hbm = functools.partial(
        pltpu.with_memory_space_constraint, memory_space=pltpu.HBM
    )
    lists = (send_list, aper_slot, aper_pattern, trace_bin, trace_count)
    half = bf16(PATTERNS // 2, samples, samples)
    shared, lower = local_call(
        functools.partial(share_kernel, tiles, bins, ROOM),
        "share",
        [HBM] * 7,
        (bf16(tiles, samples // LANES * ROOM + 2 * APER, LANES), half),
        [
            pltpu.SMEM(send_list.shape, jnp.int32),
            pltpu.VMEM(aper_slot.shape, jnp.int32),
            pltpu.VMEM(aper_pattern.shape, jnp.int32),
            pltpu.VMEM((1, trace_rows), jnp.int32),
            pltpu.VMEM((1, trace_rows), jnp.int32),
            pltpu.VMEM(traces.shape, jnp.bfloat16),
            pltpu.SemaphoreType.DMA((6,)),
            pltpu.SemaphoreType.DMA,
        ],
    )(
        in_hbm(send_list),
        in_hbm(aper_slot),
        in_hbm(aper_pattern),
        in_hbm(trace_bin[None]),
        in_hbm(trace_count[None]),
        in_hbm(traces),
        in_hbm(kernels),
    )
    landed = lax.all_to_all(shared, "mid", 0, 0)
    pattern_rows = pltpu.VMEM((bins, PATTERNS, side, samples), jnp.bfloat16)
    parts_type = bf16(PATTERNS, 2, bins, side, samples)
    start, local, gram, up, down, full, upper = local_call(
        functools.partial(first_kernel, tiles, bins, send),
        "first",
        [VMEM, VMEM, HBM],
        (
            bf16(rows, samples),
            array(rows, samples),
            bf16(bins, tiles * KEYS, tiles * KEYS),
            bf16(2 * side, samples),
            bf16(2 * side, samples),
            array(8, LANES),
            half,
        ),
        [
            pltpu.VMEM((bins, PATTERNS, tiles, CELLS, tiles * ROOM), jnp.float32),
            pattern_rows,
            pltpu.VMEM(parts_type.shape, parts_type.dtype),
            pltpu.SemaphoreType.DMA((PATTERNS // 2,)),
        ],
    )(landed, lower, in_hbm(kernels))

    path = [path_rank(m, tiles) for m in range(tiles)]
    chain = [m * offs + o for o in range(offs) for m in (path[::-1] if o % 2 else path)]
    pairs = list(zip(chain[:-1], chain[1:]))
    before = lax.ppermute(up, ("mid", "off"), pairs)
    after = lax.ppermute(down, ("mid", "off"), [(j, i) for i, j in pairs])

    flops = 2 * rows * PATTERNS * samples * samples
    ahead, mixed_ahead = local_call(
        ahead_kernel,
        "ahead",
        [VMEM] * 4,
        (bf16(*pattern_rows.shape), array(bins, PATTERNS * side, samples)),
        cost=3 * flops,
    )(local, gram, lower, upper)
    field = array(rows, samples)
    once, smooth, parts, products = local_call(
        functools.partial(second_kernel, tiles, offs),
        "second",
        [VMEM] * 10,
        (field, field, parts_type, array(8, LANES)),
        [pattern_rows],
        cost=2 * flops,
    )(start, local, gram, lower, upper, before, after, full, ahead, mixed_ahead)

    projected = local_call(last_kernel, "last", [VMEM] * 3, field, cost=2 * flops)(
        parts, lower, upper
    )
    step = 1
    while step < offs:
        partners = [(i, i ^ step) for i in range(offs)]
        products = products + lax.ppermute(products, "off", partners)
        step *= 2
    chunk = bf16(samples // LANES * 3 * bins * CELLS + 16, LANES)
    chunks = pltpu.VMEM((tiles, *chunk.shape), chunk.dtype)
    packed = local_call(
        pack_kernel, "pack", [VMEM] * 5, [chunk] * tiles, [chunks]
    )(products, start, once, smooth, projected)
    landed = swapped(packed)

    def again():
        arguments = [in_hbm(x) for x in (traces, kernels, *lists[:3])]
        arguments += [in_hbm(x[None]) for x in lists[3:]]
        *copies, bins_again, count_again = local_call(
            copy_kernel,
            "again",
            [HBM] * len(arguments),
            tuple(array(*x.shape, dtype=x.dtype) for x in arguments),
            [pltpu.SemaphoreType.DMA((len(arguments),))],
            out_specs=(HBM,) * len(arguments),
        )(*arguments)
        return *copies, bins_again[0], count_again[0]

    def placed():
        out_type = pltpu.HBM((CELLS, bins * tiles, samples), jnp.float32)
        return local_call(
            functools.partial(place_kernel, bins),
            "place",
            [VMEM] * tiles,
            (out_type, out_type),
            [chunks],
            out_specs=(VMEM, VMEM),
        )(*landed)

    return lax.cond(
        products[0, FULL] > 0.0, lambda: shards_by_tile(*again()), placed
    )


def fits_by_bin(tiles, offs, send, trace_rows, samples):
    return (
        (NOFF // offs) % (2 * tiles) == 0
        and offs & (offs - 1) == 0
        and tiles & (tiles - 1) == 0
        and tiles % TOGETHER == 0
        and send == WITHIN
        and trace_rows == LANES
        and samples % LANES == 0
    )


def solution(mesh):
    in_specs = (
        P(("mid", "off"), None),
        P(),
        P("mid", None, None),
        P(None, ("mid", "off")),
        P(None, ("mid", "off")),
        P(("mid", "off")),
        P(("mid", "off")),
    )
    out_specs = (P("mid", "off", None), P("mid", "off", None))

    def shards(traces, kernels, send_list, *lists):
        fits = fits_by_bin(
            mesh.shape["mid"], mesh.shape["off"], send_list.shape[2], *traces.shape
        )
        form = shards_by_bin if fits else shards_by_tile
        return form(traces, kernels, send_list, *lists)

    return jax.shard_map(
        shards, mesh=mesh, in_specs=in_specs, out_specs=out_specs, check_vma=False
    )
```

```python
import functools

import jax
import jax.numpy as jnp
from jax import lax
from jax.experimental import pallas as pl
from jax.experimental.pallas import tpu as pltpu
from jax.sharding import PartitionSpec as P

NOFF = 64
PATTERNS = 8
REACH = 2
APER = 8
ITERS = 2
CELLS = 8
KEYS = PATTERNS * CELLS
EARLY = 2
ROOM = 32
LANES = 128
TOGETHER = LANES // ROOM


smooth_weight = 2.0


def padded_2(x, sides, width):
    for axis, dim in sides:
        peers, length = (lax.axis_size(axis), x.shape[dim])
        up = [(i, (i + 1) % peers) for i in range(peers - 1)]
        down = [(j, i) for i, j in up]
        last = lax.slice_in_dim(x, length - width, length, axis=dim)
        first = lax.slice_in_dim(x, 0, width, axis=dim)
        before = lax.ppermute(last, axis, up)
        after = lax.ppermute(first, axis, down)
        x = jnp.concatenate([before, x, after], axis=dim)
    return x


def from_behind(x, axis, by):
    peers = lax.axis_size(axis)
    pairs = [(i, i + by) for i in range(peers) if 0 <= i + by < peers]
    return lax.ppermute(x, axis, pairs)


def direction_shift(course):
    return (course // 2 + 1) * (1 - 2 * (course % 2))


def offset_laplace(padded):
    return smooth_weight * (2.0 * padded[:, 1:-1] - padded[:, :-2] - padded[:, 2:])


def smoothing(field):
    padded = padded_2(field, (("off", 1),), 1)
    smoothed = offset_laplace(padded)
    return smoothed


def deliver(outgoing):
    arrived = [None] * (2 * REACH)
    for course in range(2 * REACH):
        arrived[course] = from_behind(outgoing[course], "mid", direction_shift(course))
    return arrived


def give_back(returning):
    landed = [None] * (2 * REACH)
    for course in range(2 * REACH):
        landed[course] = from_behind(returning[course], "mid", -direction_shift(course))
    return landed


def shards_by_tile(
    traces, kernels, send_list, aper_slot, aper_pattern, trace_bin, trace_count
):
    off_dev = NOFF // lax.axis_size("off")
    trace_rows = traces.shape[0]
    samples = traces.shape[1]
    chosen_cells = send_list[0]
    send_count = chosen_cells.shape[1]
    slot_count = CELLS + 2 * REACH * send_count
    live_mask = jnp.arange(APER, dtype=jnp.int32)[:, None] < trace_count[None, :]
    row_index = (aper_slot * off_dev + trace_bin[None, :]).reshape(-1)
    pattern_ids = jnp.arange(PATTERNS, dtype=jnp.int32)[:, None, None]
    chooser = ((aper_pattern[None] == pattern_ids) & live_mask[None]).astype(
        jnp.bfloat16
    )
    pick_rows = (
        aper_pattern * trace_rows + jnp.arange(trace_rows, dtype=jnp.int32)[None, :]
    ).reshape(-1)
    live_column = live_mask.reshape(-1, 1).astype(jnp.float32)

    def forward(field_bf):
        outgoing = [field_bf[chosen_cells[course]] for course in range(2 * REACH)]
        arrived = deliver(outgoing)
        slot_rows = jnp.concatenate([field_bf] + arrived, 0).reshape(-1, samples)
        blocks = slot_rows[row_index].reshape(APER, trace_rows, samples)
        pattern_sums = jnp.einsum(
            "pjt,jtn->ptn", chooser, blocks, preferred_element_type=jnp.float32
        ).astype(jnp.bfloat16)
        return jnp.einsum(
            "ptn,pnm->tm", pattern_sums, kernels, preferred_element_type=jnp.float32
        )

    def adjoint(values_bf):
        spread = jnp.einsum(
            "tm,pnm->ptn", values_bf, kernels, preferred_element_type=jnp.float32
        ).reshape(-1, samples)
        entries = spread[pick_rows] * live_column
        slot_sums = (
            jnp.zeros((slot_count * off_dev, samples), jnp.float32)
            .at[row_index]
            .add(entries)
        )
        slot_sums = slot_sums.reshape(slot_count, off_dev, samples)
        returning = [
            slot_sums[CELLS + course * send_count : CELLS + (course + 1) * send_count]
            for course in range(2 * REACH)
        ]
        landed = give_back(returning)
        accumulated = slot_sums[:CELLS]
        for course in range(2 * REACH):
            accumulated = accumulated.at[chosen_cells[course]].add(landed[course])
        return accumulated

    def global_total(value):
        return lax.psum(value, ("mid", "off"))

    residual = adjoint(traces)
    direction = residual
    solution = jnp.zeros_like(residual)
    norm_now = global_total(jnp.sum(residual * residual))
    for iteration in range(ITERS):
        applied = adjoint(
            forward(direction.astype(jnp.bfloat16)).astype(jnp.bfloat16)
        ) + smoothing(direction)
        step_size = norm_now / global_total(jnp.sum(direction * applied))
        solution = solution + step_size * direction
        residual = residual - step_size * applied
        if iteration + 1 < ITERS:
            norm_next = global_total(jnp.sum(residual * residual))
            direction = residual + norm_next / norm_now * direction
            norm_now = norm_next
    return (solution, residual)


def path_rank(m, tiles):
    return m ^ ((m >> 1) & 1) if tiles % 4 == 0 else m


def turns(peers):
    near, far = range(1, peers // 2), range(peers // 2, peers)
    even = [i for pair in zip(far, near) for i in pair]
    odd = [i for pair in zip(near, far) for i in pair]
    return [(0, 0), *zip(even, odd), (peers - 1, peers - 1)]


def partners(peers):
    odd, place = flipped(), lax.axis_index("mid")
    return [place ^ jnp.where(odd, j, i) for i, j in turns(peers)]


def lay_out(chunks_ref, out_refs):
    for partner, out_ref in zip(partners(len(out_refs)), out_refs):
        out_ref[...] = chunks_ref[partner]


def gather_in(landed_refs, chunks_ref):
    for partner, landed_ref in zip(partners(len(landed_refs)), landed_refs):
        chunks_ref[partner] = landed_ref[...]


def swapped(chunks):
    peers, offs = len(chunks), lax.axis_size("off")
    return list(chunks[:1]) + [
        lax.ppermute(
            chunk,
            ("mid", "off"),
            [
                (m * offs + o, (m ^ turn[o % 2]) * offs + o)
                for m in range(peers)
                for o in range(offs)
            ],
        )
        for turn, chunk in zip(turns(peers)[1:], chunks[1:])
    ]


def flipped():
    return lax.axis_index("off") % 2 > 0


def own_block(tiles):
    block = path_rank(lax.axis_index("mid"), tiles)
    return jnp.where(flipped(), tiles - 1 - block, block)


def dot_back(rows, kernel):
    return lax.dot_general(
        rows, kernel, (((1,), (1,)), ((), ())), preferred_element_type=jnp.float32
    )


SLOT, PATTERN, WITHIN, COUNT, FLAG = 0, APER, 4, 5, 6


def share_kernel(
    tiles, bins, room, sends_arg, slot_arg, pattern_arg, bin_arg, count_arg, traces_arg,
    kernels_arg, out_ref, kernels_ref, sends_ref, slot_ref, pattern_ref, bin_ref, count_ref, traces_ref,
    staged, arrived,
):
    rows, samples = traces_ref.shape
    stages = [
        pltpu.make_async_copy(arg, ref, staged.at[i])
        for i, (arg, ref) in enumerate(
            [
                (bin_arg, bin_ref),
                (slot_arg, slot_ref),
                (pattern_arg, pattern_ref),
                (count_arg, count_ref),
                (sends_arg, sends_ref),
                (traces_arg, traces_ref),
            ]
        )
    ]
    kernels = pltpu.make_async_copy(
        kernels_arg.at[:EARLY], kernels_ref, arrived
    )
    for stage in stages + [kernels]:
        stage.start()
    stages[0].wait()
    offset_bin = bin_ref[...]
    block = lax.div(offset_bin, bins)
    within = offset_bin - block * bins
    chunk = path_rank(jnp.where(flipped(), tiles - 1 - block, block), tiles)
    belongs = lax.broadcasted_iota(jnp.int32, (tiles, rows), 0) == chunk
    belongs = jnp.where(belongs, 1.0, 0.0)
    earlier = lax.broadcasted_iota(jnp.int32, (rows, rows), 0) < (
        lax.broadcasted_iota(jnp.int32, (rows, rows), 1)
    )
    rank = jnp.dot(
        belongs.astype(jnp.bfloat16),
        jnp.where(earlier, 1.0, 0.0).astype(jnp.bfloat16),
        preferred_element_type=jnp.float32,
    )
    rank = jnp.sum(rank * belongs, 0, keepdims=True).astype(jnp.int32)
    full = jnp.max(rank, axis=1, keepdims=True) >= room
    target = jnp.where(rank < room, chunk * room + rank, -1)
    picks = lax.broadcasted_iota(jnp.int32, (tiles * room, rows), 0) == target
    picks = jnp.where(picks, 1.0, 0.0).astype(jnp.bfloat16)
    place = lax.axis_index("mid")
    lane = lax.broadcasted_iota(jnp.int32, (1, LANES), 1)
    target = chunk * LANES + lax.rem(place, TOGETHER) * room + rank
    chosen = lax.broadcasted_iota(jnp.int32, (tiles * LANES, rows), 0) == (
        jnp.where(rank < room, target, -1)
    )
    chosen = jnp.where(chosen, 1.0, 0.0).astype(jnp.bfloat16)
    for stage in stages[1:5]:
        stage.wait()
    lists = jnp.concatenate(
        [
            slot_ref[...].astype(jnp.float32),
            pattern_ref[...].astype(jnp.float32),
            jnp.zeros((WITHIN, rows), jnp.float32),
            within.astype(jnp.float32),
            count_ref[...].astype(jnp.float32),
            jnp.zeros((APER - COUNT - 1, rows), jnp.float32),
        ],
        0,
    ).astype(jnp.bfloat16)
    lists = dot_back(lists, chosen)
    _, courses, send = sends_ref.shape
    line = lax.broadcasted_iota(jnp.int32, (2 * APER, LANES), 0)
    sent = jnp.zeros((2 * APER, LANES), jnp.int32)
    for course in range(courses):
        reader = lax.rem(place + direction_shift(course) + TOGETHER, TOGETHER)
        here = lax.div(lane, room) == reader
        for m in range(send):
            value = jnp.where(here, sends_ref[0, course, m], 0)
            sent += jnp.where(line == sent_row(course, send) + m, value, 0)
    past = lax.div(lane, room) == lax.rem(place + 1, TOGETHER)
    sent += jnp.where(past & (line == FLAG) & full, 1, 0)
    sent = sent.astype(jnp.float32)
    pieces = samples // LANES
    for m in range(tiles):
        own = lists[:, m * LANES : (m + 1) * LANES]
        moved = pltpu.roll(own[2 * APER :], room, 1)
        out_ref[m, pieces * room :] = (
            own[: 2 * APER] + jnp.concatenate([moved, jnp.zeros_like(moved)], 0) + sent
        ).astype(jnp.bfloat16)
    stages[5].wait()
    picked = jnp.dot(picks, traces_ref[...], preferred_element_type=jnp.float32)
    picked = picked.reshape(tiles, room, samples).astype(jnp.bfloat16)
    for i in range(pieces):
        out_ref[:, i * room : (i + 1) * room] = picked[:, :, i * LANES : (i + 1) * LANES]
    kernels.wait()


def sent_row(course, send):
    return send if course == 3 else 0


def fill_picks(tiles, bins, send, landed_ref, picks_ref):
    flags = 0
    keys = lax.broadcasted_iota(jnp.int32, (KEYS, LANES), 0)
    member = lax.div(lax.broadcasted_iota(jnp.int32, (1, LANES), 1), ROOM)
    blocks = [
        landed_ref[tile, -2 * APER :].astype(jnp.float32).astype(jnp.int32)
        for tile in range(tiles)
    ]
    for group in range(tiles // TOGETHER):
        readers = range(group * TOGETHER, (group + 1) * TOGETHER)
        lists, moved = 0, 0
        for tile in readers:
            lists += jnp.where(member == tile % TOGETHER, blocks[tile], 0)
            past = member == (tile + 1) % TOGETHER
            moved += jnp.where(past, blocks[tile][:APER], 0)
        moved = pltpu.roll(moved, LANES - ROOM, 1)
        flags += moved[FLAG : FLAG + 1]
        within, count = moved[WITHIN : WITHIN + 1], moved[COUNT : COUNT + 1]
        wanted = []
        for region in range(2 * REACH + 1):
            course = region - 1
            shift = direction_shift(course) if region else 0
            owners = [tile - shift for tile in readers if 0 <= tile - shift < tiles]
            sent = 0
            for owner in owners if region else ():
                row = sent_row(course, send)
                values = blocks[owner][row : row + send]
                sent += jnp.where(member == (owner + shift) % TOGETHER, values, 0)
            for entry in range(region, APER, 2 * REACH + 1):
                cell = lists[SLOT + entry : SLOT + entry + 1]
                if region:
                    place = cell - (CELLS + course * send)
                    cell = sent[:1]
                    for other in range(1, send):
                        cell = jnp.where(place == other, sent[other : other + 1], cell)
                pattern = lists[PATTERN + entry : PATTERN + entry + 1]
                key = jnp.where(count > entry, pattern * CELLS + cell, -1)
                for owner in owners:
                    there = member == (owner + shift) % TOGETHER
                    wanted.append((owner, jnp.where(there, key, -1)))
        for tile in range(tiles):
            for b in range(bins):
                total = jnp.zeros((KEYS, LANES), jnp.float32)
                for owner, key in wanted:
                    if owner == tile:
                        hit = keys == jnp.where(within == b, key, -1)
                        total += jnp.where(hit, 1.0, 0.0)
                picks_ref[b, :, tile, :, group * LANES : (group + 1) * LANES] = (
                    total.reshape(PATTERNS, CELLS, LANES)
                )
    return flags.astype(jnp.float32)


def two_parts(x):
    high = x.astype(jnp.bfloat16)
    low = (x - high.astype(jnp.float32)).astype(jnp.bfloat16)
    return jnp.concatenate([high, low], 0)


def store_parts(parts_ref, b, x):
    shape = (PATTERNS, *parts_ref.shape[3:])
    high = x.astype(jnp.bfloat16)
    parts_ref[:, 0, b] = high.reshape(shape)
    low = (x - high.astype(jnp.float32)).astype(jnp.bfloat16)
    parts_ref[:, 1, b] = low.reshape(shape)


def kernel_of(kernels, p):
    lower_ref, upper_ref = kernels
    return lower_ref[p] if p < EARLY else upper_ref[p - EARLY]


def back_projected_high(kernels, parts_ref):
    _, _, bins, side, samples = parts_ref.shape
    rows = bins * side
    out = jnp.zeros((rows, samples), jnp.float32)
    for p in range(PATTERNS):
        out += dot_back(parts_ref[p, 0].reshape(rows, samples), kernel_of(kernels, p))
    return out


def back_projected(kernels, parts_ref):
    _, _, bins, side, samples = parts_ref.shape
    rows = bins * side
    both = jnp.zeros((2 * rows, samples), jnp.float32)
    for p in range(PATTERNS):
        both += dot_back(
            parts_ref[p].reshape(2 * rows, samples), kernel_of(kernels, p)
        )
    return both[:rows] + both[rows:]


def project(field, kernels, rows_ref):
    bins, _, side, samples = rows_ref.shape
    rows = bins * side
    for p in range(PATTERNS):
        u = jnp.dot(field, kernel_of(kernels, p), preferred_element_type=jnp.float32)
        u = u[:rows] + u[rows:] if field.shape[0] > rows else u
        rows_ref[:, p] = u.astype(jnp.bfloat16).reshape(bins, side, samples)


def mixed(gram_ref, rows_ref, b):
    _, _, side, samples = rows_ref.shape
    return jnp.dot(
        gram_ref[b],
        rows_ref[b].reshape(PATTERNS * side, samples),
        preferred_element_type=jnp.float32,
    )


def smoothed(field, before, after):
    side = before.shape[0]
    lower = jnp.concatenate([before, field[:-side]], 0)
    upper = jnp.concatenate([field[side:], after], 0)
    return smooth_weight * (2.0 * field - lower - upper)


def first_kernel(
    tiles, bins, send, landed_ref, lower_ref, kernels_arg,
    start_ref, local_ref, gram_ref, up_ref, down_ref, full_ref, upper_ref,
    picks_ref, rows_ref, parts_ref, arrived,
):
    copies = [
        pltpu.make_async_copy(kernels_arg.at[EARLY + p], upper_ref.at[p], arrived.at[p])
        for p in range(PATTERNS - EARLY)
    ]
    for copy in copies:
        copy.start()
    kernels = (lower_ref, upper_ref)
    side = tiles * CELLS
    samples = start_ref.shape[1]
    flags = total(fill_picks(tiles, bins, send, landed_ref, picks_ref))
    full_ref[...] = jnp.broadcast_to(flags, full_ref.shape)
    traces = jnp.concatenate(
        [
            landed_ref[:, i * ROOM : (i + 1) * ROOM].reshape(-1, LANES)
            for i in range(samples // LANES)
        ],
        1,
    )
    for b in range(bins):
        picks = picks_ref[b].reshape(PATTERNS * side, -1).astype(jnp.bfloat16)
        gram_ref[b] = dot_back(picks, picks).astype(jnp.bfloat16)
        sums = jnp.dot(picks, traces, preferred_element_type=jnp.float32)
        parts_ref[:, 0, b] = sums.astype(jnp.bfloat16).reshape(PATTERNS, side, samples)
    start = jnp.zeros((bins * side, samples), jnp.float32)
    for p in range(PATTERNS):
        if p >= EARLY:
            copies[p - EARLY].wait()
        rows = parts_ref[p, 0].reshape(bins * side, samples)
        start += dot_back(rows, kernel_of(kernels, p))
    start = start.astype(jnp.bfloat16)
    start_ref[...] = start
    field = start.astype(jnp.float32)
    nothing = jnp.zeros((side, samples), jnp.float32)
    project(start, kernels, rows_ref)
    for b in range(bins):
        high = mixed(gram_ref, rows_ref, b).astype(jnp.bfloat16)
        parts_ref[:, 0, b] = high.reshape(PATTERNS, side, samples)
    local = back_projected_high(kernels, parts_ref) + smoothed(field, nothing, nothing)
    local_ref[...] = local
    up_ref[:side] = start[-side:]
    up_ref[side:] = local[-side:].astype(jnp.bfloat16)
    down_ref[:side] = start[:side]
    down_ref[side:] = local[:side].astype(jnp.bfloat16)


FULL, STEP, GROW = 4, 5, 6


def ahead_kernel(
    local_ref, gram_ref, lower_ref, upper_ref, mixed_ref, square_ref, rows_ref
):
    project(two_parts(local_ref[...]), (lower_ref, upper_ref), rows_ref)
    square = 0.0
    for b in range(rows_ref.shape[0]):
        both = mixed(gram_ref, rows_ref, b)
        mixed_ref[b] = both
        square += total(rows_ref[b].astype(jnp.float32).reshape(both.shape) * both)
    square_ref[...] = jnp.broadcast_to(square, square_ref.shape)


def second_kernel(
    tiles, offs, start_ref, local_ref, gram_ref, lower_ref, upper_ref, before_ref, after_ref,
    full_ref, mixed_ref, square_ref,
    once_ref, smooth_ref, parts_ref, sums_ref, rows_ref,
):
    bins, _, side, samples = rows_ref.shape
    start = start_ref[...].astype(jnp.float32)
    place = lax.axis_index("off") * tiles + own_block(tiles)
    ends = [place > 0, place < offs * tiles - 1]
    beyond, outer = [], []
    for end, (edge_ref, own) in enumerate(
        [(before_ref, start[:side]), (after_ref, start[-side:])]
    ):
        edge = edge_ref[...].astype(jnp.float32)
        there = jnp.where(ends[end], smooth_weight, 0.0)
        beyond.append(-smooth_weight * edge[:side])
        outer.append(edge[side:] - there * own)
    inner = [jnp.zeros(((bins - 2) * side, samples), jnp.float32)] if bins > 2 else []
    beyond = jnp.concatenate([beyond[0], *inner, beyond[1]], 0)
    once = local_ref[...] + beyond
    once_ref[...] = once
    smooth = smoothed(once, outer[0], outer[1])
    smooth_ref[...] = smooth
    project(beyond.astype(jnp.bfloat16), (lower_ref, upper_ref), rows_ref)
    square = square_ref[:1, :1]
    for b in range(bins):
        before = mixed_ref[b]
        both = before + mixed(gram_ref, rows_ref, b)
        store_parts(parts_ref, b, both)
        rows = rows_ref[b].astype(jnp.float32).reshape(both.shape)
        square += total(rows * (before + both))
    products = [
        total(start * start),
        total(start * once),
        total(once * once),
        total(once * smooth) + square,
    ]
    lane = lax.broadcasted_iota(jnp.int32, (1, LANES), 1)
    line = jnp.where(lane == FULL, full_ref[:1], 0.0)
    for i, product in enumerate(products):
        line = jnp.where(lane == i, product, line)
    sums_ref[...] = jnp.broadcast_to(line, sums_ref.shape)


def last_kernel(parts_ref, lower_ref, upper_ref, out_ref):
    out_ref[...] = back_projected((lower_ref, upper_ref), parts_ref)


def pack_kernel(sums_ref, start_ref, once_ref, smooth_ref, normal_ref, *refs):
    *out_refs, out_ref = refs
    tiles = len(out_refs)
    ss, so, oo = (sums_ref[:1, i : i + 1] for i in range(3))
    step, grow = own_scales(ss, so, oo)
    start, once = start_ref[...].astype(jnp.float32), once_ref[...]
    twice = normal_ref[...] + smooth_ref[...]
    row = 0
    for field in (start, start - step * once, grow * once - step * twice):
        samples = field.shape[1]
        field = field.reshape(-1, tiles, CELLS, samples)
        size = field.shape[0] * CELLS
        for i in range(0, samples, LANES):
            for tile in range(tiles):
                piece = field[:, tile, :, i : i + LANES].reshape(size, LANES)
                out_ref[tile, row : row + size] = piece.astype(jnp.bfloat16)
            row += size
    lane = lax.broadcasted_iota(jnp.int32, (1, LANES), 1)
    rest = jnp.where(lane == STEP, step, sums_ref[:1])
    rest = jnp.where(lane == GROW, grow, rest)
    line = lax.broadcasted_iota(jnp.int32, (16, LANES), 0)
    parts = jnp.zeros((16, LANES), jnp.float32)
    for i in range(3):
        part = rest.astype(jnp.bfloat16).astype(jnp.float32)
        rest = rest - part
        parts = jnp.where(line == i, part, parts)
    for tile in range(tiles):
        out_ref[tile, row:] = parts.astype(jnp.bfloat16)
    lay_out(out_ref, out_refs)


def total(x):
    return jnp.sum(jnp.sum(x, 0, keepdims=True), 1, keepdims=True)


def own_scales(ss, so, oo):
    step = ss / so
    step = jnp.where(step > 0.0, jnp.clip(step, 1e-8, 1e3), 1.0)
    grow = step * step * oo / ss
    return step, jnp.where(grow > 0.0, jnp.clip(grow, 0.0, 1e3), 1.0)


def place_kernel(bins, *refs):
    *landed_refs, solution_ref, residual_ref, landed_ref = refs
    gather_in(landed_refs, landed_ref)
    tiles, length, _ = landed_ref.shape
    size = bins * CELLS
    samples = solution_ref.shape[2]
    pieces = samples // LANES

    def line_of(source):
        parts = landed_ref[source, length - 16 :].astype(jnp.float32)
        return jnp.sum(parts, 0, keepdims=True)

    def vector(source, i):
        part = [
            landed_ref[source, (i * pieces + j) * size : (i * pieces + j + 1) * size]
            for j in range(pieces)
        ]
        return jnp.concatenate(part, 1).astype(jnp.float32)

    sums = sum(line_of(tile) for tile in range(tiles))
    ss, so, oo, ot = (sums[:, i : i + 1] for i in range(4))
    step_0 = ss / so
    norm_1 = step_0 * step_0 * oo - ss
    grow = 1.0 + norm_1 / ss
    step_1 = norm_1 / (grow * grow * so - 2.0 * step_0 * grow * oo + step_0 * step_0 * ot)
    near = step_0 + step_1 * grow
    far = step_1 * step_0
    fields = [[], []]
    for block in range(tiles):
        source = jnp.where(
            flipped(), path_rank(tiles - 1 - block, tiles), path_rank(block, tiles)
        )
        line = line_of(source)
        inverse = 1.0 / line[:, STEP : STEP + 1]
        there = line[:, GROW : GROW + 1]
        start, first, second = (vector(source, i) for i in range(3))
        far_once = far * inverse
        near_once = near * inverse - far_once * there * inverse
        solution = (near - far_once) * start + far_once * first
        residual = (1.0 - near_once) * start + near_once * first - far_once * second
        fields[0].append(solution.reshape(bins, CELLS, samples))
        fields[1].append(residual.reshape(bins, CELLS, samples))
    solution_ref[...] = jnp.swapaxes(jnp.concatenate(fields[0], 0), 0, 1)
    residual_ref[...] = jnp.swapaxes(jnp.concatenate(fields[1], 0), 0, 1)


def copy_kernel(*refs):
    *refs, arrived = refs
    half = len(refs) // 2
    copies = [
        pltpu.make_async_copy(refs[i], refs[half + i], arrived.at[i]) for i in range(half)
    ]
    for copy in copies:
        copy.start()
    for copy in copies:
        copy.wait()


VMEM = pl.BlockSpec(memory_space=pltpu.VMEM)
HBM = pl.BlockSpec(memory_space=pltpu.HBM)


def local_call(kernel, name, in_specs, out_shape, scratch=(), out_specs=None, cost=0):
    return pl.pallas_call(
        kernel,
        out_shape=out_shape,
        in_specs=in_specs,
        out_specs=out_specs or jax.tree.map(lambda _: VMEM, out_shape),
        scratch_shapes=list(scratch),
        cost_estimate=pl.CostEstimate(
            flops=cost, bytes_accessed=cost // 256, transcendentals=0
        )
        if cost
        else None,
        compiler_params=pltpu.CompilerParams(vmem_limit_bytes=32 * 1024 * 1024),
        name=name,
    )


def shards_by_bin(
    traces, kernels, send_list, aper_slot, aper_pattern, trace_bin, trace_count
):
    tiles, offs = lax.axis_size("mid"), lax.axis_size("off")
    bins = NOFF // offs // tiles
    trace_rows, samples = traces.shape
    send = send_list.shape[2]
    rows = bins * tiles * CELLS
    side = tiles * CELLS
    sums = bins * (CELLS + 2 * REACH * send)

    def array(*shape, dtype=jnp.float32):
        return jax.ShapeDtypeStruct(shape, dtype)

    bf16 = functools.partial(array, dtype=jnp.bfloat16)
    in_hbm = functools.partial(
        pltpu.with_memory_space_constraint, memory_space=pltpu.HBM
    )
    lists = (send_list, aper_slot, aper_pattern, trace_bin, trace_count)
    early = bf16(EARLY, samples, samples)
    shared, lower = local_call(
        functools.partial(share_kernel, tiles, bins, ROOM),
        "share",
        [HBM] * 7,
        (bf16(tiles, samples // LANES * ROOM + 2 * APER, LANES), early),
        [
            pltpu.SMEM(send_list.shape, jnp.int32),
            pltpu.VMEM(aper_slot.shape, jnp.int32),
            pltpu.VMEM(aper_pattern.shape, jnp.int32),
            pltpu.VMEM((1, trace_rows), jnp.int32),
            pltpu.VMEM((1, trace_rows), jnp.int32),
            pltpu.VMEM(traces.shape, jnp.bfloat16),
            pltpu.SemaphoreType.DMA((6,)),
            pltpu.SemaphoreType.DMA,
        ],
    )(
        in_hbm(send_list),
        in_hbm(aper_slot),
        in_hbm(aper_pattern),
        in_hbm(trace_bin[None]),
        in_hbm(trace_count[None]),
        in_hbm(traces),
        in_hbm(kernels),
    )
    landed = lax.all_to_all(shared, "mid", 0, 0)
    pattern_rows = pltpu.VMEM((bins, PATTERNS, side, samples), jnp.bfloat16)
    parts_type = bf16(PATTERNS, 2, bins, side, samples)
    start, local, gram, up, down, full, upper = local_call(
        functools.partial(first_kernel, tiles, bins, send),
        "first",
        [VMEM, VMEM, HBM],
        (
            bf16(rows, samples),
            array(rows, samples),
            bf16(bins, tiles * KEYS, tiles * KEYS),
            bf16(2 * side, samples),
            bf16(2 * side, samples),
            array(8, LANES),
            bf16(PATTERNS - EARLY, samples, samples),
        ),
        [
            pltpu.VMEM((bins, PATTERNS, tiles, CELLS, tiles * ROOM), jnp.float32),
            pattern_rows,
            pltpu.VMEM(parts_type.shape, parts_type.dtype),
            pltpu.SemaphoreType.DMA((PATTERNS - EARLY,)),
        ],
    )(landed, lower, in_hbm(kernels))

    path = [path_rank(m, tiles) for m in range(tiles)]
    chain = [m * offs + o for o in range(offs) for m in (path[::-1] if o % 2 else path)]
    pairs = list(zip(chain[:-1], chain[1:]))
    before = lax.ppermute(up, ("mid", "off"), pairs)
    after = lax.ppermute(down, ("mid", "off"), [(j, i) for i, j in pairs])

    flops = 2 * rows * PATTERNS * samples * samples
    ahead = local_call(
        ahead_kernel,
        "ahead",
        [VMEM] * 4,
        (array(bins, PATTERNS * side, samples), array(8, LANES)),
        [pattern_rows],
        cost=3 * flops,
    )(local, gram, lower, upper)
    field = array(rows, samples)
    once, smooth, parts, products = local_call(
        functools.partial(second_kernel, tiles, offs),
        "second",
        [VMEM] * 10,
        (field, field, parts_type, array(8, LANES)),
        [pattern_rows],
        cost=2 * flops,
    )(start, local, gram, lower, upper, before, after, full, *ahead)

    projected = local_call(last_kernel, "last", [VMEM] * 3, field, cost=2 * flops)(
        parts, lower, upper
    )
    addends = [products] + [
        lax.ppermute(products, "off", [(i, i ^ step) for i in range(offs)])
        for step in range(1, offs)
    ]
    while len(addends) > 1:
        addends = [a + b for a, b in zip(addends[::2], addends[1::2])]
    products = addends[0]
    chunk = bf16(samples // LANES * 3 * bins * CELLS + 16, LANES)
    chunks = pltpu.VMEM((tiles, *chunk.shape), chunk.dtype)
    packed = local_call(
        pack_kernel, "pack", [VMEM] * 5, [chunk] * tiles, [chunks]
    )(products, start, once, smooth, projected)
    landed = swapped(packed)

    def again():
        arguments = [in_hbm(x) for x in (traces, kernels, *lists[:3])]
        arguments += [in_hbm(x[None]) for x in lists[3:]]
        *copies, bins_again, count_again = local_call(
            copy_kernel,
            "again",
            [HBM] * len(arguments),
            tuple(array(*x.shape, dtype=x.dtype) for x in arguments),
            [pltpu.SemaphoreType.DMA((len(arguments),))],
            out_specs=(HBM,) * len(arguments),
        )(*arguments)
        return *copies, bins_again[0], count_again[0]

    def placed():
        out_type = pltpu.HBM((CELLS, bins * tiles, samples), jnp.float32)
        return local_call(
            functools.partial(place_kernel, bins),
            "place",
            [VMEM] * tiles,
            (out_type, out_type),
            [chunks],
            out_specs=(VMEM, VMEM),
        )(*landed)

    return lax.cond(
        products[0, FULL] > 0.0, lambda: shards_by_tile(*again()), placed
    )


def fits_by_bin(tiles, offs, send, trace_rows, samples):
    return (
        (NOFF // offs) % (2 * tiles) == 0
        and offs & (offs - 1) == 0
        and tiles & (tiles - 1) == 0
        and tiles % TOGETHER == 0
        and send == WITHIN
        and trace_rows == LANES
        and samples % LANES == 0
    )


def solution(mesh):
    in_specs = (
        P(("mid", "off"), None),
        P(),
        P("mid", None, None),
        P(None, ("mid", "off")),
        P(None, ("mid", "off")),
        P(("mid", "off")),
        P(("mid", "off")),
    )
    out_specs = (P("mid", "off", None), P("mid", "off", None))

    def shards(traces, kernels, send_list, *lists):
        fits = fits_by_bin(
            mesh.shape["mid"], mesh.shape["off"], send_list.shape[2], *traces.shape
        )
        form = shards_by_bin if fits else shards_by_tile
        return form(traces, kernels, send_list, *lists)

    return jax.shard_map(
        shards, mesh=mesh, in_specs=in_specs, out_specs=out_specs, check_vma=False
    )
```

```python
import functools

import jax
import jax.numpy as jnp
from jax import lax
from jax.experimental import pallas as pl
from jax.experimental.pallas import tpu as pltpu
from jax.sharding import PartitionSpec as P

NOFF = 64
PATTERNS = 8
REACH = 2
APER = 8
ITERS = 2
CELLS = 8
KEYS = PATTERNS * CELLS
EARLY = 3
ROOM = 32
LANES = 128
TOGETHER = LANES // ROOM


smooth_weight = 2.0


def padded_2(x, sides, width):
    for axis, dim in sides:
        peers, length = (lax.axis_size(axis), x.shape[dim])
        up = [(i, (i + 1) % peers) for i in range(peers - 1)]
        down = [(j, i) for i, j in up]
        last = lax.slice_in_dim(x, length - width, length, axis=dim)
        first = lax.slice_in_dim(x, 0, width, axis=dim)
        before = lax.ppermute(last, axis, up)
        after = lax.ppermute(first, axis, down)
        x = jnp.concatenate([before, x, after], axis=dim)
    return x


def from_behind(x, axis, by):
    peers = lax.axis_size(axis)
    pairs = [(i, i + by) for i in range(peers) if 0 <= i + by < peers]
    return lax.ppermute(x, axis, pairs)


def direction_shift(course):
    return (course // 2 + 1) * (1 - 2 * (course % 2))


def offset_laplace(padded):
    return smooth_weight * (2.0 * padded[:, 1:-1] - padded[:, :-2] - padded[:, 2:])


def smoothing(field):
    padded = padded_2(field, (("off", 1),), 1)
    smoothed = offset_laplace(padded)
    return smoothed


def deliver(outgoing):
    arrived = [None] * (2 * REACH)
    for course in range(2 * REACH):
        arrived[course] = from_behind(outgoing[course], "mid", direction_shift(course))
    return arrived


def give_back(returning):
    landed = [None] * (2 * REACH)
    for course in range(2 * REACH):
        landed[course] = from_behind(returning[course], "mid", -direction_shift(course))
    return landed


def shards_by_tile(
    traces, kernels, send_list, aper_slot, aper_pattern, trace_bin, trace_count
):
    off_dev = NOFF // lax.axis_size("off")
    trace_rows = traces.shape[0]
    samples = traces.shape[1]
    chosen_cells = send_list[0]
    send_count = chosen_cells.shape[1]
    slot_count = CELLS + 2 * REACH * send_count
    live_mask = jnp.arange(APER, dtype=jnp.int32)[:, None] < trace_count[None, :]
    row_index = (aper_slot * off_dev + trace_bin[None, :]).reshape(-1)
    pattern_ids = jnp.arange(PATTERNS, dtype=jnp.int32)[:, None, None]
    chooser = ((aper_pattern[None] == pattern_ids) & live_mask[None]).astype(
        jnp.bfloat16
    )
    pick_rows = (
        aper_pattern * trace_rows + jnp.arange(trace_rows, dtype=jnp.int32)[None, :]
    ).reshape(-1)
    live_column = live_mask.reshape(-1, 1).astype(jnp.float32)

    def forward(field_bf):
        outgoing = [field_bf[chosen_cells[course]] for course in range(2 * REACH)]
        arrived = deliver(outgoing)
        slot_rows = jnp.concatenate([field_bf] + arrived, 0).reshape(-1, samples)
        blocks = slot_rows[row_index].reshape(APER, trace_rows, samples)
        pattern_sums = jnp.einsum(
            "pjt,jtn->ptn", chooser, blocks, preferred_element_type=jnp.float32
        ).astype(jnp.bfloat16)
        return jnp.einsum(
            "ptn,pnm->tm", pattern_sums, kernels, preferred_element_type=jnp.float32
        )

    def adjoint(values_bf):
        spread = jnp.einsum(
            "tm,pnm->ptn", values_bf, kernels, preferred_element_type=jnp.float32
        ).reshape(-1, samples)
        entries = spread[pick_rows] * live_column
        slot_sums = (
            jnp.zeros((slot_count * off_dev, samples), jnp.float32)
            .at[row_index]
            .add(entries)
        )
        slot_sums = slot_sums.reshape(slot_count, off_dev, samples)
        returning = [
            slot_sums[CELLS + course * send_count : CELLS + (course + 1) * send_count]
            for course in range(2 * REACH)
        ]
        landed = give_back(returning)
        accumulated = slot_sums[:CELLS]
        for course in range(2 * REACH):
            accumulated = accumulated.at[chosen_cells[course]].add(landed[course])
        return accumulated

    def global_total(value):
        return lax.psum(value, ("mid", "off"))

    residual = adjoint(traces)
    direction = residual
    solution = jnp.zeros_like(residual)
    norm_now = global_total(jnp.sum(residual * residual))
    for iteration in range(ITERS):
        applied = adjoint(
            forward(direction.astype(jnp.bfloat16)).astype(jnp.bfloat16)
        ) + smoothing(direction)
        step_size = norm_now / global_total(jnp.sum(direction * applied))
        solution = solution + step_size * direction
        residual = residual - step_size * applied
        if iteration + 1 < ITERS:
            norm_next = global_total(jnp.sum(residual * residual))
            direction = residual + norm_next / norm_now * direction
            norm_now = norm_next
    return (solution, residual)


def path_rank(m, tiles):
    return m ^ ((m >> 1) & 1) if tiles % 4 == 0 else m


def turns(peers):
    near, far = range(1, peers // 2), range(peers // 2, peers)
    even = [i for pair in zip(far, near) for i in pair]
    odd = [i for pair in zip(near, far) for i in pair]
    return [(0, 0), *zip(even, odd), (peers - 1, peers - 1)]


def partners(peers):
    odd, place = flipped(), lax.axis_index("mid")
    return [place ^ jnp.where(odd, j, i) for i, j in turns(peers)]


def lay_out(chunks_ref, out_refs):
    for partner, out_ref in zip(partners(len(out_refs)), out_refs):
        out_ref[...] = chunks_ref[partner]


def gather_in(landed_refs, chunks_ref):
    for partner, landed_ref in zip(partners(len(landed_refs)), landed_refs):
        chunks_ref[partner] = landed_ref[...]


def swapped(chunks):
    peers, offs = len(chunks), lax.axis_size("off")
    return list(chunks[:1]) + [
        lax.ppermute(
            chunk,
            ("mid", "off"),
            [
                (m * offs + o, (m ^ turn[o % 2]) * offs + o)
                for m in range(peers)
                for o in range(offs)
            ],
        )
        for turn, chunk in zip(turns(peers)[1:], chunks[1:])
    ]


def flipped():
    return lax.axis_index("off") % 2 > 0


def own_block(tiles):
    block = path_rank(lax.axis_index("mid"), tiles)
    return jnp.where(flipped(), tiles - 1 - block, block)


def dot_back(rows, kernel):
    return lax.dot_general(
        rows, kernel, (((1,), (1,)), ((), ())), preferred_element_type=jnp.float32
    )


SLOT, PATTERN, WITHIN, COUNT, FLAG = 0, APER, 4, 5, 6


def share_kernel(
    tiles, bins, room, sends_arg, slot_arg, pattern_arg, bin_arg, count_arg, traces_arg,
    kernels_arg, out_ref, kernels_ref, sends_ref, slot_ref, pattern_ref, bin_ref, count_ref, traces_ref,
    staged, arrived,
):
    rows, samples = traces_ref.shape
    stages = [
        pltpu.make_async_copy(arg, ref, staged.at[i])
        for i, (arg, ref) in enumerate(
            [
                (bin_arg, bin_ref),
                (slot_arg, slot_ref),
                (pattern_arg, pattern_ref),
                (count_arg, count_ref),
                (sends_arg, sends_ref),
                (traces_arg, traces_ref),
            ]
        )
    ]
    kernels = pltpu.make_async_copy(
        kernels_arg.at[:EARLY], kernels_ref, arrived
    )
    for stage in stages + [kernels]:
        stage.start()
    index = lax.broadcasted_iota(jnp.int32, (tiles, rows), 0)
    earlier = lax.broadcasted_iota(jnp.int32, (rows, rows), 0) < (
        lax.broadcasted_iota(jnp.int32, (rows, rows), 1)
    )
    earlier = jnp.where(earlier, 1.0, 0.0).astype(jnp.bfloat16)
    stages[0].wait()
    offset_bin = bin_ref[...]
    block = lax.div(offset_bin, bins)
    within = offset_bin - block * bins
    chunk = path_rank(jnp.where(flipped(), tiles - 1 - block, block), tiles)
    belongs = jnp.where(index == chunk, 1.0, 0.0)
    rank = jnp.dot(
        belongs.astype(jnp.bfloat16), earlier, preferred_element_type=jnp.float32
    )
    rank = jnp.sum(rank * belongs, 0, keepdims=True).astype(jnp.int32)
    full = jnp.max(rank, axis=1, keepdims=True) >= room
    target = jnp.where(rank < room, chunk * room + rank, -1)
    picks = lax.broadcasted_iota(jnp.int32, (tiles * room, rows), 0) == target
    picks = jnp.where(picks, 1.0, 0.0).astype(jnp.bfloat16)
    place = lax.axis_index("mid")
    lane = lax.broadcasted_iota(jnp.int32, (1, LANES), 1)
    target = chunk * LANES + lax.rem(place, TOGETHER) * room + rank
    chosen = lax.broadcasted_iota(jnp.int32, (tiles * LANES, rows), 0) == (
        jnp.where(rank < room, target, -1)
    )
    chosen = jnp.where(chosen, 1.0, 0.0).astype(jnp.bfloat16)
    for stage in stages[1:5]:
        stage.wait()
    lists = jnp.concatenate(
        [
            slot_ref[...].astype(jnp.float32),
            pattern_ref[...].astype(jnp.float32),
            jnp.zeros((WITHIN, rows), jnp.float32),
            within.astype(jnp.float32),
            count_ref[...].astype(jnp.float32),
            jnp.zeros((APER - COUNT - 1, rows), jnp.float32),
        ],
        0,
    ).astype(jnp.bfloat16)
    lists = dot_back(lists, chosen)
    _, courses, send = sends_ref.shape
    line = lax.broadcasted_iota(jnp.int32, (2 * APER, LANES), 0)
    sent = jnp.zeros((2 * APER, LANES), jnp.int32)
    for course in range(courses):
        reader = lax.rem(place + direction_shift(course) + TOGETHER, TOGETHER)
        here = lax.div(lane, room) == reader
        for m in range(send):
            value = jnp.where(here, sends_ref[0, course, m], 0)
            sent += jnp.where(line == sent_row(course, send) + m, value, 0)
    past = lax.div(lane, room) == lax.rem(place + 1, TOGETHER)
    sent += jnp.where(past & (line == FLAG) & full, 1, 0)
    sent = sent.astype(jnp.float32)
    pieces = samples // LANES
    for m in range(tiles):
        own = lists[:, m * LANES : (m + 1) * LANES]
        moved = pltpu.roll(own[2 * APER :], room, 1)
        out_ref[m, pieces * room :] = (
            own[: 2 * APER] + jnp.concatenate([moved, jnp.zeros_like(moved)], 0) + sent
        ).astype(jnp.bfloat16)
    stages[5].wait()
    picked = jnp.dot(picks, traces_ref[...], preferred_element_type=jnp.float32)
    picked = picked.reshape(tiles, room, samples).astype(jnp.bfloat16)
    for i in range(pieces):
        out_ref[:, i * room : (i + 1) * room] = picked[:, :, i * LANES : (i + 1) * LANES]
    kernels.wait()


def sent_row(course, send):
    return send if course == 3 else 0


def fill_picks(tiles, bins, send, landed_ref, picks_ref):
    flags = 0
    keys = lax.broadcasted_iota(jnp.int32, (KEYS, LANES), 0)
    member = lax.div(lax.broadcasted_iota(jnp.int32, (1, LANES), 1), ROOM)
    blocks = [
        landed_ref[tile, -2 * APER :].astype(jnp.float32).astype(jnp.int32)
        for tile in range(tiles)
    ]
    for group in range(tiles // TOGETHER):
        readers = range(group * TOGETHER, (group + 1) * TOGETHER)
        lists, moved = 0, 0
        for tile in readers:
            lists += jnp.where(member == tile % TOGETHER, blocks[tile], 0)
            past = member == (tile + 1) % TOGETHER
            moved += jnp.where(past, blocks[tile][:APER], 0)
        moved = pltpu.roll(moved, LANES - ROOM, 1)
        flags += moved[FLAG : FLAG + 1]
        within, count = moved[WITHIN : WITHIN + 1], moved[COUNT : COUNT + 1]
        wanted = []
        for region in range(2 * REACH + 1):
            course = region - 1
            shift = direction_shift(course) if region else 0
            owners = [tile - shift for tile in readers if 0 <= tile - shift < tiles]
            sent = 0
            for owner in owners if region else ():
                row = sent_row(course, send)
                values = blocks[owner][row : row + send]
                sent += jnp.where(member == (owner + shift) % TOGETHER, values, 0)
            for entry in range(region, APER, 2 * REACH + 1):
                cell = lists[SLOT + entry : SLOT + entry + 1]
                if region:
                    place = cell - (CELLS + course * send)
                    cell = sent[:1]
                    for other in range(1, send):
                        cell = jnp.where(place == other, sent[other : other + 1], cell)
                pattern = lists[PATTERN + entry : PATTERN + entry + 1]
                key = jnp.where(count > entry, pattern * CELLS + cell, -1)
                for owner in owners:
                    there = member == (owner + shift) % TOGETHER
                    wanted.append((owner, jnp.where(there, key, -1)))
        for tile in range(tiles):
            for b in range(bins):
                total = jnp.zeros((KEYS, LANES), jnp.float32)
                for owner, key in wanted:
                    if owner == tile:
                        hit = keys == jnp.where(within == b, key, -1)
                        total += jnp.where(hit, 1.0, 0.0)
                picks_ref[b, :, tile, :, group * LANES : (group + 1) * LANES] = (
                    total.reshape(PATTERNS, CELLS, LANES)
                )
    return flags.astype(jnp.float32)


def two_parts(x):
    high = x.astype(jnp.bfloat16)
    low = (x - high.astype(jnp.float32)).astype(jnp.bfloat16)
    return jnp.concatenate([high, low], 0)


def store_parts(parts_ref, b, x):
    shape = (PATTERNS, *parts_ref.shape[3:])
    high = x.astype(jnp.bfloat16)
    parts_ref[:, 0, b] = high.reshape(shape)
    low = (x - high.astype(jnp.float32)).astype(jnp.bfloat16)
    parts_ref[:, 1, b] = low.reshape(shape)


def kernel_of(kernels, p):
    lower_ref, upper_ref = kernels
    return lower_ref[p] if p < EARLY else upper_ref[p - EARLY]


def back_projected(kernels, parts_ref):
    _, _, bins, side, samples = parts_ref.shape
    rows = bins * side
    both = jnp.zeros((2 * rows, samples), jnp.float32)
    for p in range(PATTERNS):
        both += dot_back(
            parts_ref[p].reshape(2 * rows, samples), kernel_of(kernels, p)
        )
    return both[:rows] + both[rows:]


def project(field, kernels, rows_ref):
    bins, _, side, samples = rows_ref.shape
    rows = bins * side
    for p in range(PATTERNS):
        u = jnp.dot(field, kernel_of(kernels, p), preferred_element_type=jnp.float32)
        u = u[:rows] + u[rows:] if field.shape[0] > rows else u
        rows_ref[:, p] = u.astype(jnp.bfloat16).reshape(bins, side, samples)


def mixed(gram_ref, rows_ref, b):
    _, _, side, samples = rows_ref.shape
    return jnp.dot(
        gram_ref[b],
        rows_ref[b].reshape(PATTERNS * side, samples),
        preferred_element_type=jnp.float32,
    )


def smoothed(field, before, after):
    side = before.shape[0]
    lower = jnp.concatenate([before, field[:-side]], 0)
    upper = jnp.concatenate([field[side:], after], 0)
    return smooth_weight * (2.0 * field - lower - upper)


def first_kernel(
    tiles, bins, send, landed_ref, lower_ref, kernels_arg,
    start_ref, local_ref, gram_ref, up_ref, down_ref, full_ref, upper_ref,
    picks_ref, rows_ref, parts_ref, arrived,
):
    copies = [
        pltpu.make_async_copy(kernels_arg.at[EARLY + p], upper_ref.at[p], arrived.at[p])
        for p in range(PATTERNS - EARLY)
    ]
    for copy in copies:
        copy.start()
    kernels = (lower_ref, upper_ref)
    side = tiles * CELLS
    samples = start_ref.shape[1]
    flags = total(fill_picks(tiles, bins, send, landed_ref, picks_ref))
    full_ref[...] = jnp.broadcast_to(flags, full_ref.shape)
    traces = jnp.concatenate(
        [
            landed_ref[:, i * ROOM : (i + 1) * ROOM].reshape(-1, LANES)
            for i in range(samples // LANES)
        ],
        1,
    )
    for b in range(bins):
        picks = picks_ref[b].reshape(PATTERNS * side, -1).astype(jnp.bfloat16)
        gram_ref[b] = dot_back(picks, picks).astype(jnp.bfloat16)
        sums = jnp.dot(picks, traces, preferred_element_type=jnp.float32)
        parts_ref[:, 0, b] = sums.astype(jnp.bfloat16).reshape(PATTERNS, side, samples)
    start = jnp.zeros((bins * side, samples), jnp.float32)
    for p in range(PATTERNS):
        if p >= EARLY:
            copies[p - EARLY].wait()
        rows = parts_ref[p, 0].reshape(bins * side, samples)
        start += dot_back(rows, kernel_of(kernels, p))
    start = start.astype(jnp.bfloat16)
    start_ref[...] = start
    field = start.astype(jnp.float32)
    nothing = jnp.zeros((side, samples), jnp.float32)
    project(start, kernels, rows_ref)
    for b in range(bins):
        store_parts(parts_ref, b, mixed(gram_ref, rows_ref, b))
    local = back_projected(kernels, parts_ref) + smoothed(field, nothing, nothing)
    local_ref[...] = local
    up_ref[:side] = start[-side:]
    up_ref[side:] = local[-side:].astype(jnp.bfloat16)
    down_ref[:side] = start[:side]
    down_ref[side:] = local[:side].astype(jnp.bfloat16)


FULL, STEP, GROW = 4, 5, 6


def ahead_kernel(local_ref, gram_ref, lower_ref, upper_ref, rows_ref, mixed_ref):
    project(two_parts(local_ref[...]), (lower_ref, upper_ref), rows_ref)
    for b in range(rows_ref.shape[0]):
        mixed_ref[b] = mixed(gram_ref, rows_ref, b)


def second_kernel(
    tiles, offs, start_ref, local_ref, gram_ref, lower_ref, upper_ref, before_ref, after_ref,
    full_ref, ahead_ref, mixed_ref,
    once_ref, smooth_ref, parts_ref, sums_ref, rows_ref,
):
    bins, _, side, samples = rows_ref.shape
    start = start_ref[...].astype(jnp.float32)
    place = lax.axis_index("off") * tiles + own_block(tiles)
    ends = [place > 0, place < offs * tiles - 1]
    beyond, outer = [], []
    for end, (edge_ref, own) in enumerate(
        [(before_ref, start[:side]), (after_ref, start[-side:])]
    ):
        edge = edge_ref[...].astype(jnp.float32)
        there = jnp.where(ends[end], smooth_weight, 0.0)
        beyond.append(-smooth_weight * edge[:side])
        outer.append(edge[side:] - there * own)
    inner = [jnp.zeros(((bins - 2) * side, samples), jnp.float32)] if bins > 2 else []
    beyond = jnp.concatenate([beyond[0], *inner, beyond[1]], 0)
    once = local_ref[...] + beyond
    once_ref[...] = once
    smooth = smoothed(once, outer[0], outer[1])
    smooth_ref[...] = smooth
    project(beyond.astype(jnp.bfloat16), (lower_ref, upper_ref), rows_ref)
    square = 0.0
    for b in range(bins):
        both = mixed_ref[b] + mixed(gram_ref, rows_ref, b)
        store_parts(parts_ref, b, both)
        rows = ahead_ref[b].astype(jnp.float32) + rows_ref[b].astype(jnp.float32)
        square += total(rows.reshape(both.shape) * both)
    products = [
        total(start * start),
        total(start * once),
        total(once * once),
        total(once * smooth) + square,
    ]
    lane = lax.broadcasted_iota(jnp.int32, (1, LANES), 1)
    line = jnp.where(lane == FULL, full_ref[:1], 0.0)
    for i, product in enumerate(products):
        line = jnp.where(lane == i, product, line)
    sums_ref[...] = jnp.broadcast_to(line, sums_ref.shape)


def last_kernel(parts_ref, lower_ref, upper_ref, out_ref):
    out_ref[...] = back_projected((lower_ref, upper_ref), parts_ref)


def pack_kernel(sums_ref, start_ref, once_ref, smooth_ref, normal_ref, *refs):
    *out_refs, out_ref = refs
    tiles = len(out_refs)
    ss, so, oo = (sums_ref[:1, i : i + 1] for i in range(3))
    step, grow = own_scales(ss, so, oo)
    start, once = start_ref[...].astype(jnp.float32), once_ref[...]
    twice = normal_ref[...] + smooth_ref[...]
    row = 0
    for field in (start, start - step * once, grow * once - step * twice):
        samples = field.shape[1]
        field = field.reshape(-1, tiles, CELLS, samples)
        size = field.shape[0] * CELLS
        for i in range(0, samples, LANES):
            for tile in range(tiles):
                piece = field[:, tile, :, i : i + LANES].reshape(size, LANES)
                out_ref[tile, row : row + size] = piece.astype(jnp.bfloat16)
            row += size
    lane = lax.broadcasted_iota(jnp.int32, (1, LANES), 1)
    rest = jnp.where(lane == STEP, step, sums_ref[:1])
    rest = jnp.where(lane == GROW, grow, rest)
    line = lax.broadcasted_iota(jnp.int32, (16, LANES), 0)
    parts = jnp.zeros((16, LANES), jnp.float32)
    for i in range(3):
        part = rest.astype(jnp.bfloat16).astype(jnp.float32)
        rest = rest - part
        parts = jnp.where(line == i, part, parts)
    for tile in range(tiles):
        out_ref[tile, row:] = parts.astype(jnp.bfloat16)
    lay_out(out_ref, out_refs)


def total(x):
    return jnp.sum(jnp.sum(x, 0, keepdims=True), 1, keepdims=True)


def own_scales(ss, so, oo):
    step = ss / so
    step = jnp.where(step > 0.0, jnp.clip(step, 1e-8, 1e3), 1.0)
    grow = step * step * oo / ss
    return step, jnp.where(grow > 0.0, jnp.clip(grow, 0.0, 1e3), 1.0)


def place_kernel(bins, *refs):
    *landed_refs, solution_out, residual_out, landed_ref, both_ref, sent = refs
    solution_ref, residual_ref = both_ref.at[0], both_ref.at[1]
    gather_in(landed_refs, landed_ref)
    tiles, length, _ = landed_ref.shape
    size = bins * CELLS
    samples = both_ref.shape[3]
    pieces = samples // LANES

    def line_of(source):
        parts = landed_ref[source, length - 16 :].astype(jnp.float32)
        return jnp.sum(parts, 0, keepdims=True)

    def vector(source, i):
        part = [
            landed_ref[source, (i * pieces + j) * size : (i * pieces + j + 1) * size]
            for j in range(pieces)
        ]
        return jnp.concatenate(part, 1).astype(jnp.float32)

    sums = sum(line_of(tile) for tile in range(tiles))
    ss, so, oo, ot = (sums[:, i : i + 1] for i in range(4))
    step_0 = ss / so
    norm_1 = step_0 * step_0 * oo - ss
    grow = 1.0 + norm_1 / ss
    step_1 = norm_1 / (grow * grow * so - 2.0 * step_0 * grow * oo + step_0 * step_0 * ot)
    near = step_0 + step_1 * grow
    far = step_1 * step_0
    sources, weights, starts = [], [], []
    solutions, residuals = [], []
    for block in range(tiles):
        source = jnp.where(
            flipped(), path_rank(tiles - 1 - block, tiles), path_rank(block, tiles)
        )
        line = line_of(source)
        inverse = 1.0 / line[:, STEP : STEP + 1]
        far_once = far * inverse
        near_once = near * inverse - far_once * line[:, GROW : GROW + 1] * inverse
        sources.append(source)
        weights.append((far_once, near_once))
        start, first = vector(source, 0), vector(source, 1)
        starts.append((start, first))
        solution = (near - far_once) * start + far_once * first
        solutions.append(solution.reshape(bins, CELLS, samples))
    solution_ref[...] = jnp.swapaxes(jnp.concatenate(solutions, 0), 0, 1)
    copies = [
        pltpu.make_async_copy(both_ref.at[i], out, sent.at[i])
        for i, out in enumerate((solution_out, residual_out))
    ]
    copies[0].start()
    for source, (far_once, near_once), (start, first) in zip(sources, weights, starts):
        second = vector(source, 2)
        residual = (1.0 - near_once) * start + near_once * first - far_once * second
        residuals.append(residual.reshape(bins, CELLS, samples))
    residual_ref[...] = jnp.swapaxes(jnp.concatenate(residuals, 0), 0, 1)
    copies[1].start()
    for copy in copies:
        copy.wait()


def copy_kernel(*refs):
    *refs, arrived = refs
    half = len(refs) // 2
    copies = [
        pltpu.make_async_copy(refs[i], refs[half + i], arrived.at[i]) for i in range(half)
    ]
    for copy in copies:
        copy.start()
    for copy in copies:
        copy.wait()


VMEM = pl.BlockSpec(memory_space=pltpu.VMEM)
HBM = pl.BlockSpec(memory_space=pltpu.HBM)


def local_call(kernel, name, in_specs, out_shape, scratch=(), out_specs=None, cost=0):
    return pl.pallas_call(
        kernel,
        out_shape=out_shape,
        in_specs=in_specs,
        out_specs=out_specs or jax.tree.map(lambda _: VMEM, out_shape),
        scratch_shapes=list(scratch),
        cost_estimate=pl.CostEstimate(
            flops=cost, bytes_accessed=cost // 256, transcendentals=0
        )
        if cost
        else None,
        compiler_params=pltpu.CompilerParams(vmem_limit_bytes=32 * 1024 * 1024),
        name=name,
    )


def shards_by_bin(
    traces, kernels, send_list, aper_slot, aper_pattern, trace_bin, trace_count
):
    tiles, offs = lax.axis_size("mid"), lax.axis_size("off")
    bins = NOFF // offs // tiles
    trace_rows, samples = traces.shape
    send = send_list.shape[2]
    rows = bins * tiles * CELLS
    side = tiles * CELLS
    sums = bins * (CELLS + 2 * REACH * send)

    def array(*shape, dtype=jnp.float32):
        return jax.ShapeDtypeStruct(shape, dtype)

    bf16 = functools.partial(array, dtype=jnp.bfloat16)
    in_hbm = functools.partial(
        pltpu.with_memory_space_constraint, memory_space=pltpu.HBM
    )
    lists = (send_list, aper_slot, aper_pattern, trace_bin, trace_count)
    early = bf16(EARLY, samples, samples)
    shared, lower = local_call(
        functools.partial(share_kernel, tiles, bins, ROOM),
        "share",
        [HBM] * 7,
        (bf16(tiles, samples // LANES * ROOM + 2 * APER, LANES), early),
        [
            pltpu.SMEM(send_list.shape, jnp.int32),
            pltpu.VMEM(aper_slot.shape, jnp.int32),
            pltpu.VMEM(aper_pattern.shape, jnp.int32),
            pltpu.VMEM((1, trace_rows), jnp.int32),
            pltpu.VMEM((1, trace_rows), jnp.int32),
            pltpu.VMEM(traces.shape, jnp.bfloat16),
            pltpu.SemaphoreType.DMA((6,)),
            pltpu.SemaphoreType.DMA,
        ],
    )(
        in_hbm(send_list),
        in_hbm(aper_slot),
        in_hbm(aper_pattern),
        in_hbm(trace_bin[None]),
        in_hbm(trace_count[None]),
        in_hbm(traces),
        in_hbm(kernels),
    )
    landed = lax.all_to_all(shared, "mid", 0, 0)
    pattern_rows = pltpu.VMEM((bins, PATTERNS, side, samples), jnp.bfloat16)
    parts_type = bf16(PATTERNS, 2, bins, side, samples)
    start, local, gram, up, down, full, upper = local_call(
        functools.partial(first_kernel, tiles, bins, send),
        "first",
        [VMEM, VMEM, HBM],
        (
            bf16(rows, samples),
            array(rows, samples),
            bf16(bins, tiles * KEYS, tiles * KEYS),
            bf16(2 * side, samples),
            bf16(2 * side, samples),
            array(8, LANES),
            bf16(PATTERNS - EARLY, samples, samples),
        ),
        [
            pltpu.VMEM((bins, PATTERNS, tiles, CELLS, tiles * ROOM), jnp.float32),
            pattern_rows,
            pltpu.VMEM(parts_type.shape, parts_type.dtype),
            pltpu.SemaphoreType.DMA((PATTERNS - EARLY,)),
        ],
    )(landed, lower, in_hbm(kernels))

    path = [path_rank(m, tiles) for m in range(tiles)]
    chain = [m * offs + o for o in range(offs) for m in (path[::-1] if o % 2 else path)]
    pairs = list(zip(chain[:-1], chain[1:]))
    before = lax.ppermute(up, ("mid", "off"), pairs)
    after = lax.ppermute(down, ("mid", "off"), [(j, i) for i, j in pairs])

    flops = 2 * rows * PATTERNS * samples * samples
    ahead, mixed_ahead = local_call(
        ahead_kernel,
        "ahead",
        [VMEM] * 4,
        (bf16(*pattern_rows.shape), array(bins, PATTERNS * side, samples)),
        cost=3 * flops,
    )(local, gram, lower, upper)
    field = array(rows, samples)
    once, smooth, parts, products = local_call(
        functools.partial(second_kernel, tiles, offs),
        "second",
        [VMEM] * 10,
        (field, field, parts_type, array(8, LANES)),
        [pattern_rows],
        cost=2 * flops,
    )(start, local, gram, lower, upper, before, after, full, ahead, mixed_ahead)

    projected = local_call(last_kernel, "last", [VMEM] * 3, field, cost=2 * flops)(
        parts, lower, upper
    )
    addends = [products] + [
        lax.ppermute(products, "off", [(i, i ^ step) for i in range(offs)])
        for step in range(1, offs)
    ]
    while len(addends) > 1:
        addends = [a + b for a, b in zip(addends[::2], addends[1::2])]
    products = addends[0]
    chunk = bf16(samples // LANES * 3 * bins * CELLS + 16, LANES)
    chunks = pltpu.VMEM((tiles, *chunk.shape), chunk.dtype)
    packed = local_call(
        pack_kernel, "pack", [VMEM] * 5, [chunk] * tiles, [chunks]
    )(products, start, once, smooth, projected)
    landed = swapped(packed)

    def again():
        arguments = [in_hbm(x) for x in (traces, kernels, *lists[:3])]
        arguments += [in_hbm(x[None]) for x in lists[3:]]
        *copies, bins_again, count_again = local_call(
            copy_kernel,
            "again",
            [HBM] * len(arguments),
            tuple(array(*x.shape, dtype=x.dtype) for x in arguments),
            [pltpu.SemaphoreType.DMA((len(arguments),))],
            out_specs=(HBM,) * len(arguments),
        )(*arguments)
        return *copies, bins_again[0], count_again[0]

    def placed():
        out_type = pltpu.HBM((CELLS, bins * tiles, samples), jnp.float32)
        return local_call(
            functools.partial(place_kernel, bins),
            "place",
            [VMEM] * tiles,
            (out_type, out_type),
            [
                chunks,
                pltpu.VMEM((2, *out_type.shape), jnp.float32),
                pltpu.SemaphoreType.DMA((2,)),
            ],
            out_specs=(HBM, HBM),
        )(*landed)

    return lax.cond(
        products[0, FULL] > 0.0, lambda: shards_by_tile(*again()), placed
    )


def fits_by_bin(tiles, offs, send, trace_rows, samples):
    return (
        (NOFF // offs) % (2 * tiles) == 0
        and offs & (offs - 1) == 0
        and tiles & (tiles - 1) == 0
        and tiles % TOGETHER == 0
        and send == WITHIN
        and trace_rows == LANES
        and samples % LANES == 0
    )


def solution(mesh):
    in_specs = (
        P(("mid", "off"), None),
        P(),
        P("mid", None, None),
        P(None, ("mid", "off")),
        P(None, ("mid", "off")),
        P(("mid", "off")),
        P(("mid", "off")),
    )
    out_specs = (P("mid", "off", None), P("mid", "off", None))

    def shards(traces, kernels, send_list, *lists):
        fits = fits_by_bin(
            mesh.shape["mid"], mesh.shape["off"], send_list.shape[2], *traces.shape
        )
        form = shards_by_bin if fits else shards_by_tile
        return form(traces, kernels, send_list, *lists)

    return jax.shard_map(
        shards, mesh=mesh, in_specs=in_specs, out_specs=out_specs, check_vma=False
    )
```

```python
import functools

import jax
import jax.numpy as jnp
from jax import lax
from jax.experimental import pallas as pl
from jax.experimental.pallas import tpu as pltpu
from jax.sharding import PartitionSpec as P

NOFF = 64
PATTERNS = 8
REACH = 2
APER = 8
ITERS = 2
CELLS = 8
KEYS = PATTERNS * CELLS
EARLY = 3
ROOM = 32
LANES = 128
TOGETHER = LANES // ROOM


smooth_weight = 2.0


def padded_2(x, sides, width):
    for axis, dim in sides:
        peers, length = (lax.axis_size(axis), x.shape[dim])
        up = [(i, (i + 1) % peers) for i in range(peers - 1)]
        down = [(j, i) for i, j in up]
        last = lax.slice_in_dim(x, length - width, length, axis=dim)
        first = lax.slice_in_dim(x, 0, width, axis=dim)
        before = lax.ppermute(last, axis, up)
        after = lax.ppermute(first, axis, down)
        x = jnp.concatenate([before, x, after], axis=dim)
    return x


def from_behind(x, axis, by):
    peers = lax.axis_size(axis)
    pairs = [(i, i + by) for i in range(peers) if 0 <= i + by < peers]
    return lax.ppermute(x, axis, pairs)


def direction_shift(course):
    return (course // 2 + 1) * (1 - 2 * (course % 2))


def offset_laplace(padded):
    return smooth_weight * (2.0 * padded[:, 1:-1] - padded[:, :-2] - padded[:, 2:])


def smoothing(field):
    padded = padded_2(field, (("off", 1),), 1)
    smoothed = offset_laplace(padded)
    return smoothed


def deliver(outgoing):
    arrived = [None] * (2 * REACH)
    for course in range(2 * REACH):
        arrived[course] = from_behind(outgoing[course], "mid", direction_shift(course))
    return arrived


def give_back(returning):
    landed = [None] * (2 * REACH)
    for course in range(2 * REACH):
        landed[course] = from_behind(returning[course], "mid", -direction_shift(course))
    return landed


def shards_by_tile(
    traces, kernels, send_list, aper_slot, aper_pattern, trace_bin, trace_count
):
    off_dev = NOFF // lax.axis_size("off")
    trace_rows = traces.shape[0]
    samples = traces.shape[1]
    chosen_cells = send_list[0]
    send_count = chosen_cells.shape[1]
    slot_count = CELLS + 2 * REACH * send_count
    live_mask = jnp.arange(APER, dtype=jnp.int32)[:, None] < trace_count[None, :]
    row_index = (aper_slot * off_dev + trace_bin[None, :]).reshape(-1)
    pattern_ids = jnp.arange(PATTERNS, dtype=jnp.int32)[:, None, None]
    chooser = ((aper_pattern[None] == pattern_ids) & live_mask[None]).astype(
        jnp.bfloat16
    )
    pick_rows = (
        aper_pattern * trace_rows + jnp.arange(trace_rows, dtype=jnp.int32)[None, :]
    ).reshape(-1)
    live_column = live_mask.reshape(-1, 1).astype(jnp.float32)

    def forward(field_bf):
        outgoing = [field_bf[chosen_cells[course]] for course in range(2 * REACH)]
        arrived = deliver(outgoing)
        slot_rows = jnp.concatenate([field_bf] + arrived, 0).reshape(-1, samples)
        blocks = slot_rows[row_index].reshape(APER, trace_rows, samples)
        pattern_sums = jnp.einsum(
            "pjt,jtn->ptn", chooser, blocks, preferred_element_type=jnp.float32
        ).astype(jnp.bfloat16)
        return jnp.einsum(
            "ptn,pnm->tm", pattern_sums, kernels, preferred_element_type=jnp.float32
        )

    def adjoint(values_bf):
        spread = jnp.einsum(
            "tm,pnm->ptn", values_bf, kernels, preferred_element_type=jnp.float32
        ).reshape(-1, samples)
        entries = spread[pick_rows] * live_column
        slot_sums = (
            jnp.zeros((slot_count * off_dev, samples), jnp.float32)
            .at[row_index]
            .add(entries)
        )
        slot_sums = slot_sums.reshape(slot_count, off_dev, samples)
        returning = [
            slot_sums[CELLS + course * send_count : CELLS + (course + 1) * send_count]
            for course in range(2 * REACH)
        ]
        landed = give_back(returning)
        accumulated = slot_sums[:CELLS]
        for course in range(2 * REACH):
            accumulated = accumulated.at[chosen_cells[course]].add(landed[course])
        return accumulated

    def global_total(value):
        return lax.psum(value, ("mid", "off"))

    residual = adjoint(traces)
    direction = residual
    solution = jnp.zeros_like(residual)
    norm_now = global_total(jnp.sum(residual * residual))
    for iteration in range(ITERS):
        applied = adjoint(
            forward(direction.astype(jnp.bfloat16)).astype(jnp.bfloat16)
        ) + smoothing(direction)
        step_size = norm_now / global_total(jnp.sum(direction * applied))
        solution = solution + step_size * direction
        residual = residual - step_size * applied
        if iteration + 1 < ITERS:
            norm_next = global_total(jnp.sum(residual * residual))
            direction = residual + norm_next / norm_now * direction
            norm_now = norm_next
    return (solution, residual)


def path_rank(m, tiles):
    return m ^ ((m >> 1) & 1) if tiles % 4 == 0 else m


def turns(peers):
    near, far = range(1, peers // 2), range(peers // 2, peers)
    even = [i for pair in zip(far, near) for i in pair]
    odd = [i for pair in zip(near, far) for i in pair]
    return [(0, 0), *zip(even, odd), (peers - 1, peers - 1)]


def partners(peers):
    odd, place = flipped(), lax.axis_index("mid")
    return [place ^ jnp.where(odd, j, i) for i, j in turns(peers)]


def lay_out(chunks_ref, out_refs):
    for partner, out_ref in zip(partners(len(out_refs)), out_refs):
        out_ref[...] = chunks_ref[partner]


def gather_in(landed_refs, chunks_ref):
    for partner, landed_ref in zip(partners(len(landed_refs)), landed_refs):
        chunks_ref[partner] = landed_ref[...]


def swapped(chunks):
    peers, offs = len(chunks), lax.axis_size("off")
    return list(chunks[:1]) + [
        lax.ppermute(
            chunk,
            ("mid", "off"),
            [
                (m * offs + o, (m ^ turn[o % 2]) * offs + o)
                for m in range(peers)
                for o in range(offs)
            ],
        )
        for turn, chunk in zip(turns(peers)[1:], chunks[1:])
    ]


def flipped():
    return lax.axis_index("off") % 2 > 0


def own_block(tiles):
    block = path_rank(lax.axis_index("mid"), tiles)
    return jnp.where(flipped(), tiles - 1 - block, block)


def dot_back(rows, kernel):
    return lax.dot_general(
        rows, kernel, (((1,), (1,)), ((), ())), preferred_element_type=jnp.float32
    )


SLOT, PATTERN, WITHIN, COUNT, FLAG = 0, APER, 4, 5, 6


def share_kernel(
    tiles, bins, room, sends_arg, slot_arg, pattern_arg, bin_arg, count_arg, traces_arg,
    kernels_arg, out_ref, kernels_ref, sends_ref, slot_ref, pattern_ref, bin_ref, count_ref, traces_ref,
    staged, arrived,
):
    rows, samples = traces_ref.shape
    stages = [
        pltpu.make_async_copy(arg, ref, staged.at[i])
        for i, (arg, ref) in enumerate(
            [
                (bin_arg, bin_ref),
                (slot_arg, slot_ref),
                (pattern_arg, pattern_ref),
                (count_arg, count_ref),
                (sends_arg, sends_ref),
                (traces_arg, traces_ref),
            ]
        )
    ]
    kernels = pltpu.make_async_copy(
        kernels_arg.at[:EARLY], kernels_ref, arrived
    )
    for stage in stages + [kernels]:
        stage.start()
    index = lax.broadcasted_iota(jnp.int32, (tiles, rows), 0)
    earlier = lax.broadcasted_iota(jnp.int32, (rows, rows), 0) < (
        lax.broadcasted_iota(jnp.int32, (rows, rows), 1)
    )
    earlier = jnp.where(earlier, 1.0, 0.0).astype(jnp.bfloat16)
    stages[0].wait()
    offset_bin = bin_ref[...]
    block = lax.div(offset_bin, bins)
    within = offset_bin - block * bins
    chunk = path_rank(jnp.where(flipped(), tiles - 1 - block, block), tiles)
    belongs = jnp.where(index == chunk, 1.0, 0.0)
    rank = jnp.dot(
        belongs.astype(jnp.bfloat16), earlier, preferred_element_type=jnp.float32
    )
    rank = jnp.sum(rank * belongs, 0, keepdims=True).astype(jnp.int32)
    full = jnp.max(rank, axis=1, keepdims=True) >= room
    target = jnp.where(rank < room, chunk * room + rank, -1)
    picks = lax.broadcasted_iota(jnp.int32, (tiles * room, rows), 0) == target
    picks = jnp.where(picks, 1.0, 0.0).astype(jnp.bfloat16)
    place = lax.axis_index("mid")
    lane = lax.broadcasted_iota(jnp.int32, (1, LANES), 1)
    target = chunk * LANES + lax.rem(place, TOGETHER) * room + rank
    chosen = lax.broadcasted_iota(jnp.int32, (tiles * LANES, rows), 0) == (
        jnp.where(rank < room, target, -1)
    )
    chosen = jnp.where(chosen, 1.0, 0.0).astype(jnp.bfloat16)
    for stage in stages[1:5]:
        stage.wait()
    lists = jnp.concatenate(
        [
            slot_ref[...].astype(jnp.float32),
            pattern_ref[...].astype(jnp.float32),
            jnp.zeros((WITHIN, rows), jnp.float32),
            within.astype(jnp.float32),
            count_ref[...].astype(jnp.float32),
            jnp.zeros((APER - COUNT - 1, rows), jnp.float32),
        ],
        0,
    ).astype(jnp.bfloat16)
    lists = dot_back(lists, chosen)
    _, courses, send = sends_ref.shape
    line = lax.broadcasted_iota(jnp.int32, (2 * APER, LANES), 0)
    sent = jnp.zeros((2 * APER, LANES), jnp.int32)
    for course in range(courses):
        reader = lax.rem(place + direction_shift(course) + TOGETHER, TOGETHER)
        here = lax.div(lane, room) == reader
        for m in range(send):
            value = jnp.where(here, sends_ref[0, course, m], 0)
            sent += jnp.where(line == sent_row(course, send) + m, value, 0)
    past = lax.div(lane, room) == lax.rem(place + 1, TOGETHER)
    sent += jnp.where(past & (line == FLAG) & full, 1, 0)
    sent = sent.astype(jnp.float32)
    pieces = samples // LANES
    for m in range(tiles):
        own = lists[:, m * LANES : (m + 1) * LANES]
        moved = pltpu.roll(own[2 * APER :], room, 1)
        out_ref[m, pieces * room :] = (
            own[: 2 * APER] + jnp.concatenate([moved, jnp.zeros_like(moved)], 0) + sent
        ).astype(jnp.bfloat16)
    stages[5].wait()
    picked = jnp.dot(picks, traces_ref[...], preferred_element_type=jnp.float32)
    picked = picked.reshape(tiles, room, samples).astype(jnp.bfloat16)
    for i in range(pieces):
        out_ref[:, i * room : (i + 1) * room] = picked[:, :, i * LANES : (i + 1) * LANES]
    kernels.wait()


def sent_row(course, send):
    return send if course == 3 else 0


def fill_picks(tiles, bins, send, landed_ref, picks_ref):
    flags = 0
    keys = lax.broadcasted_iota(jnp.int32, (KEYS, LANES), 0)
    member = lax.div(lax.broadcasted_iota(jnp.int32, (1, LANES), 1), ROOM)
    blocks = [
        landed_ref[tile, -2 * APER :].astype(jnp.float32).astype(jnp.int32)
        for tile in range(tiles)
    ]
    for group in range(tiles // TOGETHER):
        readers = range(group * TOGETHER, (group + 1) * TOGETHER)
        lists, moved = 0, 0
        for tile in readers:
            lists += jnp.where(member == tile % TOGETHER, blocks[tile], 0)
            past = member == (tile + 1) % TOGETHER
            moved += jnp.where(past, blocks[tile][:APER], 0)
        moved = pltpu.roll(moved, LANES - ROOM, 1)
        flags += moved[FLAG : FLAG + 1]
        within, count = moved[WITHIN : WITHIN + 1], moved[COUNT : COUNT + 1]
        wanted = []
        for region in range(2 * REACH + 1):
            course = region - 1
            shift = direction_shift(course) if region else 0
            owners = [tile - shift for tile in readers if 0 <= tile - shift < tiles]
            sent = 0
            for owner in owners if region else ():
                row = sent_row(course, send)
                values = blocks[owner][row : row + send]
                sent += jnp.where(member == (owner + shift) % TOGETHER, values, 0)
            for entry in range(region, APER, 2 * REACH + 1):
                cell = lists[SLOT + entry : SLOT + entry + 1]
                if region:
                    place = cell - (CELLS + course * send)
                    cell = sent[:1]
                    for other in range(1, send):
                        cell = jnp.where(place == other, sent[other : other + 1], cell)
                pattern = lists[PATTERN + entry : PATTERN + entry + 1]
                key = jnp.where(count > entry, pattern * CELLS + cell, -1)
                for owner in owners:
                    there = member == (owner + shift) % TOGETHER
                    wanted.append((owner, jnp.where(there, key, -1)))
        for tile in range(tiles):
            for b in range(bins):
                total = jnp.zeros((KEYS, LANES), jnp.float32)
                for owner, key in wanted:
                    if owner == tile:
                        hit = keys == jnp.where(within == b, key, -1)
                        total += jnp.where(hit, 1.0, 0.0)
                picks_ref[b, :, tile, :, group * LANES : (group + 1) * LANES] = (
                    total.reshape(PATTERNS, CELLS, LANES)
                )
    return flags.astype(jnp.float32)


def two_parts(x):
    high = x.astype(jnp.bfloat16)
    low = (x - high.astype(jnp.float32)).astype(jnp.bfloat16)
    return jnp.concatenate([high, low], 0)


def store_parts(parts_ref, b, x):
    shape = (PATTERNS, *parts_ref.shape[3:])
    high = x.astype(jnp.bfloat16)
    parts_ref[:, 0, b] = high.reshape(shape)
    low = (x - high.astype(jnp.float32)).astype(jnp.bfloat16)
    parts_ref[:, 1, b] = low.reshape(shape)


def kernel_of(kernels, p):
    lower_ref, upper_ref = kernels
    return lower_ref[p] if p < EARLY else upper_ref[p - EARLY]


def back_projected(kernels, parts_ref):
    _, _, bins, side, samples = parts_ref.shape
    rows = bins * side
    both = jnp.zeros((2 * rows, samples), jnp.float32)
    for p in range(PATTERNS):
        both += dot_back(
            parts_ref[p].reshape(2 * rows, samples), kernel_of(kernels, p)
        )
    return both[:rows] + both[rows:]


def project(field, kernels, rows_ref):
    bins, _, side, samples = rows_ref.shape
    rows = bins * side
    for p in range(PATTERNS):
        u = jnp.dot(field, kernel_of(kernels, p), preferred_element_type=jnp.float32)
        u = u[:rows] + u[rows:] if field.shape[0] > rows else u
        rows_ref[:, p] = u.astype(jnp.bfloat16).reshape(bins, side, samples)


def mixed(gram_ref, rows_ref, b):
    _, _, side, samples = rows_ref.shape
    return jnp.dot(
        gram_ref[b],
        rows_ref[b].reshape(PATTERNS * side, samples),
        preferred_element_type=jnp.float32,
    )


def smoothed(field, before, after):
    side = before.shape[0]
    lower = jnp.concatenate([before, field[:-side]], 0)
    upper = jnp.concatenate([field[side:], after], 0)
    return smooth_weight * (2.0 * field - lower - upper)


def first_kernel(
    tiles, bins, send, landed_ref, lower_ref, kernels_arg,
    start_ref, local_ref, gram_ref, first_swap_ref, second_swap_ref, full_ref, upper_ref,
    picks_ref, rows_ref, parts_ref, arrived,
):
    copies = [
        pltpu.make_async_copy(kernels_arg.at[EARLY + p], upper_ref.at[p], arrived.at[p])
        for p in range(PATTERNS - EARLY)
    ]
    for copy in copies:
        copy.start()
    kernels = (lower_ref, upper_ref)
    side = tiles * CELLS
    samples = start_ref.shape[1]
    flags = total(fill_picks(tiles, bins, send, landed_ref, picks_ref))
    full_ref[...] = jnp.broadcast_to(flags, full_ref.shape)
    traces = jnp.concatenate(
        [
            landed_ref[:, i * ROOM : (i + 1) * ROOM].reshape(-1, LANES)
            for i in range(samples // LANES)
        ],
        1,
    )
    for b in range(bins):
        picks = picks_ref[b].reshape(PATTERNS * side, -1).astype(jnp.bfloat16)
        gram_ref[b] = dot_back(picks, picks).astype(jnp.bfloat16)
        sums = jnp.dot(picks, traces, preferred_element_type=jnp.float32)
        parts_ref[:, 0, b] = sums.astype(jnp.bfloat16).reshape(PATTERNS, side, samples)
    start = jnp.zeros((bins * side, samples), jnp.float32)
    for p in range(PATTERNS):
        if p >= EARLY:
            copies[p - EARLY].wait()
        rows = parts_ref[p, 0].reshape(bins * side, samples)
        start += dot_back(rows, kernel_of(kernels, p))
    start = start.astype(jnp.bfloat16)
    start_ref[...] = start
    field = start.astype(jnp.float32)
    nothing = jnp.zeros((side, samples), jnp.float32)
    project(start, kernels, rows_ref)
    for b in range(bins):
        store_parts(parts_ref, b, mixed(gram_ref, rows_ref, b))
    local = back_projected(kernels, parts_ref) + smoothed(field, nothing, nothing)
    local_ref[...] = local
    local = local.astype(jnp.bfloat16)
    odd = own_block(tiles) % 2 > 0
    for out_ref, to_after in ((first_swap_ref, ~odd), (second_swap_ref, odd)):
        out_ref[:side] = jnp.where(to_after, start[-side:], start[:side])
        out_ref[side:] = jnp.where(to_after, local[-side:], local[:side])


FULL, STEP, GROW = 4, 5, 6


def ahead_kernel(local_ref, gram_ref, lower_ref, upper_ref, rows_ref, mixed_ref):
    project(two_parts(local_ref[...]), (lower_ref, upper_ref), rows_ref)
    for b in range(rows_ref.shape[0]):
        mixed_ref[b] = mixed(gram_ref, rows_ref, b)


def second_kernel(
    tiles, offs, start_ref, local_ref, gram_ref, lower_ref, upper_ref, first_swap_ref,
    second_swap_ref, full_ref, ahead_ref, mixed_ref,
    once_ref, smooth_ref, parts_ref, sums_ref, rows_ref,
):
    bins, _, side, samples = rows_ref.shape
    start = start_ref[...].astype(jnp.float32)
    place = lax.axis_index("off") * tiles + own_block(tiles)
    ends = [place > 0, place < offs * tiles - 1]
    odd = own_block(tiles) % 2 > 0
    first = first_swap_ref[...].astype(jnp.float32)
    second = second_swap_ref[...].astype(jnp.float32)
    edges = [jnp.where(odd, first, second), jnp.where(odd, second, first)]
    beyond, outer = [], []
    for end, (edge, own) in enumerate(zip(edges, (start[:side], start[-side:]))):
        there = jnp.where(ends[end], smooth_weight, 0.0)
        beyond.append(-smooth_weight * edge[:side])
        outer.append(edge[side:] - there * own)
    inner = [jnp.zeros(((bins - 2) * side, samples), jnp.float32)] if bins > 2 else []
    beyond = jnp.concatenate([beyond[0], *inner, beyond[1]], 0)
    once = local_ref[...] + beyond
    once_ref[...] = once
    smooth = smoothed(once, outer[0], outer[1])
    smooth_ref[...] = smooth
    project(beyond.astype(jnp.bfloat16), (lower_ref, upper_ref), rows_ref)
    square = 0.0
    for b in range(bins):
        both = mixed_ref[b] + mixed(gram_ref, rows_ref, b)
        store_parts(parts_ref, b, both)
        rows = ahead_ref[b].astype(jnp.float32) + rows_ref[b].astype(jnp.float32)
        square += total(rows.reshape(both.shape) * both)
    products = [
        total(start * start),
        total(start * once),
        total(once * once),
        total(once * smooth) + square,
    ]
    lane = lax.broadcasted_iota(jnp.int32, (1, LANES), 1)
    line = jnp.where(lane == FULL, full_ref[:1], 0.0)
    for i, product in enumerate(products):
        line = jnp.where(lane == i, product, line)
    sums_ref[...] = jnp.broadcast_to(line, sums_ref.shape)


def last_kernel(parts_ref, lower_ref, upper_ref, out_ref):
    out_ref[...] = back_projected((lower_ref, upper_ref), parts_ref)


def pack_kernel(sums_ref, start_ref, once_ref, smooth_ref, normal_ref, *refs):
    *out_refs, out_ref = refs
    tiles = len(out_refs)
    ss, so, oo = (sums_ref[:1, i : i + 1] for i in range(3))
    step, grow = own_scales(ss, so, oo)
    start, once = start_ref[...].astype(jnp.float32), once_ref[...]
    twice = normal_ref[...] + smooth_ref[...]
    row = 0
    for field in (start, start - step * once, grow * once - step * twice):
        samples = field.shape[1]
        field = field.reshape(-1, tiles, CELLS, samples)
        size = field.shape[0] * CELLS
        for i in range(0, samples, LANES):
            for tile in range(tiles):
                piece = field[:, tile, :, i : i + LANES].reshape(size, LANES)
                out_ref[tile, row : row + size] = piece.astype(jnp.bfloat16)
            row += size
    lane = lax.broadcasted_iota(jnp.int32, (1, LANES), 1)
    rest = jnp.where(lane == STEP, step, sums_ref[:1])
    rest = jnp.where(lane == GROW, grow, rest)
    line = lax.broadcasted_iota(jnp.int32, (16, LANES), 0)
    parts = jnp.zeros((16, LANES), jnp.float32)
    for i in range(3):
        part = rest.astype(jnp.bfloat16).astype(jnp.float32)
        rest = rest - part
        parts = jnp.where(line == i, part, parts)
    for tile in range(tiles):
        out_ref[tile, row:] = parts.astype(jnp.bfloat16)
    lay_out(out_ref, out_refs)


def total(x):
    return jnp.sum(jnp.sum(x, 0, keepdims=True), 1, keepdims=True)


def own_scales(ss, so, oo):
    step = ss / so
    step = jnp.where(step > 0.0, jnp.clip(step, 1e-8, 1e3), 1.0)
    grow = step * step * oo / ss
    return step, jnp.where(grow > 0.0, jnp.clip(grow, 0.0, 1e3), 1.0)


def place_kernel(bins, *refs):
    *landed_refs, solution_ref, residual_ref, landed_ref = refs
    gather_in(landed_refs, landed_ref)
    tiles, length, _ = landed_ref.shape
    size = bins * CELLS
    samples = solution_ref.shape[2]
    pieces = samples // LANES

    def line_of(source):
        parts = landed_ref[source, length - 16 :].astype(jnp.float32)
        return jnp.sum(parts, 0, keepdims=True)

    def vector(source, i):
        part = [
            landed_ref[source, (i * pieces + j) * size : (i * pieces + j + 1) * size]
            for j in range(pieces)
        ]
        return jnp.concatenate(part, 1).astype(jnp.float32)

    sums = sum(line_of(tile) for tile in range(tiles))
    ss, so, oo, ot = (sums[:, i : i + 1] for i in range(4))
    step_0 = ss / so
    norm_1 = step_0 * step_0 * oo - ss
    grow = 1.0 + norm_1 / ss
    step_1 = norm_1 / (grow * grow * so - 2.0 * step_0 * grow * oo + step_0 * step_0 * ot)
    near = step_0 + step_1 * grow
    far = step_1 * step_0
    fields = [[], []]
    for block in range(tiles):
        source = jnp.where(
            flipped(), path_rank(tiles - 1 - block, tiles), path_rank(block, tiles)
        )
        line = line_of(source)
        inverse = 1.0 / line[:, STEP : STEP + 1]
        there = line[:, GROW : GROW + 1]
        start, first, second = (vector(source, i) for i in range(3))
        far_once = far * inverse
        near_once = near * inverse - far_once * there * inverse
        solution = (near - far_once) * start + far_once * first
        residual = (1.0 - near_once) * start + near_once * first - far_once * second
        fields[0].append(solution.reshape(bins, CELLS, samples))
        fields[1].append(residual.reshape(bins, CELLS, samples))
    solution_ref[...] = jnp.swapaxes(jnp.concatenate(fields[0], 0), 0, 1)
    residual_ref[...] = jnp.swapaxes(jnp.concatenate(fields[1], 0), 0, 1)


def copy_kernel(*refs):
    *refs, arrived = refs
    half = len(refs) // 2
    copies = [
        pltpu.make_async_copy(refs[i], refs[half + i], arrived.at[i]) for i in range(half)
    ]
    for copy in copies:
        copy.start()
    for copy in copies:
        copy.wait()


VMEM = pl.BlockSpec(memory_space=pltpu.VMEM)
HBM = pl.BlockSpec(memory_space=pltpu.HBM)


def local_call(kernel, name, in_specs, out_shape, scratch=(), out_specs=None, cost=0):
    return pl.pallas_call(
        kernel,
        out_shape=out_shape,
        in_specs=in_specs,
        out_specs=out_specs or jax.tree.map(lambda _: VMEM, out_shape),
        scratch_shapes=list(scratch),
        cost_estimate=pl.CostEstimate(
            flops=cost, bytes_accessed=cost // 256, transcendentals=0
        )
        if cost
        else None,
        compiler_params=pltpu.CompilerParams(vmem_limit_bytes=32 * 1024 * 1024),
        name=name,
    )


def shards_by_bin(
    traces, kernels, send_list, aper_slot, aper_pattern, trace_bin, trace_count
):
    tiles, offs = lax.axis_size("mid"), lax.axis_size("off")
    bins = NOFF // offs // tiles
    trace_rows, samples = traces.shape
    send = send_list.shape[2]
    rows = bins * tiles * CELLS
    side = tiles * CELLS
    sums = bins * (CELLS + 2 * REACH * send)

    def array(*shape, dtype=jnp.float32):
        return jax.ShapeDtypeStruct(shape, dtype)

    bf16 = functools.partial(array, dtype=jnp.bfloat16)
    in_hbm = functools.partial(
        pltpu.with_memory_space_constraint, memory_space=pltpu.HBM
    )
    lists = (send_list, aper_slot, aper_pattern, trace_bin, trace_count)
    early = bf16(EARLY, samples, samples)
    shared, lower = local_call(
        functools.partial(share_kernel, tiles, bins, ROOM),
        "share",
        [HBM] * 7,
        (bf16(tiles, samples // LANES * ROOM + 2 * APER, LANES), early),
        [
            pltpu.SMEM(send_list.shape, jnp.int32),
            pltpu.VMEM(aper_slot.shape, jnp.int32),
            pltpu.VMEM(aper_pattern.shape, jnp.int32),
            pltpu.VMEM((1, trace_rows), jnp.int32),
            pltpu.VMEM((1, trace_rows), jnp.int32),
            pltpu.VMEM(traces.shape, jnp.bfloat16),
            pltpu.SemaphoreType.DMA((6,)),
            pltpu.SemaphoreType.DMA,
        ],
    )(
        in_hbm(send_list),
        in_hbm(aper_slot),
        in_hbm(aper_pattern),
        in_hbm(trace_bin[None]),
        in_hbm(trace_count[None]),
        in_hbm(traces),
        in_hbm(kernels),
    )
    landed = lax.all_to_all(shared, "mid", 0, 0)
    pattern_rows = pltpu.VMEM((bins, PATTERNS, side, samples), jnp.bfloat16)
    parts_type = bf16(PATTERNS, 2, bins, side, samples)
    start, local, gram, *swaps, full, upper = local_call(
        functools.partial(first_kernel, tiles, bins, send),
        "first",
        [VMEM, VMEM, HBM],
        (
            bf16(rows, samples),
            array(rows, samples),
            bf16(bins, tiles * KEYS, tiles * KEYS),
            bf16(2 * side, samples),
            bf16(2 * side, samples),
            array(8, LANES),
            bf16(PATTERNS - EARLY, samples, samples),
        ),
        [
            pltpu.VMEM((bins, PATTERNS, tiles, CELLS, tiles * ROOM), jnp.float32),
            pattern_rows,
            pltpu.VMEM(parts_type.shape, parts_type.dtype),
            pltpu.SemaphoreType.DMA((PATTERNS - EARLY,)),
        ],
    )(landed, lower, in_hbm(kernels))

    path = [path_rank(m, tiles) for m in range(tiles)]
    chain = [m * offs + o for o in range(offs) for m in (path[::-1] if o % 2 else path)]
    swaps = [
        lax.ppermute(
            x,
            ("mid", "off"),
            [
                pair
                for i, j in zip(chain[first:-1:2], chain[first + 1 :: 2])
                for pair in ((i, j), (j, i))
            ],
        )
        for first, x in enumerate(swaps)
    ]

    flops = 2 * rows * PATTERNS * samples * samples
    ahead, mixed_ahead = local_call(
        ahead_kernel,
        "ahead",
        [VMEM] * 4,
        (bf16(*pattern_rows.shape), array(bins, PATTERNS * side, samples)),
        cost=3 * flops,
    )(local, gram, lower, upper)
    field = array(rows, samples)
    once, smooth, parts, products = local_call(
        functools.partial(second_kernel, tiles, offs),
        "second",
        [VMEM] * 10,
        (field, field, parts_type, array(8, LANES)),
        [pattern_rows],
        cost=2 * flops,
    )(start, local, gram, lower, upper, *swaps, full, ahead, mixed_ahead)

    projected = local_call(last_kernel, "last", [VMEM] * 3, field, cost=2 * flops)(
        parts, lower, upper
    )
    addends = [products] + [
        lax.ppermute(products, "off", [(i, i ^ step) for i in range(offs)])
        for step in range(1, offs)
    ]
    while len(addends) > 1:
        addends = [a + b for a, b in zip(addends[::2], addends[1::2])]
    products = addends[0]
    chunk = bf16(samples // LANES * 3 * bins * CELLS + 16, LANES)
    chunks = pltpu.VMEM((tiles, *chunk.shape), chunk.dtype)
    packed = local_call(
        pack_kernel, "pack", [VMEM] * 5, [chunk] * tiles, [chunks]
    )(products, start, once, smooth, projected)
    landed = swapped(packed)

    def again():
        arguments = [in_hbm(x) for x in (traces, kernels, *lists[:3])]
        arguments += [in_hbm(x[None]) for x in lists[3:]]
        *copies, bins_again, count_again = local_call(
            copy_kernel,
            "again",
            [HBM] * len(arguments),
            tuple(array(*x.shape, dtype=x.dtype) for x in arguments),
            [pltpu.SemaphoreType.DMA((len(arguments),))],
            out_specs=(HBM,) * len(arguments),
        )(*arguments)
        return *copies, bins_again[0], count_again[0]

    def placed():
        out_type = pltpu.HBM((CELLS, bins * tiles, samples), jnp.float32)
        return local_call(
            functools.partial(place_kernel, bins),
            "place",
            [VMEM] * tiles,
            (out_type, out_type),
            [chunks],
            out_specs=(VMEM, VMEM),
        )(*landed)

    return lax.cond(
        products[0, FULL] > 0.0, lambda: shards_by_tile(*again()), placed
    )


def fits_by_bin(tiles, offs, send, trace_rows, samples):
    return (
        (NOFF // offs) % (2 * tiles) == 0
        and offs & (offs - 1) == 0
        and tiles & (tiles - 1) == 0
        and tiles % TOGETHER == 0
        and send == WITHIN
        and trace_rows == LANES
        and samples % LANES == 0
    )


def solution(mesh):
    in_specs = (
        P(("mid", "off"), None),
        P(),
        P("mid", None, None),
        P(None, ("mid", "off")),
        P(None, ("mid", "off")),
        P(("mid", "off")),
        P(("mid", "off")),
    )
    out_specs = (P("mid", "off", None), P("mid", "off", None))

    def shards(traces, kernels, send_list, *lists):
        fits = fits_by_bin(
            mesh.shape["mid"], mesh.shape["off"], send_list.shape[2], *traces.shape
        )
        form = shards_by_bin if fits else shards_by_tile
        return form(traces, kernels, send_list, *lists)

    return jax.shard_map(
        shards, mesh=mesh, in_specs=in_specs, out_specs=out_specs, check_vma=False
    )
```

```python
import functools

import jax
import jax.numpy as jnp
from jax import lax
from jax.experimental import pallas as pl
from jax.experimental.pallas import tpu as pltpu
from jax.sharding import PartitionSpec as P

NOFF = 64
PATTERNS = 8
REACH = 2
APER = 8
ITERS = 2
CELLS = 8
KEYS = PATTERNS * CELLS
EARLY = 3
ROOM = 32
LANES = 128
TOGETHER = LANES // ROOM


smooth_weight = 2.0


def padded_2(x, sides, width):
    for axis, dim in sides:
        peers, length = (lax.axis_size(axis), x.shape[dim])
        up = [(i, (i + 1) % peers) for i in range(peers - 1)]
        down = [(j, i) for i, j in up]
        last = lax.slice_in_dim(x, length - width, length, axis=dim)
        first = lax.slice_in_dim(x, 0, width, axis=dim)
        before = lax.ppermute(last, axis, up)
        after = lax.ppermute(first, axis, down)
        x = jnp.concatenate([before, x, after], axis=dim)
    return x


def from_behind(x, axis, by):
    peers = lax.axis_size(axis)
    pairs = [(i, i + by) for i in range(peers) if 0 <= i + by < peers]
    return lax.ppermute(x, axis, pairs)


def direction_shift(course):
    return (course // 2 + 1) * (1 - 2 * (course % 2))


def offset_laplace(padded):
    return smooth_weight * (2.0 * padded[:, 1:-1] - padded[:, :-2] - padded[:, 2:])


def smoothing(field):
    padded = padded_2(field, (("off", 1),), 1)
    smoothed = offset_laplace(padded)
    return smoothed


def deliver(outgoing):
    arrived = [None] * (2 * REACH)
    for course in range(2 * REACH):
        arrived[course] = from_behind(outgoing[course], "mid", direction_shift(course))
    return arrived


def give_back(returning):
    landed = [None] * (2 * REACH)
    for course in range(2 * REACH):
        landed[course] = from_behind(returning[course], "mid", -direction_shift(course))
    return landed


def shards_by_tile(
    traces, kernels, send_list, aper_slot, aper_pattern, trace_bin, trace_count
):
    off_dev = NOFF // lax.axis_size("off")
    trace_rows = traces.shape[0]
    samples = traces.shape[1]
    chosen_cells = send_list[0]
    send_count = chosen_cells.shape[1]
    slot_count = CELLS + 2 * REACH * send_count
    live_mask = jnp.arange(APER, dtype=jnp.int32)[:, None] < trace_count[None, :]
    row_index = (aper_slot * off_dev + trace_bin[None, :]).reshape(-1)
    pattern_ids = jnp.arange(PATTERNS, dtype=jnp.int32)[:, None, None]
    chooser = ((aper_pattern[None] == pattern_ids) & live_mask[None]).astype(
        jnp.bfloat16
    )
    pick_rows = (
        aper_pattern * trace_rows + jnp.arange(trace_rows, dtype=jnp.int32)[None, :]
    ).reshape(-1)
    live_column = live_mask.reshape(-1, 1).astype(jnp.float32)

    def forward(field_bf):
        outgoing = [field_bf[chosen_cells[course]] for course in range(2 * REACH)]
        arrived = deliver(outgoing)
        slot_rows = jnp.concatenate([field_bf] + arrived, 0).reshape(-1, samples)
        blocks = slot_rows[row_index].reshape(APER, trace_rows, samples)
        pattern_sums = jnp.einsum(
            "pjt,jtn->ptn", chooser, blocks, preferred_element_type=jnp.float32
        ).astype(jnp.bfloat16)
        return jnp.einsum(
            "ptn,pnm->tm", pattern_sums, kernels, preferred_element_type=jnp.float32
        )

    def adjoint(values_bf):
        spread = jnp.einsum(
            "tm,pnm->ptn", values_bf, kernels, preferred_element_type=jnp.float32
        ).reshape(-1, samples)
        entries = spread[pick_rows] * live_column
        slot_sums = (
            jnp.zeros((slot_count * off_dev, samples), jnp.float32)
            .at[row_index]
            .add(entries)
        )
        slot_sums = slot_sums.reshape(slot_count, off_dev, samples)
        returning = [
            slot_sums[CELLS + course * send_count : CELLS + (course + 1) * send_count]
            for course in range(2 * REACH)
        ]
        landed = give_back(returning)
        accumulated = slot_sums[:CELLS]
        for course in range(2 * REACH):
            accumulated = accumulated.at[chosen_cells[course]].add(landed[course])
        return accumulated

    def global_total(value):
        return lax.psum(value, ("mid", "off"))

    residual = adjoint(traces)
    direction = residual
    solution = jnp.zeros_like(residual)
    norm_now = global_total(jnp.sum(residual * residual))
    for iteration in range(ITERS):
        applied = adjoint(
            forward(direction.astype(jnp.bfloat16)).astype(jnp.bfloat16)
        ) + smoothing(direction)
        step_size = norm_now / global_total(jnp.sum(direction * applied))
        solution = solution + step_size * direction
        residual = residual - step_size * applied
        if iteration + 1 < ITERS:
            norm_next = global_total(jnp.sum(residual * residual))
            direction = residual + norm_next / norm_now * direction
            norm_now = norm_next
    return (solution, residual)


def path_rank(m, tiles):
    return m ^ ((m >> 1) & 1) if tiles % 4 == 0 else m


def turns(peers):
    near, far = range(1, peers // 2), range(peers // 2, peers)
    even = [i for pair in zip(far, near) for i in pair]
    odd = [i for pair in zip(near, far) for i in pair]
    return [(0, 0), *zip(even, odd), (peers - 1, peers - 1)]


def partners(peers):
    odd, place = flipped(), lax.axis_index("mid")
    return [place ^ jnp.where(odd, j, i) for i, j in turns(peers)]


def lay_out(chunks_ref, out_refs):
    for partner, out_ref in zip(partners(len(out_refs)), out_refs):
        out_ref[...] = chunks_ref[partner]


def gather_in(landed_refs, chunks_ref):
    for partner, landed_ref in zip(partners(len(landed_refs)), landed_refs):
        chunks_ref[partner] = landed_ref[...]


def swapped(chunks):
    peers, offs = len(chunks), lax.axis_size("off")
    return list(chunks[:1]) + [
        lax.ppermute(
            chunk,
            ("mid", "off"),
            [
                (m * offs + o, (m ^ turn[o % 2]) * offs + o)
                for m in range(peers)
                for o in range(offs)
            ],
        )
        for turn, chunk in zip(turns(peers)[1:], chunks[1:])
    ]


def flipped():
    return lax.axis_index("off") % 2 > 0


def own_block(tiles):
    block = path_rank(lax.axis_index("mid"), tiles)
    return jnp.where(flipped(), tiles - 1 - block, block)


def dot_back(rows, kernel):
    return lax.dot_general(
        rows, kernel, (((1,), (1,)), ((), ())), preferred_element_type=jnp.float32
    )


SLOT, PATTERN, WITHIN, COUNT, FLAG = 0, APER, 4, 5, 6


def share_kernel(
    tiles, bins, room, sends_arg, slot_arg, pattern_arg, bin_arg, count_arg, traces_arg,
    kernels_arg, out_ref, kernels_ref, sends_ref, slot_ref, pattern_ref, bin_ref, count_ref, traces_ref,
    staged, arrived,
):
    rows, samples = traces_ref.shape
    stages = [
        pltpu.make_async_copy(arg, ref, staged.at[i])
        for i, (arg, ref) in enumerate(
            [
                (bin_arg, bin_ref),
                (slot_arg, slot_ref),
                (pattern_arg, pattern_ref),
                (count_arg, count_ref),
                (sends_arg, sends_ref),
                (traces_arg, traces_ref),
            ]
        )
    ]
    kernels = pltpu.make_async_copy(
        kernels_arg.at[:EARLY], kernels_ref, arrived
    )
    for stage in stages + [kernels]:
        stage.start()
    index = lax.broadcasted_iota(jnp.int32, (tiles, rows), 0)
    earlier = lax.broadcasted_iota(jnp.int32, (rows, rows), 0) < (
        lax.broadcasted_iota(jnp.int32, (rows, rows), 1)
    )
    earlier = jnp.where(earlier, 1.0, 0.0).astype(jnp.bfloat16)
    stages[0].wait()
    offset_bin = bin_ref[...]
    block = lax.div(offset_bin, bins)
    within = offset_bin - block * bins
    chunk = path_rank(jnp.where(flipped(), tiles - 1 - block, block), tiles)
    belongs = jnp.where(index == chunk, 1.0, 0.0)
    rank = jnp.dot(
        belongs.astype(jnp.bfloat16), earlier, preferred_element_type=jnp.float32
    )
    rank = jnp.sum(rank * belongs, 0, keepdims=True).astype(jnp.int32)
    full = jnp.max(rank, axis=1, keepdims=True) >= room
    target = jnp.where(rank < room, chunk * room + rank, -1)
    picks = lax.broadcasted_iota(jnp.int32, (tiles * room, rows), 0) == target
    picks = jnp.where(picks, 1.0, 0.0).astype(jnp.bfloat16)
    place = lax.axis_index("mid")
    lane = lax.broadcasted_iota(jnp.int32, (1, LANES), 1)
    target = chunk * LANES + lax.rem(place, TOGETHER) * room + rank
    chosen = lax.broadcasted_iota(jnp.int32, (tiles * LANES, rows), 0) == (
        jnp.where(rank < room, target, -1)
    )
    chosen = jnp.where(chosen, 1.0, 0.0).astype(jnp.bfloat16)
    for stage in stages[1:5]:
        stage.wait()
    lists = jnp.concatenate(
        [
            slot_ref[...].astype(jnp.float32),
            pattern_ref[...].astype(jnp.float32),
            jnp.zeros((WITHIN, rows), jnp.float32),
            within.astype(jnp.float32),
            count_ref[...].astype(jnp.float32),
            jnp.zeros((APER - COUNT - 1, rows), jnp.float32),
        ],
        0,
    ).astype(jnp.bfloat16)
    lists = dot_back(lists, chosen)
    _, courses, send = sends_ref.shape
    line = lax.broadcasted_iota(jnp.int32, (2 * APER, LANES), 0)
    sent = jnp.zeros((2 * APER, LANES), jnp.int32)
    for course in range(courses):
        reader = lax.rem(place + direction_shift(course) + TOGETHER, TOGETHER)
        here = lax.div(lane, room) == reader
        for m in range(send):
            value = jnp.where(here, sends_ref[0, course, m], 0)
            sent += jnp.where(line == sent_row(course, send) + m, value, 0)
    past = lax.div(lane, room) == lax.rem(place + 1, TOGETHER)
    sent += jnp.where(past & (line == FLAG) & full, 1, 0)
    sent = sent.astype(jnp.float32)
    pieces = samples // LANES
    for m in range(tiles):
        own = lists[:, m * LANES : (m + 1) * LANES]
        moved = pltpu.roll(own[2 * APER :], room, 1)
        out_ref[m, pieces * room :] = (
            own[: 2 * APER] + jnp.concatenate([moved, jnp.zeros_like(moved)], 0) + sent
        ).astype(jnp.bfloat16)
    stages[5].wait()
    picked = jnp.dot(picks, traces_ref[...], preferred_element_type=jnp.float32)
    picked = picked.reshape(tiles, room, samples).astype(jnp.bfloat16)
    for i in range(pieces):
        out_ref[:, i * room : (i + 1) * room] = picked[:, :, i * LANES : (i + 1) * LANES]
    kernels.wait()


def sent_row(course, send):
    return send if course == 3 else 0


def fill_picks(tiles, bins, send, landed_ref, picks_ref):
    flags = 0
    keys = lax.broadcasted_iota(jnp.int32, (KEYS, LANES), 0)
    member = lax.div(lax.broadcasted_iota(jnp.int32, (1, LANES), 1), ROOM)
    blocks = [
        landed_ref[tile, -2 * APER :].astype(jnp.float32).astype(jnp.int32)
        for tile in range(tiles)
    ]
    for group in range(tiles // TOGETHER):
        readers = range(group * TOGETHER, (group + 1) * TOGETHER)
        lists, moved = 0, 0
        for tile in readers:
            lists += jnp.where(member == tile % TOGETHER, blocks[tile], 0)
            past = member == (tile + 1) % TOGETHER
            moved += jnp.where(past, blocks[tile][:APER], 0)
        moved = pltpu.roll(moved, LANES - ROOM, 1)
        flags += moved[FLAG : FLAG + 1]
        within, count = moved[WITHIN : WITHIN + 1], moved[COUNT : COUNT + 1]
        wanted = []
        for region in range(2 * REACH + 1):
            course = region - 1
            shift = direction_shift(course) if region else 0
            owners = [tile - shift for tile in readers if 0 <= tile - shift < tiles]
            sent = 0
            for owner in owners if region else ():
                row = sent_row(course, send)
                values = blocks[owner][row : row + send]
                sent += jnp.where(member == (owner + shift) % TOGETHER, values, 0)
            for entry in range(region, APER, 2 * REACH + 1):
                cell = lists[SLOT + entry : SLOT + entry + 1]
                if region:
                    place = cell - (CELLS + course * send)
                    cell = sent[:1]
                    for other in range(1, send):
                        cell = jnp.where(place == other, sent[other : other + 1], cell)
                pattern = lists[PATTERN + entry : PATTERN + entry + 1]
                key = jnp.where(count > entry, pattern * CELLS + cell, -1)
                for owner in owners:
                    there = member == (owner + shift) % TOGETHER
                    wanted.append((owner, jnp.where(there, key, -1)))
        for tile in range(tiles):
            for b in range(bins):
                total = jnp.zeros((KEYS, LANES), jnp.float32)
                for owner, key in wanted:
                    if owner == tile:
                        hit = keys == jnp.where(within == b, key, -1)
                        total += jnp.where(hit, 1.0, 0.0)
                picks_ref[b, :, tile, :, group * LANES : (group + 1) * LANES] = (
                    total.reshape(PATTERNS, CELLS, LANES)
                )
    return flags.astype(jnp.float32)


def two_parts(x):
    high = x.astype(jnp.bfloat16)
    low = (x - high.astype(jnp.float32)).astype(jnp.bfloat16)
    return jnp.concatenate([high, low], 0)


def store_parts(parts_ref, b, x):
    shape = (PATTERNS, *parts_ref.shape[3:])
    high = x.astype(jnp.bfloat16)
    parts_ref[:, 0, b] = high.reshape(shape)
    low = (x - high.astype(jnp.float32)).astype(jnp.bfloat16)
    parts_ref[:, 1, b] = low.reshape(shape)


def kernel_of(kernels, p):
    lower_ref, upper_ref = kernels
    return lower_ref[p] if p < EARLY else upper_ref[p - EARLY]


def back_projected(kernels, parts_ref):
    _, _, bins, side, samples = parts_ref.shape
    rows = bins * side
    both = jnp.zeros((2 * rows, samples), jnp.float32)
    for p in range(PATTERNS):
        both += dot_back(
            parts_ref[p].reshape(2 * rows, samples), kernel_of(kernels, p)
        )
    return both[:rows] + both[rows:]


def project(field, kernels, rows_ref):
    bins, _, side, samples = rows_ref.shape
    rows = bins * side
    for p in range(PATTERNS):
        u = jnp.dot(field, kernel_of(kernels, p), preferred_element_type=jnp.float32)
        u = u[:rows] + u[rows:] if field.shape[0] > rows else u
        rows_ref[:, p] = u.astype(jnp.bfloat16).reshape(bins, side, samples)


def mixed(gram_ref, rows_ref, b):
    _, _, side, samples = rows_ref.shape
    return jnp.dot(
        gram_ref[b],
        rows_ref[b].reshape(PATTERNS * side, samples),
        preferred_element_type=jnp.float32,
    )


def smoothed(field, before, after):
    side = before.shape[0]
    lower = jnp.concatenate([before, field[:-side]], 0)
    upper = jnp.concatenate([field[side:], after], 0)
    return smooth_weight * (2.0 * field - lower - upper)


def store_edges(out_refs, tiles, field):
    side = tiles * CELLS
    odd = own_block(tiles) % 2 > 0
    for out_ref, to_after in zip(out_refs, (~odd, odd)):
        out_ref[...] = jnp.where(to_after, field[-side:], field[:side])


def edges_beyond(landed_refs, tiles):
    odd = own_block(tiles) % 2 > 0
    first, second = (ref[...].astype(jnp.float32) for ref in landed_refs)
    return jnp.where(odd, first, second), jnp.where(odd, second, first)


def first_kernel(
    tiles, bins, send, landed_ref, lower_ref, kernels_arg,
    start_ref, picks_ref, first_swap_ref, second_swap_ref, full_ref, upper_ref,
    counts_ref, parts_ref, arrived,
):
    copies = [
        pltpu.make_async_copy(kernels_arg.at[EARLY + p], upper_ref.at[p], arrived.at[p])
        for p in range(PATTERNS - EARLY)
    ]
    for copy in copies:
        copy.start()
    kernels = (lower_ref, upper_ref)
    side = tiles * CELLS
    samples = start_ref.shape[1]
    flags = total(fill_picks(tiles, bins, send, landed_ref, counts_ref))
    full_ref[...] = jnp.broadcast_to(flags, full_ref.shape)
    traces = jnp.concatenate(
        [
            landed_ref[:, i * ROOM : (i + 1) * ROOM].reshape(-1, LANES)
            for i in range(samples // LANES)
        ],
        1,
    )
    for b in range(bins):
        picks = counts_ref[b].reshape(PATTERNS * side, -1).astype(jnp.bfloat16)
        picks_ref[b] = picks
        sums = jnp.dot(picks, traces, preferred_element_type=jnp.float32)
        parts_ref[:, b] = sums.astype(jnp.bfloat16).reshape(PATTERNS, side, samples)
    start = jnp.zeros((bins * side, samples), jnp.float32)
    for p in range(PATTERNS):
        if p >= EARLY:
            copies[p - EARLY].wait()
        rows = parts_ref[p].reshape(bins * side, samples)
        start += dot_back(rows, kernel_of(kernels, p))
    start = start.astype(jnp.bfloat16)
    start_ref[...] = start
    store_edges((first_swap_ref, second_swap_ref), tiles, start)


def local_kernel(
    start_ref, picks_ref, lower_ref, upper_ref, local_ref, gram_ref, rows_ref, parts_ref
):
    bins, _, side, samples = rows_ref.shape
    kernels = (lower_ref, upper_ref)
    for b in range(bins):
        gram_ref[b] = dot_back(picks_ref[b], picks_ref[b]).astype(jnp.bfloat16)
    project(start_ref[...], kernels, rows_ref)
    for b in range(bins):
        store_parts(parts_ref, b, mixed(gram_ref, rows_ref, b))
    nothing = jnp.zeros((side, samples), jnp.float32)
    local_ref[...] = back_projected(kernels, parts_ref) + smoothed(
        start_ref[...].astype(jnp.float32), nothing, nothing
    )


def complete_kernel(tiles, local_ref, first_ref, second_ref, once_ref, *out_refs):
    before, after = edges_beyond((first_ref, second_ref), tiles)
    side = before.shape[0]
    local = local_ref[...]
    inner = [local[side:-side]] if local.shape[0] > 2 * side else []
    first = local[:side] - smooth_weight * before
    last = local[-side:] - smooth_weight * after
    once_ref[...] = jnp.concatenate([first, *inner, last], 0)
    store_edges(
        out_refs, tiles, jnp.concatenate([first, last], 0).astype(jnp.bfloat16)
    )


FULL, STEP, GROW = 4, 5, 6


def mix_kernel(
    once_ref, gram_ref, lower_ref, upper_ref, parts_ref, square_ref, rows_ref
):
    project(two_parts(once_ref[...]), (lower_ref, upper_ref), rows_ref)
    square = 0.0
    for b in range(rows_ref.shape[0]):
        both = mixed(gram_ref, rows_ref, b)
        store_parts(parts_ref, b, both)
        square += total(rows_ref[b].astype(jnp.float32).reshape(both.shape) * both)
    square_ref[...] = jnp.broadcast_to(square, square_ref.shape)


def sums_kernel(
    tiles, start_ref, once_ref, first_ref, second_ref, square_ref, full_ref,
    smooth_ref, sums_ref,
):
    start, once = start_ref[...].astype(jnp.float32), once_ref[...]
    smooth = smoothed(once, *edges_beyond((first_ref, second_ref), tiles))
    smooth_ref[...] = smooth
    products = [
        total(start * start),
        total(start * once),
        total(once * once),
        total(once * smooth) + square_ref[:1, :1],
    ]
    lane = lax.broadcasted_iota(jnp.int32, (1, LANES), 1)
    line = jnp.where(lane == FULL, full_ref[:1], 0.0)
    for i, product in enumerate(products):
        line = jnp.where(lane == i, product, line)
    sums_ref[...] = jnp.broadcast_to(line, sums_ref.shape)


def last_kernel(parts_ref, lower_ref, upper_ref, out_ref):
    out_ref[...] = back_projected((lower_ref, upper_ref), parts_ref)


def pack_kernel(sums_ref, start_ref, once_ref, smooth_ref, normal_ref, *refs):
    *out_refs, out_ref = refs
    tiles = len(out_refs)
    ss, so, oo = (sums_ref[:1, i : i + 1] for i in range(3))
    step, grow = own_scales(ss, so, oo)
    start, once = start_ref[...].astype(jnp.float32), once_ref[...]
    twice = normal_ref[...] + smooth_ref[...]
    row = 0
    for field in (start, start - step * once, grow * once - step * twice):
        samples = field.shape[1]
        field = field.reshape(-1, tiles, CELLS, samples)
        size = field.shape[0] * CELLS
        for i in range(0, samples, LANES):
            for tile in range(tiles):
                piece = field[:, tile, :, i : i + LANES].reshape(size, LANES)
                out_ref[tile, row : row + size] = piece.astype(jnp.bfloat16)
            row += size
    lane = lax.broadcasted_iota(jnp.int32, (1, LANES), 1)
    rest = jnp.where(lane == STEP, step, sums_ref[:1])
    rest = jnp.where(lane == GROW, grow, rest)
    line = lax.broadcasted_iota(jnp.int32, (16, LANES), 0)
    parts = jnp.zeros((16, LANES), jnp.float32)
    for i in range(3):
        part = rest.astype(jnp.bfloat16).astype(jnp.float32)
        rest = rest - part
        parts = jnp.where(line == i, part, parts)
    for tile in range(tiles):
        out_ref[tile, row:] = parts.astype(jnp.bfloat16)
    lay_out(out_ref, out_refs)


def total(x):
    return jnp.sum(jnp.sum(x, 0, keepdims=True), 1, keepdims=True)


def own_scales(ss, so, oo):
    step = ss / so
    step = jnp.where(step > 0.0, jnp.clip(step, 1e-8, 1e3), 1.0)
    grow = step * step * oo / ss
    return step, jnp.where(grow > 0.0, jnp.clip(grow, 0.0, 1e3), 1.0)


def place_kernel(bins, *refs):
    *landed_refs, solution_ref, residual_ref, landed_ref = refs
    gather_in(landed_refs, landed_ref)
    tiles, length, _ = landed_ref.shape
    size = bins * CELLS
    samples = solution_ref.shape[2]
    pieces = samples // LANES

    def line_of(source):
        parts = landed_ref[source, length - 16 :].astype(jnp.float32)
        return jnp.sum(parts, 0, keepdims=True)

    def vector(source, i):
        part = [
            landed_ref[source, (i * pieces + j) * size : (i * pieces + j + 1) * size]
            for j in range(pieces)
        ]
        return jnp.concatenate(part, 1).astype(jnp.float32)

    sums = sum(line_of(tile) for tile in range(tiles))
    ss, so, oo, ot = (sums[:, i : i + 1] for i in range(4))
    step_0 = ss / so
    norm_1 = step_0 * step_0 * oo - ss
    grow = 1.0 + norm_1 / ss
    step_1 = norm_1 / (grow * grow * so - 2.0 * step_0 * grow * oo + step_0 * step_0 * ot)
    near = step_0 + step_1 * grow
    far = step_1 * step_0
    fields = [[], []]
    for block in range(tiles):
        source = jnp.where(
            flipped(), path_rank(tiles - 1 - block, tiles), path_rank(block, tiles)
        )
        line = line_of(source)
        inverse = 1.0 / line[:, STEP : STEP + 1]
        there = line[:, GROW : GROW + 1]
        start, first, second = (vector(source, i) for i in range(3))
        far_once = far * inverse
        near_once = near * inverse - far_once * there * inverse
        solution = (near - far_once) * start + far_once * first
        residual = (1.0 - near_once) * start + near_once * first - far_once * second
        fields[0].append(solution.reshape(bins, CELLS, samples))
        fields[1].append(residual.reshape(bins, CELLS, samples))
    solution_ref[...] = jnp.swapaxes(jnp.concatenate(fields[0], 0), 0, 1)
    residual_ref[...] = jnp.swapaxes(jnp.concatenate(fields[1], 0), 0, 1)


def copy_kernel(*refs):
    *refs, arrived = refs
    half = len(refs) // 2
    copies = [
        pltpu.make_async_copy(refs[i], refs[half + i], arrived.at[i]) for i in range(half)
    ]
    for copy in copies:
        copy.start()
    for copy in copies:
        copy.wait()


VMEM = pl.BlockSpec(memory_space=pltpu.VMEM)
HBM = pl.BlockSpec(memory_space=pltpu.HBM)


def local_call(kernel, name, in_specs, out_shape, scratch=(), out_specs=None, cost=0):
    return pl.pallas_call(
        kernel,
        out_shape=out_shape,
        in_specs=in_specs,
        out_specs=out_specs or jax.tree.map(lambda _: VMEM, out_shape),
        scratch_shapes=list(scratch),
        cost_estimate=pl.CostEstimate(
            flops=cost, bytes_accessed=cost // 256, transcendentals=0
        )
        if cost
        else None,
        compiler_params=pltpu.CompilerParams(vmem_limit_bytes=32 * 1024 * 1024),
        name=name,
    )


def shards_by_bin(
    traces, kernels, send_list, aper_slot, aper_pattern, trace_bin, trace_count
):
    tiles, offs = lax.axis_size("mid"), lax.axis_size("off")
    bins = NOFF // offs // tiles
    trace_rows, samples = traces.shape
    send = send_list.shape[2]
    rows = bins * tiles * CELLS
    side = tiles * CELLS
    sums = bins * (CELLS + 2 * REACH * send)

    def array(*shape, dtype=jnp.float32):
        return jax.ShapeDtypeStruct(shape, dtype)

    bf16 = functools.partial(array, dtype=jnp.bfloat16)
    in_hbm = functools.partial(
        pltpu.with_memory_space_constraint, memory_space=pltpu.HBM
    )
    lists = (send_list, aper_slot, aper_pattern, trace_bin, trace_count)
    early = bf16(EARLY, samples, samples)
    shared, lower = local_call(
        functools.partial(share_kernel, tiles, bins, ROOM),
        "share",
        [HBM] * 7,
        (bf16(tiles, samples // LANES * ROOM + 2 * APER, LANES), early),
        [
            pltpu.SMEM(send_list.shape, jnp.int32),
            pltpu.VMEM(aper_slot.shape, jnp.int32),
            pltpu.VMEM(aper_pattern.shape, jnp.int32),
            pltpu.VMEM((1, trace_rows), jnp.int32),
            pltpu.VMEM((1, trace_rows), jnp.int32),
            pltpu.VMEM(traces.shape, jnp.bfloat16),
            pltpu.SemaphoreType.DMA((6,)),
            pltpu.SemaphoreType.DMA,
        ],
    )(
        in_hbm(send_list),
        in_hbm(aper_slot),
        in_hbm(aper_pattern),
        in_hbm(trace_bin[None]),
        in_hbm(trace_count[None]),
        in_hbm(traces),
        in_hbm(kernels),
    )
    landed = lax.all_to_all(shared, "mid", 0, 0)
    flops = 2 * rows * PATTERNS * samples * samples
    pattern_rows = pltpu.VMEM((bins, PATTERNS, side, samples), jnp.bfloat16)
    parts_type = bf16(PATTERNS, 2, bins, side, samples)
    parts = pltpu.VMEM(parts_type.shape, parts_type.dtype)
    field, edge = array(rows, samples), bf16(side, samples)
    start, picks, *edges, full, upper = local_call(
        functools.partial(first_kernel, tiles, bins, send),
        "first",
        [VMEM, VMEM, HBM],
        (
            bf16(rows, samples),
            bf16(bins, PATTERNS * side, tiles * ROOM),
            edge,
            edge,
            array(8, LANES),
            bf16(PATTERNS - EARLY, samples, samples),
        ),
        [
            pltpu.VMEM((bins, PATTERNS, tiles, CELLS, tiles * ROOM), jnp.float32),
            pltpu.VMEM((PATTERNS, bins, side, samples), jnp.bfloat16),
            pltpu.SemaphoreType.DMA((PATTERNS - EARLY,)),
        ],
    )(landed, lower, in_hbm(kernels))

    path = [path_rank(m, tiles) for m in range(tiles)]
    chain = [m * offs + o for o in range(offs) for m in (path[::-1] if o % 2 else path)]

    def swapped_edges(edges):
        return [
            lax.ppermute(
                x,
                ("mid", "off"),
                [
                    pair
                    for i, j in zip(chain[first:-1:2], chain[first + 1 :: 2])
                    for pair in ((i, j), (j, i))
                ],
            )
            for first, x in enumerate(edges)
        ]

    beyond = swapped_edges(edges)
    local, gram = local_call(
        local_kernel,
        "local",
        [VMEM] * 4,
        (field, bf16(bins, PATTERNS * side, PATTERNS * side)),
        [pattern_rows, parts],
        cost=4 * flops,
    )(start, picks, lower, upper)
    once, *edges = local_call(
        functools.partial(complete_kernel, tiles),
        "complete",
        [VMEM] * 3,
        (field, edge, edge),
    )(local, *beyond)
    beyond = swapped_edges(edges)
    parts, square = local_call(
        mix_kernel,
        "mix",
        [VMEM] * 4,
        (parts_type, array(8, LANES)),
        [pattern_rows],
        cost=3 * flops,
    )(once, gram, lower, upper)
    smooth, products = local_call(
        functools.partial(sums_kernel, tiles),
        "sums",
        [VMEM] * 6,
        (field, array(8, LANES)),
    )(start, once, *beyond, square, full)
    projected = local_call(last_kernel, "last", [VMEM] * 3, field, cost=2 * flops)(
        parts, lower, upper
    )
    addends = [products] + [
        lax.ppermute(products, "off", [(i, i ^ step) for i in range(offs)])
        for step in range(1, offs)
    ]
    while len(addends) > 1:
        addends = [a + b for a, b in zip(addends[::2], addends[1::2])]
    products = addends[0]
    chunk = bf16(samples // LANES * 3 * bins * CELLS + 16, LANES)
    chunks = pltpu.VMEM((tiles, *chunk.shape), chunk.dtype)
    packed = local_call(
        pack_kernel, "pack", [VMEM] * 5, [chunk] * tiles, [chunks]
    )(products, start, once, smooth, projected)
    landed = swapped(packed)

    def again():
        arguments = [in_hbm(x) for x in (traces, kernels, *lists[:3])]
        arguments += [in_hbm(x[None]) for x in lists[3:]]
        *copies, bins_again, count_again = local_call(
            copy_kernel,
            "again",
            [HBM] * len(arguments),
            tuple(array(*x.shape, dtype=x.dtype) for x in arguments),
            [pltpu.SemaphoreType.DMA((len(arguments),))],
            out_specs=(HBM,) * len(arguments),
        )(*arguments)
        return *copies, bins_again[0], count_again[0]

    def placed():
        out_type = pltpu.HBM((CELLS, bins * tiles, samples), jnp.float32)
        return local_call(
            functools.partial(place_kernel, bins),
            "place",
            [VMEM] * tiles,
            (out_type, out_type),
            [chunks],
            out_specs=(VMEM, VMEM),
        )(*landed)

    return lax.cond(
        products[0, FULL] > 0.0, lambda: shards_by_tile(*again()), placed
    )


def fits_by_bin(tiles, offs, send, trace_rows, samples):
    return (
        (NOFF // offs) % (2 * tiles) == 0
        and offs & (offs - 1) == 0
        and tiles & (tiles - 1) == 0
        and tiles % TOGETHER == 0
        and send == WITHIN
        and trace_rows == LANES
        and samples % LANES == 0
    )


def solution(mesh):
    in_specs = (
        P(("mid", "off"), None),
        P(),
        P("mid", None, None),
        P(None, ("mid", "off")),
        P(None, ("mid", "off")),
        P(("mid", "off")),
        P(("mid", "off")),
    )
    out_specs = (P("mid", "off", None), P("mid", "off", None))

    def shards(traces, kernels, send_list, *lists):
        fits = fits_by_bin(
            mesh.shape["mid"], mesh.shape["off"], send_list.shape[2], *traces.shape
        )
        form = shards_by_bin if fits else shards_by_tile
        return form(traces, kernels, send_list, *lists)

    return jax.shard_map(
        shards, mesh=mesh, in_specs=in_specs, out_specs=out_specs, check_vma=False
    )
```

```python
import functools

import jax
import jax.numpy as jnp
from jax import lax
from jax.experimental import pallas as pl
from jax.experimental.pallas import tpu as pltpu
from jax.sharding import PartitionSpec as P

NOFF = 64
PATTERNS = 8
REACH = 2
APER = 8
ITERS = 2
CELLS = 8
KEYS = PATTERNS * CELLS
EARLY = 3
ROOM = 32
LANES = 128
TOGETHER = LANES // ROOM


smooth_weight = 2.0


def padded_2(x, sides, width):
    for axis, dim in sides:
        peers, length = (lax.axis_size(axis), x.shape[dim])
        up = [(i, (i + 1) % peers) for i in range(peers - 1)]
        down = [(j, i) for i, j in up]
        last = lax.slice_in_dim(x, length - width, length, axis=dim)
        first = lax.slice_in_dim(x, 0, width, axis=dim)
        before = lax.ppermute(last, axis, up)
        after = lax.ppermute(first, axis, down)
        x = jnp.concatenate([before, x, after], axis=dim)
    return x


def from_behind(x, axis, by):
    peers = lax.axis_size(axis)
    pairs = [(i, i + by) for i in range(peers) if 0 <= i + by < peers]
    return lax.ppermute(x, axis, pairs)


def direction_shift(course):
    return (course // 2 + 1) * (1 - 2 * (course % 2))


def offset_laplace(padded):
    return smooth_weight * (2.0 * padded[:, 1:-1] - padded[:, :-2] - padded[:, 2:])


def smoothing(field):
    padded = padded_2(field, (("off", 1),), 1)
    smoothed = offset_laplace(padded)
    return smoothed


def deliver(outgoing):
    arrived = [None] * (2 * REACH)
    for course in range(2 * REACH):
        arrived[course] = from_behind(outgoing[course], "mid", direction_shift(course))
    return arrived


def give_back(returning):
    landed = [None] * (2 * REACH)
    for course in range(2 * REACH):
        landed[course] = from_behind(returning[course], "mid", -direction_shift(course))
    return landed


def shards_by_tile(
    traces, kernels, send_list, aper_slot, aper_pattern, trace_bin, trace_count
):
    off_dev = NOFF // lax.axis_size("off")
    trace_rows = traces.shape[0]
    samples = traces.shape[1]
    chosen_cells = send_list[0]
    send_count = chosen_cells.shape[1]
    slot_count = CELLS + 2 * REACH * send_count
    live_mask = jnp.arange(APER, dtype=jnp.int32)[:, None] < trace_count[None, :]
    row_index = (aper_slot * off_dev + trace_bin[None, :]).reshape(-1)
    pattern_ids = jnp.arange(PATTERNS, dtype=jnp.int32)[:, None, None]
    chooser = ((aper_pattern[None] == pattern_ids) & live_mask[None]).astype(
        jnp.bfloat16
    )
    pick_rows = (
        aper_pattern * trace_rows + jnp.arange(trace_rows, dtype=jnp.int32)[None, :]
    ).reshape(-1)
    live_column = live_mask.reshape(-1, 1).astype(jnp.float32)

    def forward(field_bf):
        outgoing = [field_bf[chosen_cells[course]] for course in range(2 * REACH)]
        arrived = deliver(outgoing)
        slot_rows = jnp.concatenate([field_bf] + arrived, 0).reshape(-1, samples)
        blocks = slot_rows[row_index].reshape(APER, trace_rows, samples)
        pattern_sums = jnp.einsum(
            "pjt,jtn->ptn", chooser, blocks, preferred_element_type=jnp.float32
        ).astype(jnp.bfloat16)
        return jnp.einsum(
            "ptn,pnm->tm", pattern_sums, kernels, preferred_element_type=jnp.float32
        )

    def adjoint(values_bf):
        spread = jnp.einsum(
            "tm,pnm->ptn", values_bf, kernels, preferred_element_type=jnp.float32
        ).reshape(-1, samples)
        entries = spread[pick_rows] * live_column
        slot_sums = (
            jnp.zeros((slot_count * off_dev, samples), jnp.float32)
            .at[row_index]
            .add(entries)
        )
        slot_sums = slot_sums.reshape(slot_count, off_dev, samples)
        returning = [
            slot_sums[CELLS + course * send_count : CELLS + (course + 1) * send_count]
            for course in range(2 * REACH)
        ]
        landed = give_back(returning)
        accumulated = slot_sums[:CELLS]
        for course in range(2 * REACH):
            accumulated = accumulated.at[chosen_cells[course]].add(landed[course])
        return accumulated

    def global_total(value):
        return lax.psum(value, ("mid", "off"))

    residual = adjoint(traces)
    direction = residual
    solution = jnp.zeros_like(residual)
    norm_now = global_total(jnp.sum(residual * residual))
    for iteration in range(ITERS):
        applied = adjoint(
            forward(direction.astype(jnp.bfloat16)).astype(jnp.bfloat16)
        ) + smoothing(direction)
        step_size = norm_now / global_total(jnp.sum(direction * applied))
        solution = solution + step_size * direction
        residual = residual - step_size * applied
        if iteration + 1 < ITERS:
            norm_next = global_total(jnp.sum(residual * residual))
            direction = residual + norm_next / norm_now * direction
            norm_now = norm_next
    return (solution, residual)


def path_rank(m, tiles):
    return m ^ ((m >> 1) & 1) if tiles % 4 == 0 else m


def turns(peers):
    near, far = range(1, peers // 2), range(peers // 2, peers)
    even = [i for pair in zip(near, far) for i in pair]
    odd = [i for pair in zip(far, near) for i in pair]
    return [(0, 0), *zip(even, odd), (peers - 1, peers - 1)]


def partners(peers):
    odd, place = flipped(), lax.axis_index("mid")
    return [place ^ jnp.where(odd, j, i) for i, j in turns(peers)]


def lay_out(chunks_ref, out_refs):
    for partner, out_ref in zip(partners(len(out_refs)), out_refs):
        out_ref[...] = chunks_ref[partner]


def gather_in(landed_refs, chunks_ref):
    for partner, landed_ref in zip(partners(len(landed_refs)), landed_refs):
        chunks_ref[partner] = landed_ref[...]


def swapped(chunks):
    peers, offs = len(chunks), lax.axis_size("off")
    return list(chunks[:1]) + [
        lax.ppermute(
            chunk,
            ("mid", "off"),
            [
                (m * offs + o, (m ^ turn[o % 2]) * offs + o)
                for m in range(peers)
                for o in range(offs)
            ],
        )
        for turn, chunk in zip(turns(peers)[1:], chunks[1:])
    ]


def flipped():
    return lax.axis_index("off") % 2 > 0


def own_block(tiles):
    block = path_rank(lax.axis_index("mid"), tiles)
    return jnp.where(flipped(), tiles - 1 - block, block)


def dot_back(rows, kernel):
    return lax.dot_general(
        rows, kernel, (((1,), (1,)), ((), ())), preferred_element_type=jnp.float32
    )


SLOT, PATTERN, WITHIN, COUNT, FLAG = 0, APER, 4, 5, 6


def share_kernel(
    tiles, bins, room, sends_arg, slot_arg, pattern_arg, bin_arg, count_arg, traces_arg,
    kernels_arg, out_ref, kernels_ref, sends_ref, slot_ref, pattern_ref, bin_ref, count_ref, traces_ref,
    staged, arrived,
):
    rows, samples = traces_ref.shape
    stages = [
        pltpu.make_async_copy(arg, ref, staged.at[i])
        for i, (arg, ref) in enumerate(
            [
                (bin_arg, bin_ref),
                (slot_arg, slot_ref),
                (pattern_arg, pattern_ref),
                (count_arg, count_ref),
                (sends_arg, sends_ref),
                (traces_arg, traces_ref),
            ]
        )
    ]
    kernels = pltpu.make_async_copy(
        kernels_arg.at[:EARLY], kernels_ref, arrived
    )
    for stage in stages + [kernels]:
        stage.start()
    index = lax.broadcasted_iota(jnp.int32, (tiles, rows), 0)
    earlier = lax.broadcasted_iota(jnp.int32, (rows, rows), 0) < (
        lax.broadcasted_iota(jnp.int32, (rows, rows), 1)
    )
    earlier = jnp.where(earlier, 1.0, 0.0).astype(jnp.bfloat16)
    stages[0].wait()
    offset_bin = bin_ref[...]
    block = lax.div(offset_bin, bins)
    within = offset_bin - block * bins
    chunk = path_rank(jnp.where(flipped(), tiles - 1 - block, block), tiles)
    belongs = jnp.where(index == chunk, 1.0, 0.0)
    rank = jnp.dot(
        belongs.astype(jnp.bfloat16), earlier, preferred_element_type=jnp.float32
    )
    rank = jnp.sum(rank * belongs, 0, keepdims=True).astype(jnp.int32)
    full = jnp.max(rank, axis=1, keepdims=True) >= room
    target = jnp.where(rank < room, chunk * room + rank, -1)
    picks = lax.broadcasted_iota(jnp.int32, (tiles * room, rows), 0) == target
    picks = jnp.where(picks, 1.0, 0.0).astype(jnp.bfloat16)
    place = lax.axis_index("mid")
    lane = lax.broadcasted_iota(jnp.int32, (1, LANES), 1)
    target = chunk * LANES + lax.rem(place, TOGETHER) * room + rank
    chosen = lax.broadcasted_iota(jnp.int32, (tiles * LANES, rows), 0) == (
        jnp.where(rank < room, target, -1)
    )
    chosen = jnp.where(chosen, 1.0, 0.0).astype(jnp.bfloat16)
    for stage in stages[1:5]:
        stage.wait()
    lists = jnp.concatenate(
        [
            slot_ref[...].astype(jnp.float32),
            pattern_ref[...].astype(jnp.float32),
            jnp.zeros((WITHIN, rows), jnp.float32),
            within.astype(jnp.float32),
            count_ref[...].astype(jnp.float32),
            jnp.zeros((APER - COUNT - 1, rows), jnp.float32),
        ],
        0,
    ).astype(jnp.bfloat16)
    lists = dot_back(lists, chosen)
    _, courses, send = sends_ref.shape
    line = lax.broadcasted_iota(jnp.int32, (2 * APER, LANES), 0)
    sent = jnp.zeros((2 * APER, LANES), jnp.int32)
    for course in range(courses):
        reader = lax.rem(place + direction_shift(course) + TOGETHER, TOGETHER)
        here = lax.div(lane, room) == reader
        for m in range(send):
            value = jnp.where(here, sends_ref[0, course, m], 0)
            sent += jnp.where(line == sent_row(course, send) + m, value, 0)
    past = lax.div(lane, room) == lax.rem(place + 1, TOGETHER)
    sent += jnp.where(past & (line == FLAG) & full, 1, 0)
    sent = sent.astype(jnp.float32)
    pieces = samples // LANES
    for m in range(tiles):
        own = lists[:, m * LANES : (m + 1) * LANES]
        moved = pltpu.roll(own[2 * APER :], room, 1)
        out_ref[m, pieces * room :] = (
            own[: 2 * APER] + jnp.concatenate([moved, jnp.zeros_like(moved)], 0) + sent
        ).astype(jnp.bfloat16)
    stages[5].wait()
    picked = jnp.dot(picks, traces_ref[...], preferred_element_type=jnp.float32)
    picked = picked.reshape(tiles, room, samples).astype(jnp.bfloat16)
    for i in range(pieces):
        out_ref[:, i * room : (i + 1) * room] = picked[:, :, i * LANES : (i + 1) * LANES]
    kernels.wait()


def sent_row(course, send):
    return send if course == 3 else 0


def fill_picks(tiles, bins, send, landed_ref, picks_ref):
    flags = 0
    keys = lax.broadcasted_iota(jnp.int32, (KEYS, LANES), 0)
    member = lax.div(lax.broadcasted_iota(jnp.int32, (1, LANES), 1), ROOM)
    blocks = [
        landed_ref[tile, -2 * APER :].astype(jnp.float32).astype(jnp.int32)
        for tile in range(tiles)
    ]
    for group in range(tiles // TOGETHER):
        readers = range(group * TOGETHER, (group + 1) * TOGETHER)
        lists, moved = 0, 0
        for tile in readers:
            lists += jnp.where(member == tile % TOGETHER, blocks[tile], 0)
            past = member == (tile + 1) % TOGETHER
            moved += jnp.where(past, blocks[tile][:APER], 0)
        moved = pltpu.roll(moved, LANES - ROOM, 1)
        flags += moved[FLAG : FLAG + 1]
        within, count = moved[WITHIN : WITHIN + 1], moved[COUNT : COUNT + 1]
        wanted = []
        for region in range(2 * REACH + 1):
            course = region - 1
            shift = direction_shift(course) if region else 0
            owners = [tile - shift for tile in readers if 0 <= tile - shift < tiles]
            sent = 0
            for owner in owners if region else ():
                row = sent_row(course, send)
                values = blocks[owner][row : row + send]
                sent += jnp.where(member == (owner + shift) % TOGETHER, values, 0)
            for entry in range(region, APER, 2 * REACH + 1):
                cell = lists[SLOT + entry : SLOT + entry + 1]
                if region:
                    place = cell - (CELLS + course * send)
                    cell = sent[:1]
                    for other in range(1, send):
                        cell = jnp.where(place == other, sent[other : other + 1], cell)
                pattern = lists[PATTERN + entry : PATTERN + entry + 1]
                key = jnp.where(count > entry, pattern * CELLS + cell, -1)
                for owner in owners:
                    there = member == (owner + shift) % TOGETHER
                    wanted.append((owner, jnp.where(there, key, -1)))
        for tile in range(tiles):
            for b in range(bins):
                total = jnp.zeros((KEYS, LANES), jnp.float32)
                for owner, key in wanted:
                    if owner == tile:
                        hit = keys == jnp.where(within == b, key, -1)
                        total += jnp.where(hit, 1.0, 0.0)
                picks_ref[b, :, tile, :, group * LANES : (group + 1) * LANES] = (
                    total.reshape(PATTERNS, CELLS, LANES)
                )
    return flags.astype(jnp.float32)


def two_parts(x):
    high = x.astype(jnp.bfloat16)
    low = (x - high.astype(jnp.float32)).astype(jnp.bfloat16)
    return jnp.concatenate([high, low], 0)


def store_parts(parts_ref, b, x):
    shape = (PATTERNS, *parts_ref.shape[3:])
    high = x.astype(jnp.bfloat16)
    parts_ref[:, 0, b] = high.reshape(shape)
    low = (x - high.astype(jnp.float32)).astype(jnp.bfloat16)
    parts_ref[:, 1, b] = low.reshape(shape)


def kernel_of(kernels, p):
    lower_ref, upper_ref = kernels
    return lower_ref[p] if p < EARLY else upper_ref[p - EARLY]


def back_projected(kernels, parts_ref):
    _, _, bins, side, samples = parts_ref.shape
    rows = bins * side
    both = jnp.zeros((2 * rows, samples), jnp.float32)
    for p in range(PATTERNS):
        both += dot_back(
            parts_ref[p].reshape(2 * rows, samples), kernel_of(kernels, p)
        )
    return both[:rows] + both[rows:]


def project(field, kernels, rows_ref):
    bins, _, side, samples = rows_ref.shape
    rows = bins * side
    for p in range(PATTERNS):
        u = jnp.dot(field, kernel_of(kernels, p), preferred_element_type=jnp.float32)
        u = u[:rows] + u[rows:] if field.shape[0] > rows else u
        rows_ref[:, p] = u.astype(jnp.bfloat16).reshape(bins, side, samples)


def mixed(gram_ref, rows_ref, b):
    _, _, side, samples = rows_ref.shape
    return jnp.dot(
        gram_ref[b],
        rows_ref[b].reshape(PATTERNS * side, samples),
        preferred_element_type=jnp.float32,
    )


def smoothed(field, before, after):
    side = before.shape[0]
    lower = jnp.concatenate([before, field[:-side]], 0)
    upper = jnp.concatenate([field[side:], after], 0)
    return smooth_weight * (2.0 * field - lower - upper)


def first_kernel(
    tiles, bins, send, landed_ref, lower_ref, kernels_arg,
    start_ref, local_ref, gram_ref, first_swap_ref, second_swap_ref, full_ref, upper_ref,
    picks_ref, rows_ref, parts_ref, arrived,
):
    copies = [
        pltpu.make_async_copy(kernels_arg.at[EARLY + p], upper_ref.at[p], arrived.at[p])
        for p in range(PATTERNS - EARLY)
    ]
    for copy in copies:
        copy.start()
    kernels = (lower_ref, upper_ref)
    side = tiles * CELLS
    samples = start_ref.shape[1]
    flags = total(fill_picks(tiles, bins, send, landed_ref, picks_ref))
    full_ref[...] = jnp.broadcast_to(flags, full_ref.shape)
    traces = jnp.concatenate(
        [
            landed_ref[:, i * ROOM : (i + 1) * ROOM].reshape(-1, LANES)
            for i in range(samples // LANES)
        ],
        1,
    )
    for b in range(bins):
        picks = picks_ref[b].reshape(PATTERNS * side, -1).astype(jnp.bfloat16)
        gram_ref[b] = dot_back(picks, picks).astype(jnp.bfloat16)
        sums = jnp.dot(picks, traces, preferred_element_type=jnp.float32)
        parts_ref[:, 0, b] = sums.astype(jnp.bfloat16).reshape(PATTERNS, side, samples)
    start = jnp.zeros((bins * side, samples), jnp.float32)
    for p in range(PATTERNS):
        if p >= EARLY:
            copies[p - EARLY].wait()
        rows = parts_ref[p, 0].reshape(bins * side, samples)
        start += dot_back(rows, kernel_of(kernels, p))
    start = start.astype(jnp.bfloat16)
    start_ref[...] = start
    field = start.astype(jnp.float32)
    nothing = jnp.zeros((side, samples), jnp.float32)
    project(start, kernels, rows_ref)
    for b in range(bins):
        store_parts(parts_ref, b, mixed(gram_ref, rows_ref, b))
    local = back_projected(kernels, parts_ref) + smoothed(field, nothing, nothing)
    local_ref[...] = local
    local = local.astype(jnp.bfloat16)
    odd = own_block(tiles) % 2 > 0
    for out_ref, to_after in ((first_swap_ref, odd), (second_swap_ref, ~odd)):
        out_ref[:side] = jnp.where(to_after, start[-side:], start[:side])
        out_ref[side:] = jnp.where(to_after, local[-side:], local[:side])


FULL, STEP, GROW = 4, 5, 6


def ahead_kernel(local_ref, gram_ref, lower_ref, upper_ref, rows_ref, mixed_ref):
    project(two_parts(local_ref[...]), (lower_ref, upper_ref), rows_ref)
    for b in range(rows_ref.shape[0]):
        mixed_ref[b] = mixed(gram_ref, rows_ref, b)


def second_kernel(
    tiles, offs, start_ref, local_ref, gram_ref, lower_ref, upper_ref, first_swap_ref,
    second_swap_ref, full_ref, ahead_ref, mixed_ref,
    once_ref, smooth_ref, parts_ref, sums_ref, rows_ref,
):
    bins, _, side, samples = rows_ref.shape
    start = start_ref[...].astype(jnp.float32)
    place = lax.axis_index("off") * tiles + own_block(tiles)
    ends = [place > 0, place < offs * tiles - 1]
    odd = own_block(tiles) % 2 > 0
    first = first_swap_ref[...].astype(jnp.float32)
    second = second_swap_ref[...].astype(jnp.float32)
    edges = [jnp.where(odd, second, first), jnp.where(odd, first, second)]
    beyond, outer = [], []
    for end, (edge, own) in enumerate(zip(edges, (start[:side], start[-side:]))):
        there = jnp.where(ends[end], smooth_weight, 0.0)
        beyond.append(-smooth_weight * edge[:side])
        outer.append(edge[side:] - there * own)
    inner = [jnp.zeros(((bins - 2) * side, samples), jnp.float32)] if bins > 2 else []
    beyond = jnp.concatenate([beyond[0], *inner, beyond[1]], 0)
    once = local_ref[...] + beyond
    once_ref[...] = once
    smooth = smoothed(once, outer[0], outer[1])
    smooth_ref[...] = smooth
    project(beyond.astype(jnp.bfloat16), (lower_ref, upper_ref), rows_ref)
    square = 0.0
    for b in range(bins):
        both = mixed_ref[b] + mixed(gram_ref, rows_ref, b)
        store_parts(parts_ref, b, both)
        rows = ahead_ref[b].astype(jnp.float32) + rows_ref[b].astype(jnp.float32)
        square += total(rows.reshape(both.shape) * both)
    products = [
        total(start * start),
        total(start * once),
        total(once * once),
        total(once * smooth) + square,
    ]
    lane = lax.broadcasted_iota(jnp.int32, (1, LANES), 1)
    line = jnp.where(lane == FULL, full_ref[:1], 0.0)
    for i, product in enumerate(products):
        line = jnp.where(lane == i, product, line)
    sums_ref[...] = jnp.broadcast_to(line, sums_ref.shape)


def last_kernel(parts_ref, lower_ref, upper_ref, out_ref):
    out_ref[...] = back_projected((lower_ref, upper_ref), parts_ref)


def pack_kernel(sums_ref, start_ref, once_ref, smooth_ref, normal_ref, *refs):
    *out_refs, out_ref = refs
    tiles = len(out_refs)
    ss, so, oo = (sums_ref[:1, i : i + 1] for i in range(3))
    step, grow = own_scales(ss, so, oo)
    start, once = start_ref[...].astype(jnp.float32), once_ref[...]
    twice = normal_ref[...] + smooth_ref[...]
    row = 0
    for field in (start, start - step * once, grow * once - step * twice):
        samples = field.shape[1]
        field = field.reshape(-1, tiles, CELLS, samples)
        size = field.shape[0] * CELLS
        for i in range(0, samples, LANES):
            for tile in range(tiles):
                piece = field[:, tile, :, i : i + LANES].reshape(size, LANES)
                out_ref[tile, row : row + size] = piece.astype(jnp.bfloat16)
            row += size
    lane = lax.broadcasted_iota(jnp.int32, (1, LANES), 1)
    rest = jnp.where(lane == STEP, step, sums_ref[:1])
    rest = jnp.where(lane == GROW, grow, rest)
    line = lax.broadcasted_iota(jnp.int32, (16, LANES), 0)
    parts = jnp.zeros((16, LANES), jnp.float32)
    for i in range(3):
        part = rest.astype(jnp.bfloat16).astype(jnp.float32)
        rest = rest - part
        parts = jnp.where(line == i, part, parts)
    for tile in range(tiles):
        out_ref[tile, row:] = parts.astype(jnp.bfloat16)
    lay_out(out_ref, out_refs)


def total(x):
    return jnp.sum(jnp.sum(x, 0, keepdims=True), 1, keepdims=True)


def own_scales(ss, so, oo):
    step = ss / so
    step = jnp.where(step > 0.0, jnp.clip(step, 1e-8, 1e3), 1.0)
    grow = step * step * oo / ss
    return step, jnp.where(grow > 0.0, jnp.clip(grow, 0.0, 1e3), 1.0)


def place_kernel(bins, *refs):
    *landed_refs, solution_ref, residual_ref, landed_ref = refs
    gather_in(landed_refs, landed_ref)
    tiles, length, _ = landed_ref.shape
    size = bins * CELLS
    samples = solution_ref.shape[2]
    pieces = samples // LANES

    def line_of(source):
        parts = landed_ref[source, length - 16 :].astype(jnp.float32)
        return jnp.sum(parts, 0, keepdims=True)

    def vector(source, i):
        part = [
            landed_ref[source, (i * pieces + j) * size : (i * pieces + j + 1) * size]
            for j in range(pieces)
        ]
        return jnp.concatenate(part, 1).astype(jnp.float32)

    sums = sum(line_of(tile) for tile in range(tiles))
    ss, so, oo, ot = (sums[:, i : i + 1] for i in range(4))
    step_0 = ss / so
    norm_1 = step_0 * step_0 * oo - ss
    grow = 1.0 + norm_1 / ss
    step_1 = norm_1 / (grow * grow * so - 2.0 * step_0 * grow * oo + step_0 * step_0 * ot)
    near = step_0 + step_1 * grow
    far = step_1 * step_0
    fields = [[], []]
    for block in range(tiles):
        source = jnp.where(
            flipped(), path_rank(tiles - 1 - block, tiles), path_rank(block, tiles)
        )
        line = line_of(source)
        inverse = 1.0 / line[:, STEP : STEP + 1]
        there = line[:, GROW : GROW + 1]
        start, first, second = (vector(source, i) for i in range(3))
        far_once = far * inverse
        near_once = near * inverse - far_once * there * inverse
        solution = (near - far_once) * start + far_once * first
        residual = (1.0 - near_once) * start + near_once * first - far_once * second
        fields[0].append(solution.reshape(bins, CELLS, samples))
        fields[1].append(residual.reshape(bins, CELLS, samples))
    solution_ref[...] = jnp.swapaxes(jnp.concatenate(fields[0], 0), 0, 1)
    residual_ref[...] = jnp.swapaxes(jnp.concatenate(fields[1], 0), 0, 1)


def copy_kernel(*refs):
    *refs, arrived = refs
    half = len(refs) // 2
    copies = [
        pltpu.make_async_copy(refs[i], refs[half + i], arrived.at[i]) for i in range(half)
    ]
    for copy in copies:
        copy.start()
    for copy in copies:
        copy.wait()


VMEM = pl.BlockSpec(memory_space=pltpu.VMEM)
HBM = pl.BlockSpec(memory_space=pltpu.HBM)


def local_call(kernel, name, in_specs, out_shape, scratch=(), out_specs=None, cost=0):
    return pl.pallas_call(
        kernel,
        out_shape=out_shape,
        in_specs=in_specs,
        out_specs=out_specs or jax.tree.map(lambda _: VMEM, out_shape),
        scratch_shapes=list(scratch),
        cost_estimate=pl.CostEstimate(
            flops=cost, bytes_accessed=cost // 256, transcendentals=0
        )
        if cost
        else None,
        compiler_params=pltpu.CompilerParams(vmem_limit_bytes=32 * 1024 * 1024),
        name=name,
    )


def shards_by_bin(
    traces, kernels, send_list, aper_slot, aper_pattern, trace_bin, trace_count
):
    tiles, offs = lax.axis_size("mid"), lax.axis_size("off")
    bins = NOFF // offs // tiles
    trace_rows, samples = traces.shape
    send = send_list.shape[2]
    rows = bins * tiles * CELLS
    side = tiles * CELLS
    sums = bins * (CELLS + 2 * REACH * send)

    def array(*shape, dtype=jnp.float32):
        return jax.ShapeDtypeStruct(shape, dtype)

    bf16 = functools.partial(array, dtype=jnp.bfloat16)
    in_hbm = functools.partial(
        pltpu.with_memory_space_constraint, memory_space=pltpu.HBM
    )
    lists = (send_list, aper_slot, aper_pattern, trace_bin, trace_count)
    early = bf16(EARLY, samples, samples)
    shared, lower = local_call(
        functools.partial(share_kernel, tiles, bins, ROOM),
        "share",
        [HBM] * 7,
        (bf16(tiles, samples // LANES * ROOM + 2 * APER, LANES), early),
        [
            pltpu.SMEM(send_list.shape, jnp.int32),
            pltpu.VMEM(aper_slot.shape, jnp.int32),
            pltpu.VMEM(aper_pattern.shape, jnp.int32),
            pltpu.VMEM((1, trace_rows), jnp.int32),
            pltpu.VMEM((1, trace_rows), jnp.int32),
            pltpu.VMEM(traces.shape, jnp.bfloat16),
            pltpu.SemaphoreType.DMA((6,)),
            pltpu.SemaphoreType.DMA,
        ],
    )(
        in_hbm(send_list),
        in_hbm(aper_slot),
        in_hbm(aper_pattern),
        in_hbm(trace_bin[None]),
        in_hbm(trace_count[None]),
        in_hbm(traces),
        in_hbm(kernels),
    )
    landed = lax.all_to_all(shared, "mid", 0, 0)
    pattern_rows = pltpu.VMEM((bins, PATTERNS, side, samples), jnp.bfloat16)
    parts_type = bf16(PATTERNS, 2, bins, side, samples)
    start, local, gram, *swaps, full, upper = local_call(
        functools.partial(first_kernel, tiles, bins, send),
        "first",
        [VMEM, VMEM, HBM],
        (
            bf16(rows, samples),
            array(rows, samples),
            bf16(bins, tiles * KEYS, tiles * KEYS),
            bf16(2 * side, samples),
            bf16(2 * side, samples),
            array(8, LANES),
            bf16(PATTERNS - EARLY, samples, samples),
        ),
        [
            pltpu.VMEM((bins, PATTERNS, tiles, CELLS, tiles * ROOM), jnp.float32),
            pattern_rows,
            pltpu.VMEM(parts_type.shape, parts_type.dtype),
            pltpu.SemaphoreType.DMA((PATTERNS - EARLY,)),
        ],
    )(landed, lower, in_hbm(kernels))

    path = [path_rank(m, tiles) for m in range(tiles)]
    chain = [m * offs + o for o in range(offs) for m in (path[::-1] if o % 2 else path)]
    swaps = [
        lax.ppermute(
            x,
            ("mid", "off"),
            [
                pair
                for i, j in zip(chain[first:-1:2], chain[first + 1 :: 2])
                for pair in ((i, j), (j, i))
            ],
        )
        for first, x in zip((1, 0), swaps)
    ]

    flops = 2 * rows * PATTERNS * samples * samples
    ahead, mixed_ahead = local_call(
        ahead_kernel,
        "ahead",
        [VMEM] * 4,
        (bf16(*pattern_rows.shape), array(bins, PATTERNS * side, samples)),
        cost=3 * flops,
    )(local, gram, lower, upper)
    field = array(rows, samples)
    once, smooth, parts, products = local_call(
        functools.partial(second_kernel, tiles, offs),
        "second",
        [VMEM] * 10,
        (field, field, parts_type, array(8, LANES)),
        [pattern_rows],
        cost=2 * flops,
    )(start, local, gram, lower, upper, *swaps, full, ahead, mixed_ahead)

    projected = local_call(last_kernel, "last", [VMEM] * 3, field, cost=2 * flops)(
        parts, lower, upper
    )
    addends = [products] + [
        lax.ppermute(products, "off", [(i, i ^ step) for i in range(offs)])
        for step in range(1, offs)
    ]
    while len(addends) > 1:
        addends = [a + b for a, b in zip(addends[::2], addends[1::2])]
    products = addends[0]
    chunk = bf16(samples // LANES * 3 * bins * CELLS + 16, LANES)
    chunks = pltpu.VMEM((tiles, *chunk.shape), chunk.dtype)
    packed = local_call(
        pack_kernel, "pack", [VMEM] * 5, [chunk] * tiles, [chunks]
    )(products, start, once, smooth, projected)
    landed = swapped(packed)

    def again():
        arguments = [in_hbm(x) for x in (traces, kernels, *lists[:3])]
        arguments += [in_hbm(x[None]) for x in lists[3:]]
        *copies, bins_again, count_again = local_call(
            copy_kernel,
            "again",
            [HBM] * len(arguments),
            tuple(array(*x.shape, dtype=x.dtype) for x in arguments),
            [pltpu.SemaphoreType.DMA((len(arguments),))],
            out_specs=(HBM,) * len(arguments),
        )(*arguments)
        return *copies, bins_again[0], count_again[0]

    def placed():
        out_type = pltpu.HBM((CELLS, bins * tiles, samples), jnp.float32)
        return local_call(
            functools.partial(place_kernel, bins),
            "place",
            [VMEM] * tiles,
            (out_type, out_type),
            [chunks],
            out_specs=(VMEM, VMEM),
        )(*landed)

    return lax.cond(
        products[0, FULL] > 0.0, lambda: shards_by_tile(*again()), placed
    )


def fits_by_bin(tiles, offs, send, trace_rows, samples):
    return (
        (NOFF // offs) % (2 * tiles) == 0
        and offs & (offs - 1) == 0
        and tiles & (tiles - 1) == 0
        and tiles % TOGETHER == 0
        and send == WITHIN
        and trace_rows == LANES
        and samples % LANES == 0
    )


def solution(mesh):
    in_specs = (
        P(("mid", "off"), None),
        P(),
        P("mid", None, None),
        P(None, ("mid", "off")),
        P(None, ("mid", "off")),
        P(("mid", "off")),
        P(("mid", "off")),
    )
    out_specs = (P("mid", "off", None), P("mid", "off", None))

    def shards(traces, kernels, send_list, *lists):
        fits = fits_by_bin(
            mesh.shape["mid"], mesh.shape["off"], send_list.shape[2], *traces.shape
        )
        form = shards_by_bin if fits else shards_by_tile
        return form(traces, kernels, send_list, *lists)

    return jax.shard_map(
        shards, mesh=mesh, in_specs=in_specs, out_specs=out_specs, check_vma=False
    )
```

```python
import functools

import jax
import jax.numpy as jnp
from jax import lax
from jax.experimental import pallas as pl
from jax.experimental.pallas import tpu as pltpu
from jax.sharding import PartitionSpec as P

NOFF = 64
PATTERNS = 8
REACH = 2
APER = 8
ITERS = 2
CELLS = 8
KEYS = PATTERNS * CELLS
EARLY = 3
ROOM = 32
LANES = 128
TOGETHER = LANES // ROOM


smooth_weight = 2.0


def padded_2(x, sides, width):
    for axis, dim in sides:
        peers, length = (lax.axis_size(axis), x.shape[dim])
        up = [(i, (i + 1) % peers) for i in range(peers - 1)]
        down = [(j, i) for i, j in up]
        last = lax.slice_in_dim(x, length - width, length, axis=dim)
        first = lax.slice_in_dim(x, 0, width, axis=dim)
        before = lax.ppermute(last, axis, up)
        after = lax.ppermute(first, axis, down)
        x = jnp.concatenate([before, x, after], axis=dim)
    return x


def from_behind(x, axis, by):
    peers = lax.axis_size(axis)
    pairs = [(i, i + by) for i in range(peers) if 0 <= i + by < peers]
    return lax.ppermute(x, axis, pairs)


def direction_shift(course):
    return (course // 2 + 1) * (1 - 2 * (course % 2))


def offset_laplace(padded):
    return smooth_weight * (2.0 * padded[:, 1:-1] - padded[:, :-2] - padded[:, 2:])


def smoothing(field):
    padded = padded_2(field, (("off", 1),), 1)
    smoothed = offset_laplace(padded)
    return smoothed


def deliver(outgoing):
    arrived = [None] * (2 * REACH)
    for course in range(2 * REACH):
        arrived[course] = from_behind(outgoing[course], "mid", direction_shift(course))
    return arrived


def give_back(returning):
    landed = [None] * (2 * REACH)
    for course in range(2 * REACH):
        landed[course] = from_behind(returning[course], "mid", -direction_shift(course))
    return landed


def shards_by_tile(
    traces, kernels, send_list, aper_slot, aper_pattern, trace_bin, trace_count
):
    off_dev = NOFF // lax.axis_size("off")
    trace_rows = traces.shape[0]
    samples = traces.shape[1]
    chosen_cells = send_list[0]
    send_count = chosen_cells.shape[1]
    slot_count = CELLS + 2 * REACH * send_count
    live_mask = jnp.arange(APER, dtype=jnp.int32)[:, None] < trace_count[None, :]
    row_index = (aper_slot * off_dev + trace_bin[None, :]).reshape(-1)
    pattern_ids = jnp.arange(PATTERNS, dtype=jnp.int32)[:, None, None]
    chooser = ((aper_pattern[None] == pattern_ids) & live_mask[None]).astype(
        jnp.bfloat16
    )
    pick_rows = (
        aper_pattern * trace_rows + jnp.arange(trace_rows, dtype=jnp.int32)[None, :]
    ).reshape(-1)
    live_column = live_mask.reshape(-1, 1).astype(jnp.float32)

    def forward(field_bf):
        outgoing = [field_bf[chosen_cells[course]] for course in range(2 * REACH)]
        arrived = deliver(outgoing)
        slot_rows = jnp.concatenate([field_bf] + arrived, 0).reshape(-1, samples)
        blocks = slot_rows[row_index].reshape(APER, trace_rows, samples)
        pattern_sums = jnp.einsum(
            "pjt,jtn->ptn", chooser, blocks, preferred_element_type=jnp.float32
        ).astype(jnp.bfloat16)
        return jnp.einsum(
            "ptn,pnm->tm", pattern_sums, kernels, preferred_element_type=jnp.float32
        )

    def adjoint(values_bf):
        spread = jnp.einsum(
            "tm,pnm->ptn", values_bf, kernels, preferred_element_type=jnp.float32
        ).reshape(-1, samples)
        entries = spread[pick_rows] * live_column
        slot_sums = (
            jnp.zeros((slot_count * off_dev, samples), jnp.float32)
            .at[row_index]
            .add(entries)
        )
        slot_sums = slot_sums.reshape(slot_count, off_dev, samples)
        returning = [
            slot_sums[CELLS + course * send_count : CELLS + (course + 1) * send_count]
            for course in range(2 * REACH)
        ]
        landed = give_back(returning)
        accumulated = slot_sums[:CELLS]
        for course in range(2 * REACH):
            accumulated = accumulated.at[chosen_cells[course]].add(landed[course])
        return accumulated

    def global_total(value):
        return lax.psum(value, ("mid", "off"))

    residual = adjoint(traces)
    direction = residual
    solution = jnp.zeros_like(residual)
    norm_now = global_total(jnp.sum(residual * residual))
    for iteration in range(ITERS):
        applied = adjoint(
            forward(direction.astype(jnp.bfloat16)).astype(jnp.bfloat16)
        ) + smoothing(direction)
        step_size = norm_now / global_total(jnp.sum(direction * applied))
        solution = solution + step_size * direction
        residual = residual - step_size * applied
        if iteration + 1 < ITERS:
            norm_next = global_total(jnp.sum(residual * residual))
            direction = residual + norm_next / norm_now * direction
            norm_now = norm_next
    return (solution, residual)


def path_rank(m, tiles):
    return m ^ ((m >> 1) & 1) if tiles % 4 == 0 else m


def turns(peers):
    near, far = range(1, peers // 2), range(peers - 1, peers // 2, -1)
    even = [i for pair in zip(far, near) for i in pair]
    odd = [i for pair in zip(near, far) for i in pair]
    return [(0, 0), *zip(even, odd), (peers // 2, peers // 2)]


def partners(peers):
    odd, place = flipped(), lax.axis_index("mid")
    return [place ^ jnp.where(odd, j, i) for i, j in turns(peers)]


def lay_out(chunks_ref, out_refs):
    for partner, out_ref in zip(partners(len(out_refs)), out_refs):
        out_ref[...] = chunks_ref[partner]


def gather_in(landed_refs, chunks_ref):
    for partner, landed_ref in zip(partners(len(landed_refs)), landed_refs):
        chunks_ref[partner] = landed_ref[...]


def swapped(chunks):
    peers, offs = len(chunks), lax.axis_size("off")
    return list(chunks[:1]) + [
        lax.ppermute(
            chunk,
            ("mid", "off"),
            [
                (m * offs + o, (m ^ turn[o % 2]) * offs + o)
                for m in range(peers)
                for o in range(offs)
            ],
        )
        for turn, chunk in zip(turns(peers)[1:], chunks[1:])
    ]


def flipped():
    return lax.axis_index("off") % 2 > 0


def own_block(tiles):
    block = path_rank(lax.axis_index("mid"), tiles)
    return jnp.where(flipped(), tiles - 1 - block, block)


def dot_back(rows, kernel):
    return lax.dot_general(
        rows, kernel, (((1,), (1,)), ((), ())), preferred_element_type=jnp.float32
    )


SLOT, PATTERN, WITHIN, COUNT, FLAG = 0, APER, 4, 5, 6


def share_kernel(
    tiles, bins, room, sends_arg, slot_arg, pattern_arg, bin_arg, count_arg, traces_arg,
    kernels_arg, out_ref, kernels_ref, sends_ref, slot_ref, pattern_ref, bin_ref, count_ref, traces_ref,
    staged, arrived,
):
    rows, samples = traces_ref.shape
    stages = [
        pltpu.make_async_copy(arg, ref, staged.at[i])
        for i, (arg, ref) in enumerate(
            [
                (bin_arg, bin_ref),
                (slot_arg, slot_ref),
                (pattern_arg, pattern_ref),
                (count_arg, count_ref),
                (sends_arg, sends_ref),
                (traces_arg, traces_ref),
            ]
        )
    ]
    kernels = pltpu.make_async_copy(
        kernels_arg.at[:EARLY], kernels_ref, arrived
    )
    for stage in stages + [kernels]:
        stage.start()
    index = lax.broadcasted_iota(jnp.int32, (tiles, rows), 0)
    earlier = lax.broadcasted_iota(jnp.int32, (rows, rows), 0) < (
        lax.broadcasted_iota(jnp.int32, (rows, rows), 1)
    )
    earlier = jnp.where(earlier, 1.0, 0.0).astype(jnp.bfloat16)
    stages[0].wait()
    offset_bin = bin_ref[...]
    block = lax.div(offset_bin, bins)
    within = offset_bin - block * bins
    chunk = path_rank(jnp.where(flipped(), tiles - 1 - block, block), tiles)
    belongs = jnp.where(index == chunk, 1.0, 0.0)
    rank = jnp.dot(
        belongs.astype(jnp.bfloat16), earlier, preferred_element_type=jnp.float32
    )
    rank = jnp.sum(rank * belongs, 0, keepdims=True).astype(jnp.int32)
    full = jnp.max(rank, axis=1, keepdims=True) >= room
    target = jnp.where(rank < room, chunk * room + rank, -1)
    picks = lax.broadcasted_iota(jnp.int32, (tiles * room, rows), 0) == target
    picks = jnp.where(picks, 1.0, 0.0).astype(jnp.bfloat16)
    place = lax.axis_index("mid")
    lane = lax.broadcasted_iota(jnp.int32, (1, LANES), 1)
    target = chunk * LANES + lax.rem(place, TOGETHER) * room + rank
    chosen = lax.broadcasted_iota(jnp.int32, (tiles * LANES, rows), 0) == (
        jnp.where(rank < room, target, -1)
    )
    chosen = jnp.where(chosen, 1.0, 0.0).astype(jnp.bfloat16)
    for stage in stages[1:5]:
        stage.wait()
    lists = jnp.concatenate(
        [
            slot_ref[...].astype(jnp.float32),
            pattern_ref[...].astype(jnp.float32),
            jnp.zeros((WITHIN, rows), jnp.float32),
            within.astype(jnp.float32),
            count_ref[...].astype(jnp.float32),
            jnp.zeros((APER - COUNT - 1, rows), jnp.float32),
        ],
        0,
    ).astype(jnp.bfloat16)
    lists = dot_back(lists, chosen)
    _, courses, send = sends_ref.shape
    line = lax.broadcasted_iota(jnp.int32, (2 * APER, LANES), 0)
    sent = jnp.zeros((2 * APER, LANES), jnp.int32)
    for course in range(courses):
        reader = lax.rem(place + direction_shift(course) + TOGETHER, TOGETHER)
        here = lax.div(lane, room) == reader
        for m in range(send):
            value = jnp.where(here, sends_ref[0, course, m], 0)
            sent += jnp.where(line == sent_row(course, send) + m, value, 0)
    past = lax.div(lane, room) == lax.rem(place + 1, TOGETHER)
    sent += jnp.where(past & (line == FLAG) & full, 1, 0)
    sent = sent.astype(jnp.float32)
    pieces = samples // LANES
    for m in range(tiles):
        own = lists[:, m * LANES : (m + 1) * LANES]
        moved = pltpu.roll(own[2 * APER :], room, 1)
        out_ref[m, pieces * room :] = (
            own[: 2 * APER] + jnp.concatenate([moved, jnp.zeros_like(moved)], 0) + sent
        ).astype(jnp.bfloat16)
    stages[5].wait()
    picked = jnp.dot(picks, traces_ref[...], preferred_element_type=jnp.float32)
    picked = picked.reshape(tiles, room, samples).astype(jnp.bfloat16)
    for i in range(pieces):
        out_ref[:, i * room : (i + 1) * room] = picked[:, :, i * LANES : (i + 1) * LANES]
    kernels.wait()


def sent_row(course, send):
    return send if course == 3 else 0


def fill_picks(tiles, bins, send, landed_ref, picks_ref):
    flags = 0
    keys = lax.broadcasted_iota(jnp.int32, (KEYS, LANES), 0)
    member = lax.div(lax.broadcasted_iota(jnp.int32, (1, LANES), 1), ROOM)
    blocks = [
        landed_ref[tile, -2 * APER :].astype(jnp.float32).astype(jnp.int32)
        for tile in range(tiles)
    ]
    for group in range(tiles // TOGETHER):
        readers = range(group * TOGETHER, (group + 1) * TOGETHER)
        lists, moved = 0, 0
        for tile in readers:
            lists += jnp.where(member == tile % TOGETHER, blocks[tile], 0)
            past = member == (tile + 1) % TOGETHER
            moved += jnp.where(past, blocks[tile][:APER], 0)
        moved = pltpu.roll(moved, LANES - ROOM, 1)
        flags += moved[FLAG : FLAG + 1]
        within, count = moved[WITHIN : WITHIN + 1], moved[COUNT : COUNT + 1]
        wanted = []
        for region in range(2 * REACH + 1):
            course = region - 1
            shift = direction_shift(course) if region else 0
            owners = [tile - shift for tile in readers if 0 <= tile - shift < tiles]
            sent = 0
            for owner in owners if region else ():
                row = sent_row(course, send)
                values = blocks[owner][row : row + send]
                sent += jnp.where(member == (owner + shift) % TOGETHER, values, 0)
            for entry in range(region, APER, 2 * REACH + 1):
                cell = lists[SLOT + entry : SLOT + entry + 1]
                if region:
                    place = cell - (CELLS + course * send)
                    cell = sent[:1]
                    for other in range(1, send):
                        cell = jnp.where(place == other, sent[other : other + 1], cell)
                pattern = lists[PATTERN + entry : PATTERN + entry + 1]
                key = jnp.where(count > entry, pattern * CELLS + cell, -1)
                for owner in owners:
                    there = member == (owner + shift) % TOGETHER
                    wanted.append((owner, jnp.where(there, key, -1)))
        for tile in range(tiles):
            for b in range(bins):
                total = jnp.zeros((KEYS, LANES), jnp.float32)
                for owner, key in wanted:
                    if owner == tile:
                        hit = keys == jnp.where(within == b, key, -1)
                        total += jnp.where(hit, 1.0, 0.0)
                picks_ref[b, :, tile, :, group * LANES : (group + 1) * LANES] = (
                    total.reshape(PATTERNS, CELLS, LANES)
                )
    return flags.astype(jnp.float32)


def two_parts(x):
    high = x.astype(jnp.bfloat16)
    low = (x - high.astype(jnp.float32)).astype(jnp.bfloat16)
    return jnp.concatenate([high, low], 0)


def store_parts(parts_ref, b, x):
    shape = (PATTERNS, *parts_ref.shape[3:])
    high = x.astype(jnp.bfloat16)
    parts_ref[:, 0, b] = high.reshape(shape)
    low = (x - high.astype(jnp.float32)).astype(jnp.bfloat16)
    parts_ref[:, 1, b] = low.reshape(shape)


def kernel_of(kernels, p):
    lower_ref, upper_ref = kernels
    return lower_ref[p] if p < EARLY else upper_ref[p - EARLY]


def back_projected(kernels, parts_ref):
    _, _, bins, side, samples = parts_ref.shape
    rows = bins * side
    both = jnp.zeros((2 * rows, samples), jnp.float32)
    for p in range(PATTERNS):
        both += dot_back(
            parts_ref[p].reshape(2 * rows, samples), kernel_of(kernels, p)
        )
    return both[:rows] + both[rows:]


def project(field, kernels, rows_ref):
    bins, _, side, samples = rows_ref.shape
    rows = bins * side
    for p in range(PATTERNS):
        u = jnp.dot(field, kernel_of(kernels, p), preferred_element_type=jnp.float32)
        u = u[:rows] + u[rows:] if field.shape[0] > rows else u
        rows_ref[:, p] = u.astype(jnp.bfloat16).reshape(bins, side, samples)


def mixed(gram_ref, rows_ref, b):
    _, _, side, samples = rows_ref.shape
    return jnp.dot(
        gram_ref[b],
        rows_ref[b].reshape(PATTERNS * side, samples),
        preferred_element_type=jnp.float32,
    )


def smoothed(field, before, after):
    side = before.shape[0]
    lower = jnp.concatenate([before, field[:-side]], 0)
    upper = jnp.concatenate([field[side:], after], 0)
    return smooth_weight * (2.0 * field - lower - upper)


def first_kernel(
    tiles, bins, send, landed_ref, lower_ref, kernels_arg,
    start_ref, local_ref, gram_ref, first_swap_ref, second_swap_ref, full_ref, upper_ref,
    picks_ref, rows_ref, parts_ref, arrived,
):
    copies = [
        pltpu.make_async_copy(kernels_arg.at[EARLY + p], upper_ref.at[p], arrived.at[p])
        for p in range(PATTERNS - EARLY)
    ]
    for copy in copies:
        copy.start()
    kernels = (lower_ref, upper_ref)
    side = tiles * CELLS
    samples = start_ref.shape[1]
    flags = total(fill_picks(tiles, bins, send, landed_ref, picks_ref))
    full_ref[...] = jnp.broadcast_to(flags, full_ref.shape)
    traces = jnp.concatenate(
        [
            landed_ref[:, i * ROOM : (i + 1) * ROOM].reshape(-1, LANES)
            for i in range(samples // LANES)
        ],
        1,
    )
    for b in range(bins):
        picks = picks_ref[b].reshape(PATTERNS * side, -1).astype(jnp.bfloat16)
        gram_ref[b] = dot_back(picks, picks).astype(jnp.bfloat16)
        sums = jnp.dot(picks, traces, preferred_element_type=jnp.float32)
        parts_ref[:, 0, b] = sums.astype(jnp.bfloat16).reshape(PATTERNS, side, samples)
    start = jnp.zeros((bins * side, samples), jnp.float32)
    for p in range(PATTERNS):
        if p >= EARLY:
            copies[p - EARLY].wait()
        rows = parts_ref[p, 0].reshape(bins * side, samples)
        start += dot_back(rows, kernel_of(kernels, p))
    start = start.astype(jnp.bfloat16)
    start_ref[...] = start
    field = start.astype(jnp.float32)
    nothing = jnp.zeros((side, samples), jnp.float32)
    project(start, kernels, rows_ref)
    for b in range(bins):
        store_parts(parts_ref, b, mixed(gram_ref, rows_ref, b))
    local = back_projected(kernels, parts_ref) + smoothed(field, nothing, nothing)
    local_ref[...] = local
    local = local.astype(jnp.bfloat16)
    odd = own_block(tiles) % 2 > 0
    for out_ref, to_after in ((first_swap_ref, ~odd), (second_swap_ref, odd)):
        out_ref[:side] = jnp.where(to_after, start[-side:], start[:side])
        out_ref[side:] = jnp.where(to_after, local[-side:], local[:side])


FULL, STEP, GROW = 4, 5, 6


def ahead_kernel(local_ref, gram_ref, lower_ref, upper_ref, rows_ref, mixed_ref):
    project(two_parts(local_ref[...]), (lower_ref, upper_ref), rows_ref)
    for b in range(rows_ref.shape[0]):
        mixed_ref[b] = mixed(gram_ref, rows_ref, b)


def second_kernel(
    tiles, offs, start_ref, local_ref, gram_ref, lower_ref, upper_ref, first_swap_ref,
    second_swap_ref, full_ref, ahead_ref, mixed_ref,
    once_ref, smooth_ref, parts_ref, sums_ref, rows_ref,
):
    bins, _, side, samples = rows_ref.shape
    start = start_ref[...].astype(jnp.float32)
    place = lax.axis_index("off") * tiles + own_block(tiles)
    ends = [place > 0, place < offs * tiles - 1]
    odd = own_block(tiles) % 2 > 0
    first = first_swap_ref[...].astype(jnp.float32)
    second = second_swap_ref[...].astype(jnp.float32)
    edges = [jnp.where(odd, first, second), jnp.where(odd, second, first)]
    beyond, outer = [], []
    for end, (edge, own) in enumerate(zip(edges, (start[:side], start[-side:]))):
        there = jnp.where(ends[end], smooth_weight, 0.0)
        beyond.append(-smooth_weight * edge[:side])
        outer.append(edge[side:] - there * own)
    inner = [jnp.zeros(((bins - 2) * side, samples), jnp.float32)] if bins > 2 else []
    beyond = jnp.concatenate([beyond[0], *inner, beyond[1]], 0)
    once = local_ref[...] + beyond
    once_ref[...] = once
    smooth = smoothed(once, outer[0], outer[1])
    smooth_ref[...] = smooth
    project(beyond.astype(jnp.bfloat16), (lower_ref, upper_ref), rows_ref)
    square = 0.0
    for b in range(bins):
        both = mixed_ref[b] + mixed(gram_ref, rows_ref, b)
        store_parts(parts_ref, b, both)
        rows = ahead_ref[b].astype(jnp.float32) + rows_ref[b].astype(jnp.float32)
        square += total(rows.reshape(both.shape) * both)
    products = [
        total(start * start),
        total(start * once),
        total(once * once),
        total(once * smooth) + square,
    ]
    lane = lax.broadcasted_iota(jnp.int32, (1, LANES), 1)
    line = jnp.where(lane == FULL, full_ref[:1], 0.0)
    for i, product in enumerate(products):
        line = jnp.where(lane == i, product, line)
    sums_ref[...] = jnp.broadcast_to(line, sums_ref.shape)


def last_kernel(parts_ref, lower_ref, upper_ref, out_ref):
    out_ref[...] = back_projected((lower_ref, upper_ref), parts_ref)


def pack_kernel(sums_ref, start_ref, once_ref, smooth_ref, normal_ref, *refs):
    *out_refs, out_ref = refs
    tiles = len(out_refs)
    ss, so, oo = (sums_ref[:1, i : i + 1] for i in range(3))
    step, grow = own_scales(ss, so, oo)
    start, once = start_ref[...].astype(jnp.float32), once_ref[...]
    twice = normal_ref[...] + smooth_ref[...]
    row = 0
    for field in (start, start - step * once, grow * once - step * twice):
        samples = field.shape[1]
        field = field.reshape(-1, tiles, CELLS, samples)
        size = field.shape[0] * CELLS
        for i in range(0, samples, LANES):
            for tile in range(tiles):
                piece = field[:, tile, :, i : i + LANES].reshape(size, LANES)
                out_ref[tile, row : row + size] = piece.astype(jnp.bfloat16)
            row += size
    lane = lax.broadcasted_iota(jnp.int32, (1, LANES), 1)
    rest = jnp.where(lane == STEP, step, sums_ref[:1])
    rest = jnp.where(lane == GROW, grow, rest)
    line = lax.broadcasted_iota(jnp.int32, (16, LANES), 0)
    parts = jnp.zeros((16, LANES), jnp.float32)
    for i in range(3):
        part = rest.astype(jnp.bfloat16).astype(jnp.float32)
        rest = rest - part
        parts = jnp.where(line == i, part, parts)
    for tile in range(tiles):
        out_ref[tile, row:] = parts.astype(jnp.bfloat16)
    lay_out(out_ref, out_refs)


def total(x):
    return jnp.sum(jnp.sum(x, 0, keepdims=True), 1, keepdims=True)


def own_scales(ss, so, oo):
    step = ss / so
    step = jnp.where(step > 0.0, jnp.clip(step, 1e-8, 1e3), 1.0)
    grow = step * step * oo / ss
    return step, jnp.where(grow > 0.0, jnp.clip(grow, 0.0, 1e3), 1.0)


def place_kernel(bins, *refs):
    *landed_refs, solution_ref, residual_ref, landed_ref = refs
    gather_in(landed_refs, landed_ref)
    tiles, length, _ = landed_ref.shape
    size = bins * CELLS
    samples = solution_ref.shape[2]
    pieces = samples // LANES

    def line_of(source):
        parts = landed_ref[source, length - 16 :].astype(jnp.float32)
        return jnp.sum(parts, 0, keepdims=True)

    def vector(source, i):
        part = [
            landed_ref[source, (i * pieces + j) * size : (i * pieces + j + 1) * size]
            for j in range(pieces)
        ]
        return jnp.concatenate(part, 1).astype(jnp.float32)

    sums = sum(line_of(tile) for tile in range(tiles))
    ss, so, oo, ot = (sums[:, i : i + 1] for i in range(4))
    step_0 = ss / so
    norm_1 = step_0 * step_0 * oo - ss
    grow = 1.0 + norm_1 / ss
    step_1 = norm_1 / (grow * grow * so - 2.0 * step_0 * grow * oo + step_0 * step_0 * ot)
    near = step_0 + step_1 * grow
    far = step_1 * step_0
    fields = [[], []]
    for block in range(tiles):
        source = jnp.where(
            flipped(), path_rank(tiles - 1 - block, tiles), path_rank(block, tiles)
        )
        line = line_of(source)
        inverse = 1.0 / line[:, STEP : STEP + 1]
        there = line[:, GROW : GROW + 1]
        start, first, second = (vector(source, i) for i in range(3))
        far_once = far * inverse
        near_once = near * inverse - far_once * there * inverse
        solution = (near - far_once) * start + far_once * first
        residual = (1.0 - near_once) * start + near_once * first - far_once * second
        fields[0].append(solution.reshape(bins, CELLS, samples))
        fields[1].append(residual.reshape(bins, CELLS, samples))
    solution_ref[...] = jnp.swapaxes(jnp.concatenate(fields[0], 0), 0, 1)
    residual_ref[...] = jnp.swapaxes(jnp.concatenate(fields[1], 0), 0, 1)


def copy_kernel(*refs):
    *refs, arrived = refs
    half = len(refs) // 2
    copies = [
        pltpu.make_async_copy(refs[i], refs[half + i], arrived.at[i]) for i in range(half)
    ]
    for copy in copies:
        copy.start()
    for copy in copies:
        copy.wait()


VMEM = pl.BlockSpec(memory_space=pltpu.VMEM)
HBM = pl.BlockSpec(memory_space=pltpu.HBM)


def local_call(kernel, name, in_specs, out_shape, scratch=(), out_specs=None, cost=0):
    return pl.pallas_call(
        kernel,
        out_shape=out_shape,
        in_specs=in_specs,
        out_specs=out_specs or jax.tree.map(lambda _: VMEM, out_shape),
        scratch_shapes=list(scratch),
        cost_estimate=pl.CostEstimate(
            flops=cost, bytes_accessed=cost // 256, transcendentals=0
        )
        if cost
        else None,
        compiler_params=pltpu.CompilerParams(vmem_limit_bytes=32 * 1024 * 1024),
        name=name,
    )


def shards_by_bin(
    traces, kernels, send_list, aper_slot, aper_pattern, trace_bin, trace_count
):
    tiles, offs = lax.axis_size("mid"), lax.axis_size("off")
    bins = NOFF // offs // tiles
    trace_rows, samples = traces.shape
    send = send_list.shape[2]
    rows = bins * tiles * CELLS
    side = tiles * CELLS
    sums = bins * (CELLS + 2 * REACH * send)

    def array(*shape, dtype=jnp.float32):
        return jax.ShapeDtypeStruct(shape, dtype)

    bf16 = functools.partial(array, dtype=jnp.bfloat16)
    in_hbm = functools.partial(
        pltpu.with_memory_space_constraint, memory_space=pltpu.HBM
    )
    lists = (send_list, aper_slot, aper_pattern, trace_bin, trace_count)
    early = bf16(EARLY, samples, samples)
    shared, lower = local_call(
        functools.partial(share_kernel, tiles, bins, ROOM),
        "share",
        [HBM] * 7,
        (bf16(tiles, samples // LANES * ROOM + 2 * APER, LANES), early),
        [
            pltpu.SMEM(send_list.shape, jnp.int32),
            pltpu.VMEM(aper_slot.shape, jnp.int32),
            pltpu.VMEM(aper_pattern.shape, jnp.int32),
            pltpu.VMEM((1, trace_rows), jnp.int32),
            pltpu.VMEM((1, trace_rows), jnp.int32),
            pltpu.VMEM(traces.shape, jnp.bfloat16),
            pltpu.SemaphoreType.DMA((6,)),
            pltpu.SemaphoreType.DMA,
        ],
    )(
        in_hbm(send_list),
        in_hbm(aper_slot),
        in_hbm(aper_pattern),
        in_hbm(trace_bin[None]),
        in_hbm(trace_count[None]),
        in_hbm(traces),
        in_hbm(kernels),
    )
    landed = lax.all_to_all(shared, "mid", 0, 0)
    pattern_rows = pltpu.VMEM((bins, PATTERNS, side, samples), jnp.bfloat16)
    parts_type = bf16(PATTERNS, 2, bins, side, samples)
    start, local, gram, *swaps, full, upper = local_call(
        functools.partial(first_kernel, tiles, bins, send),
        "first",
        [VMEM, VMEM, HBM],
        (
            bf16(rows, samples),
            array(rows, samples),
            bf16(bins, tiles * KEYS, tiles * KEYS),
            bf16(2 * side, samples),
            bf16(2 * side, samples),
            array(8, LANES),
            bf16(PATTERNS - EARLY, samples, samples),
        ),
        [
            pltpu.VMEM((bins, PATTERNS, tiles, CELLS, tiles * ROOM), jnp.float32),
            pattern_rows,
            pltpu.VMEM(parts_type.shape, parts_type.dtype),
            pltpu.SemaphoreType.DMA((PATTERNS - EARLY,)),
        ],
    )(landed, lower, in_hbm(kernels))

    path = [path_rank(m, tiles) for m in range(tiles)]
    chain = [m * offs + o for o in range(offs) for m in (path[::-1] if o % 2 else path)]
    swaps = [
        lax.ppermute(
            x,
            ("mid", "off"),
            [
                pair
                for i, j in zip(chain[first:-1:2], chain[first + 1 :: 2])
                for pair in ((i, j), (j, i))
            ],
        )
        for first, x in enumerate(swaps)
    ]

    flops = 2 * rows * PATTERNS * samples * samples
    ahead, mixed_ahead = local_call(
        ahead_kernel,
        "ahead",
        [VMEM] * 4,
        (bf16(*pattern_rows.shape), array(bins, PATTERNS * side, samples)),
        cost=3 * flops,
    )(local, gram, lower, upper)
    field = array(rows, samples)
    once, smooth, parts, products = local_call(
        functools.partial(second_kernel, tiles, offs),
        "second",
        [VMEM] * 10,
        (field, field, parts_type, array(8, LANES)),
        [pattern_rows],
        cost=2 * flops,
    )(start, local, gram, lower, upper, *swaps, full, ahead, mixed_ahead)

    projected = local_call(last_kernel, "last", [VMEM] * 3, field, cost=2 * flops)(
        parts, lower, upper
    )
    addends = [products] + [
        lax.ppermute(products, "off", [(i, i ^ step) for i in range(offs)])
        for step in range(1, offs)
    ]
    while len(addends) > 1:
        addends = [a + b for a, b in zip(addends[::2], addends[1::2])]
    products = addends[0]
    chunk = bf16(samples // LANES * 3 * bins * CELLS + 16, LANES)
    chunks = pltpu.VMEM((tiles, *chunk.shape), chunk.dtype)
    packed = local_call(
        pack_kernel, "pack", [VMEM] * 5, [chunk] * tiles, [chunks]
    )(products, start, once, smooth, projected)
    landed = swapped(packed)

    def again():
        arguments = [in_hbm(x) for x in (traces, kernels, *lists[:3])]
        arguments += [in_hbm(x[None]) for x in lists[3:]]
        *copies, bins_again, count_again = local_call(
            copy_kernel,
            "again",
            [HBM] * len(arguments),
            tuple(array(*x.shape, dtype=x.dtype) for x in arguments),
            [pltpu.SemaphoreType.DMA((len(arguments),))],
            out_specs=(HBM,) * len(arguments),
        )(*arguments)
        return *copies, bins_again[0], count_again[0]

    def placed():
        out_type = pltpu.HBM((CELLS, bins * tiles, samples), jnp.float32)
        return local_call(
            functools.partial(place_kernel, bins),
            "place",
            [VMEM] * tiles,
            (out_type, out_type),
            [chunks],
            out_specs=(VMEM, VMEM),
        )(*landed)

    return lax.cond(
        products[0, FULL] > 0.0, lambda: shards_by_tile(*again()), placed
    )


def fits_by_bin(tiles, offs, send, trace_rows, samples):
    return (
        (NOFF // offs) % (2 * tiles) == 0
        and offs & (offs - 1) == 0
        and tiles & (tiles - 1) == 0
        and tiles % TOGETHER == 0
        and send == WITHIN
        and trace_rows == LANES
        and samples % LANES == 0
    )


def solution(mesh):
    in_specs = (
        P(("mid", "off"), None),
        P(),
        P("mid", None, None),
        P(None, ("mid", "off")),
        P(None, ("mid", "off")),
        P(("mid", "off")),
        P(("mid", "off")),
    )
    out_specs = (P("mid", "off", None), P("mid", "off", None))

    def shards(traces, kernels, send_list, *lists):
        fits = fits_by_bin(
            mesh.shape["mid"], mesh.shape["off"], send_list.shape[2], *traces.shape
        )
        form = shards_by_bin if fits else shards_by_tile
        return form(traces, kernels, send_list, *lists)

    return jax.shard_map(
        shards, mesh=mesh, in_specs=in_specs, out_specs=out_specs, check_vma=False
    )
```

```python
import functools

import jax
import jax.numpy as jnp
from jax import lax
from jax.experimental import pallas as pl
from jax.experimental.pallas import tpu as pltpu
from jax.sharding import PartitionSpec as P

NOFF = 64
PATTERNS = 8
REACH = 2
APER = 8
ITERS = 2
CELLS = 8
KEYS = PATTERNS * CELLS
EARLY = 3
ROOM = 32
LANES = 128
TOGETHER = LANES // ROOM


smooth_weight = 2.0


def padded_2(x, sides, width):
    for axis, dim in sides:
        peers, length = (lax.axis_size(axis), x.shape[dim])
        up = [(i, (i + 1) % peers) for i in range(peers - 1)]
        down = [(j, i) for i, j in up]
        last = lax.slice_in_dim(x, length - width, length, axis=dim)
        first = lax.slice_in_dim(x, 0, width, axis=dim)
        before = lax.ppermute(last, axis, up)
        after = lax.ppermute(first, axis, down)
        x = jnp.concatenate([before, x, after], axis=dim)
    return x


def from_behind(x, axis, by):
    peers = lax.axis_size(axis)
    pairs = [(i, i + by) for i in range(peers) if 0 <= i + by < peers]
    return lax.ppermute(x, axis, pairs)


def direction_shift(course):
    return (course // 2 + 1) * (1 - 2 * (course % 2))


def offset_laplace(padded):
    return smooth_weight * (2.0 * padded[:, 1:-1] - padded[:, :-2] - padded[:, 2:])


def smoothing(field):
    padded = padded_2(field, (("off", 1),), 1)
    smoothed = offset_laplace(padded)
    return smoothed


def deliver(outgoing):
    arrived = [None] * (2 * REACH)
    for course in range(2 * REACH):
        arrived[course] = from_behind(outgoing[course], "mid", direction_shift(course))
    return arrived


def give_back(returning):
    landed = [None] * (2 * REACH)
    for course in range(2 * REACH):
        landed[course] = from_behind(returning[course], "mid", -direction_shift(course))
    return landed


def shards_by_tile(
    traces, kernels, send_list, aper_slot, aper_pattern, trace_bin, trace_count
):
    off_dev = NOFF // lax.axis_size("off")
    trace_rows = traces.shape[0]
    samples = traces.shape[1]
    chosen_cells = send_list[0]
    send_count = chosen_cells.shape[1]
    slot_count = CELLS + 2 * REACH * send_count
    live_mask = jnp.arange(APER, dtype=jnp.int32)[:, None] < trace_count[None, :]
    row_index = (aper_slot * off_dev + trace_bin[None, :]).reshape(-1)
    pattern_ids = jnp.arange(PATTERNS, dtype=jnp.int32)[:, None, None]
    chooser = ((aper_pattern[None] == pattern_ids) & live_mask[None]).astype(
        jnp.bfloat16
    )
    pick_rows = (
        aper_pattern * trace_rows + jnp.arange(trace_rows, dtype=jnp.int32)[None, :]
    ).reshape(-1)
    live_column = live_mask.reshape(-1, 1).astype(jnp.float32)

    def forward(field_bf):
        outgoing = [field_bf[chosen_cells[course]] for course in range(2 * REACH)]
        arrived = deliver(outgoing)
        slot_rows = jnp.concatenate([field_bf] + arrived, 0).reshape(-1, samples)
        blocks = slot_rows[row_index].reshape(APER, trace_rows, samples)
        pattern_sums = jnp.einsum(
            "pjt,jtn->ptn", chooser, blocks, preferred_element_type=jnp.float32
        ).astype(jnp.bfloat16)
        return jnp.einsum(
            "ptn,pnm->tm", pattern_sums, kernels, preferred_element_type=jnp.float32
        )

    def adjoint(values_bf):
        spread = jnp.einsum(
            "tm,pnm->ptn", values_bf, kernels, preferred_element_type=jnp.float32
        ).reshape(-1, samples)
        entries = spread[pick_rows] * live_column
        slot_sums = (
            jnp.zeros((slot_count * off_dev, samples), jnp.float32)
            .at[row_index]
            .add(entries)
        )
        slot_sums = slot_sums.reshape(slot_count, off_dev, samples)
        returning = [
            slot_sums[CELLS + course * send_count : CELLS + (course + 1) * send_count]
            for course in range(2 * REACH)
        ]
        landed = give_back(returning)
        accumulated = slot_sums[:CELLS]
        for course in range(2 * REACH):
            accumulated = accumulated.at[chosen_cells[course]].add(landed[course])
        return accumulated

    def global_total(value):
        return lax.psum(value, ("mid", "off"))

    residual = adjoint(traces)
    direction = residual
    solution = jnp.zeros_like(residual)
    norm_now = global_total(jnp.sum(residual * residual))
    for iteration in range(ITERS):
        applied = adjoint(
            forward(direction.astype(jnp.bfloat16)).astype(jnp.bfloat16)
        ) + smoothing(direction)
        step_size = norm_now / global_total(jnp.sum(direction * applied))
        solution = solution + step_size * direction
        residual = residual - step_size * applied
        if iteration + 1 < ITERS:
            norm_next = global_total(jnp.sum(residual * residual))
            direction = residual + norm_next / norm_now * direction
            norm_now = norm_next
    return (solution, residual)


def path_rank(m, tiles):
    return m ^ ((m >> 1) & 1) if tiles % 4 == 0 else m


def turns(peers):
    near, far = range(1, peers // 2), range(peers // 2, peers)
    even = [i for pair in zip(far, near) for i in pair]
    odd = [i for pair in zip(near, far) for i in pair]
    return [(0, 0), *zip(even, odd), (peers - 1, peers - 1)]


def partners(peers):
    odd, place = flipped(), lax.axis_index("mid")
    return [place ^ jnp.where(odd, j, i) for i, j in turns(peers)]


def lay_out(chunks_ref, out_refs):
    for partner, out_ref in zip(partners(len(out_refs)), out_refs):
        out_ref[...] = chunks_ref[partner]


def gather_in(landed_refs, chunks_ref):
    for partner, landed_ref in zip(partners(len(landed_refs)), landed_refs):
        chunks_ref[partner] = landed_ref[...]


def swapped(chunks):
    peers, offs = len(chunks), lax.axis_size("off")
    return list(chunks[:1]) + [
        lax.ppermute(
            chunk,
            ("mid", "off"),
            [
                (m * offs + o, (m ^ turn[o % 2]) * offs + o)
                for m in range(peers)
                for o in range(offs)
            ],
        )
        for turn, chunk in zip(turns(peers)[1:], chunks[1:])
    ]


def flipped():
    return lax.axis_index("off") % 2 > 0


def own_block(tiles):
    block = path_rank(lax.axis_index("mid"), tiles)
    return jnp.where(flipped(), tiles - 1 - block, block)


def dot_back(rows, kernel):
    return lax.dot_general(
        rows, kernel, (((1,), (1,)), ((), ())), preferred_element_type=jnp.float32
    )


SLOT, PATTERN, WITHIN, COUNT, FLAG = 0, APER, 4, 5, 6


def share_kernel(
    tiles, bins, room, sends_arg, slot_arg, pattern_arg, bin_arg, count_arg, traces_arg,
    kernels_arg, out_ref, kernels_ref, sends_ref, slot_ref, pattern_ref, bin_ref, count_ref, traces_ref,
    staged, arrived,
):
    rows, samples = traces_ref.shape
    stages = [
        pltpu.make_async_copy(arg, ref, staged.at[i])
        for i, (arg, ref) in enumerate(
            [
                (bin_arg, bin_ref),
                (slot_arg, slot_ref),
                (pattern_arg, pattern_ref),
                (count_arg, count_ref),
                (sends_arg, sends_ref),
                (traces_arg, traces_ref),
            ]
        )
    ]
    kernels, others = (
        pltpu.make_async_copy(kernels_arg.at[some], kernels_ref.at[some], arrived.at[i])
        for i, some in enumerate((pl.ds(0, EARLY), pl.ds(EARLY, PATTERNS - EARLY)))
    )
    for stage in stages + [kernels]:
        stage.start()

    @pl.when(flipped())
    def _():
        others.start()

    index = lax.broadcasted_iota(jnp.int32, (tiles, rows), 0)
    earlier = lax.broadcasted_iota(jnp.int32, (rows, rows), 0) < (
        lax.broadcasted_iota(jnp.int32, (rows, rows), 1)
    )
    earlier = jnp.where(earlier, 1.0, 0.0).astype(jnp.bfloat16)
    stages[0].wait()
    offset_bin = bin_ref[...]
    block = lax.div(offset_bin, bins)
    within = offset_bin - block * bins
    chunk = path_rank(jnp.where(flipped(), tiles - 1 - block, block), tiles)
    belongs = jnp.where(index == chunk, 1.0, 0.0)
    rank = jnp.dot(
        belongs.astype(jnp.bfloat16), earlier, preferred_element_type=jnp.float32
    )
    rank = jnp.sum(rank * belongs, 0, keepdims=True).astype(jnp.int32)
    full = jnp.max(rank, axis=1, keepdims=True) >= room
    target = jnp.where(rank < room, chunk * room + rank, -1)
    picks = lax.broadcasted_iota(jnp.int32, (tiles * room, rows), 0) == target
    picks = jnp.where(picks, 1.0, 0.0).astype(jnp.bfloat16)
    place = lax.axis_index("mid")
    lane = lax.broadcasted_iota(jnp.int32, (1, LANES), 1)
    target = chunk * LANES + lax.rem(place, TOGETHER) * room + rank
    chosen = lax.broadcasted_iota(jnp.int32, (tiles * LANES, rows), 0) == (
        jnp.where(rank < room, target, -1)
    )
    chosen = jnp.where(chosen, 1.0, 0.0).astype(jnp.bfloat16)
    for stage in stages[1:5]:
        stage.wait()
    lists = jnp.concatenate(
        [
            slot_ref[...].astype(jnp.float32),
            pattern_ref[...].astype(jnp.float32),
            jnp.zeros((WITHIN, rows), jnp.float32),
            within.astype(jnp.float32),
            count_ref[...].astype(jnp.float32),
            jnp.zeros((APER - COUNT - 1, rows), jnp.float32),
        ],
        0,
    ).astype(jnp.bfloat16)
    lists = dot_back(lists, chosen)
    _, courses, send = sends_ref.shape
    line = lax.broadcasted_iota(jnp.int32, (2 * APER, LANES), 0)
    sent = jnp.zeros((2 * APER, LANES), jnp.int32)
    for course in range(courses):
        reader = lax.rem(place + direction_shift(course) + TOGETHER, TOGETHER)
        here = lax.div(lane, room) == reader
        for m in range(send):
            value = jnp.where(here, sends_ref[0, course, m], 0)
            sent += jnp.where(line == sent_row(course, send) + m, value, 0)
    past = lax.div(lane, room) == lax.rem(place + 1, TOGETHER)
    sent += jnp.where(past & (line == FLAG) & full, 1, 0)
    sent = sent.astype(jnp.float32)
    pieces = samples // LANES
    for m in range(tiles):
        own = lists[:, m * LANES : (m + 1) * LANES]
        moved = pltpu.roll(own[2 * APER :], room, 1)
        out_ref[m, pieces * room :] = (
            own[: 2 * APER] + jnp.concatenate([moved, jnp.zeros_like(moved)], 0) + sent
        ).astype(jnp.bfloat16)
    stages[5].wait()
    picked = jnp.dot(picks, traces_ref[...], preferred_element_type=jnp.float32)
    picked = picked.reshape(tiles, room, samples).astype(jnp.bfloat16)
    for i in range(pieces):
        out_ref[:, i * room : (i + 1) * room] = picked[:, :, i * LANES : (i + 1) * LANES]
    kernels.wait()

    @pl.when(flipped())
    def _():
        others.wait()


def sent_row(course, send):
    return send if course == 3 else 0


def fill_picks(tiles, bins, send, landed_ref, picks_ref):
    flags = 0
    keys = lax.broadcasted_iota(jnp.int32, (KEYS, LANES), 0)
    member = lax.div(lax.broadcasted_iota(jnp.int32, (1, LANES), 1), ROOM)
    blocks = [
        landed_ref[tile, -2 * APER :].astype(jnp.float32).astype(jnp.int32)
        for tile in range(tiles)
    ]
    for group in range(tiles // TOGETHER):
        readers = range(group * TOGETHER, (group + 1) * TOGETHER)
        lists, moved = 0, 0
        for tile in readers:
            lists += jnp.where(member == tile % TOGETHER, blocks[tile], 0)
            past = member == (tile + 1) % TOGETHER
            moved += jnp.where(past, blocks[tile][:APER], 0)
        moved = pltpu.roll(moved, LANES - ROOM, 1)
        flags += moved[FLAG : FLAG + 1]
        within, count = moved[WITHIN : WITHIN + 1], moved[COUNT : COUNT + 1]
        wanted = []
        for region in range(2 * REACH + 1):
            course = region - 1
            shift = direction_shift(course) if region else 0
            owners = [tile - shift for tile in readers if 0 <= tile - shift < tiles]
            sent = 0
            for owner in owners if region else ():
                row = sent_row(course, send)
                values = blocks[owner][row : row + send]
                sent += jnp.where(member == (owner + shift) % TOGETHER, values, 0)
            for entry in range(region, APER, 2 * REACH + 1):
                cell = lists[SLOT + entry : SLOT + entry + 1]
                if region:
                    place = cell - (CELLS + course * send)
                    cell = sent[:1]
                    for other in range(1, send):
                        cell = jnp.where(place == other, sent[other : other + 1], cell)
                pattern = lists[PATTERN + entry : PATTERN + entry + 1]
                key = jnp.where(count > entry, pattern * CELLS + cell, -1)
                for owner in owners:
                    there = member == (owner + shift) % TOGETHER
                    wanted.append((owner, jnp.where(there, key, -1)))
        for tile in range(tiles):
            for b in range(bins):
                total = jnp.zeros((KEYS, LANES), jnp.float32)
                for owner, key in wanted:
                    if owner == tile:
                        hit = keys == jnp.where(within == b, key, -1)
                        total += jnp.where(hit, 1.0, 0.0)
                picks_ref[b, :, tile, :, group * LANES : (group + 1) * LANES] = (
                    total.reshape(PATTERNS, CELLS, LANES)
                )
    return flags.astype(jnp.float32)


def two_parts(x):
    high = x.astype(jnp.bfloat16)
    low = (x - high.astype(jnp.float32)).astype(jnp.bfloat16)
    return jnp.concatenate([high, low], 0)


def store_parts(parts_ref, b, x):
    shape = (PATTERNS, *parts_ref.shape[3:])
    high = x.astype(jnp.bfloat16)
    parts_ref[:, 0, b] = high.reshape(shape)
    low = (x - high.astype(jnp.float32)).astype(jnp.bfloat16)
    parts_ref[:, 1, b] = low.reshape(shape)


def back_projected(kernels_ref, parts_ref):
    _, _, bins, side, samples = parts_ref.shape
    rows = bins * side
    both = jnp.zeros((2 * rows, samples), jnp.float32)
    for p in range(PATTERNS):
        both += dot_back(
            parts_ref[p].reshape(2 * rows, samples), kernels_ref[p]
        )
    return both[:rows] + both[rows:]


def project(field, kernels_ref, rows_ref):
    bins, _, side, samples = rows_ref.shape
    rows = bins * side
    for p in range(PATTERNS):
        u = jnp.dot(field, kernels_ref[p], preferred_element_type=jnp.float32)
        u = u[:rows] + u[rows:] if field.shape[0] > rows else u
        rows_ref[:, p] = u.astype(jnp.bfloat16).reshape(bins, side, samples)


def mixed(gram_ref, rows_ref, b):
    _, _, side, samples = rows_ref.shape
    return jnp.dot(
        gram_ref[b],
        rows_ref[b].reshape(PATTERNS * side, samples),
        preferred_element_type=jnp.float32,
    )


def smoothed(field, before, after):
    side = before.shape[0]
    lower = jnp.concatenate([before, field[:-side]], 0)
    upper = jnp.concatenate([field[side:], after], 0)
    return smooth_weight * (2.0 * field - lower - upper)


def first_kernel(
    tiles, bins, send, landed_ref, _, kernels_arg,
    start_ref, local_ref, gram_ref, first_swap_ref, second_swap_ref, full_ref, kernels_ref,
    picks_ref, rows_ref, parts_ref, arrived,
):
    copies = [
        pltpu.make_async_copy(
            kernels_arg.at[EARLY + p], kernels_ref.at[EARLY + p], arrived.at[p]
        )
        for p in range(PATTERNS - EARLY)
    ]

    @pl.when(~flipped())
    def _():
        for copy in copies:
            copy.start()

    side = tiles * CELLS
    samples = start_ref.shape[1]
    flags = total(fill_picks(tiles, bins, send, landed_ref, picks_ref))
    full_ref[...] = jnp.broadcast_to(flags, full_ref.shape)
    traces = jnp.concatenate(
        [
            landed_ref[:, i * ROOM : (i + 1) * ROOM].reshape(-1, LANES)
            for i in range(samples // LANES)
        ],
        1,
    )
    for b in range(bins):
        picks = picks_ref[b].reshape(PATTERNS * side, -1).astype(jnp.bfloat16)
        gram_ref[b] = dot_back(picks, picks).astype(jnp.bfloat16)
        sums = jnp.dot(picks, traces, preferred_element_type=jnp.float32)
        parts_ref[:, 0, b] = sums.astype(jnp.bfloat16).reshape(PATTERNS, side, samples)
    start = jnp.zeros((bins * side, samples), jnp.float32)
    for p in range(PATTERNS):
        if p >= EARLY:
            pl.when(~flipped())(copies[p - EARLY].wait)
        rows = parts_ref[p, 0].reshape(bins * side, samples)
        start += dot_back(rows, kernels_ref[p])
    start = start.astype(jnp.bfloat16)
    start_ref[...] = start
    field = start.astype(jnp.float32)
    nothing = jnp.zeros((side, samples), jnp.float32)
    project(start, kernels_ref, rows_ref)
    for b in range(bins):
        store_parts(parts_ref, b, mixed(gram_ref, rows_ref, b))
    local = back_projected(kernels_ref, parts_ref) + smoothed(field, nothing, nothing)
    local_ref[...] = local
    local = local.astype(jnp.bfloat16)
    odd = own_block(tiles) % 2 > 0
    for out_ref, to_after in ((first_swap_ref, ~odd), (second_swap_ref, odd)):
        out_ref[:side] = jnp.where(to_after, start[-side:], start[:side])
        out_ref[side:] = jnp.where(to_after, local[-side:], local[:side])


FULL, STEP, GROW = 4, 5, 6


def ahead_kernel(local_ref, gram_ref, kernels_ref, rows_ref, mixed_ref):
    project(two_parts(local_ref[...]), kernels_ref, rows_ref)
    for b in range(rows_ref.shape[0]):
        mixed_ref[b] = mixed(gram_ref, rows_ref, b)


def second_kernel(
    tiles, offs, start_ref, local_ref, gram_ref, kernels_ref, first_swap_ref,
    second_swap_ref, full_ref, ahead_ref, mixed_ref,
    once_ref, smooth_ref, parts_ref, sums_ref, rows_ref,
):
    bins, _, side, samples = rows_ref.shape
    start = start_ref[...].astype(jnp.float32)
    place = lax.axis_index("off") * tiles + own_block(tiles)
    ends = [place > 0, place < offs * tiles - 1]
    odd = own_block(tiles) % 2 > 0
    first = first_swap_ref[...].astype(jnp.float32)
    second = second_swap_ref[...].astype(jnp.float32)
    edges = [jnp.where(odd, first, second), jnp.where(odd, second, first)]
    beyond, outer = [], []
    for end, (edge, own) in enumerate(zip(edges, (start[:side], start[-side:]))):
        there = jnp.where(ends[end], smooth_weight, 0.0)
        beyond.append(-smooth_weight * edge[:side])
        outer.append(edge[side:] - there * own)
    inner = [jnp.zeros(((bins - 2) * side, samples), jnp.float32)] if bins > 2 else []
    beyond = jnp.concatenate([beyond[0], *inner, beyond[1]], 0)
    once = local_ref[...] + beyond
    once_ref[...] = once
    smooth = smoothed(once, outer[0], outer[1])
    smooth_ref[...] = smooth
    project(beyond.astype(jnp.bfloat16), kernels_ref, rows_ref)
    square = 0.0
    for b in range(bins):
        both = mixed_ref[b] + mixed(gram_ref, rows_ref, b)
        store_parts(parts_ref, b, both)
        rows = ahead_ref[b].astype(jnp.float32) + rows_ref[b].astype(jnp.float32)
        square += total(rows.reshape(both.shape) * both)
    products = [
        total(start * start),
        total(start * once),
        total(once * once),
        total(once * smooth) + square,
    ]
    lane = lax.broadcasted_iota(jnp.int32, (1, LANES), 1)
    line = jnp.where(lane == FULL, full_ref[:1], 0.0)
    for i, product in enumerate(products):
        line = jnp.where(lane == i, product, line)
    sums_ref[...] = jnp.broadcast_to(line, sums_ref.shape)


def last_kernel(parts_ref, kernels_ref, out_ref):
    out_ref[...] = back_projected(kernels_ref, parts_ref)


def pack_kernel(sums_ref, start_ref, once_ref, smooth_ref, normal_ref, *refs):
    *out_refs, out_ref = refs
    tiles = len(out_refs)
    ss, so, oo = (sums_ref[:1, i : i + 1] for i in range(3))
    step, grow = own_scales(ss, so, oo)
    start, once = start_ref[...].astype(jnp.float32), once_ref[...]
    twice = normal_ref[...] + smooth_ref[...]
    row = 0
    for field in (start, start - step * once, grow * once - step * twice):
        samples = field.shape[1]
        field = field.reshape(-1, tiles, CELLS, samples)
        size = field.shape[0] * CELLS
        for i in range(0, samples, LANES):
            for tile in range(tiles):
                piece = field[:, tile, :, i : i + LANES].reshape(size, LANES)
                out_ref[tile, row : row + size] = piece.astype(jnp.bfloat16)
            row += size
    lane = lax.broadcasted_iota(jnp.int32, (1, LANES), 1)
    rest = jnp.where(lane == STEP, step, sums_ref[:1])
    rest = jnp.where(lane == GROW, grow, rest)
    line = lax.broadcasted_iota(jnp.int32, (16, LANES), 0)
    parts = jnp.zeros((16, LANES), jnp.float32)
    for i in range(3):
        part = rest.astype(jnp.bfloat16).astype(jnp.float32)
        rest = rest - part
        parts = jnp.where(line == i, part, parts)
    for tile in range(tiles):
        out_ref[tile, row:] = parts.astype(jnp.bfloat16)
    lay_out(out_ref, out_refs)


def total(x):
    return jnp.sum(jnp.sum(x, 0, keepdims=True), 1, keepdims=True)


def own_scales(ss, so, oo):
    step = ss / so
    step = jnp.where(step > 0.0, jnp.clip(step, 1e-8, 1e3), 1.0)
    grow = step * step * oo / ss
    return step, jnp.where(grow > 0.0, jnp.clip(grow, 0.0, 1e3), 1.0)


def place_kernel(bins, *refs):
    *landed_refs, solution_ref, residual_ref, landed_ref = refs
    gather_in(landed_refs, landed_ref)
    tiles, length, _ = landed_ref.shape
    size = bins * CELLS
    samples = solution_ref.shape[2]
    pieces = samples // LANES

    def line_of(source):
        parts = landed_ref[source, length - 16 :].astype(jnp.float32)
        return jnp.sum(parts, 0, keepdims=True)

    def vector(source, i):
        part = [
            landed_ref[source, (i * pieces + j) * size : (i * pieces + j + 1) * size]
            for j in range(pieces)
        ]
        return jnp.concatenate(part, 1).astype(jnp.float32)

    sums = sum(line_of(tile) for tile in range(tiles))
    ss, so, oo, ot = (sums[:, i : i + 1] for i in range(4))
    step_0 = ss / so
    norm_1 = step_0 * step_0 * oo - ss
    grow = 1.0 + norm_1 / ss
    step_1 = norm_1 / (grow * grow * so - 2.0 * step_0 * grow * oo + step_0 * step_0 * ot)
    near = step_0 + step_1 * grow
    far = step_1 * step_0
    fields = [[], []]
    for block in range(tiles):
        source = jnp.where(
            flipped(), path_rank(tiles - 1 - block, tiles), path_rank(block, tiles)
        )
        line = line_of(source)
        inverse = 1.0 / line[:, STEP : STEP + 1]
        there = line[:, GROW : GROW + 1]
        start, first, second = (vector(source, i) for i in range(3))
        far_once = far * inverse
        near_once = near * inverse - far_once * there * inverse
        solution = (near - far_once) * start + far_once * first
        residual = (1.0 - near_once) * start + near_once * first - far_once * second
        fields[0].append(solution.reshape(bins, CELLS, samples))
        fields[1].append(residual.reshape(bins, CELLS, samples))
    solution_ref[...] = jnp.swapaxes(jnp.concatenate(fields[0], 0), 0, 1)
    residual_ref[...] = jnp.swapaxes(jnp.concatenate(fields[1], 0), 0, 1)


def copy_kernel(*refs):
    *refs, arrived = refs
    half = len(refs) // 2
    copies = [
        pltpu.make_async_copy(refs[i], refs[half + i], arrived.at[i]) for i in range(half)
    ]
    for copy in copies:
        copy.start()
    for copy in copies:
        copy.wait()


VMEM = pl.BlockSpec(memory_space=pltpu.VMEM)
HBM = pl.BlockSpec(memory_space=pltpu.HBM)


def local_call(kernel, name, in_specs, out_shape, scratch=(), out_specs=None, cost=0, aliases=None):
    return pl.pallas_call(
        kernel,
        out_shape=out_shape,
        in_specs=in_specs,
        out_specs=out_specs or jax.tree.map(lambda _: VMEM, out_shape),
        scratch_shapes=list(scratch),
        input_output_aliases=aliases or {},
        cost_estimate=pl.CostEstimate(
            flops=cost, bytes_accessed=cost // 256, transcendentals=0
        )
        if cost
        else None,
        compiler_params=pltpu.CompilerParams(vmem_limit_bytes=32 * 1024 * 1024),
        name=name,
    )


def shards_by_bin(
    traces, kernels, send_list, aper_slot, aper_pattern, trace_bin, trace_count
):
    tiles, offs = lax.axis_size("mid"), lax.axis_size("off")
    bins = NOFF // offs // tiles
    trace_rows, samples = traces.shape
    send = send_list.shape[2]
    rows = bins * tiles * CELLS
    side = tiles * CELLS
    sums = bins * (CELLS + 2 * REACH * send)

    def array(*shape, dtype=jnp.float32):
        return jax.ShapeDtypeStruct(shape, dtype)

    bf16 = functools.partial(array, dtype=jnp.bfloat16)
    in_hbm = functools.partial(
        pltpu.with_memory_space_constraint, memory_space=pltpu.HBM
    )
    lists = (send_list, aper_slot, aper_pattern, trace_bin, trace_count)
    held_type = bf16(*kernels.shape)
    shared, held = local_call(
        functools.partial(share_kernel, tiles, bins, ROOM),
        "share",
        [HBM] * 7,
        (bf16(tiles, samples // LANES * ROOM + 2 * APER, LANES), held_type),
        [
            pltpu.SMEM(send_list.shape, jnp.int32),
            pltpu.VMEM(aper_slot.shape, jnp.int32),
            pltpu.VMEM(aper_pattern.shape, jnp.int32),
            pltpu.VMEM((1, trace_rows), jnp.int32),
            pltpu.VMEM((1, trace_rows), jnp.int32),
            pltpu.VMEM(traces.shape, jnp.bfloat16),
            pltpu.SemaphoreType.DMA((6,)),
            pltpu.SemaphoreType.DMA((2,)),
        ],
    )(
        in_hbm(send_list),
        in_hbm(aper_slot),
        in_hbm(aper_pattern),
        in_hbm(trace_bin[None]),
        in_hbm(trace_count[None]),
        in_hbm(traces),
        in_hbm(kernels),
    )
    landed = lax.all_to_all(shared, "mid", 0, 0)
    pattern_rows = pltpu.VMEM((bins, PATTERNS, side, samples), jnp.bfloat16)
    parts_type = bf16(PATTERNS, 2, bins, side, samples)
    start, local, gram, *swaps, full, held = local_call(
        functools.partial(first_kernel, tiles, bins, send),
        "first",
        [VMEM, VMEM, HBM],
        (
            bf16(rows, samples),
            array(rows, samples),
            bf16(bins, tiles * KEYS, tiles * KEYS),
            bf16(2 * side, samples),
            bf16(2 * side, samples),
            array(8, LANES),
            held_type,
        ),
        [
            pltpu.VMEM((bins, PATTERNS, tiles, CELLS, tiles * ROOM), jnp.float32),
            pattern_rows,
            pltpu.VMEM(parts_type.shape, parts_type.dtype),
            pltpu.SemaphoreType.DMA((PATTERNS - EARLY,)),
        ],
        aliases={1: 6},
    )(landed, held, in_hbm(kernels))

    path = [path_rank(m, tiles) for m in range(tiles)]
    chain = [m * offs + o for o in range(offs) for m in (path[::-1] if o % 2 else path)]
    swaps = [
        lax.ppermute(
            x,
            ("mid", "off"),
            [
                pair
                for i, j in zip(chain[first:-1:2], chain[first + 1 :: 2])
                for pair in ((i, j), (j, i))
            ],
        )
        for first, x in enumerate(swaps)
    ]

    flops = 2 * rows * PATTERNS * samples * samples
    ahead, mixed_ahead = local_call(
        ahead_kernel,
        "ahead",
        [VMEM] * 3,
        (bf16(*pattern_rows.shape), array(bins, PATTERNS * side, samples)),
        cost=3 * flops,
    )(local, gram, held)
    field = array(rows, samples)
    once, smooth, parts, products = local_call(
        functools.partial(second_kernel, tiles, offs),
        "second",
        [VMEM] * 9,
        (field, field, parts_type, array(8, LANES)),
        [pattern_rows],
        cost=2 * flops,
    )(start, local, gram, held, *swaps, full, ahead, mixed_ahead)

    projected = local_call(last_kernel, "last", [VMEM] * 2, field, cost=2 * flops)(
        parts, held
    )
    addends = [products] + [
        lax.ppermute(products, "off", [(i, i ^ step) for i in range(offs)])
        for step in range(1, offs)
    ]
    while len(addends) > 1:
        addends = [a + b for a, b in zip(addends[::2], addends[1::2])]
    products = addends[0]
    chunk = bf16(samples // LANES * 3 * bins * CELLS + 16, LANES)
    chunks = pltpu.VMEM((tiles, *chunk.shape), chunk.dtype)
    packed = local_call(
        pack_kernel, "pack", [VMEM] * 5, [chunk] * tiles, [chunks]
    )(products, start, once, smooth, projected)
    landed = swapped(packed)

    def again():
        arguments = [in_hbm(x) for x in (traces, kernels, *lists[:3])]
        arguments += [in_hbm(x[None]) for x in lists[3:]]
        *copies, bins_again, count_again = local_call(
            copy_kernel,
            "again",
            [HBM] * len(arguments),
            tuple(array(*x.shape, dtype=x.dtype) for x in arguments),
            [pltpu.SemaphoreType.DMA((len(arguments),))],
            out_specs=(HBM,) * len(arguments),
        )(*arguments)
        return *copies, bins_again[0], count_again[0]

    def placed():
        out_type = pltpu.HBM((CELLS, bins * tiles, samples), jnp.float32)
        return local_call(
            functools.partial(place_kernel, bins),
            "place",
            [VMEM] * tiles,
            (out_type, out_type),
            [chunks],
            out_specs=(VMEM, VMEM),
        )(*landed)

    return lax.cond(
        products[0, FULL] > 0.0, lambda: shards_by_tile(*again()), placed
    )


def fits_by_bin(tiles, offs, send, trace_rows, samples):
    return (
        (NOFF // offs) % (2 * tiles) == 0
        and offs & (offs - 1) == 0
        and tiles & (tiles - 1) == 0
        and tiles % TOGETHER == 0
        and send == WITHIN
        and trace_rows == LANES
        and samples % LANES == 0
    )


def solution(mesh):
    in_specs = (
        P(("mid", "off"), None),
        P(),
        P("mid", None, None),
        P(None, ("mid", "off")),
        P(None, ("mid", "off")),
        P(("mid", "off")),
        P(("mid", "off")),
    )
    out_specs = (P("mid", "off", None), P("mid", "off", None))

    def shards(traces, kernels, send_list, *lists):
        fits = fits_by_bin(
            mesh.shape["mid"], mesh.shape["off"], send_list.shape[2], *traces.shape
        )
        form = shards_by_bin if fits else shards_by_tile
        return form(traces, kernels, send_list, *lists)

    return jax.shard_map(
        shards, mesh=mesh, in_specs=in_specs, out_specs=out_specs, check_vma=False
    )
```

```python
import functools

import jax
import jax.numpy as jnp
from jax import lax
from jax.experimental import pallas as pl
from jax.experimental.pallas import tpu as pltpu
from jax.sharding import PartitionSpec as P

NOFF = 64
PATTERNS = 8
REACH = 2
APER = 8
ITERS = 2
CELLS = 8
KEYS = PATTERNS * CELLS
EARLY = 3
ROOM = 32
LANES = 128
TOGETHER = LANES // ROOM


smooth_weight = 2.0


def padded_2(x, sides, width):
    for axis, dim in sides:
        peers, length = (lax.axis_size(axis), x.shape[dim])
        up = [(i, (i + 1) % peers) for i in range(peers - 1)]
        down = [(j, i) for i, j in up]
        last = lax.slice_in_dim(x, length - width, length, axis=dim)
        first = lax.slice_in_dim(x, 0, width, axis=dim)
        before = lax.ppermute(last, axis, up)
        after = lax.ppermute(first, axis, down)
        x = jnp.concatenate([before, x, after], axis=dim)
    return x


def from_behind(x, axis, by):
    peers = lax.axis_size(axis)
    pairs = [(i, i + by) for i in range(peers) if 0 <= i + by < peers]
    return lax.ppermute(x, axis, pairs)


def direction_shift(course):
    return (course // 2 + 1) * (1 - 2 * (course % 2))


def offset_laplace(padded):
    return smooth_weight * (2.0 * padded[:, 1:-1] - padded[:, :-2] - padded[:, 2:])


def smoothing(field):
    padded = padded_2(field, (("off", 1),), 1)
    smoothed = offset_laplace(padded)
    return smoothed


def deliver(outgoing):
    arrived = [None] * (2 * REACH)
    for course in range(2 * REACH):
        arrived[course] = from_behind(outgoing[course], "mid", direction_shift(course))
    return arrived


def give_back(returning):
    landed = [None] * (2 * REACH)
    for course in range(2 * REACH):
        landed[course] = from_behind(returning[course], "mid", -direction_shift(course))
    return landed


def shards_by_tile(
    traces, kernels, send_list, aper_slot, aper_pattern, trace_bin, trace_count
):
    off_dev = NOFF // lax.axis_size("off")
    trace_rows = traces.shape[0]
    samples = traces.shape[1]
    chosen_cells = send_list[0]
    send_count = chosen_cells.shape[1]
    slot_count = CELLS + 2 * REACH * send_count
    live_mask = jnp.arange(APER, dtype=jnp.int32)[:, None] < trace_count[None, :]
    row_index = (aper_slot * off_dev + trace_bin[None, :]).reshape(-1)
    pattern_ids = jnp.arange(PATTERNS, dtype=jnp.int32)[:, None, None]
    chooser = ((aper_pattern[None] == pattern_ids) & live_mask[None]).astype(
        jnp.bfloat16
    )
    pick_rows = (
        aper_pattern * trace_rows + jnp.arange(trace_rows, dtype=jnp.int32)[None, :]
    ).reshape(-1)
    live_column = live_mask.reshape(-1, 1).astype(jnp.float32)

    def forward(field_bf):
        outgoing = [field_bf[chosen_cells[course]] for course in range(2 * REACH)]
        arrived = deliver(outgoing)
        slot_rows = jnp.concatenate([field_bf] + arrived, 0).reshape(-1, samples)
        blocks = slot_rows[row_index].reshape(APER, trace_rows, samples)
        pattern_sums = jnp.einsum(
            "pjt,jtn->ptn", chooser, blocks, preferred_element_type=jnp.float32
        ).astype(jnp.bfloat16)
        return jnp.einsum(
            "ptn,pnm->tm", pattern_sums, kernels, preferred_element_type=jnp.float32
        )

    def adjoint(values_bf):
        spread = jnp.einsum(
            "tm,pnm->ptn", values_bf, kernels, preferred_element_type=jnp.float32
        ).reshape(-1, samples)
        entries = spread[pick_rows] * live_column
        slot_sums = (
            jnp.zeros((slot_count * off_dev, samples), jnp.float32)
            .at[row_index]
            .add(entries)
        )
        slot_sums = slot_sums.reshape(slot_count, off_dev, samples)
        returning = [
            slot_sums[CELLS + course * send_count : CELLS + (course + 1) * send_count]
            for course in range(2 * REACH)
        ]
        landed = give_back(returning)
        accumulated = slot_sums[:CELLS]
        for course in range(2 * REACH):
            accumulated = accumulated.at[chosen_cells[course]].add(landed[course])
        return accumulated

    def global_total(value):
        return lax.psum(value, ("mid", "off"))

    residual = adjoint(traces)
    direction = residual
    solution = jnp.zeros_like(residual)
    norm_now = global_total(jnp.sum(residual * residual))
    for iteration in range(ITERS):
        applied = adjoint(
            forward(direction.astype(jnp.bfloat16)).astype(jnp.bfloat16)
        ) + smoothing(direction)
        step_size = norm_now / global_total(jnp.sum(direction * applied))
        solution = solution + step_size * direction
        residual = residual - step_size * applied
        if iteration + 1 < ITERS:
            norm_next = global_total(jnp.sum(residual * residual))
            direction = residual + norm_next / norm_now * direction
            norm_now = norm_next
    return (solution, residual)


def path_rank(m, tiles):
    return m ^ ((m >> 1) & 1) if tiles % 4 == 0 else m


def turns(peers):
    near, far = range(1, peers // 2), range(peers // 2, peers)
    even = [i for pair in zip(far, near) for i in pair]
    odd = [i for pair in zip(near, far) for i in pair]
    return [(0, 0), *zip(even, odd), (peers - 1, peers - 1)]


def partners(peers):
    odd, place = flipped(), lax.axis_index("mid")
    return [place ^ jnp.where(odd, j, i) for i, j in turns(peers)]


def lay_out(chunks_ref, out_refs):
    for partner, out_ref in zip(partners(len(out_refs)), out_refs):
        out_ref[...] = chunks_ref[partner]


def gather_in(landed_refs, chunks_ref):
    for partner, landed_ref in zip(partners(len(landed_refs)), landed_refs):
        chunks_ref[partner] = landed_ref[...]


def swapped(chunks):
    peers, offs = len(chunks), lax.axis_size("off")
    return list(chunks[:1]) + [
        lax.ppermute(
            chunk,
            ("mid", "off"),
            [
                (m * offs + o, (m ^ turn[o % 2]) * offs + o)
                for m in range(peers)
                for o in range(offs)
            ],
        )
        for turn, chunk in zip(turns(peers)[1:], chunks[1:])
    ]


def flipped():
    return lax.axis_index("off") % 2 > 0


def own_block(tiles):
    block = path_rank(lax.axis_index("mid"), tiles)
    return jnp.where(flipped(), tiles - 1 - block, block)


def dot_back(rows, kernel):
    return lax.dot_general(
        rows, kernel, (((1,), (1,)), ((), ())), preferred_element_type=jnp.float32
    )


SLOT, PATTERN, WITHIN, COUNT, FLAG = 0, APER, 4, 5, 6


def share_kernel(
    tiles, bins, room, sends_arg, slot_arg, pattern_arg, bin_arg, count_arg, traces_arg,
    kernels_arg, out_ref, kernels_ref, sends_ref, slot_ref, pattern_ref, bin_ref, count_ref, traces_ref,
    staged, arrived,
):
    rows, samples = traces_ref.shape
    stages = [
        pltpu.make_async_copy(arg, ref, staged.at[i])
        for i, (arg, ref) in enumerate(
            [
                (bin_arg, bin_ref),
                (slot_arg, slot_ref),
                (pattern_arg, pattern_ref),
                (count_arg, count_ref),
                (sends_arg, sends_ref),
                (traces_arg, traces_ref),
            ]
        )
    ]
    kernels = pltpu.make_async_copy(
        kernels_arg.at[:EARLY], kernels_ref, arrived
    )
    for stage in stages + [kernels]:
        stage.start()
    index = lax.broadcasted_iota(jnp.int32, (tiles, rows), 0)
    earlier = lax.broadcasted_iota(jnp.int32, (rows, rows), 0) < (
        lax.broadcasted_iota(jnp.int32, (rows, rows), 1)
    )
    earlier = jnp.where(earlier, 1.0, 0.0).astype(jnp.bfloat16)
    stages[0].wait()
    offset_bin = bin_ref[...]
    block = lax.div(offset_bin, bins)
    within = offset_bin - block * bins
    chunk = path_rank(jnp.where(flipped(), tiles - 1 - block, block), tiles)
    belongs = jnp.where(index == chunk, 1.0, 0.0)
    rank = jnp.dot(
        belongs.astype(jnp.bfloat16), earlier, preferred_element_type=jnp.float32
    )
    rank = jnp.sum(rank * belongs, 0, keepdims=True).astype(jnp.int32)
    full = jnp.max(rank, axis=1, keepdims=True) >= room
    target = jnp.where(rank < room, chunk * room + rank, -1)
    picks = lax.broadcasted_iota(jnp.int32, (tiles * room, rows), 0) == target
    picks = jnp.where(picks, 1.0, 0.0).astype(jnp.bfloat16)
    place = lax.axis_index("mid")
    lane = lax.broadcasted_iota(jnp.int32, (1, LANES), 1)
    target = chunk * LANES + lax.rem(place, TOGETHER) * room + rank
    chosen = lax.broadcasted_iota(jnp.int32, (tiles * LANES, rows), 0) == (
        jnp.where(rank < room, target, -1)
    )
    chosen = jnp.where(chosen, 1.0, 0.0).astype(jnp.bfloat16)
    for stage in stages[1:5]:
        stage.wait()
    lists = jnp.concatenate(
        [
            slot_ref[...].astype(jnp.float32),
            pattern_ref[...].astype(jnp.float32),
            jnp.zeros((WITHIN, rows), jnp.float32),
            within.astype(jnp.float32),
            count_ref[...].astype(jnp.float32),
            jnp.zeros((APER - COUNT - 1, rows), jnp.float32),
        ],
        0,
    ).astype(jnp.bfloat16)
    lists = dot_back(lists, chosen)
    _, courses, send = sends_ref.shape
    line = lax.broadcasted_iota(jnp.int32, (2 * APER, LANES), 0)
    sent = jnp.zeros((2 * APER, LANES), jnp.int32)
    for course in range(courses):
        reader = lax.rem(place + direction_shift(course) + TOGETHER, TOGETHER)
        here = lax.div(lane, room) == reader
        for m in range(send):
            value = jnp.where(here, sends_ref[0, course, m], 0)
            sent += jnp.where(line == sent_row(course, send) + m, value, 0)
    past = lax.div(lane, room) == lax.rem(place + 1, TOGETHER)
    sent += jnp.where(past & (line == FLAG) & full, 1, 0)
    sent = sent.astype(jnp.float32)
    pieces = samples // LANES
    for m in range(tiles):
        own = lists[:, m * LANES : (m + 1) * LANES]
        moved = pltpu.roll(own[2 * APER :], room, 1)
        out_ref[m, pieces * room :] = (
            own[: 2 * APER] + jnp.concatenate([moved, jnp.zeros_like(moved)], 0) + sent
        ).astype(jnp.bfloat16)
    stages[5].wait()
    picked = jnp.dot(picks, traces_ref[...], preferred_element_type=jnp.float32)
    picked = picked.reshape(tiles, room, samples).astype(jnp.bfloat16)
    for i in range(pieces):
        out_ref[:, i * room : (i + 1) * room] = picked[:, :, i * LANES : (i + 1) * LANES]
    kernels.wait()


def sent_row(course, send):
    return send if course == 3 else 0


def fill_picks(tiles, bins, send, landed_ref, picks_ref):
    flags = 0
    keys = lax.broadcasted_iota(jnp.int32, (KEYS, LANES), 0)
    member = lax.div(lax.broadcasted_iota(jnp.int32, (1, LANES), 1), ROOM)
    blocks = [
        landed_ref[tile, -2 * APER :].astype(jnp.float32).astype(jnp.int32)
        for tile in range(tiles)
    ]
    for group in range(tiles // TOGETHER):
        readers = range(group * TOGETHER, (group + 1) * TOGETHER)
        lists, moved = 0, 0
        for tile in readers:
            lists += jnp.where(member == tile % TOGETHER, blocks[tile], 0)
            past = member == (tile + 1) % TOGETHER
            moved += jnp.where(past, blocks[tile][:APER], 0)
        moved = pltpu.roll(moved, LANES - ROOM, 1)
        flags += moved[FLAG : FLAG + 1]
        within, count = moved[WITHIN : WITHIN + 1], moved[COUNT : COUNT + 1]
        wanted = []
        for region in range(2 * REACH + 1):
            course = region - 1
            shift = direction_shift(course) if region else 0
            owners = [tile - shift for tile in readers if 0 <= tile - shift < tiles]
            sent = 0
            for owner in owners if region else ():
                row = sent_row(course, send)
                values = blocks[owner][row : row + send]
                sent += jnp.where(member == (owner + shift) % TOGETHER, values, 0)
            for entry in range(region, APER, 2 * REACH + 1):
                cell = lists[SLOT + entry : SLOT + entry + 1]
                if region:
                    place = cell - (CELLS + course * send)
                    cell = sent[:1]
                    for other in range(1, send):
                        cell = jnp.where(place == other, sent[other : other + 1], cell)
                pattern = lists[PATTERN + entry : PATTERN + entry + 1]
                key = jnp.where(count > entry, pattern * CELLS + cell, -1)
                for owner in owners:
                    there = member == (owner + shift) % TOGETHER
                    wanted.append((owner, jnp.where(there, key, -1)))
        for tile in range(tiles):
            for b in range(bins):
                total = jnp.zeros((KEYS, LANES), jnp.float32)
                for owner, key in wanted:
                    if owner == tile:
                        hit = keys == jnp.where(within == b, key, -1)
                        total += jnp.where(hit, 1.0, 0.0)
                picks_ref[b, :, tile, :, group * LANES : (group + 1) * LANES] = (
                    total.reshape(PATTERNS, CELLS, LANES)
                )
    return flags.astype(jnp.float32)


def two_parts(x):
    high = x.astype(jnp.bfloat16)
    low = (x - high.astype(jnp.float32)).astype(jnp.bfloat16)
    return jnp.concatenate([high, low], 0)


def store_parts(parts_ref, b, x):
    shape = (PATTERNS, *parts_ref.shape[3:])
    high = x.astype(jnp.bfloat16)
    parts_ref[:, 0, b] = high.reshape(shape)
    low = (x - high.astype(jnp.float32)).astype(jnp.bfloat16)
    parts_ref[:, 1, b] = low.reshape(shape)


def kernel_of(kernels, p):
    lower_ref, upper_ref = kernels
    return lower_ref[p] if p < EARLY else upper_ref[p - EARLY]


def back_projected(kernels, parts_ref):
    _, _, bins, side, samples = parts_ref.shape
    rows = bins * side
    both = jnp.zeros((2 * rows, samples), jnp.float32)
    for p in range(PATTERNS):
        both += dot_back(
            parts_ref[p].reshape(2 * rows, samples), kernel_of(kernels, p)
        )
    return both[:rows] + both[rows:]


def project(field, kernels, rows_ref):
    bins, _, side, samples = rows_ref.shape
    rows = bins * side
    for p in range(PATTERNS):
        u = jnp.dot(field, kernel_of(kernels, p), preferred_element_type=jnp.float32)
        u = u[:rows] + u[rows:] if field.shape[0] > rows else u
        rows_ref[:, p] = u.astype(jnp.bfloat16).reshape(bins, side, samples)


def mixed(gram_ref, rows_ref, b):
    _, _, side, samples = rows_ref.shape
    return jnp.dot(
        gram_ref[b],
        rows_ref[b].reshape(PATTERNS * side, samples),
        preferred_element_type=jnp.float32,
    )


def smoothed(field, before, after):
    side = before.shape[0]
    lower = jnp.concatenate([before, field[:-side]], 0)
    upper = jnp.concatenate([field[side:], after], 0)
    return smooth_weight * (2.0 * field - lower - upper)


def first_kernel(
    tiles, bins, send, landed_ref, lower_ref, kernels_arg,
    start_ref, local_ref, gram_ref, first_swap_ref, second_swap_ref, full_ref, upper_ref,
    picks_ref, rows_ref, parts_ref, arrived,
):
    copies = [
        pltpu.make_async_copy(kernels_arg.at[EARLY + p], upper_ref.at[p], arrived.at[p])
        for p in range(PATTERNS - EARLY)
    ]
    for copy in copies:
        copy.start()
    kernels = (lower_ref, upper_ref)
    side = tiles * CELLS
    samples = start_ref.shape[1]
    flags = total(fill_picks(tiles, bins, send, landed_ref, picks_ref))
    full_ref[...] = jnp.broadcast_to(flags, full_ref.shape)
    traces = jnp.concatenate(
        [
            landed_ref[:, i * ROOM : (i + 1) * ROOM].reshape(-1, LANES)
            for i in range(samples // LANES)
        ],
        1,
    )
    for b in range(bins):
        picks = picks_ref[b].reshape(PATTERNS * side, -1).astype(jnp.bfloat16)
        gram_ref[b] = dot_back(picks, picks).astype(jnp.bfloat16)
        sums = jnp.dot(picks, traces, preferred_element_type=jnp.float32)
        parts_ref[:, 0, b] = sums.astype(jnp.bfloat16).reshape(PATTERNS, side, samples)
    start = jnp.zeros((bins * side, samples), jnp.float32)
    for p in range(PATTERNS):
        if p >= EARLY:
            copies[p - EARLY].wait()
        rows = parts_ref[p, 0].reshape(bins * side, samples)
        start += dot_back(rows, kernel_of(kernels, p))
    start = start.astype(jnp.bfloat16)
    start_ref[...] = start
    field = start.astype(jnp.float32)
    nothing = jnp.zeros((side, samples), jnp.float32)
    project(start, kernels, rows_ref)
    for b in range(bins):
        store_parts(parts_ref, b, mixed(gram_ref, rows_ref, b))
    local = back_projected(kernels, parts_ref) + smoothed(field, nothing, nothing)
    local_ref[...] = local
    local = local.astype(jnp.bfloat16)
    odd = own_block(tiles) % 2 > 0
    for out_ref, to_after in ((first_swap_ref, ~odd), (second_swap_ref, odd)):
        out_ref[:side] = jnp.where(to_after, start[-side:], start[:side])
        out_ref[side:] = jnp.where(to_after, local[-side:], local[:side])


FULL, STEP, GROW = 4, 5, 6


def ahead_kernel(local_ref, gram_ref, lower_ref, upper_ref, rows_ref, mixed_ref):
    project(two_parts(local_ref[...]), (lower_ref, upper_ref), rows_ref)
    for b in range(rows_ref.shape[0]):
        mixed_ref[b] = mixed(gram_ref, rows_ref, b)


def second_kernel(
    tiles, offs, start_ref, local_ref, gram_ref, lower_ref, upper_ref, first_swap_ref,
    second_swap_ref, full_ref, ahead_ref, mixed_ref,
    once_ref, smooth_ref, both_ref, sums_ref, rows_ref,
):
    bins, _, side, samples = rows_ref.shape
    start = start_ref[...].astype(jnp.float32)
    place = lax.axis_index("off") * tiles + own_block(tiles)
    ends = [place > 0, place < offs * tiles - 1]
    odd = own_block(tiles) % 2 > 0
    first = first_swap_ref[...].astype(jnp.float32)
    second = second_swap_ref[...].astype(jnp.float32)
    edges = [jnp.where(odd, first, second), jnp.where(odd, second, first)]
    beyond, outer = [], []
    for end, (edge, own) in enumerate(zip(edges, (start[:side], start[-side:]))):
        there = jnp.where(ends[end], smooth_weight, 0.0)
        beyond.append(-smooth_weight * edge[:side])
        outer.append(edge[side:] - there * own)
    inner = [jnp.zeros(((bins - 2) * side, samples), jnp.float32)] if bins > 2 else []
    beyond = jnp.concatenate([beyond[0], *inner, beyond[1]], 0)
    once = local_ref[...] + beyond
    once_ref[...] = once
    smooth = smoothed(once, outer[0], outer[1])
    smooth_ref[...] = smooth
    project(beyond.astype(jnp.bfloat16), (lower_ref, upper_ref), rows_ref)
    square = 0.0
    for b in range(bins):
        both = mixed_ref[b] + mixed(gram_ref, rows_ref, b)
        both_ref[b] = both
        rows = ahead_ref[b].astype(jnp.float32) + rows_ref[b].astype(jnp.float32)
        square += total(rows.reshape(both.shape) * both)
    products = [
        total(start * start),
        total(start * once),
        total(once * once),
        total(once * smooth) + square,
    ]
    lane = lax.broadcasted_iota(jnp.int32, (1, LANES), 1)
    line = jnp.where(lane == FULL, full_ref[:1], 0.0)
    for i, product in enumerate(products):
        line = jnp.where(lane == i, product, line)
    sums_ref[...] = jnp.broadcast_to(line, sums_ref.shape)


def last_kernel(both_ref, lower_ref, upper_ref, out_ref):
    rows, samples = out_ref.shape
    bins = both_ref.shape[0]
    side = rows // bins
    out = jnp.zeros((2 * rows, samples), jnp.float32)
    for p in range(PATTERNS):
        z = both_ref[:, p * side : (p + 1) * side].reshape(rows, samples)
        out += dot_back(two_parts(z), kernel_of((lower_ref, upper_ref), p))
    out_ref[...] = out[:rows] + out[rows:]


def pack_kernel(sums_ref, start_ref, once_ref, smooth_ref, normal_ref, *refs):
    *out_refs, out_ref = refs
    tiles = len(out_refs)
    ss, so, oo = (sums_ref[:1, i : i + 1] for i in range(3))
    step, grow = own_scales(ss, so, oo)
    start, once = start_ref[...].astype(jnp.float32), once_ref[...]
    twice = normal_ref[...] + smooth_ref[...]
    row = 0
    for field in (start, start - step * once, grow * once - step * twice):
        samples = field.shape[1]
        field = field.reshape(-1, tiles, CELLS, samples)
        size = field.shape[0] * CELLS
        for i in range(0, samples, LANES):
            for tile in range(tiles):
                piece = field[:, tile, :, i : i + LANES].reshape(size, LANES)
                out_ref[tile, row : row + size] = piece.astype(jnp.bfloat16)
            row += size
    lane = lax.broadcasted_iota(jnp.int32, (1, LANES), 1)
    rest = jnp.where(lane == STEP, step, sums_ref[:1])
    rest = jnp.where(lane == GROW, grow, rest)
    line = lax.broadcasted_iota(jnp.int32, (16, LANES), 0)
    parts = jnp.zeros((16, LANES), jnp.float32)
    for i in range(3):
        part = rest.astype(jnp.bfloat16).astype(jnp.float32)
        rest = rest - part
        parts = jnp.where(line == i, part, parts)
    for tile in range(tiles):
        out_ref[tile, row:] = parts.astype(jnp.bfloat16)
    lay_out(out_ref, out_refs)


def total(x):
    return jnp.sum(jnp.sum(x, 0, keepdims=True), 1, keepdims=True)


def own_scales(ss, so, oo):
    step = ss / so
    step = jnp.where(step > 0.0, jnp.clip(step, 1e-8, 1e3), 1.0)
    grow = step * step * oo / ss
    return step, jnp.where(grow > 0.0, jnp.clip(grow, 0.0, 1e3), 1.0)


def place_kernel(bins, *refs):
    *landed_refs, solution_ref, residual_ref, landed_ref = refs
    gather_in(landed_refs, landed_ref)
    tiles, length, _ = landed_ref.shape
    size = bins * CELLS
    samples = solution_ref.shape[2]
    pieces = samples // LANES

    def line_of(source):
        parts = landed_ref[source, length - 16 :].astype(jnp.float32)
        return jnp.sum(parts, 0, keepdims=True)

    def vector(source, i):
        part = [
            landed_ref[source, (i * pieces + j) * size : (i * pieces + j + 1) * size]
            for j in range(pieces)
        ]
        return jnp.concatenate(part, 1).astype(jnp.float32)

    sums = sum(line_of(tile) for tile in range(tiles))
    ss, so, oo, ot = (sums[:, i : i + 1] for i in range(4))
    step_0 = ss / so
    norm_1 = step_0 * step_0 * oo - ss
    grow = 1.0 + norm_1 / ss
    step_1 = norm_1 / (grow * grow * so - 2.0 * step_0 * grow * oo + step_0 * step_0 * ot)
    near = step_0 + step_1 * grow
    far = step_1 * step_0
    fields = [[], []]
    for block in range(tiles):
        source = jnp.where(
            flipped(), path_rank(tiles - 1 - block, tiles), path_rank(block, tiles)
        )
        line = line_of(source)
        inverse = 1.0 / line[:, STEP : STEP + 1]
        there = line[:, GROW : GROW + 1]
        start, first, second = (vector(source, i) for i in range(3))
        far_once = far * inverse
        near_once = near * inverse - far_once * there * inverse
        solution = (near - far_once) * start + far_once * first
        residual = (1.0 - near_once) * start + near_once * first - far_once * second
        fields[0].append(solution.reshape(bins, CELLS, samples))
        fields[1].append(residual.reshape(bins, CELLS, samples))
    solution_ref[...] = jnp.swapaxes(jnp.concatenate(fields[0], 0), 0, 1)
    residual_ref[...] = jnp.swapaxes(jnp.concatenate(fields[1], 0), 0, 1)


def copy_kernel(*refs):
    *refs, arrived = refs
    half = len(refs) // 2
    copies = [
        pltpu.make_async_copy(refs[i], refs[half + i], arrived.at[i]) for i in range(half)
    ]
    for copy in copies:
        copy.start()
    for copy in copies:
        copy.wait()


VMEM = pl.BlockSpec(memory_space=pltpu.VMEM)
HBM = pl.BlockSpec(memory_space=pltpu.HBM)


def local_call(kernel, name, in_specs, out_shape, scratch=(), out_specs=None, cost=0):
    return pl.pallas_call(
        kernel,
        out_shape=out_shape,
        in_specs=in_specs,
        out_specs=out_specs or jax.tree.map(lambda _: VMEM, out_shape),
        scratch_shapes=list(scratch),
        cost_estimate=pl.CostEstimate(
            flops=cost, bytes_accessed=cost // 256, transcendentals=0
        )
        if cost
        else None,
        compiler_params=pltpu.CompilerParams(vmem_limit_bytes=32 * 1024 * 1024),
        name=name,
    )


def shards_by_bin(
    traces, kernels, send_list, aper_slot, aper_pattern, trace_bin, trace_count
):
    tiles, offs = lax.axis_size("mid"), lax.axis_size("off")
    bins = NOFF // offs // tiles
    trace_rows, samples = traces.shape
    send = send_list.shape[2]
    rows = bins * tiles * CELLS
    side = tiles * CELLS
    sums = bins * (CELLS + 2 * REACH * send)

    def array(*shape, dtype=jnp.float32):
        return jax.ShapeDtypeStruct(shape, dtype)

    bf16 = functools.partial(array, dtype=jnp.bfloat16)
    in_hbm = functools.partial(
        pltpu.with_memory_space_constraint, memory_space=pltpu.HBM
    )
    lists = (send_list, aper_slot, aper_pattern, trace_bin, trace_count)
    early = bf16(EARLY, samples, samples)
    shared, lower = local_call(
        functools.partial(share_kernel, tiles, bins, ROOM),
        "share",
        [HBM] * 7,
        (bf16(tiles, samples // LANES * ROOM + 2 * APER, LANES), early),
        [
            pltpu.SMEM(send_list.shape, jnp.int32),
            pltpu.VMEM(aper_slot.shape, jnp.int32),
            pltpu.VMEM(aper_pattern.shape, jnp.int32),
            pltpu.VMEM((1, trace_rows), jnp.int32),
            pltpu.VMEM((1, trace_rows), jnp.int32),
            pltpu.VMEM(traces.shape, jnp.bfloat16),
            pltpu.SemaphoreType.DMA((6,)),
            pltpu.SemaphoreType.DMA,
        ],
    )(
        in_hbm(send_list),
        in_hbm(aper_slot),
        in_hbm(aper_pattern),
        in_hbm(trace_bin[None]),
        in_hbm(trace_count[None]),
        in_hbm(traces),
        in_hbm(kernels),
    )
    landed = lax.all_to_all(shared, "mid", 0, 0)
    pattern_rows = pltpu.VMEM((bins, PATTERNS, side, samples), jnp.bfloat16)
    parts_type = bf16(PATTERNS, 2, bins, side, samples)
    start, local, gram, *swaps, full, upper = local_call(
        functools.partial(first_kernel, tiles, bins, send),
        "first",
        [VMEM, VMEM, HBM],
        (
            bf16(rows, samples),
            array(rows, samples),
            bf16(bins, tiles * KEYS, tiles * KEYS),
            bf16(2 * side, samples),
            bf16(2 * side, samples),
            array(8, LANES),
            bf16(PATTERNS - EARLY, samples, samples),
        ),
        [
            pltpu.VMEM((bins, PATTERNS, tiles, CELLS, tiles * ROOM), jnp.float32),
            pattern_rows,
            pltpu.VMEM(parts_type.shape, parts_type.dtype),
            pltpu.SemaphoreType.DMA((PATTERNS - EARLY,)),
        ],
    )(landed, lower, in_hbm(kernels))

    path = [path_rank(m, tiles) for m in range(tiles)]
    chain = [m * offs + o for o in range(offs) for m in (path[::-1] if o % 2 else path)]
    swaps = [
        lax.ppermute(
            x,
            ("mid", "off"),
            [
                pair
                for i, j in zip(chain[first:-1:2], chain[first + 1 :: 2])
                for pair in ((i, j), (j, i))
            ],
        )
        for first, x in enumerate(swaps)
    ]

    flops = 2 * rows * PATTERNS * samples * samples
    ahead, mixed_ahead = local_call(
        ahead_kernel,
        "ahead",
        [VMEM] * 4,
        (bf16(*pattern_rows.shape), array(bins, PATTERNS * side, samples)),
        cost=3 * flops,
    )(local, gram, lower, upper)
    field = array(rows, samples)
    once, smooth, parts, products = local_call(
        functools.partial(second_kernel, tiles, offs),
        "second",
        [VMEM] * 10,
        (field, field, array(bins, PATTERNS * side, samples), array(8, LANES)),
        [pattern_rows],
        cost=2 * flops,
    )(start, local, gram, lower, upper, *swaps, full, ahead, mixed_ahead)

    projected = local_call(last_kernel, "last", [VMEM] * 3, field, cost=2 * flops)(
        parts, lower, upper
    )
    addends = [products] + [
        lax.ppermute(products, "off", [(i, i ^ step) for i in range(offs)])
        for step in range(1, offs)
    ]
    while len(addends) > 1:
        addends = [a + b for a, b in zip(addends[::2], addends[1::2])]
    products = addends[0]
    chunk = bf16(samples // LANES * 3 * bins * CELLS + 16, LANES)
    chunks = pltpu.VMEM((tiles, *chunk.shape), chunk.dtype)
    packed = local_call(
        pack_kernel, "pack", [VMEM] * 5, [chunk] * tiles, [chunks]
    )(products, start, once, smooth, projected)
    landed = swapped(packed)

    def again():
        arguments = [in_hbm(x) for x in (traces, kernels, *lists[:3])]
        arguments += [in_hbm(x[None]) for x in lists[3:]]
        *copies, bins_again, count_again = local_call(
            copy_kernel,
            "again",
            [HBM] * len(arguments),
            tuple(array(*x.shape, dtype=x.dtype) for x in arguments),
            [pltpu.SemaphoreType.DMA((len(arguments),))],
            out_specs=(HBM,) * len(arguments),
        )(*arguments)
        return *copies, bins_again[0], count_again[0]

    def placed():
        out_type = pltpu.HBM((CELLS, bins * tiles, samples), jnp.float32)
        return local_call(
            functools.partial(place_kernel, bins),
            "place",
            [VMEM] * tiles,
            (out_type, out_type),
            [chunks],
            out_specs=(VMEM, VMEM),
        )(*landed)

    return lax.cond(
        products[0, FULL] > 0.0, lambda: shards_by_tile(*again()), placed
    )


def fits_by_bin(tiles, offs, send, trace_rows, samples):
    return (
        (NOFF // offs) % (2 * tiles) == 0
        and offs & (offs - 1) == 0
        and tiles & (tiles - 1) == 0
        and tiles % TOGETHER == 0
        and send == WITHIN
        and trace_rows == LANES
        and samples % LANES == 0
    )


def solution(mesh):
    in_specs = (
        P(("mid", "off"), None),
        P(),
        P("mid", None, None),
        P(None, ("mid", "off")),
        P(None, ("mid", "off")),
        P(("mid", "off")),
        P(("mid", "off")),
    )
    out_specs = (P("mid", "off", None), P("mid", "off", None))

    def shards(traces, kernels, send_list, *lists):
        fits = fits_by_bin(
            mesh.shape["mid"], mesh.shape["off"], send_list.shape[2], *traces.shape
        )
        form = shards_by_bin if fits else shards_by_tile
        return form(traces, kernels, send_list, *lists)

    return jax.shard_map(
        shards, mesh=mesh, in_specs=in_specs, out_specs=out_specs, check_vma=False
    )
```

```python
import functools

import jax
import jax.numpy as jnp
from jax import lax
from jax.experimental import pallas as pl
from jax.experimental.pallas import tpu as pltpu
from jax.sharding import PartitionSpec as P

NOFF = 64
PATTERNS = 8
REACH = 2
APER = 8
ITERS = 2
CELLS = 8
KEYS = PATTERNS * CELLS
EARLY = 3
ROOM = 32
LANES = 128
TOGETHER = LANES // ROOM


smooth_weight = 2.0


def padded_2(x, sides, width):
    for axis, dim in sides:
        peers, length = (lax.axis_size(axis), x.shape[dim])
        up = [(i, (i + 1) % peers) for i in range(peers - 1)]
        down = [(j, i) for i, j in up]
        last = lax.slice_in_dim(x, length - width, length, axis=dim)
        first = lax.slice_in_dim(x, 0, width, axis=dim)
        before = lax.ppermute(last, axis, up)
        after = lax.ppermute(first, axis, down)
        x = jnp.concatenate([before, x, after], axis=dim)
    return x


def from_behind(x, axis, by):
    peers = lax.axis_size(axis)
    pairs = [(i, i + by) for i in range(peers) if 0 <= i + by < peers]
    return lax.ppermute(x, axis, pairs)


def direction_shift(course):
    return (course // 2 + 1) * (1 - 2 * (course % 2))


def offset_laplace(padded):
    return smooth_weight * (2.0 * padded[:, 1:-1] - padded[:, :-2] - padded[:, 2:])


def smoothing(field):
    padded = padded_2(field, (("off", 1),), 1)
    smoothed = offset_laplace(padded)
    return smoothed


def deliver(outgoing):
    arrived = [None] * (2 * REACH)
    for course in range(2 * REACH):
        arrived[course] = from_behind(outgoing[course], "mid", direction_shift(course))
    return arrived


def give_back(returning):
    landed = [None] * (2 * REACH)
    for course in range(2 * REACH):
        landed[course] = from_behind(returning[course], "mid", -direction_shift(course))
    return landed


def shards_by_tile(
    traces, kernels, send_list, aper_slot, aper_pattern, trace_bin, trace_count
):
    off_dev = NOFF // lax.axis_size("off")
    trace_rows = traces.shape[0]
    samples = traces.shape[1]
    chosen_cells = send_list[0]
    send_count = chosen_cells.shape[1]
    slot_count = CELLS + 2 * REACH * send_count
    live_mask = jnp.arange(APER, dtype=jnp.int32)[:, None] < trace_count[None, :]
    row_index = (aper_slot * off_dev + trace_bin[None, :]).reshape(-1)
    pattern_ids = jnp.arange(PATTERNS, dtype=jnp.int32)[:, None, None]
    chooser = ((aper_pattern[None] == pattern_ids) & live_mask[None]).astype(
        jnp.bfloat16
    )
    pick_rows = (
        aper_pattern * trace_rows + jnp.arange(trace_rows, dtype=jnp.int32)[None, :]
    ).reshape(-1)
    live_column = live_mask.reshape(-1, 1).astype(jnp.float32)

    def forward(field_bf):
        outgoing = [field_bf[chosen_cells[course]] for course in range(2 * REACH)]
        arrived = deliver(outgoing)
        slot_rows = jnp.concatenate([field_bf] + arrived, 0).reshape(-1, samples)
        blocks = slot_rows[row_index].reshape(APER, trace_rows, samples)
        pattern_sums = jnp.einsum(
            "pjt,jtn->ptn", chooser, blocks, preferred_element_type=jnp.float32
        ).astype(jnp.bfloat16)
        return jnp.einsum(
            "ptn,pnm->tm", pattern_sums, kernels, preferred_element_type=jnp.float32
        )

    def adjoint(values_bf):
        spread = jnp.einsum(
            "tm,pnm->ptn", values_bf, kernels, preferred_element_type=jnp.float32
        ).reshape(-1, samples)
        entries = spread[pick_rows] * live_column
        slot_sums = (
            jnp.zeros((slot_count * off_dev, samples), jnp.float32)
            .at[row_index]
            .add(entries)
        )
        slot_sums = slot_sums.reshape(slot_count, off_dev, samples)
        returning = [
            slot_sums[CELLS + course * send_count : CELLS + (course + 1) * send_count]
            for course in range(2 * REACH)
        ]
        landed = give_back(returning)
        accumulated = slot_sums[:CELLS]
        for course in range(2 * REACH):
            accumulated = accumulated.at[chosen_cells[course]].add(landed[course])
        return accumulated

    def global_total(value):
        return lax.psum(value, ("mid", "off"))

    residual = adjoint(traces)
    direction = residual
    solution = jnp.zeros_like(residual)
    norm_now = global_total(jnp.sum(residual * residual))
    for iteration in range(ITERS):
        applied = adjoint(
            forward(direction.astype(jnp.bfloat16)).astype(jnp.bfloat16)
        ) + smoothing(direction)
        step_size = norm_now / global_total(jnp.sum(direction * applied))
        solution = solution + step_size * direction
        residual = residual - step_size * applied
        if iteration + 1 < ITERS:
            norm_next = global_total(jnp.sum(residual * residual))
            direction = residual + norm_next / norm_now * direction
            norm_now = norm_next
    return (solution, residual)


def path_rank(m, tiles):
    return m ^ ((m >> 1) & 1) if tiles % 4 == 0 else m


def turns(peers):
    near, far = range(1, peers // 2), range(peers // 2, peers)
    even = [i for pair in zip(far, near) for i in pair]
    odd = [i for pair in zip(near, far) for i in pair]
    return [(0, 0), *zip(even, odd), (peers - 1, peers - 1)]


def partners(peers):
    odd, place = flipped(), lax.axis_index("mid")
    return [place ^ jnp.where(odd, j, i) for i, j in turns(peers)]


def lay_out(chunks_ref, out_refs):
    for partner, out_ref in zip(partners(len(out_refs)), out_refs):
        out_ref[...] = chunks_ref[partner]


def gather_in(landed_refs, chunks_ref):
    for partner, landed_ref in zip(partners(len(landed_refs)), landed_refs):
        chunks_ref[partner] = landed_ref[...]


def swapped(chunks):
    peers, offs = len(chunks), lax.axis_size("off")
    return list(chunks[:1]) + [
        lax.ppermute(
            chunk,
            ("mid", "off"),
            [
                (m * offs + o, (m ^ turn[o % 2]) * offs + o)
                for m in range(peers)
                for o in range(offs)
            ],
        )
        for turn, chunk in zip(turns(peers)[1:], chunks[1:])
    ]


def flipped():
    return lax.axis_index("off") % 2 > 0


def own_block(tiles):
    block = path_rank(lax.axis_index("mid"), tiles)
    return jnp.where(flipped(), tiles - 1 - block, block)


def dot_back(rows, kernel):
    return lax.dot_general(
        rows, kernel, (((1,), (1,)), ((), ())), preferred_element_type=jnp.float32
    )


SLOT, PATTERN, WITHIN, COUNT, FLAG = 0, APER, 4, 5, 6


def share_kernel(
    tiles, bins, room, sends_arg, slot_arg, pattern_arg, bin_arg, count_arg, traces_arg,
    kernels_arg, out_ref, kernels_ref, sends_ref, slot_ref, pattern_ref, bin_ref, count_ref, traces_ref,
    staged, arrived,
):
    rows, samples = traces_ref.shape
    stages = [
        pltpu.make_async_copy(arg, ref, staged.at[i])
        for i, (arg, ref) in enumerate(
            [
                (bin_arg, bin_ref),
                (slot_arg, slot_ref),
                (pattern_arg, pattern_ref),
                (count_arg, count_ref),
                (sends_arg, sends_ref),
                (traces_arg, traces_ref),
            ]
        )
    ]
    kernels = pltpu.make_async_copy(
        kernels_arg.at[:EARLY], kernels_ref, arrived
    )
    for stage in stages + [kernels]:
        stage.start()
    index = lax.broadcasted_iota(jnp.int32, (tiles, rows), 0)
    earlier = lax.broadcasted_iota(jnp.int32, (rows, rows), 0) < (
        lax.broadcasted_iota(jnp.int32, (rows, rows), 1)
    )
    earlier = jnp.where(earlier, 1.0, 0.0).astype(jnp.bfloat16)
    stages[0].wait()
    offset_bin = bin_ref[...]
    block = lax.div(offset_bin, bins)
    within = offset_bin - block * bins
    chunk = path_rank(jnp.where(flipped(), tiles - 1 - block, block), tiles)
    belongs = jnp.where(index == chunk, 1.0, 0.0)
    rank = jnp.dot(
        belongs.astype(jnp.bfloat16), earlier, preferred_element_type=jnp.float32
    )
    rank = jnp.sum(rank * belongs, 0, keepdims=True).astype(jnp.int32)
    full = jnp.max(rank, axis=1, keepdims=True) >= room
    target = jnp.where(rank < room, chunk * room + rank, -1)
    picks = lax.broadcasted_iota(jnp.int32, (tiles * room, rows), 0) == target
    picks = jnp.where(picks, 1.0, 0.0).astype(jnp.bfloat16)
    place = lax.axis_index("mid")
    lane = lax.broadcasted_iota(jnp.int32, (1, LANES), 1)
    for stage in stages[1:5]:
        stage.wait()
    lists = jnp.concatenate(
        [
            slot_ref[...].astype(jnp.float32),
            pattern_ref[...].astype(jnp.float32),
            jnp.zeros((WITHIN, rows), jnp.float32),
            within.astype(jnp.float32),
            count_ref[...].astype(jnp.float32),
            jnp.zeros((APER - COUNT - 1, rows), jnp.float32),
        ],
        0,
    ).astype(jnp.bfloat16)
    lists = dot_back(lists, picks)
    own_lanes = lax.rem(place, TOGETHER)
    member = lax.div(lane, room)
    _, courses, send = sends_ref.shape
    line = lax.broadcasted_iota(jnp.int32, (2 * APER, LANES), 0)
    sent = jnp.zeros((2 * APER, LANES), jnp.int32)
    for course in range(courses):
        reader = lax.rem(place + direction_shift(course) + TOGETHER, TOGETHER)
        here = lax.div(lane, room) == reader
        for m in range(send):
            value = jnp.where(here, sends_ref[0, course, m], 0)
            sent += jnp.where(line == sent_row(course, send) + m, value, 0)
    past = lax.div(lane, room) == lax.rem(place + 1, TOGETHER)
    sent += jnp.where(past & (line == FLAG) & full, 1, 0)
    sent = sent.astype(jnp.float32)
    pieces = samples // LANES
    for m in range(tiles):
        own = lists[:, m // TOGETHER * LANES : (m // TOGETHER + 1) * LANES]
        shift = lax.rem((own_lanes - m % TOGETHER + TOGETHER) * room, LANES)
        own = jnp.where(member == own_lanes, pltpu.roll(own, shift, 1), 0.0)
        moved = pltpu.roll(own[2 * APER :], room, 1)
        out_ref[m, pieces * room :] = (
            own[: 2 * APER] + jnp.concatenate([moved, jnp.zeros_like(moved)], 0) + sent
        ).astype(jnp.bfloat16)
    stages[5].wait()
    picked = jnp.dot(picks, traces_ref[...], preferred_element_type=jnp.float32)
    picked = picked.reshape(tiles, room, samples).astype(jnp.bfloat16)
    for i in range(pieces):
        out_ref[:, i * room : (i + 1) * room] = picked[:, :, i * LANES : (i + 1) * LANES]
    kernels.wait()


def sent_row(course, send):
    return send if course == 3 else 0


def fill_picks(tiles, bins, send, landed_ref, picks_ref):
    flags = 0
    keys = lax.broadcasted_iota(jnp.int32, (KEYS, LANES), 0)
    member = lax.div(lax.broadcasted_iota(jnp.int32, (1, LANES), 1), ROOM)
    blocks = [
        landed_ref[tile, -2 * APER :].astype(jnp.float32).astype(jnp.int32)
        for tile in range(tiles)
    ]
    for group in range(tiles // TOGETHER):
        readers = range(group * TOGETHER, (group + 1) * TOGETHER)
        lists, moved = 0, 0
        for tile in readers:
            lists += jnp.where(member == tile % TOGETHER, blocks[tile], 0)
            past = member == (tile + 1) % TOGETHER
            moved += jnp.where(past, blocks[tile][:APER], 0)
        moved = pltpu.roll(moved, LANES - ROOM, 1)
        flags += moved[FLAG : FLAG + 1]
        within, count = moved[WITHIN : WITHIN + 1], moved[COUNT : COUNT + 1]
        wanted = []
        for region in range(2 * REACH + 1):
            course = region - 1
            shift = direction_shift(course) if region else 0
            owners = [tile - shift for tile in readers if 0 <= tile - shift < tiles]
            sent = 0
            for owner in owners if region else ():
                row = sent_row(course, send)
                values = blocks[owner][row : row + send]
                sent += jnp.where(member == (owner + shift) % TOGETHER, values, 0)
            for entry in range(region, APER, 2 * REACH + 1):
                cell = lists[SLOT + entry : SLOT + entry + 1]
                if region:
                    place = cell - (CELLS + course * send)
                    cell = sent[:1]
                    for other in range(1, send):
                        cell = jnp.where(place == other, sent[other : other + 1], cell)
                pattern = lists[PATTERN + entry : PATTERN + entry + 1]
                key = jnp.where(count > entry, pattern * CELLS + cell, -1)
                for owner in owners:
                    there = member == (owner + shift) % TOGETHER
                    wanted.append((owner, jnp.where(there, key, -1)))
        for tile in range(tiles):
            for b in range(bins):
                total = jnp.zeros((KEYS, LANES), jnp.float32)
                for owner, key in wanted:
                    if owner == tile:
                        hit = keys == jnp.where(within == b, key, -1)
                        total += jnp.where(hit, 1.0, 0.0)
                picks_ref[b, :, tile, :, group * LANES : (group + 1) * LANES] = (
                    total.reshape(PATTERNS, CELLS, LANES)
                )
    return flags.astype(jnp.float32)


def two_parts(x):
    high = x.astype(jnp.bfloat16)
    low = (x - high.astype(jnp.float32)).astype(jnp.bfloat16)
    return jnp.concatenate([high, low], 0)


def store_parts(parts_ref, b, x):
    shape = (PATTERNS, *parts_ref.shape[3:])
    high = x.astype(jnp.bfloat16)
    parts_ref[:, 0, b] = high.reshape(shape)
    low = (x - high.astype(jnp.float32)).astype(jnp.bfloat16)
    parts_ref[:, 1, b] = low.reshape(shape)


def kernel_of(kernels, p):
    lower_ref, upper_ref = kernels
    return lower_ref[p] if p < EARLY else upper_ref[p - EARLY]


def back_projected(kernels, parts_ref):
    _, _, bins, side, samples = parts_ref.shape
    rows = bins * side
    both = jnp.zeros((2 * rows, samples), jnp.float32)
    for p in range(PATTERNS):
        both += dot_back(
            parts_ref[p].reshape(2 * rows, samples), kernel_of(kernels, p)
        )
    return both[:rows] + both[rows:]


def project(field, kernels, rows_ref):
    bins, _, side, samples = rows_ref.shape
    rows = bins * side
    for p in range(PATTERNS):
        u = jnp.dot(field, kernel_of(kernels, p), preferred_element_type=jnp.float32)
        u = u[:rows] + u[rows:] if field.shape[0] > rows else u
        rows_ref[:, p] = u.astype(jnp.bfloat16).reshape(bins, side, samples)


def mixed(gram_ref, rows_ref, b):
    _, _, side, samples = rows_ref.shape
    return jnp.dot(
        gram_ref[b],
        rows_ref[b].reshape(PATTERNS * side, samples),
        preferred_element_type=jnp.float32,
    )


def smoothed(field, before, after):
    side = before.shape[0]
    lower = jnp.concatenate([before, field[:-side]], 0)
    upper = jnp.concatenate([field[side:], after], 0)
    return smooth_weight * (2.0 * field - lower - upper)


def first_kernel(
    tiles, bins, send, landed_ref, lower_ref, kernels_arg,
    start_ref, local_ref, gram_ref, first_swap_ref, second_swap_ref, full_ref, upper_ref,
    picks_ref, rows_ref, parts_ref, arrived,
):
    copies = [
        pltpu.make_async_copy(kernels_arg.at[EARLY + p], upper_ref.at[p], arrived.at[p])
        for p in range(PATTERNS - EARLY)
    ]
    for copy in copies:
        copy.start()
    kernels = (lower_ref, upper_ref)
    side = tiles * CELLS
    samples = start_ref.shape[1]
    flags = total(fill_picks(tiles, bins, send, landed_ref, picks_ref))
    full_ref[...] = jnp.broadcast_to(flags, full_ref.shape)
    traces = jnp.concatenate(
        [
            landed_ref[:, i * ROOM : (i + 1) * ROOM].reshape(-1, LANES)
            for i in range(samples // LANES)
        ],
        1,
    )
    for b in range(bins):
        picks = picks_ref[b].reshape(PATTERNS * side, -1).astype(jnp.bfloat16)
        gram_ref[b] = dot_back(picks, picks).astype(jnp.bfloat16)
        sums = jnp.dot(picks, traces, preferred_element_type=jnp.float32)
        parts_ref[:, 0, b] = sums.astype(jnp.bfloat16).reshape(PATTERNS, side, samples)
    start = jnp.zeros((bins * side, samples), jnp.float32)
    for p in range(PATTERNS):
        if p >= EARLY:
            copies[p - EARLY].wait()
        rows = parts_ref[p, 0].reshape(bins * side, samples)
        start += dot_back(rows, kernel_of(kernels, p))
    start = start.astype(jnp.bfloat16)
    start_ref[...] = start
    field = start.astype(jnp.float32)
    nothing = jnp.zeros((side, samples), jnp.float32)
    project(start, kernels, rows_ref)
    for b in range(bins):
        store_parts(parts_ref, b, mixed(gram_ref, rows_ref, b))
    local = back_projected(kernels, parts_ref) + smoothed(field, nothing, nothing)
    local_ref[...] = local
    local = local.astype(jnp.bfloat16)
    odd = own_block(tiles) % 2 > 0
    for out_ref, to_after in ((first_swap_ref, ~odd), (second_swap_ref, odd)):
        out_ref[:side] = jnp.where(to_after, start[-side:], start[:side])
        out_ref[side:] = jnp.where(to_after, local[-side:], local[:side])


FULL, STEP, GROW = 4, 5, 6


def ahead_kernel(local_ref, gram_ref, lower_ref, upper_ref, rows_ref, mixed_ref):
    project(two_parts(local_ref[...]), (lower_ref, upper_ref), rows_ref)
    for b in range(rows_ref.shape[0]):
        mixed_ref[b] = mixed(gram_ref, rows_ref, b)


def second_kernel(
    tiles, offs, start_ref, local_ref, gram_ref, lower_ref, upper_ref, first_swap_ref,
    second_swap_ref, full_ref, ahead_ref, mixed_ref,
    once_ref, smooth_ref, both_ref, sums_ref, rows_ref,
):
    bins, _, side, samples = rows_ref.shape
    start = start_ref[...].astype(jnp.float32)
    place = lax.axis_index("off") * tiles + own_block(tiles)
    ends = [place > 0, place < offs * tiles - 1]
    odd = own_block(tiles) % 2 > 0
    first = first_swap_ref[...].astype(jnp.float32)
    second = second_swap_ref[...].astype(jnp.float32)
    edges = [jnp.where(odd, first, second), jnp.where(odd, second, first)]
    beyond, outer = [], []
    for end, (edge, own) in enumerate(zip(edges, (start[:side], start[-side:]))):
        there = jnp.where(ends[end], smooth_weight, 0.0)
        beyond.append(-smooth_weight * edge[:side])
        outer.append(edge[side:] - there * own)
    inner = [jnp.zeros(((bins - 2) * side, samples), jnp.float32)] if bins > 2 else []
    beyond = jnp.concatenate([beyond[0], *inner, beyond[1]], 0)
    once = local_ref[...] + beyond
    once_ref[...] = once
    smooth = smoothed(once, outer[0], outer[1])
    smooth_ref[...] = smooth
    project(beyond.astype(jnp.bfloat16), (lower_ref, upper_ref), rows_ref)
    square = 0.0
    for b in range(bins):
        both = mixed_ref[b] + mixed(gram_ref, rows_ref, b)
        both_ref[b] = both
        rows = ahead_ref[b].astype(jnp.float32) + rows_ref[b].astype(jnp.float32)
        square += total(rows.reshape(both.shape) * both)
    products = [
        total(start * start),
        total(start * once),
        total(once * once),
        total(once * smooth) + square,
    ]
    lane = lax.broadcasted_iota(jnp.int32, (1, LANES), 1)
    line = jnp.where(lane == FULL, full_ref[:1], 0.0)
    for i, product in enumerate(products):
        line = jnp.where(lane == i, product, line)
    sums_ref[...] = jnp.broadcast_to(line, sums_ref.shape)


def last_kernel(both_ref, lower_ref, upper_ref, out_ref):
    rows, samples = out_ref.shape
    bins = both_ref.shape[0]
    side = rows // bins
    out = jnp.zeros((2 * rows, samples), jnp.float32)
    for p in range(PATTERNS):
        z = both_ref[:, p * side : (p + 1) * side].reshape(rows, samples)
        out += dot_back(two_parts(z), kernel_of((lower_ref, upper_ref), p))
    out_ref[...] = out[:rows] + out[rows:]


def pack_kernel(sums_ref, start_ref, once_ref, smooth_ref, normal_ref, *refs):
    *out_refs, out_ref = refs
    tiles = len(out_refs)
    ss, so, oo = (sums_ref[:1, i : i + 1] for i in range(3))
    step, grow = own_scales(ss, so, oo)
    start, once = start_ref[...].astype(jnp.float32), once_ref[...]
    twice = normal_ref[...] + smooth_ref[...]
    row = 0
    for field in (start, start - step * once, grow * once - step * twice):
        samples = field.shape[1]
        field = field.reshape(-1, tiles, CELLS, samples)
        size = field.shape[0] * CELLS
        for i in range(0, samples, LANES):
            for tile in range(tiles):
                piece = field[:, tile, :, i : i + LANES].reshape(size, LANES)
                out_ref[tile, row : row + size] = piece.astype(jnp.bfloat16)
            row += size
    lane = lax.broadcasted_iota(jnp.int32, (1, LANES), 1)
    rest = jnp.where(lane == STEP, step, sums_ref[:1])
    rest = jnp.where(lane == GROW, grow, rest)
    line = lax.broadcasted_iota(jnp.int32, (16, LANES), 0)
    parts = jnp.zeros((16, LANES), jnp.float32)
    for i in range(3):
        part = rest.astype(jnp.bfloat16).astype(jnp.float32)
        rest = rest - part
        parts = jnp.where(line == i, part, parts)
    for tile in range(tiles):
        out_ref[tile, row:] = parts.astype(jnp.bfloat16)
    lay_out(out_ref, out_refs)


def total(x):
    return jnp.sum(jnp.sum(x, 0, keepdims=True), 1, keepdims=True)


def own_scales(ss, so, oo):
    step = ss / so
    step = jnp.where(step > 0.0, jnp.clip(step, 1e-8, 1e3), 1.0)
    grow = step * step * oo / ss
    return step, jnp.where(grow > 0.0, jnp.clip(grow, 0.0, 1e3), 1.0)


def place_kernel(bins, *refs):
    *landed_refs, solution_ref, residual_ref, landed_ref = refs
    gather_in(landed_refs, landed_ref)
    tiles, length, _ = landed_ref.shape
    size = bins * CELLS
    samples = solution_ref.shape[2]
    pieces = samples // LANES

    def line_of(source):
        parts = landed_ref[source, length - 16 :].astype(jnp.float32)
        return jnp.sum(parts, 0, keepdims=True)

    def vector(source, i):
        part = [
            landed_ref[source, (i * pieces + j) * size : (i * pieces + j + 1) * size]
            for j in range(pieces)
        ]
        return jnp.concatenate(part, 1).astype(jnp.float32)

    sums = sum(line_of(tile) for tile in range(tiles))
    ss, so, oo, ot = (sums[:, i : i + 1] for i in range(4))
    step_0 = ss / so
    norm_1 = step_0 * step_0 * oo - ss
    grow = 1.0 + norm_1 / ss
    step_1 = norm_1 / (grow * grow * so - 2.0 * step_0 * grow * oo + step_0 * step_0 * ot)
    near = step_0 + step_1 * grow
    far = step_1 * step_0
    fields = [[], []]
    for block in range(tiles):
        source = jnp.where(
            flipped(), path_rank(tiles - 1 - block, tiles), path_rank(block, tiles)
        )
        line = line_of(source)
        inverse = 1.0 / line[:, STEP : STEP + 1]
        there = line[:, GROW : GROW + 1]
        start, first, second = (vector(source, i) for i in range(3))
        far_once = far * inverse
        near_once = near * inverse - far_once * there * inverse
        solution = (near - far_once) * start + far_once * first
        residual = (1.0 - near_once) * start + near_once * first - far_once * second
        fields[0].append(solution.reshape(bins, CELLS, samples))
        fields[1].append(residual.reshape(bins, CELLS, samples))
    solution_ref[...] = jnp.swapaxes(jnp.concatenate(fields[0], 0), 0, 1)
    residual_ref[...] = jnp.swapaxes(jnp.concatenate(fields[1], 0), 0, 1)


def copy_kernel(*refs):
    *refs, arrived = refs
    half = len(refs) // 2
    copies = [
        pltpu.make_async_copy(refs[i], refs[half + i], arrived.at[i]) for i in range(half)
    ]
    for copy in copies:
        copy.start()
    for copy in copies:
        copy.wait()


VMEM = pl.BlockSpec(memory_space=pltpu.VMEM)
HBM = pl.BlockSpec(memory_space=pltpu.HBM)


def local_call(kernel, name, in_specs, out_shape, scratch=(), out_specs=None, cost=0):
    return pl.pallas_call(
        kernel,
        out_shape=out_shape,
        in_specs=in_specs,
        out_specs=out_specs or jax.tree.map(lambda _: VMEM, out_shape),
        scratch_shapes=list(scratch),
        cost_estimate=pl.CostEstimate(
            flops=cost, bytes_accessed=cost // 256, transcendentals=0
        )
        if cost
        else None,
        compiler_params=pltpu.CompilerParams(vmem_limit_bytes=32 * 1024 * 1024),
        name=name,
    )


def shards_by_bin(
    traces, kernels, send_list, aper_slot, aper_pattern, trace_bin, trace_count
):
    tiles, offs = lax.axis_size("mid"), lax.axis_size("off")
    bins = NOFF // offs // tiles
    trace_rows, samples = traces.shape
    send = send_list.shape[2]
    rows = bins * tiles * CELLS
    side = tiles * CELLS
    sums = bins * (CELLS + 2 * REACH * send)

    def array(*shape, dtype=jnp.float32):
        return jax.ShapeDtypeStruct(shape, dtype)

    bf16 = functools.partial(array, dtype=jnp.bfloat16)
    in_hbm = functools.partial(
        pltpu.with_memory_space_constraint, memory_space=pltpu.HBM
    )
    lists = (send_list, aper_slot, aper_pattern, trace_bin, trace_count)
    early = bf16(EARLY, samples, samples)
    shared, lower = local_call(
        functools.partial(share_kernel, tiles, bins, ROOM),
        "share",
        [HBM] * 7,
        (bf16(tiles, samples // LANES * ROOM + 2 * APER, LANES), early),
        [
            pltpu.SMEM(send_list.shape, jnp.int32),
            pltpu.VMEM(aper_slot.shape, jnp.int32),
            pltpu.VMEM(aper_pattern.shape, jnp.int32),
            pltpu.VMEM((1, trace_rows), jnp.int32),
            pltpu.VMEM((1, trace_rows), jnp.int32),
            pltpu.VMEM(traces.shape, jnp.bfloat16),
            pltpu.SemaphoreType.DMA((6,)),
            pltpu.SemaphoreType.DMA,
        ],
    )(
        in_hbm(send_list),
        in_hbm(aper_slot),
        in_hbm(aper_pattern),
        in_hbm(trace_bin[None]),
        in_hbm(trace_count[None]),
        in_hbm(traces),
        in_hbm(kernels),
    )
    landed = lax.all_to_all(shared, "mid", 0, 0)
    pattern_rows = pltpu.VMEM((bins, PATTERNS, side, samples), jnp.bfloat16)
    parts_type = bf16(PATTERNS, 2, bins, side, samples)
    start, local, gram, *swaps, full, upper = local_call(
        functools.partial(first_kernel, tiles, bins, send),
        "first",
        [VMEM, VMEM, HBM],
        (
            bf16(rows, samples),
            array(rows, samples),
            bf16(bins, tiles * KEYS, tiles * KEYS),
            bf16(2 * side, samples),
            bf16(2 * side, samples),
            array(8, LANES),
            bf16(PATTERNS - EARLY, samples, samples),
        ),
        [
            pltpu.VMEM((bins, PATTERNS, tiles, CELLS, tiles * ROOM), jnp.float32),
            pattern_rows,
            pltpu.VMEM(parts_type.shape, parts_type.dtype),
            pltpu.SemaphoreType.DMA((PATTERNS - EARLY,)),
        ],
    )(landed, lower, in_hbm(kernels))

    path = [path_rank(m, tiles) for m in range(tiles)]
    chain = [m * offs + o for o in range(offs) for m in (path[::-1] if o % 2 else path)]
    swaps = [
        lax.ppermute(
            x,
            ("mid", "off"),
            [
                pair
                for i, j in zip(chain[first:-1:2], chain[first + 1 :: 2])
                for pair in ((i, j), (j, i))
            ],
        )
        for first, x in enumerate(swaps)
    ]

    flops = 2 * rows * PATTERNS * samples * samples
    ahead, mixed_ahead = local_call(
        ahead_kernel,
        "ahead",
        [VMEM] * 4,
        (bf16(*pattern_rows.shape), array(bins, PATTERNS * side, samples)),
        cost=3 * flops,
    )(local, gram, lower, upper)
    field = array(rows, samples)
    once, smooth, parts, products = local_call(
        functools.partial(second_kernel, tiles, offs),
        "second",
        [VMEM] * 10,
        (field, field, array(bins, PATTERNS * side, samples), array(8, LANES)),
        [pattern_rows],
        cost=2 * flops,
    )(start, local, gram, lower, upper, *swaps, full, ahead, mixed_ahead)

    projected = local_call(last_kernel, "last", [VMEM] * 3, field, cost=2 * flops)(
        parts, lower, upper
    )
    addends = [products] + [
        lax.ppermute(products, "off", [(i, i ^ step) for i in range(offs)])
        for step in range(1, offs)
    ]
    while len(addends) > 1:
        addends = [a + b for a, b in zip(addends[::2], addends[1::2])]
    products = addends[0]
    chunk = bf16(samples // LANES * 3 * bins * CELLS + 16, LANES)
    chunks = pltpu.VMEM((tiles, *chunk.shape), chunk.dtype)
    packed = local_call(
        pack_kernel, "pack", [VMEM] * 5, [chunk] * tiles, [chunks]
    )(products, start, once, smooth, projected)
    landed = swapped(packed)

    def again():
        arguments = [in_hbm(x) for x in (traces, kernels, *lists[:3])]
        arguments += [in_hbm(x[None]) for x in lists[3:]]
        *copies, bins_again, count_again = local_call(
            copy_kernel,
            "again",
            [HBM] * len(arguments),
            tuple(array(*x.shape, dtype=x.dtype) for x in arguments),
            [pltpu.SemaphoreType.DMA((len(arguments),))],
            out_specs=(HBM,) * len(arguments),
        )(*arguments)
        return *copies, bins_again[0], count_again[0]

    def placed():
        out_type = pltpu.HBM((CELLS, bins * tiles, samples), jnp.float32)
        return local_call(
            functools.partial(place_kernel, bins),
            "place",
            [VMEM] * tiles,
            (out_type, out_type),
            [chunks],
            out_specs=(VMEM, VMEM),
        )(*landed)

    return lax.cond(
        products[0, FULL] > 0.0, lambda: shards_by_tile(*again()), placed
    )


def fits_by_bin(tiles, offs, send, trace_rows, samples):
    return (
        (NOFF // offs) % (2 * tiles) == 0
        and offs & (offs - 1) == 0
        and tiles & (tiles - 1) == 0
        and tiles % TOGETHER == 0
        and send == WITHIN
        and trace_rows == LANES
        and samples % LANES == 0
    )


def solution(mesh):
    in_specs = (
        P(("mid", "off"), None),
        P(),
        P("mid", None, None),
        P(None, ("mid", "off")),
        P(None, ("mid", "off")),
        P(("mid", "off")),
        P(("mid", "off")),
    )
    out_specs = (P("mid", "off", None), P("mid", "off", None))

    def shards(traces, kernels, send_list, *lists):
        fits = fits_by_bin(
            mesh.shape["mid"], mesh.shape["off"], send_list.shape[2], *traces.shape
        )
        form = shards_by_bin if fits else shards_by_tile
        return form(traces, kernels, send_list, *lists)

    return jax.shard_map(
        shards, mesh=mesh, in_specs=in_specs, out_specs=out_specs, check_vma=False
    )
```

```python
import functools

import jax
import jax.numpy as jnp
from jax import lax
from jax.experimental import pallas as pl
from jax.experimental.pallas import tpu as pltpu
from jax.sharding import PartitionSpec as P

NOFF = 64
PATTERNS = 8
REACH = 2
APER = 8
ITERS = 2
CELLS = 8
KEYS = PATTERNS * CELLS
EARLY = 3
ROOM = 32
LANES = 128
TOGETHER = LANES // ROOM


smooth_weight = 2.0


def padded_2(x, sides, width):
    for axis, dim in sides:
        peers, length = (lax.axis_size(axis), x.shape[dim])
        up = [(i, (i + 1) % peers) for i in range(peers - 1)]
        down = [(j, i) for i, j in up]
        last = lax.slice_in_dim(x, length - width, length, axis=dim)
        first = lax.slice_in_dim(x, 0, width, axis=dim)
        before = lax.ppermute(last, axis, up)
        after = lax.ppermute(first, axis, down)
        x = jnp.concatenate([before, x, after], axis=dim)
    return x


def from_behind(x, axis, by):
    peers = lax.axis_size(axis)
    pairs = [(i, i + by) for i in range(peers) if 0 <= i + by < peers]
    return lax.ppermute(x, axis, pairs)


def direction_shift(course):
    return (course // 2 + 1) * (1 - 2 * (course % 2))


def offset_laplace(padded):
    return smooth_weight * (2.0 * padded[:, 1:-1] - padded[:, :-2] - padded[:, 2:])


def smoothing(field):
    padded = padded_2(field, (("off", 1),), 1)
    smoothed = offset_laplace(padded)
    return smoothed


def deliver(outgoing):
    arrived = [None] * (2 * REACH)
    for course in range(2 * REACH):
        arrived[course] = from_behind(outgoing[course], "mid", direction_shift(course))
    return arrived


def give_back(returning):
    landed = [None] * (2 * REACH)
    for course in range(2 * REACH):
        landed[course] = from_behind(returning[course], "mid", -direction_shift(course))
    return landed


def shards_by_tile(
    traces, kernels, send_list, aper_slot, aper_pattern, trace_bin, trace_count
):
    off_dev = NOFF // lax.axis_size("off")
    trace_rows = traces.shape[0]
    samples = traces.shape[1]
    chosen_cells = send_list[0]
    send_count = chosen_cells.shape[1]
    slot_count = CELLS + 2 * REACH * send_count
    live_mask = jnp.arange(APER, dtype=jnp.int32)[:, None] < trace_count[None, :]
    row_index = (aper_slot * off_dev + trace_bin[None, :]).reshape(-1)
    pattern_ids = jnp.arange(PATTERNS, dtype=jnp.int32)[:, None, None]
    chooser = ((aper_pattern[None] == pattern_ids) & live_mask[None]).astype(
        jnp.bfloat16
    )
    pick_rows = (
        aper_pattern * trace_rows + jnp.arange(trace_rows, dtype=jnp.int32)[None, :]
    ).reshape(-1)
    live_column = live_mask.reshape(-1, 1).astype(jnp.float32)

    def forward(field_bf):
        outgoing = [field_bf[chosen_cells[course]] for course in range(2 * REACH)]
        arrived = deliver(outgoing)
        slot_rows = jnp.concatenate([field_bf] + arrived, 0).reshape(-1, samples)
        blocks = slot_rows[row_index].reshape(APER, trace_rows, samples)
        pattern_sums = jnp.einsum(
            "pjt,jtn->ptn", chooser, blocks, preferred_element_type=jnp.float32
        ).astype(jnp.bfloat16)
        return jnp.einsum(
            "ptn,pnm->tm", pattern_sums, kernels, preferred_element_type=jnp.float32
        )

    def adjoint(values_bf):
        spread = jnp.einsum(
            "tm,pnm->ptn", values_bf, kernels, preferred_element_type=jnp.float32
        ).reshape(-1, samples)
        entries = spread[pick_rows] * live_column
        slot_sums = (
            jnp.zeros((slot_count * off_dev, samples), jnp.float32)
            .at[row_index]
            .add(entries)
        )
        slot_sums = slot_sums.reshape(slot_count, off_dev, samples)
        returning = [
            slot_sums[CELLS + course * send_count : CELLS + (course + 1) * send_count]
            for course in range(2 * REACH)
        ]
        landed = give_back(returning)
        accumulated = slot_sums[:CELLS]
        for course in range(2 * REACH):
            accumulated = accumulated.at[chosen_cells[course]].add(landed[course])
        return accumulated

    def global_total(value):
        return lax.psum(value, ("mid", "off"))

    residual = adjoint(traces)
    direction = residual
    solution = jnp.zeros_like(residual)
    norm_now = global_total(jnp.sum(residual * residual))
    for iteration in range(ITERS):
        applied = adjoint(
            forward(direction.astype(jnp.bfloat16)).astype(jnp.bfloat16)
        ) + smoothing(direction)
        step_size = norm_now / global_total(jnp.sum(direction * applied))
        solution = solution + step_size * direction
        residual = residual - step_size * applied
        if iteration + 1 < ITERS:
            norm_next = global_total(jnp.sum(residual * residual))
            direction = residual + norm_next / norm_now * direction
            norm_now = norm_next
    return (solution, residual)


def path_rank(m, tiles):
    return m ^ ((m >> 1) & 1) if tiles % 4 == 0 else m


def turns(peers):
    near, far = range(1, peers // 2), range(peers // 2, peers)
    even = [i for pair in zip(far, near) for i in pair]
    odd = [i for pair in zip(near, far) for i in pair]
    return [(0, 0), *zip(even, odd), (peers - 1, peers - 1)]


def partners(peers):
    odd, place = flipped(), lax.axis_index("mid")
    return [place ^ jnp.where(odd, j, i) for i, j in turns(peers)]


def lay_out(chunks_ref, out_refs):
    for partner, out_ref in zip(partners(len(out_refs)), out_refs):
        out_ref[...] = chunks_ref[partner]


def gather_in(landed_refs, chunks_ref):
    for partner, landed_ref in zip(partners(len(landed_refs)), landed_refs):
        chunks_ref[partner] = landed_ref[...]


def swapped(chunks):
    peers, offs = len(chunks), lax.axis_size("off")
    return list(chunks[:1]) + [
        lax.ppermute(
            chunk,
            ("mid", "off"),
            [
                (m * offs + o, (m ^ turn[o % 2]) * offs + o)
                for m in range(peers)
                for o in range(offs)
            ],
        )
        for turn, chunk in zip(turns(peers)[1:], chunks[1:])
    ]


def flipped():
    return lax.axis_index("off") % 2 > 0


def own_block(tiles):
    block = path_rank(lax.axis_index("mid"), tiles)
    return jnp.where(flipped(), tiles - 1 - block, block)


def dot_back(rows, kernel):
    return lax.dot_general(
        rows, kernel, (((1,), (1,)), ((), ())), preferred_element_type=jnp.float32
    )


SLOT, PATTERN, WITHIN, COUNT, FLAG = 0, APER, 4, 5, 6


def share_kernel(
    tiles, bins, room, sends_arg, slot_arg, pattern_arg, bin_arg, count_arg, traces_arg,
    kernels_arg, out_ref, kernels_ref, sends_ref, slot_ref, pattern_ref, bin_ref, count_ref, traces_ref,
    staged, arrived,
):
    rows, samples = traces_ref.shape
    stages = [
        pltpu.make_async_copy(arg, ref, staged.at[i])
        for i, (arg, ref) in enumerate(
            [
                (bin_arg, bin_ref),
                (slot_arg, slot_ref),
                (pattern_arg, pattern_ref),
                (count_arg, count_ref),
                (sends_arg, sends_ref),
                (traces_arg, traces_ref),
            ]
        )
    ]
    half = samples // 2
    kernels = [
        pltpu.make_async_copy(
            kernels_arg.at[p, pl.ds(i * half, half)],
            kernels_ref.at[p, pl.ds(i * half, half)],
            arrived.at[2 * p + i],
        )
        for p in range(EARLY)
        for i in range(2)
    ]
    for stage in stages + kernels:
        stage.start()
    index = lax.broadcasted_iota(jnp.int32, (tiles, rows), 0)
    earlier = lax.broadcasted_iota(jnp.int32, (rows, rows), 0) < (
        lax.broadcasted_iota(jnp.int32, (rows, rows), 1)
    )
    earlier = jnp.where(earlier, 1.0, 0.0).astype(jnp.bfloat16)
    stages[0].wait()
    offset_bin = bin_ref[...]
    block = lax.div(offset_bin, bins)
    within = offset_bin - block * bins
    chunk = path_rank(jnp.where(flipped(), tiles - 1 - block, block), tiles)
    belongs = jnp.where(index == chunk, 1.0, 0.0)
    rank = jnp.dot(
        belongs.astype(jnp.bfloat16), earlier, preferred_element_type=jnp.float32
    )
    rank = jnp.sum(rank * belongs, 0, keepdims=True).astype(jnp.int32)
    full = jnp.max(rank, axis=1, keepdims=True) >= room
    target = jnp.where(rank < room, chunk * room + rank, -1)
    picks = lax.broadcasted_iota(jnp.int32, (tiles * room, rows), 0) == target
    picks = jnp.where(picks, 1.0, 0.0).astype(jnp.bfloat16)
    place = lax.axis_index("mid")
    lane = lax.broadcasted_iota(jnp.int32, (1, LANES), 1)
    for stage in stages[1:5]:
        stage.wait()
    lists = jnp.concatenate(
        [
            slot_ref[...].astype(jnp.float32),
            pattern_ref[...].astype(jnp.float32),
            jnp.zeros((WITHIN, rows), jnp.float32),
            within.astype(jnp.float32),
            count_ref[...].astype(jnp.float32),
            jnp.zeros((APER - COUNT - 1, rows), jnp.float32),
        ],
        0,
    ).astype(jnp.bfloat16)
    lists = dot_back(lists, picks)
    own_lanes = lax.rem(place, TOGETHER)
    member = lax.div(lane, room)
    _, courses, send = sends_ref.shape
    line = lax.broadcasted_iota(jnp.int32, (2 * APER, LANES), 0)
    sent = jnp.zeros((2 * APER, LANES), jnp.int32)
    for course in range(courses):
        reader = lax.rem(place + direction_shift(course) + TOGETHER, TOGETHER)
        here = lax.div(lane, room) == reader
        for m in range(send):
            value = jnp.where(here, sends_ref[0, course, m], 0)
            sent += jnp.where(line == sent_row(course, send) + m, value, 0)
    past = lax.div(lane, room) == lax.rem(place + 1, TOGETHER)
    sent += jnp.where(past & (line == FLAG) & full, 1, 0)
    sent = sent.astype(jnp.float32)
    pieces = samples // LANES
    for m in range(tiles):
        own = lists[:, m // TOGETHER * LANES : (m // TOGETHER + 1) * LANES]
        shift = lax.rem((own_lanes - m % TOGETHER + TOGETHER) * room, LANES)
        own = jnp.where(member == own_lanes, pltpu.roll(own, shift, 1), 0.0)
        moved = pltpu.roll(own[2 * APER :], room, 1)
        out_ref[m, pieces * room :] = (
            own[: 2 * APER] + jnp.concatenate([moved, jnp.zeros_like(moved)], 0) + sent
        ).astype(jnp.bfloat16)
    stages[5].wait()
    picked = jnp.dot(picks, traces_ref[...], preferred_element_type=jnp.float32)
    picked = picked.reshape(tiles, room, samples).astype(jnp.bfloat16)
    for i in range(pieces):
        out_ref[:, i * room : (i + 1) * room] = picked[:, :, i * LANES : (i + 1) * LANES]
    for copy in kernels:
        copy.wait()


def sent_row(course, send):
    return send if course == 3 else 0


def fill_picks(tiles, bins, send, landed_ref, picks_ref):
    flags = 0
    keys = lax.broadcasted_iota(jnp.int32, (KEYS, LANES), 0)
    member = lax.div(lax.broadcasted_iota(jnp.int32, (1, LANES), 1), ROOM)
    blocks = [
        landed_ref[tile, -2 * APER :].astype(jnp.float32).astype(jnp.int32)
        for tile in range(tiles)
    ]
    for group in range(tiles // TOGETHER):
        readers = range(group * TOGETHER, (group + 1) * TOGETHER)
        lists, moved = 0, 0
        for tile in readers:
            lists += jnp.where(member == tile % TOGETHER, blocks[tile], 0)
            past = member == (tile + 1) % TOGETHER
            moved += jnp.where(past, blocks[tile][:APER], 0)
        moved = pltpu.roll(moved, LANES - ROOM, 1)
        flags += moved[FLAG : FLAG + 1]
        within, count = moved[WITHIN : WITHIN + 1], moved[COUNT : COUNT + 1]
        wanted = []
        for region in range(2 * REACH + 1):
            course = region - 1
            shift = direction_shift(course) if region else 0
            owners = [tile - shift for tile in readers if 0 <= tile - shift < tiles]
            sent = 0
            for owner in owners if region else ():
                row = sent_row(course, send)
                values = blocks[owner][row : row + send]
                sent += jnp.where(member == (owner + shift) % TOGETHER, values, 0)
            for entry in range(region, APER, 2 * REACH + 1):
                cell = lists[SLOT + entry : SLOT + entry + 1]
                if region:
                    place = cell - (CELLS + course * send)
                    cell = sent[:1]
                    for other in range(1, send):
                        cell = jnp.where(place == other, sent[other : other + 1], cell)
                pattern = lists[PATTERN + entry : PATTERN + entry + 1]
                key = jnp.where(count > entry, pattern * CELLS + cell, -1)
                for owner in owners:
                    there = member == (owner + shift) % TOGETHER
                    wanted.append((owner, jnp.where(there, key, -1)))
        for tile in range(tiles):
            for b in range(bins):
                total = jnp.zeros((KEYS, LANES), jnp.float32)
                for owner, key in wanted:
                    if owner == tile:
                        hit = keys == jnp.where(within == b, key, -1)
                        total += jnp.where(hit, 1.0, 0.0)
                picks_ref[b, :, tile, :, group * LANES : (group + 1) * LANES] = (
                    total.reshape(PATTERNS, CELLS, LANES)
                )
    return flags.astype(jnp.float32)


def two_parts(x):
    high = x.astype(jnp.bfloat16)
    low = (x - high.astype(jnp.float32)).astype(jnp.bfloat16)
    return jnp.concatenate([high, low], 0)


def store_parts(parts_ref, b, x):
    shape = (PATTERNS, *parts_ref.shape[3:])
    high = x.astype(jnp.bfloat16)
    parts_ref[:, 0, b] = high.reshape(shape)
    low = (x - high.astype(jnp.float32)).astype(jnp.bfloat16)
    parts_ref[:, 1, b] = low.reshape(shape)


def kernel_of(kernels, p):
    lower_ref, upper_ref = kernels
    return lower_ref[p] if p < EARLY else upper_ref[p - EARLY]


def back_projected(kernels, parts_ref):
    _, _, bins, side, samples = parts_ref.shape
    rows = bins * side
    both = jnp.zeros((2 * rows, samples), jnp.float32)
    for p in range(PATTERNS):
        both += dot_back(
            parts_ref[p].reshape(2 * rows, samples), kernel_of(kernels, p)
        )
    return both[:rows] + both[rows:]


def project(field, kernels, rows_ref):
    bins, _, side, samples = rows_ref.shape
    rows = bins * side
    for p in range(PATTERNS):
        u = jnp.dot(field, kernel_of(kernels, p), preferred_element_type=jnp.float32)
        u = u[:rows] + u[rows:] if field.shape[0] > rows else u
        rows_ref[:, p] = u.astype(jnp.bfloat16).reshape(bins, side, samples)


def mixed(gram_ref, rows_ref, b):
    _, _, side, samples = rows_ref.shape
    return jnp.dot(
        gram_ref[b],
        rows_ref[b].reshape(PATTERNS * side, samples),
        preferred_element_type=jnp.float32,
    )


def smoothed(field, before, after):
    side = before.shape[0]
    lower = jnp.concatenate([before, field[:-side]], 0)
    upper = jnp.concatenate([field[side:], after], 0)
    return smooth_weight * (2.0 * field - lower - upper)


def first_kernel(
    tiles, bins, send, landed_ref, lower_ref, kernels_arg,
    start_ref, local_ref, gram_ref, first_swap_ref, second_swap_ref, full_ref, upper_ref,
    picks_ref, rows_ref, parts_ref, arrived,
):
    copies = [
        pltpu.make_async_copy(kernels_arg.at[EARLY + p], upper_ref.at[p], arrived.at[p])
        for p in range(PATTERNS - EARLY)
    ]
    for copy in copies:
        copy.start()
    kernels = (lower_ref, upper_ref)
    side = tiles * CELLS
    samples = start_ref.shape[1]
    flags = total(fill_picks(tiles, bins, send, landed_ref, picks_ref))
    full_ref[...] = jnp.broadcast_to(flags, full_ref.shape)
    traces = jnp.concatenate(
        [
            landed_ref[:, i * ROOM : (i + 1) * ROOM].reshape(-1, LANES)
            for i in range(samples // LANES)
        ],
        1,
    )
    for b in range(bins):
        picks = picks_ref[b].reshape(PATTERNS * side, -1).astype(jnp.bfloat16)
        gram_ref[b] = dot_back(picks, picks).astype(jnp.bfloat16)
        sums = jnp.dot(picks, traces, preferred_element_type=jnp.float32)
        parts_ref[:, 0, b] = sums.astype(jnp.bfloat16).reshape(PATTERNS, side, samples)
    start = jnp.zeros((bins * side, samples), jnp.float32)
    for p in range(PATTERNS):
        if p >= EARLY:
            copies[p - EARLY].wait()
        rows = parts_ref[p, 0].reshape(bins * side, samples)
        start += dot_back(rows, kernel_of(kernels, p))
    start = start.astype(jnp.bfloat16)
    start_ref[...] = start
    field = start.astype(jnp.float32)
    nothing = jnp.zeros((side, samples), jnp.float32)
    project(start, kernels, rows_ref)
    for b in range(bins):
        store_parts(parts_ref, b, mixed(gram_ref, rows_ref, b))
    local = back_projected(kernels, parts_ref) + smoothed(field, nothing, nothing)
    local_ref[...] = local
    local = local.astype(jnp.bfloat16)
    odd = own_block(tiles) % 2 > 0
    for out_ref, to_after in ((first_swap_ref, ~odd), (second_swap_ref, odd)):
        out_ref[:side] = jnp.where(to_after, start[-side:], start[:side])
        out_ref[side:] = jnp.where(to_after, local[-side:], local[:side])


FULL, STEP, GROW = 4, 5, 6


def ahead_kernel(local_ref, gram_ref, lower_ref, upper_ref, rows_ref, mixed_ref):
    project(two_parts(local_ref[...]), (lower_ref, upper_ref), rows_ref)
    for b in range(rows_ref.shape[0]):
        mixed_ref[b] = mixed(gram_ref, rows_ref, b)


def second_kernel(
    tiles, offs, start_ref, local_ref, gram_ref, lower_ref, upper_ref, first_swap_ref,
    second_swap_ref, full_ref, ahead_ref, mixed_ref,
    once_ref, smooth_ref, both_ref, sums_ref, rows_ref,
):
    bins, _, side, samples = rows_ref.shape
    start = start_ref[...].astype(jnp.float32)
    place = lax.axis_index("off") * tiles + own_block(tiles)
    ends = [place > 0, place < offs * tiles - 1]
    odd = own_block(tiles) % 2 > 0
    first = first_swap_ref[...].astype(jnp.float32)
    second = second_swap_ref[...].astype(jnp.float32)
    edges = [jnp.where(odd, first, second), jnp.where(odd, second, first)]
    beyond, outer = [], []
    for end, (edge, own) in enumerate(zip(edges, (start[:side], start[-side:]))):
        there = jnp.where(ends[end], smooth_weight, 0.0)
        beyond.append(-smooth_weight * edge[:side])
        outer.append(edge[side:] - there * own)
    inner = [jnp.zeros(((bins - 2) * side, samples), jnp.float32)] if bins > 2 else []
    beyond = jnp.concatenate([beyond[0], *inner, beyond[1]], 0)
    once = local_ref[...] + beyond
    once_ref[...] = once
    smooth = smoothed(once, outer[0], outer[1])
    smooth_ref[...] = smooth
    project(beyond.astype(jnp.bfloat16), (lower_ref, upper_ref), rows_ref)
    square = 0.0
    for b in range(bins):
        both = mixed_ref[b] + mixed(gram_ref, rows_ref, b)
        both_ref[b] = both
        rows = ahead_ref[b].astype(jnp.float32) + rows_ref[b].astype(jnp.float32)
        square += total(rows.reshape(both.shape) * both)
    products = [
        total(start * start),
        total(start * once),
        total(once * once),
        total(once * smooth) + square,
    ]
    lane = lax.broadcasted_iota(jnp.int32, (1, LANES), 1)
    line = jnp.where(lane == FULL, full_ref[:1], 0.0)
    for i, product in enumerate(products):
        line = jnp.where(lane == i, product, line)
    sums_ref[...] = jnp.broadcast_to(line, sums_ref.shape)


def last_kernel(both_ref, lower_ref, upper_ref, out_ref):
    rows, samples = out_ref.shape
    bins = both_ref.shape[0]
    side = rows // bins
    out = jnp.zeros((2 * rows, samples), jnp.float32)
    for p in range(PATTERNS):
        z = both_ref[:, p * side : (p + 1) * side].reshape(rows, samples)
        out += dot_back(two_parts(z), kernel_of((lower_ref, upper_ref), p))
    out_ref[...] = out[:rows] + out[rows:]


def pack_kernel(sums_ref, start_ref, once_ref, smooth_ref, normal_ref, *refs):
    *out_refs, out_ref = refs
    tiles = len(out_refs)
    ss, so, oo = (sums_ref[:1, i : i + 1] for i in range(3))
    step, grow = own_scales(ss, so, oo)
    start, once = start_ref[...].astype(jnp.float32), once_ref[...]
    twice = normal_ref[...] + smooth_ref[...]
    row = 0
    for field in (start, start - step * once, grow * once - step * twice):
        samples = field.shape[1]
        field = field.reshape(-1, tiles, CELLS, samples)
        size = field.shape[0] * CELLS
        for i in range(0, samples, LANES):
            for tile in range(tiles):
                piece = field[:, tile, :, i : i + LANES].reshape(size, LANES)
                out_ref[tile, row : row + size] = piece.astype(jnp.bfloat16)
            row += size
    lane = lax.broadcasted_iota(jnp.int32, (1, LANES), 1)
    rest = jnp.where(lane == STEP, step, sums_ref[:1])
    rest = jnp.where(lane == GROW, grow, rest)
    line = lax.broadcasted_iota(jnp.int32, (16, LANES), 0)
    parts = jnp.zeros((16, LANES), jnp.float32)
    for i in range(3):
        part = rest.astype(jnp.bfloat16).astype(jnp.float32)
        rest = rest - part
        parts = jnp.where(line == i, part, parts)
    for tile in range(tiles):
        out_ref[tile, row:] = parts.astype(jnp.bfloat16)
    lay_out(out_ref, out_refs)


def total(x):
    return jnp.sum(jnp.sum(x, 0, keepdims=True), 1, keepdims=True)


def own_scales(ss, so, oo):
    step = ss / so
    step = jnp.where(step > 0.0, jnp.clip(step, 1e-8, 1e3), 1.0)
    grow = step * step * oo / ss
    return step, jnp.where(grow > 0.0, jnp.clip(grow, 0.0, 1e3), 1.0)


def place_kernel(bins, *refs):
    *landed_refs, solution_ref, residual_ref, landed_ref = refs
    gather_in(landed_refs, landed_ref)
    tiles, length, _ = landed_ref.shape
    size = bins * CELLS
    samples = solution_ref.shape[2]
    pieces = samples // LANES

    def line_of(source):
        parts = landed_ref[source, length - 16 :].astype(jnp.float32)
        return jnp.sum(parts, 0, keepdims=True)

    def vector(source, i):
        part = [
            landed_ref[source, (i * pieces + j) * size : (i * pieces + j + 1) * size]
            for j in range(pieces)
        ]
        return jnp.concatenate(part, 1).astype(jnp.float32)

    sums = sum(line_of(tile) for tile in range(tiles))
    ss, so, oo, ot = (sums[:, i : i + 1] for i in range(4))
    step_0 = ss / so
    norm_1 = step_0 * step_0 * oo - ss
    grow = 1.0 + norm_1 / ss
    step_1 = norm_1 / (grow * grow * so - 2.0 * step_0 * grow * oo + step_0 * step_0 * ot)
    near = step_0 + step_1 * grow
    far = step_1 * step_0
    fields = [[], []]
    for block in range(tiles):
        source = jnp.where(
            flipped(), path_rank(tiles - 1 - block, tiles), path_rank(block, tiles)
        )
        line = line_of(source)
        inverse = 1.0 / line[:, STEP : STEP + 1]
        there = line[:, GROW : GROW + 1]
        start, first, second = (vector(source, i) for i in range(3))
        far_once = far * inverse
        near_once = near * inverse - far_once * there * inverse
        solution = (near - far_once) * start + far_once * first
        residual = (1.0 - near_once) * start + near_once * first - far_once * second
        fields[0].append(solution.reshape(bins, CELLS, samples))
        fields[1].append(residual.reshape(bins, CELLS, samples))
    solution_ref[...] = jnp.swapaxes(jnp.concatenate(fields[0], 0), 0, 1)
    residual_ref[...] = jnp.swapaxes(jnp.concatenate(fields[1], 0), 0, 1)


def copy_kernel(*refs):
    *refs, arrived = refs
    half = len(refs) // 2
    copies = [
        pltpu.make_async_copy(refs[i], refs[half + i], arrived.at[i]) for i in range(half)
    ]
    for copy in copies:
        copy.start()
    for copy in copies:
        copy.wait()


VMEM = pl.BlockSpec(memory_space=pltpu.VMEM)
HBM = pl.BlockSpec(memory_space=pltpu.HBM)


def local_call(kernel, name, in_specs, out_shape, scratch=(), out_specs=None, cost=0):
    return pl.pallas_call(
        kernel,
        out_shape=out_shape,
        in_specs=in_specs,
        out_specs=out_specs or jax.tree.map(lambda _: VMEM, out_shape),
        scratch_shapes=list(scratch),
        cost_estimate=pl.CostEstimate(
            flops=cost, bytes_accessed=cost // 256, transcendentals=0
        )
        if cost
        else None,
        compiler_params=pltpu.CompilerParams(vmem_limit_bytes=32 * 1024 * 1024),
        name=name,
    )


def shards_by_bin(
    traces, kernels, send_list, aper_slot, aper_pattern, trace_bin, trace_count
):
    tiles, offs = lax.axis_size("mid"), lax.axis_size("off")
    bins = NOFF // offs // tiles
    trace_rows, samples = traces.shape
    send = send_list.shape[2]
    rows = bins * tiles * CELLS
    side = tiles * CELLS
    sums = bins * (CELLS + 2 * REACH * send)

    def array(*shape, dtype=jnp.float32):
        return jax.ShapeDtypeStruct(shape, dtype)

    bf16 = functools.partial(array, dtype=jnp.bfloat16)
    in_hbm = functools.partial(
        pltpu.with_memory_space_constraint, memory_space=pltpu.HBM
    )
    lists = (send_list, aper_slot, aper_pattern, trace_bin, trace_count)
    early = bf16(EARLY, samples, samples)
    shared, lower = local_call(
        functools.partial(share_kernel, tiles, bins, ROOM),
        "share",
        [HBM] * 7,
        (bf16(tiles, samples // LANES * ROOM + 2 * APER, LANES), early),
        [
            pltpu.SMEM(send_list.shape, jnp.int32),
            pltpu.VMEM(aper_slot.shape, jnp.int32),
            pltpu.VMEM(aper_pattern.shape, jnp.int32),
            pltpu.VMEM((1, trace_rows), jnp.int32),
            pltpu.VMEM((1, trace_rows), jnp.int32),
            pltpu.VMEM(traces.shape, jnp.bfloat16),
            pltpu.SemaphoreType.DMA((6,)),
            pltpu.SemaphoreType.DMA((2 * EARLY,)),
        ],
    )(
        in_hbm(send_list),
        in_hbm(aper_slot),
        in_hbm(aper_pattern),
        in_hbm(trace_bin[None]),
        in_hbm(trace_count[None]),
        in_hbm(traces),
        in_hbm(kernels),
    )
    landed = lax.all_to_all(shared, "mid", 0, 0)
    pattern_rows = pltpu.VMEM((bins, PATTERNS, side, samples), jnp.bfloat16)
    parts_type = bf16(PATTERNS, 2, bins, side, samples)
    start, local, gram, *swaps, full, upper = local_call(
        functools.partial(first_kernel, tiles, bins, send),
        "first",
        [VMEM, VMEM, HBM],
        (
            bf16(rows, samples),
            array(rows, samples),
            bf16(bins, tiles * KEYS, tiles * KEYS),
            bf16(2 * side, samples),
            bf16(2 * side, samples),
            array(8, LANES),
            bf16(PATTERNS - EARLY, samples, samples),
        ),
        [
            pltpu.VMEM((bins, PATTERNS, tiles, CELLS, tiles * ROOM), jnp.float32),
            pattern_rows,
            pltpu.VMEM(parts_type.shape, parts_type.dtype),
            pltpu.SemaphoreType.DMA((PATTERNS - EARLY,)),
        ],
    )(landed, lower, in_hbm(kernels))

    path = [path_rank(m, tiles) for m in range(tiles)]
    chain = [m * offs + o for o in range(offs) for m in (path[::-1] if o % 2 else path)]
    swaps = [
        lax.ppermute(
            x,
            ("mid", "off"),
            [
                pair
                for i, j in zip(chain[first:-1:2], chain[first + 1 :: 2])
                for pair in ((i, j), (j, i))
            ],
        )
        for first, x in enumerate(swaps)
    ]

    flops = 2 * rows * PATTERNS * samples * samples
    ahead, mixed_ahead = local_call(
        ahead_kernel,
        "ahead",
        [VMEM] * 4,
        (bf16(*pattern_rows.shape), array(bins, PATTERNS * side, samples)),
        cost=3 * flops,
    )(local, gram, lower, upper)
    field = array(rows, samples)
    once, smooth, parts, products = local_call(
        functools.partial(second_kernel, tiles, offs),
        "second",
        [VMEM] * 10,
        (field, field, array(bins, PATTERNS * side, samples), array(8, LANES)),
        [pattern_rows],
        cost=2 * flops,
    )(start, local, gram, lower, upper, *swaps, full, ahead, mixed_ahead)

    projected = local_call(last_kernel, "last", [VMEM] * 3, field, cost=2 * flops)(
        parts, lower, upper
    )
    addends = [products] + [
        lax.ppermute(products, "off", [(i, i ^ step) for i in range(offs)])
        for step in range(1, offs)
    ]
    while len(addends) > 1:
        addends = [a + b for a, b in zip(addends[::2], addends[1::2])]
    products = addends[0]
    chunk = bf16(samples // LANES * 3 * bins * CELLS + 16, LANES)
    chunks = pltpu.VMEM((tiles, *chunk.shape), chunk.dtype)
    packed = local_call(
        pack_kernel, "pack", [VMEM] * 5, [chunk] * tiles, [chunks]
    )(products, start, once, smooth, projected)
    landed = swapped(packed)

    def again():
        arguments = [in_hbm(x) for x in (traces, kernels, *lists[:3])]
        arguments += [in_hbm(x[None]) for x in lists[3:]]
        *copies, bins_again, count_again = local_call(
            copy_kernel,
            "again",
            [HBM] * len(arguments),
            tuple(array(*x.shape, dtype=x.dtype) for x in arguments),
            [pltpu.SemaphoreType.DMA((len(arguments),))],
            out_specs=(HBM,) * len(arguments),
        )(*arguments)
        return *copies, bins_again[0], count_again[0]

    def placed():
        out_type = pltpu.HBM((CELLS, bins * tiles, samples), jnp.float32)
        return local_call(
            functools.partial(place_kernel, bins),
            "place",
            [VMEM] * tiles,
            (out_type, out_type),
            [chunks],
            out_specs=(VMEM, VMEM),
        )(*landed)

    return lax.cond(
        products[0, FULL] > 0.0, lambda: shards_by_tile(*again()), placed
    )


def fits_by_bin(tiles, offs, send, trace_rows, samples):
    return (
        (NOFF // offs) % (2 * tiles) == 0
        and offs & (offs - 1) == 0
        and tiles & (tiles - 1) == 0
        and tiles % TOGETHER == 0
        and send == WITHIN
        and trace_rows == LANES
        and samples % LANES == 0
    )


def solution(mesh):
    in_specs = (
        P(("mid", "off"), None),
        P(),
        P("mid", None, None),
        P(None, ("mid", "off")),
        P(None, ("mid", "off")),
        P(("mid", "off")),
        P(("mid", "off")),
    )
    out_specs = (P("mid", "off", None), P("mid", "off", None))

    def shards(traces, kernels, send_list, *lists):
        fits = fits_by_bin(
            mesh.shape["mid"], mesh.shape["off"], send_list.shape[2], *traces.shape
        )
        form = shards_by_bin if fits else shards_by_tile
        return form(traces, kernels, send_list, *lists)

    return jax.shard_map(
        shards, mesh=mesh, in_specs=in_specs, out_specs=out_specs, check_vma=False
    )
```
